32 devices in a mesh: seq: 16 (over z, y, x), head: 2 (over core).
Axes of the slice: x: 2, y: 2, z: 4, core: 2. Of those that a mesh axis runs over, the one named last changes fastest.
Arguments:
- layer_input: float32 [4096, 2048], P('seq'), may hold values from -6 to 6
- doc_start: int32 [4096], P('seq'), may hold values from 0 to 4095, as said below
- mixer_gain: float32 [2048], replicated, may hold values from 0.5 to 1.5
- ffn_gain: float32 [2048], replicated, may hold values from 0.5 to 1.5
- z_weight: bfloat16 [2048, 3072], P('seq', 'head'), may hold values from -0.125 to 0.125
- x_weight: bfloat16 [2048, 3072], P('seq', 'head'), may hold values from -0.125 to 0.125
- bc_weight: bfloat16 [2048, 512], P('seq'), may hold values from -0.0068359375 to 0.0068359375
- dt_weight: bfloat16 [2048, 48], P('seq', 'head'), may hold values from -0.125 to 0.125
- q_weight: bfloat16 [2048, 1024], P('seq', 'head'), may hold values from -0.125 to 0.125
- k_weight: bfloat16 [2048, 256], P('seq', 'head'), may hold values from -0.125 to 0.125
- v_weight: bfloat16 [2048, 256], P('seq', 'head'), may hold values from -0.125 to 0.125
- o_weight: bfloat16 [2048, 1024], P('seq', 'head'), may hold values from -1.5 to 1.5
- out_weight: bfloat16 [2048, 3072], P('seq', 'head'), may hold values from -0.109375 to 0.109375
- gate_weight: bfloat16 [2048, 4096], P('seq', 'head'), may hold values from -0.125 to 0.125
- up_weight: bfloat16 [2048, 4096], P('seq', 'head'), may hold values from -0.125 to 0.125
- down_weight: bfloat16 [2048, 4096], P('seq', 'head'), may hold values from -0.09375 to 0.09375
- conv_inner: float32 [4, 3072], P(None, 'head'), may hold values from -3 to 3
- conv_state: float32 [4, 512], replicated, may hold values from -3 to 3
- decay_log: float32 [48], P('head'), may hold values from -16 to -2
- dt_bias: float32 [48], P('head'), may hold values from -1.5 to 0.5
- skip_coef: float32 [48], P('head'), may hold values from 0.5 to 1.5
- ssm_gain: float32 [3072], P('head'), may hold values from 0.5 to 1.5
- cotangent: float32 [4096, 2048], P('seq'), may hold values from -6 to 6
Outputs:
- layer_out: float32 [4096, 2048], P('seq')
- grad_input: float32 [4096, 2048], P('seq')
- grad_mixer_gain: float32 [2048], P('seq')
- grad_ffn_gain: float32 [2048], P('seq')
- grad_z_weight: float32 [2048, 3072], P('seq', 'head')
- grad_x_weight: float32 [2048, 3072], P('seq', 'head')
- grad_bc_weight: float32 [2048, 512], P('seq')
- grad_dt_weight: float32 [2048, 48], P('seq', 'head')
- grad_q_weight: float32 [2048, 1024], P('seq', 'head')
- grad_k_weight: float32 [2048, 256], P('seq', 'head')
- grad_v_weight: float32 [2048, 256], P('seq', 'head')
- grad_o_weight: float32 [2048, 1024], P('seq', 'head')
- grad_out_weight: float32 [2048, 3072], P('seq', 'head')
- grad_gate_weight: float32 [2048, 4096], P('seq', 'head')
- grad_up_weight: float32 [2048, 4096], P('seq', 'head')
- grad_down_weight: float32 [2048, 4096], P('seq', 'head')
- grad_conv_inner: float32 [4, 3072], P(None, 'head')
- grad_conv_state: float32 [4, 512], replicated
- grad_decay_log: float32 [48], P('head')
- grad_dt_bias: float32 [48], P('head')
- grad_skip_coef: float32 [48], P('head')
- grad_ssm_gain: float32 [3072], P('head')
The draws below stay inside these ranges and needn't reach their ends.
Inputs may be any that keep to these rules, and one draw needn't show every extreme that they name: `doc_start`: documents are contiguous: entries never fall, each is at most its token's position, and a token whose entry equals its position begins a document; the first document begins at 0.
All inputs are finite; a program needn't handle non-finite values.
Results may differ from the reference program's by a relative error of at most 0.017.
Values may be sent and summed in bfloat16 or wider, within the bound.
A program may use at most 448 MiB of HBM per device.

```python
import jax
import jax.numpy as jnp
from jax import lax

D = 2048
H = 48
P_SIZE = 64
N = 256
QH = 8
KVH = 2
HD = 128
FF = 4096
K = 4
TOK_DEV = 256
TOKENS = 4096
DSSM = 3072


def draw_doc_start(key, part):
    key = jax.random.fold_in(key, 11)
    first_key, second_key, length_key = jax.random.split(key, 3)
    early_cut = jax.random.randint(first_key, (), TOKENS // 8, TOKENS // 4 + 1)
    late_cut = jax.random.randint(second_key, (), 5 * TOKENS // 8, 3 * TOKENS // 4 + 1)
    count = max(64, TOKENS // 128)
    powers = jax.random.randint(length_key, (count,), 0, 9)
    lengths = jnp.left_shift(jnp.full((count,), 32, jnp.int32), powers)
    tail_starts = late_cut + jnp.cumsum(lengths)
    places = jnp.arange(TOKENS, dtype=jnp.int32)
    tail_marks = jnp.zeros((TOKENS,), jnp.int32).at[tail_starts].set(1, mode='drop')
    begins = (tail_marks > 0) | (places == 0) | (places == early_cut) | (places == late_cut) | (places == TOKENS - 1)
    marks = jnp.where(begins, places, 0).astype(jnp.int32)
    return lax.cummax(marks, axis=0)


def draw_decay_log(key, part):
    key = jax.random.fold_in(key, 7)
    pick_key, slow_key, fast_key = jax.random.split(key, 3)
    share = 0.5
    slow = jax.random.uniform(pick_key, (H,)) < share
    slow_rate = jnp.exp(jax.random.uniform(slow_key, (H,), minval=jnp.log(0.3), maxval=jnp.log(3.0))) / TOKENS
    fast_rate = jnp.exp(jax.random.uniform(fast_key, (H,), minval=jnp.log(0.03), maxval=jnp.log(0.1)))
    return jnp.log(jnp.where(slow, slow_rate, fast_rate)).astype(jnp.float32)


def level_of(own_key, dims, cuts, smallest, high):
    factor_of, own = 1.0, jax.random.fold_in(own_key, 6)
    for position, shards_of in cuts:
        heights = jnp.exp(jax.random.uniform(jax.random.fold_in(own, position), (shards_of,), jnp.float32, smallest / len(cuts), high / len(cuts)))
        factor_of = factor_of * jnp.repeat(heights, dims[position] // shards_of).reshape([-1 if axis == position else 1 for axis in range(len(dims))])
    return factor_of


def gaussian(own_key, shape, deviation, limit, cuts=(), kind=jnp.bfloat16):
    drawn = deviation * jax.random.normal(own_key, shape, jnp.float32)
    if cuts:
        drawn = drawn * level_of(own_key, shape, cuts, -0.22, 0.18)
    return jnp.clip(drawn, -limit, limit).astype(kind)


def setup_inputs(seed: int = 0) -> dict:
    streams_of = jax.random.split(jax.random.key(seed), 24)
    return {
        "layer_input": gaussian(streams_of[0], (TOKENS, D), 1.0, 6.0, ((0, 16),), jnp.float32),
        "doc_start": draw_doc_start(jax.random.fold_in(streams_of[23], 71), 0),
        "mixer_gain": jnp.clip(1.0 + 0.1 * jax.random.normal(streams_of[2], (D,), jnp.float32), 0.5, 1.5),
        "ffn_gain": jnp.clip(1.0 + 0.1 * jax.random.normal(streams_of[3], (D,), jnp.float32), 0.5, 1.5),
        "z_weight": gaussian(streams_of[4], (D, DSSM), D ** -0.5, 0.125, ((0, 16), (1, 2))),
        "x_weight": gaussian(streams_of[5], (D, DSSM), D ** -0.5, 0.125, ((0, 16), (1, 2))),
        "bc_weight": gaussian(streams_of[6], (D, 2 * N), (400 * D) ** -0.5, 0.0068359375, ((0, 16),)),
        "dt_weight": gaussian(streams_of[7], (D, H), D ** -0.5, 0.125, ((0, 16), (1, 2))),
        "q_weight": gaussian(streams_of[8], (D, QH * HD), D ** -0.5, 0.125, ((0, 16), (1, 2))),
        "k_weight": gaussian(streams_of[9], (D, KVH * HD), D ** -0.5, 0.125, ((0, 16), (1, 2))),
        "v_weight": gaussian(streams_of[10], (D, KVH * HD), D ** -0.5, 0.125, ((0, 16), (1, 2))),
        "o_weight": gaussian(streams_of[11], (D, QH * HD), (QH * HD // 64) ** -0.5, 1.5, ((0, 16), (1, 2))),
        "out_weight": gaussian(streams_of[12], (D, DSSM), DSSM ** -0.5, 0.109375, ((0, 16), (1, 2))),
        "gate_weight": gaussian(streams_of[13], (D, FF), D ** -0.5, 0.125, ((0, 16), (1, 2))),
        "up_weight": gaussian(streams_of[14], (D, FF), D ** -0.5, 0.125, ((0, 16), (1, 2))),
        "down_weight": gaussian(streams_of[15], (D, FF), FF ** -0.5, 0.09375, ((0, 16), (1, 2))),
        "conv_inner": gaussian(streams_of[16], (K, DSSM), 0.5, 3.0, ((1, 2),), jnp.float32),
        "conv_state": gaussian(streams_of[17], (K, 2 * N), 0.5, 3.0, (), jnp.float32),
        "decay_log": draw_decay_log(jax.random.fold_in(streams_of[23], 71), 0),
        "dt_bias": jnp.clip(-1.5 + 2.0 * jax.random.uniform(streams_of[19], (H,), jnp.float32) ** level_of(streams_of[19], (H,), ((0, 2),), -0.2, 0.2), -1.5, 0.5),
        "skip_coef": jnp.clip(0.5 + 1.0 * jax.random.uniform(streams_of[20], (H,), jnp.float32) ** level_of(streams_of[20], (H,), ((0, 2),), -0.2, 0.2), 0.5, 1.5),
        "ssm_gain": jnp.clip(1.0 + 0.1 * jax.random.normal(streams_of[21], (DSSM,), jnp.float32), 0.5, 1.5),
        "cotangent": gaussian(streams_of[22], (TOKENS, D), 1.0, 6.0, ((0, 16),), jnp.float32),
    }


@jax.custom_vjp
def low(v):
    return lax.optimization_barrier(v.astype(jnp.bfloat16)).astype(jnp.float32)

@jax.custom_vjp
def low_back(v):
    return v

def low_keep(v):
    return (low(v), None)

def low_pass(kept, grad):
    return (grad,)

def back_keep(v):
    return (v, None)

def back_low(kept, grad):
    return (low(grad),)
low.defvjp(low_keep, low_pass)
low_back.defvjp(back_keep, back_low)
highest = lax.Precision.HIGHEST
rope_base = 10000.0
norm_eps = 1e-05

def rms_scale(values, gain):
    return values * lax.rsqrt(lax.optimization_barrier(jnp.mean(values * values, axis=-1, keepdims=True)) + norm_eps) * gain

def rotate(values, offsets):
    half = values.shape[-1] // 2
    freqs = rope_base ** (-2.0 * jnp.arange(half, dtype=values.dtype) / values.shape[-1])
    angles = offsets.astype(values.dtype)[:, None] * freqs[None, :]
    cosine = jnp.cos(angles)[:, None, :]
    sine = jnp.sin(angles)[:, None, :]
    first = values[..., :half]
    second = values[..., half:]
    return jnp.concatenate([first * cosine - second * sine, second * cosine + first * sine], axis=-1)

def causal_conv(padded, taps, starts, places):
    width = taps.shape[0]
    length = starts.shape[0]
    total = jnp.zeros((length, padded.shape[1]), padded.dtype)
    for lag in range(width):
        valid = (places - (width - 1 - lag) >= starts)[:, None]
        total = total + jnp.where(valid, padded[lag:lag + length] * taps[lag][None, :], 0.0)
    return total

def ssd_block(state, block):
    inner, b_rows, c_rows, step_size, log_decay, starts, places = block
    cum_decay = jnp.cumsum(log_decay, axis=0)
    visible = (starts[:, None] <= places[None, :]) & (places[None, :] <= places[:, None])
    spans = cum_decay[:, None, :] - cum_decay[None, :, :]
    weights = jnp.where(visible[:, :, None], jnp.exp(jnp.where(visible[:, :, None], spans, 0.0)), 0.0)
    intersection = jnp.dot(c_rows, b_rows.T, precision=highest)
    driven = inner * step_size[:, :, None]
    mixed = jnp.einsum('ijh,jhp->ihp', weights * intersection[:, :, None], driven, precision=highest)
    carried = (starts < places[0]).astype(inner.dtype)
    decay_in = jnp.exp(cum_decay) * carried[:, None]
    from_state = jnp.einsum('in,hpn->ihp', c_rows, state, precision=highest) * decay_in[:, :, None]
    closing = jnp.where((starts[-1] <= places)[:, None], jnp.exp(cum_decay[-1][None, :] - cum_decay), 0.0)
    new_state = state * decay_in[-1][:, None, None] + jnp.einsum('jh,jhp,jn->hpn', closing, driven, b_rows, precision=highest)
    return (new_state, mixed + from_state)

def attend(queries, keys, values, starts, places):
    group = queries.shape[1] // keys.shape[1]
    keys_all = jnp.repeat(keys, group, axis=1)
    values_all = jnp.repeat(values, group, axis=1)
    rows = min(512, queries.shape[0])
    blocks = queries.shape[0] // rows

    def one_block(pieces):
        q_block, s_block, p_block = pieces
        scores = low_back(jnp.einsum('qhd,khd->hqk', q_block, keys_all, precision=highest))
        visible = (places[None, :] >= s_block[:, None]) & (places[None, :] <= p_block[:, None])
        scores = jnp.where(visible[None], scores, -jnp.inf)
        probs = low(jax.nn.softmax(scores, axis=-1))
        return jnp.einsum('hqk,khd->qhd', probs, values_all, precision=highest)
    result = lax.map(jax.checkpoint(one_block), (queries.reshape(blocks, rows, queries.shape[1], queries.shape[2]), starts.reshape(blocks, rows), places.reshape(blocks, rows)))
    return result.reshape(queries.shape)

def reference(layer_input, doc_start, mixer_gain, ffn_gain, z_weight, x_weight, bc_weight, dt_weight, q_weight, k_weight, v_weight, o_weight, out_weight, gate_weight, up_weight, down_weight, conv_inner, conv_state, decay_log, dt_bias, skip_coef, ssm_gain, cotangent):
    places = jnp.arange(TOKENS, dtype=jnp.int32)
    offsets = places - doc_start
    block_len = min(128, TOK_DEV)
    blocks = TOKENS // block_len

    def layer(layer_input, mixer_gain, ffn_gain, z_weight, x_weight, bc_weight, dt_weight, q_weight, k_weight, v_weight, o_weight, out_weight, gate_weight, up_weight, down_weight, conv_inner, conv_state, decay_log, dt_bias, skip_coef, ssm_gain):
        normed = low(rms_scale(layer_input, mixer_gain))
        z_part = low_back(jnp.dot(normed, z_weight, precision=highest))
        inner_pre = low_back(jnp.dot(normed, x_weight, precision=highest))
        state_pre = low_back(jnp.dot(normed, bc_weight, precision=highest))
        step_raw = low_back(jnp.dot(normed, dt_weight, precision=highest))
        rim_inner = jnp.zeros((K - 1, inner_pre.shape[1]), jnp.float32)
        rim_state = jnp.zeros((K - 1, state_pre.shape[1]), jnp.float32)
        conv_x = jax.nn.silu(causal_conv(jnp.concatenate([rim_inner, inner_pre], axis=0), conv_inner, doc_start, places))
        conv_bc = jax.nn.silu(causal_conv(jnp.concatenate([rim_state, state_pre], axis=0), conv_state, doc_start, places))
        step_size = jax.nn.softplus(step_raw + dt_bias)
        log_decay = -jnp.exp(decay_log) * step_size
        inner_heads = conv_x.reshape(TOKENS, H, P_SIZE)
        pieces = (inner_heads.reshape(blocks, block_len, H, P_SIZE), conv_bc[:, :N].reshape(blocks, block_len, N), conv_bc[:, N:].reshape(blocks, block_len, N), step_size.reshape(blocks, block_len, H), log_decay.reshape(blocks, block_len, H), doc_start.reshape(blocks, block_len), places.reshape(blocks, block_len))
        _, outputs = lax.scan(jax.checkpoint(ssd_block), jnp.zeros((H, P_SIZE, N), jnp.float32), pieces)
        ssm_out = outputs.reshape(TOKENS, H, P_SIZE) + skip_coef[None, :, None] * inner_heads
        gated = ssm_out * jax.nn.silu(z_part.reshape(TOKENS, H, P_SIZE))
        scaled = gated * lax.rsqrt(lax.optimization_barrier(jnp.mean(gated * gated, axis=-1, keepdims=True)) + norm_eps) * ssm_gain.reshape(H, P_SIZE)
        ssm_low = low(scaled.reshape(TOKENS, H * P_SIZE))
        mamba = jnp.dot(ssm_low, out_weight.T, precision=highest)
        queries = low_back(jnp.dot(normed, q_weight, precision=highest)).reshape(TOKENS, QH, HD)
        keys = low_back(jnp.dot(normed, k_weight, precision=highest)).reshape(TOKENS, KVH, HD)
        values = low_back(jnp.dot(normed, v_weight, precision=highest)).reshape(TOKENS, KVH, HD)
        query_low = low(rotate(queries, offsets) * HD ** (-0.5))
        key_low = low(rotate(keys, offsets))
        value_low = low(values)
        attended = low(low_back(attend(query_low, key_low, value_low, doc_start, places).reshape(TOKENS, QH * HD)))
        attn = jnp.dot(attended, o_weight.T, precision=highest)
        hidden = layer_input + low_back(mamba + attn)
        second = low(rms_scale(hidden, ffn_gain))
        gate_pre = low_back(jnp.dot(second, gate_weight, precision=highest))
        up_pre = low_back(jnp.dot(second, up_weight, precision=highest))
        activated = low(jax.nn.silu(gate_pre) * up_pre)
        return hidden + low_back(jnp.dot(activated, down_weight.T, precision=highest))
    floats = (layer_input, mixer_gain, ffn_gain, z_weight, x_weight, bc_weight, dt_weight, q_weight, k_weight, v_weight, o_weight, out_weight, gate_weight, up_weight, down_weight, conv_inner, conv_state, decay_log, dt_bias, skip_coef, ssm_gain)
    floats = tuple((item.astype(jnp.float32) for item in floats))
    layer_out, layer_back = jax.vjp(layer, *floats)
    g_input, g_mixer, g_ffn, g_z, g_x, g_bc, g_dt, g_q, g_k, g_v, g_o, g_out, g_gate, g_up, g_down, g_conv_inner, g_conv_state, g_decay, g_bias, g_skip, g_ssm = layer_back(cotangent)
    return (layer_out, g_input, g_mixer, g_ffn, g_z, g_x, g_bc, g_dt, g_q, g_k, g_v, g_o, g_out, g_gate, g_up, g_down, g_conv_inner, g_conv_state, g_decay, g_bias, g_skip, g_ssm)
```

```python
import jax
import jax.numpy as jnp
from jax import lax
from jax.sharding import Mesh, PartitionSpec as P

P_SIZE = 64
N = 256
HD = 128
K = 4
G = 4
CHUNK = 128

highest = lax.Precision.HIGHEST
rope_base = 10000.0
norm_eps = 1e-05
bf16 = jnp.bfloat16
f32 = jnp.float32


def dot(a, b, ca, cb):
    return lax.dot_general(a, b, (((ca,), (cb,)), ((), ())), preferred_element_type=f32)


def exact(text, *operands):
    return jnp.einsum(text, *operands, precision=highest, preferred_element_type=f32)


def d_silu(v):
    s = jax.nn.sigmoid(v)
    return s * (1.0 + v * (1.0 - s))


def shifted(block, axis, distance):
    count = lax.axis_size(axis)
    route = [(i - distance, i) for i in range(count) if 0 <= i - distance < count]
    return lax.ppermute(block, axis, route)


def rope_tables(offsets, first, count):
    half = HD // 2
    index = (first + jnp.arange(count)).astype(f32)
    freqs = rope_base ** (-2.0 * index / HD)
    angles = offsets.astype(f32)[:, None] * freqs[None, :]
    return jnp.cos(angles), jnp.sin(angles)


def turn(v, cosine, sine):
    half = v.shape[-1] // 2
    a, b = v[:, :half], v[:, half:]
    return jnp.concatenate([a * cosine - b * sine, b * cosine + a * sine], axis=-1)


def conv_parts(padded, starts, places):
    length = starts.shape[0]
    parts = []
    for lag in range(K):
        valid = (places - (K - 1 - lag) >= starts)[:, None]
        parts.append(jnp.where(valid, padded[lag : lag + length], 0.0))
    return parts


def conv_back(grad, padded, taps, starts, places):
    length = starts.shape[0]
    total = jnp.zeros_like(padded)
    tap_grads = []
    for lag in range(K):
        valid = (places - (K - 1 - lag) >= starts)[:, None]
        g = jnp.where(valid, grad, 0.0)
        total = total + jnp.pad(g * taps[lag][None, :], ((lag, K - 1 - lag), (0, 0)))
        tap_grads.append(jnp.sum(g * padded[lag : lag + length], axis=0))
    return total, jnp.stack(tap_grads)


def on_device(
    layer_input, doc_start, mixer_gain, ffn_gain,
    z_weight, x_weight, bc_weight, dt_weight, q_weight, k_weight, v_weight,
    o_weight, out_weight, gate_weight, up_weight, down_weight,
    conv_inner, conv_state, decay_log, dt_bias, skip_coef, ssm_gain, cotangent,
):
    tokens, width = layer_input.shape
    rows = z_weight.shape[0]
    planes = lax.axis_size("z")
    cores = lax.axis_size("head")
    zi, pi, hi = (lax.axis_index(a) for a in ("z", "p", "head"))
    T = tokens * G
    total_tokens = T * planes
    offset = zi * T
    places = offset + jnp.arange(T, dtype=jnp.int32)
    starts = lax.all_gather(doc_start, "p", axis=0, tiled=True)
    heads = decay_log.shape[0] // G
    chan = heads * P_SIZE
    bcs = 2 * N // cores // G
    quarter_half = HD // 2 // G

    def my_slice(v, size, index, axis):
        return lax.dynamic_slice_in_dim(v, index * size, size, axis)

    taps_inner = my_slice(conv_inner, chan, pi, 1)
    taps_state = my_slice(conv_state, bcs, hi * G + pi, 1)
    rates = my_slice(decay_log, heads, pi, 0)
    bias = my_slice(dt_bias, heads, pi, 0)
    skip = my_slice(skip_coef, heads, pi, 0)
    gain_s = my_slice(ssm_gain, chan, pi, 0)

    def cut(w):
        return w.reshape(rows, G, -1)

    bc_mine = lax.dynamic_slice_in_dim(bc_weight, hi * (2 * N // cores), 2 * N // cores, 1)
    k_cut = jnp.moveaxis(k_weight.reshape(rows, 2, G, quarter_half), 2, 1).reshape(rows, G, -1)
    a_parts = [cut(z_weight), cut(x_weight), cut(q_weight), cut(bc_mine), k_cut, cut(v_weight), cut(dt_weight)]
    a_sizes = [a.shape[-1] for a in a_parts]
    a_cols = sum(a_sizes)
    pad = -a_cols % 128
    a_parts.append(jnp.zeros((rows, G, pad), bf16))
    a_at = [sum(a_sizes[:i]) for i in range(len(a_sizes))]

    def gather(parts):
        w = jnp.moveaxis(jnp.concatenate(parts, axis=2), 1, 0)
        w = lax.all_to_all(w, "p", 0, 0, tiled=True)
        return lax.all_gather(w.reshape(G * rows, -1), "z", axis=0, tiled=True)

    def scatter(grad):
        g = lax.psum_scatter(grad.astype(bf16), "z", scatter_dimension=0, tiled=True)
        g = lax.all_to_all(g.reshape(G, rows, -1), "p", 0, 0, tiled=True)
        return jnp.moveaxis(g, 0, 1).astype(f32)

    wa = gather(a_parts)
    wb = gather([cut(out_weight), cut(o_weight)])
    wc = gather([cut(gate_weight), cut(up_weight)])
    wd = gather([cut(down_weight)])

    r1 = lax.rsqrt(jnp.mean(layer_input * layer_input, axis=-1, keepdims=True) + norm_eps)
    first_own = (layer_input * r1 * mixer_gain).astype(bf16)
    first = lax.all_gather(first_own, "p", axis=0, tiled=True)
    out_low = lax.all_gather(cotangent.astype(bf16), "p", axis=0, tiled=True)
    pa = dot(first, wa, 1, 0)
    z_part, inner_pre, q_proj, bc_pre, k_proj, v_proj, step_raw = (
        pa[:, a : a + s] for a, s in zip(a_at, a_sizes)
    )
    edge = K - 1
    rim_inner, rim_bc = shifted((inner_pre[T - edge :], bc_pre[T - edge :]), "z", 1)
    pad_inner = jnp.concatenate([rim_inner, inner_pre], axis=0)
    pad_bc = jnp.concatenate([rim_bc, bc_pre], axis=0)
    cv_x = sum(p * t[None, :] for p, t in zip(conv_parts(pad_inner, starts, places), taps_inner))
    cv_bc = sum(p * t[None, :] for p, t in zip(conv_parts(pad_bc, starts, places), taps_state))
    conv_x = jax.nn.silu(cv_x)
    bc_low = jax.nn.silu(cv_bc).astype(bf16)
    bc_all = lax.all_gather(bc_low, ("head", "p"), axis=1, tiled=True)
    step = jax.nn.softplus(step_raw + bias)
    log_decay = -jnp.exp(rates) * step

    L = CHUNK
    nc = T // L
    lower = (jnp.arange(L)[:, None] >= jnp.arange(L)[None, :]).astype(f32)
    b_rows = bc_all[:, :N].astype(f32).reshape(nc, L, N)
    c_rows = bc_all[:, N:].astype(f32).reshape(nc, L, N)

    def by_head(v):
        return v.reshape(nc, L, heads, P_SIZE).transpose(0, 2, 1, 3)

    def by_token(v):
        return v.transpose(0, 2, 1, 3).reshape(T, chan)

    xh = by_head(conv_x)
    step_h = step.reshape(nc, L, heads).transpose(0, 2, 1)
    la_h = log_decay.reshape(nc, L, heads).transpose(0, 2, 1)
    cs = exact("ij,chj->chi", lower, la_h)
    st = starts.reshape(nc, L)
    pl_ = places.reshape(nc, L)
    visible = (st[:, :, None] <= pl_[:, None, :]) & (pl_[:, None, :] <= pl_[:, :, None])
    span = cs[:, :, :, None] - cs[:, :, None, :]
    weights = jnp.where(visible[:, None], jnp.exp(jnp.where(visible[:, None], span, 0.0)), 0.0)
    inter = exact("cin,cjn->cij", c_rows, b_rows)
    mix = weights * inter[:, None]
    driven = xh * step_h[..., None]
    carried = (st < pl_[:, :1]).astype(f32)
    decay_in = jnp.exp(cs) * carried[:, None, :]
    closing = jnp.where((st[:, -1:] <= pl_)[:, None, :], jnp.exp(cs[:, :, -1:] - cs), 0.0)
    dtot = decay_in[:, :, -1]
    local = exact("chjp,cjn->chpn", driven * closing[..., None], b_rows)
    entering = []
    state = jnp.zeros((heads, P_SIZE, N), f32)
    through = jnp.ones((heads,), f32)
    reach = []
    for c in range(nc):
        entering.append(state)
        reach.append(through)
        state = state * dtot[c][:, None, None] + local[c]
        through = through * dtot[c]
    everyone = lax.all_gather(state.astype(bf16), "z", axis=0)
    factors = lax.all_gather(through, "z", axis=0)
    before = jnp.zeros((heads, P_SIZE, N), f32)
    for k in range(planes - 1):
        new = before * factors[k][:, None, None] + everyone[k].astype(f32)
        before = jnp.where(k < zi, new, before)
    state_in = jnp.stack([s + before * r[:, None, None] for s, r in zip(entering, reach)])
    y_off = exact("cin,chpn->chip", c_rows, state_in) * decay_in[..., None]
    y_scan = exact("chij,chjp->chip", mix, driven) + y_off
    y_h = y_scan + skip[None, :, None, None] * xh

    ssm = by_token(y_h)
    same_head = (jnp.arange(chan)[:, None] // P_SIZE == jnp.arange(heads)[None, :]).astype(f32)

    def head_mean(v):
        return jnp.repeat(jnp.mean(v.reshape(T, heads, P_SIZE), axis=-1), P_SIZE, axis=1)

    sz = jax.nn.silu(z_part)
    gated = ssm * sz
    r_s = lax.rsqrt(head_mean(gated * gated) + norm_eps)
    ssm_low = (gated * r_s * gain_s).astype(bf16)

    offsets = places - starts
    cos_q, sin_q = rope_tables(offsets, 0, HD // 2)
    cos_k, sin_k = rope_tables(offsets, pi * quarter_half, quarter_half)
    scale = HD ** (-0.5)
    query = (turn(q_proj, cos_q, sin_q) * scale).astype(bf16)
    kv_own = jnp.concatenate([turn(k_proj, cos_k, sin_k).astype(bf16), v_proj.astype(bf16)], axis=1)
    kv_all = lax.all_gather(kv_own, ("z", "p"), axis=0)
    kv_all = kv_all.reshape(planes, G, T, 4, quarter_half)
    keys = kv_all[:, :, :, :2].transpose(0, 2, 3, 1, 4).reshape(total_tokens, HD)
    values = kv_all[:, :, :, 2:].reshape(planes, G, T, 2 * quarter_half).transpose(0, 2, 1, 3).reshape(total_tokens, HD)
    key_len = min(512, total_tokens)
    first_block = starts[0] // key_len
    last_block = (offset + T - 1) // key_len

    def key_block(index):
        begin = index * key_len
        kb = lax.dynamic_slice_in_dim(keys, begin, key_len, 0)
        vb = lax.dynamic_slice_in_dim(values, begin, key_len, 0)
        at = begin + jnp.arange(key_len, dtype=jnp.int32)
        seen = (at[None, :] >= starts[:, None]) & (at[None, :] <= places[:, None])
        return kb, vb, seen, dot(query, kb, 1, 1)

    def running(index, carry):
        peak, mass = carry
        _, _, seen, scores = key_block(index)
        new = jnp.maximum(peak, jnp.max(jnp.where(seen, scores, -1e30), axis=-1))
        mass = mass * jnp.exp(peak - new) + jnp.sum(jnp.where(seen, jnp.exp(scores - new[:, None]), 0.0), axis=-1)
        return new, mass

    peak, mass = lax.fori_loop(
        first_block, last_block + 1, running, (jnp.full((T,), -1e30, f32), jnp.zeros((T,), f32))
    )
    log_mass = peak + jnp.log(mass)

    def weighted(index, total):
        _, vb, seen, scores = key_block(index)
        probs = jnp.where(seen, jnp.exp(scores - log_mass[:, None]), 0.0).astype(bf16)
        return total + dot(probs, vb, 1, 0)

    attended = lax.fori_loop(first_block, last_block + 1, weighted, jnp.zeros((T, HD), f32))
    att_low = attended.astype(bf16)

    def plane_sum(part):
        mine = lax.psum_scatter(part.astype(bf16), "p", scatter_dimension=0, tiled=True)
        return lax.psum(mine, "head").astype(f32)

    both_low = jnp.concatenate([ssm_low, att_low], axis=1)
    hidden = layer_input + plane_sum(dot(both_low, wb, 1, 1))
    r2 = lax.rsqrt(jnp.mean(hidden * hidden, axis=-1, keepdims=True) + norm_eps)
    second = lax.all_gather((hidden * r2 * ffn_gain).astype(bf16), "p", axis=0, tiled=True)
    pc = dot(second, wc, 1, 0)
    ff = pc.shape[1] // 2
    gate_pre, up_pre = pc[:, :ff], pc[:, ff:]
    s_gate = jax.nn.silu(gate_pre)
    act_low = (s_gate * up_pre).astype(bf16)
    layer_out = hidden + plane_sum(dot(act_low, wd, 1, 1))

    grad_d = dot(out_low, act_low, 0, 0)
    d_act = dot(out_low, wd, 1, 0)
    gu_low = jnp.concatenate([d_act * up_pre * d_silu(gate_pre), d_act * s_gate], axis=1).astype(bf16)
    grad_c = dot(second, gu_low, 0, 0)
    d_second = plane_sum(dot(gu_low, wc, 1, 1))
    u2 = d_second * ffn_gain
    d_hidden = cotangent + r2 * u2 - hidden * r2**3 * jnp.mean(u2 * hidden, axis=-1, keepdims=True)
    grad_ffn = jnp.sum(d_second * hidden * r2, axis=0)
    branch = lax.all_gather(d_hidden.astype(bf16), "p", axis=0, tiled=True)
    grad_b = dot(branch, both_low, 0, 0)
    d_both = dot(branch, wb, 1, 0)
    d_norm_s, d_att = d_both[:, :chan], d_both[:, chan:].astype(bf16)

    grad_gain_s = jnp.sum(d_norm_s * gated * r_s, axis=0)
    u_s = d_norm_s * gain_s
    d_gated = r_s * u_s - gated * r_s**3 * head_mean(u_s * gated)
    d_z = d_gated * ssm * d_silu(z_part)
    dy = by_head(d_gated * sz)
    dy_in = dy * decay_in[..., None]
    from_chunk = exact("chip,cin->chpn", dy_in, c_rows)
    zero_state = jnp.zeros((heads, P_SIZE, N), f32)
    g = zero_state
    leaving = [None] * nc
    for c in reversed(range(nc)):
        leaving[c] = g
        g = g * dtot[c][:, None, None] + from_chunk[c]
    every_grad = lax.all_gather(g.astype(bf16), "z", axis=0)
    after = zero_state
    for k in reversed(range(1, planes)):
        new = after * factors[k][:, None, None] + every_grad[k].astype(f32)
        after = jnp.where(k > zi, new, after)
    scale_c = jnp.ones((heads,), f32)
    d_state = [None] * nc
    for c in reversed(range(nc)):
        d_state[c] = leaving[c] + after * scale_c[:, None, None]
        scale_c = scale_c * dtot[c]
    d_state = jnp.stack(d_state)
    d_mix = exact("chip,chjp->chij", dy, driven)
    d_inter = jnp.sum(weights * d_mix, axis=1)
    d_c = exact("cij,cjn->cin", d_inter, b_rows) + exact("chip,chpn->cin", dy_in, state_in)
    closed = driven * closing[..., None]
    d_b = exact("cij,cin->cjn", d_inter, c_rows) + exact("chpn,chjp->cjn", d_state, closed)
    d_driven = exact("chij,chip->chjp", mix, dy) + closing[..., None] * exact("chpn,cjn->chjp", d_state, b_rows)
    d_closing = jnp.sum(closed * exact("chpn,cjn->chjp", d_state, b_rows), axis=-1)
    d_cs = jnp.sum(dy * y_scan, axis=-1) - jnp.sum(driven * d_driven, axis=-1)
    d_total = jnp.sum(d_closing, axis=-1) + dtot * jnp.sum(d_state * state_in, axis=(2, 3))
    d_la = exact("ji,chj->chi", lower, d_cs) + d_total[:, :, None]
    d_step = jnp.sum(d_driven * xh, axis=-1)
    dx = by_token(d_driven * step_h[..., None] + skip[None, :, None, None] * dy)
    grad_skip = jnp.sum(dy * xh, axis=(0, 2, 3))
    d_raw = (d_step - jnp.exp(rates)[None, :, None] * d_la).transpose(0, 2, 1).reshape(T, heads)
    d_raw = d_raw * jax.nn.sigmoid(step_raw + bias)
    grad_bias = jnp.sum(d_raw, axis=0)
    grad_rates = jnp.sum(d_la * la_h, axis=(0, 2))
    d_bc_all = jnp.concatenate([d_b.reshape(T, N), d_c.reshape(T, N)], axis=1).astype(bf16)
    d_bc = lax.psum_scatter(d_bc_all, ("head", "p"), scatter_dimension=1, tiled=True).astype(f32)
    pad_g, grad_conv_inner = conv_back(dx * d_silu(cv_x), pad_inner, taps_inner, starts, places)
    pad_h, grad_conv_state = conv_back(d_bc * d_silu(cv_bc), pad_bc, taps_state, starts, places)
    next_g, next_h = shifted((pad_g[:edge], pad_h[:edge]), "z", -1)
    d_inner_pre = pad_g[edge:] + jnp.pad(next_g, ((T - edge, 0), (0, 0)))
    d_bc_pre = pad_h[edge:] + jnp.pad(next_h, ((T - edge, 0), (0, 0)))

    balance = jnp.sum(d_att.astype(f32) * attended, axis=-1, keepdims=True)

    def grads(index, carry):
        d_query, d_keys, d_values = carry
        kb, vb, seen, scores = key_block(index)
        probs = jnp.where(seen, jnp.exp(scores - log_mass[:, None]), 0.0)
        d_scores = (probs * (dot(d_att, vb, 1, 1) - balance)).astype(bf16)
        d_query = d_query + dot(d_scores, kb, 1, 0)
        d_keys = lax.dynamic_update_slice_in_dim(d_keys, dot(d_scores, query, 0, 0), index * key_len, 0)
        d_values = lax.dynamic_update_slice_in_dim(d_values, dot(probs.astype(bf16), d_att, 0, 0), index * key_len, 0)
        return d_query, d_keys, d_values

    zero_keys = jnp.zeros((total_tokens, HD), f32)
    d_query, d_keys, d_values = lax.fori_loop(
        first_block, last_block + 1, grads, (jnp.zeros((T, HD), f32), zero_keys, zero_keys)
    )
    dk_cut = d_keys.astype(bf16).reshape(planes, T, 2, G, quarter_half).transpose(0, 3, 1, 2, 4)
    dv_cut = d_values.astype(bf16).reshape(planes, T, G, 2 * quarter_half).transpose(0, 2, 1, 3)
    dkv = jnp.concatenate([dk_cut.reshape(planes, G, T, -1), dv_cut], axis=-1).reshape(planes * G, T, -1)
    dkv = jnp.sum(lax.all_to_all(dkv, ("z", "p"), 0, 0, tiled=True).astype(f32), axis=0)
    d_q = turn(d_query, cos_q, -sin_q) * scale
    d_k = turn(dkv[:, : 2 * quarter_half], cos_k, -sin_k)
    d_v = dkv[:, 2 * quarter_half :]

    da_low = jnp.concatenate(
        [d_z, d_inner_pre, d_q, d_bc_pre, d_k, d_v, d_raw, jnp.zeros((T, pad), f32)], axis=1
    ).astype(bf16)
    grad_a = dot(first, da_low, 0, 0)
    d_first = plane_sum(dot(da_low, wa, 1, 1))
    u1 = d_first * mixer_gain
    grad_input = d_hidden + r1 * u1 - layer_input * r1**3 * jnp.mean(u1 * layer_input, axis=-1, keepdims=True)
    grad_mixer = jnp.sum(d_first * layer_input * r1, axis=0)

    ga, gb, gc, gd = (scatter(g) for g in (grad_a, grad_b, grad_c, grad_d))
    g_z, g_x, g_q, g_bc, g_k, g_v, g_dt = (ga[:, :, a : a + s] for a, s in zip(a_at, a_sizes))
    g_k = jnp.moveaxis(g_k.reshape(rows, G, 2, quarter_half), 1, 2)
    g_bc = lax.all_gather(g_bc.reshape(rows, -1).astype(bf16), "head", axis=1, tiled=True).astype(f32)

    small = [grad_conv_inner, grad_conv_state, grad_rates, grad_bias, grad_skip, grad_gain_s]
    flat = jnp.concatenate([s.reshape(-1) for s in small])
    every = jnp.sum(lax.all_gather(flat, ("z", "p", "head")).reshape(planes, G, cores, -1), axis=0)
    mine = lax.dynamic_index_in_dim(every, hi, 1, False)
    at = [0]
    for s in small:
        at.append(at[-1] + s.size)
    pieces = [mine[:, a:b] for a, b in zip(at, at[1:])]
    o_conv_inner = jnp.moveaxis(pieces[0].reshape(G, K, chan), 0, 1).reshape(K, G * chan)
    o_conv_state = every[:, :, at[1] : at[2]].reshape(G, cores, K, bcs).transpose(2, 1, 0, 3).reshape(K, 2 * N)
    gains = lax.psum_scatter(jnp.stack([grad_mixer, grad_ffn]), ("z", "p"), scatter_dimension=1, tiled=True)

    def whole(g):
        return g.reshape(rows, -1)

    return (
        layer_out, grad_input, gains[0], gains[1],
        whole(g_z), whole(g_x), g_bc, whole(g_dt), whole(g_q), whole(g_k), whole(g_v),
        whole(gb[:, :, chan:]), whole(gb[:, :, :chan]),
        whole(gc[:, :, :ff]), whole(gc[:, :, ff:]), whole(gd),
        o_conv_inner, o_conv_state,
        pieces[2].reshape(-1), pieces[3].reshape(-1), pieces[4].reshape(-1), pieces[5].reshape(-1),
    )


def solution(mesh):
    seq, cores = mesh.shape["seq"], mesh.shape["head"]
    planes = Mesh(mesh.devices.reshape(seq // G, G, cores), ("z", "p", "head"))
    s = ("z", "p")
    both, row, head, whole = P(s, "head"), P(s, None), P("head"), P()
    placed = (
        row, P(s), whole, whole, both, both, row, both, both, both, both, both, both, both, both, both,
        P(None, "head"), whole, head, head, head, head, row,
    )
    return jax.shard_map(
        on_device,
        mesh=planes,
        in_specs=placed,
        out_specs=(
            row, row, P(s), P(s), both, both, row, both, both, both, both, both, both, both, both, both,
            P(None, "head"), whole, head, head, head, head,
        ),
        check_vma=False,
    )
```

```python
import functools

import jax
import jax.numpy as jnp
from jax import lax
from jax.experimental import pallas as pl
from jax.experimental.pallas import tpu as pltpu
from jax.sharding import Mesh, PartitionSpec as P

P_SIZE = 64
N = 256
HD = 128
K = 4
G = 4
CHUNK = 128
RIM = 16

highest = lax.Precision.HIGHEST
rope_base = 10000.0
norm_eps = 1e-05
bf16 = jnp.bfloat16
f32 = jnp.float32
MESH = pl.DeviceIdType.MESH
HBM = pl.BlockSpec(memory_space=pl.ANY)
VMEM = pl.BlockSpec(memory_space=pltpu.VMEM)
DMA = pltpu.SemaphoreType.DMA


def rcopy(src, dst, send, recv, **where):
    return pltpu.make_async_remote_copy(
        src_ref=src, dst_ref=dst, send_sem=send, recv_sem=recv, device_id=where, device_id_type=MESH
    )


def here():
    return lax.axis_index("z"), lax.axis_index("p"), lax.axis_index("head")


def ring(p, d):
    return lax.rem(p + d + G, G)


def greet(*partners):
    barrier = pltpu.get_barrier_semaphore()
    for where in partners:
        pl.semaphore_signal(barrier, inc=1, device_id=where, device_id_type=MESH)
    pl.semaphore_wait(barrier, len(partners))


def plane_partners(p, c):
    return [{"p": ring(p, d)} for d in range(1, G)] + [{"head": 1 - c}]


def line_partners(z, planes):
    return [{"z": lax.rem(z + d, planes)} for d in range(1, planes)]


def slot_at(p, c, rows, base=0):
    return pl.ds(pl.multiple_of(base + (p * 2 + c) * rows, 16), rows)


class Spread:
    sems = [DMA((3,)), DMA((3,)), DMA((4,)), DMA((4,)), DMA(())]

    def __init__(self, block, out, at, sems):
        self.block, self.out, self.at = block, out, at
        self.s1, self.r1, self.s2, self.r2, self.keep = sems
        _, self.p, self.c = here()

    def over(self, d):
        spot = self.out.at[self.at(self.p, self.c)]
        return rcopy(self.block, spot, self.s1.at[d - 1], self.r1.at[d - 1], p=ring(self.p, d))

    def across(self, d):
        spot = self.out.at[self.at(ring(self.p, -d), self.c)]
        return rcopy(spot if d else self.block, spot, self.s2.at[d], self.r2.at[d], head=1 - self.c)

    def mine(self):
        return pltpu.make_async_copy(self.block, self.out.at[self.at(self.p, self.c)], self.keep)

    def start(self):
        for d in (1, 2, 3):
            self.over(d).start()
        self.across(0).start()
        self.mine().start()

    def pass_on(self):
        for d in (1, 3, 2):
            self.over(d).wait_recv()
            self.across(d).start()

    def finish(self):
        self.mine().wait()
        for d in (1, 2, 3):
            self.over(d).wait_send()
        for d in (0, 1, 2, 3):
            self.across(d).wait()


class Collect:
    @staticmethod
    def scratch(rows, width):
        return [
            pltpu.VMEM((4, rows, width), bf16), pltpu.VMEM((3, rows, width), bf16), pltpu.VMEM((3, rows, width), bf16),
            pltpu.VMEM((rows, width), f32), DMA((4,)), DMA((4,)), DMA((3,)), DMA((3,)),
        ]

    def __init__(self, part, at, scratch, strip=16):
        self.part, self.at = part, at
        self.cx, self.out, self.rx, self.total, self.s1, self.r1, self.s2, self.r2 = scratch
        self.strip = strip
        _, self.p, self.c = here()

    def across(self, d):
        spot = self.part.at[self.at(ring(self.p, d), 1 - self.c)]
        return rcopy(spot, self.cx.at[d], self.s1.at[d], self.r1.at[d], head=1 - self.c)

    def over(self, d):
        return rcopy(self.out.at[d - 1], self.rx.at[d - 1], self.s2.at[d - 1], self.r2.at[d - 1], p=ring(self.p, d))

    def strips(self, body):
        def one(i, carry):
            body(pl.ds(pl.multiple_of(i * self.strip, self.strip), self.strip), i * self.strip)
            return carry

        lax.fori_loop(0, self.total.shape[0] // self.strip, one, 0)

    def start(self):
        for d in (2, 1, 3, 0):
            self.across(d).start()

    def middle(self):
        for d in (2, 1, 3, 0):
            self.across(d).wait_recv()
            first = self.at(ring(self.p, d), self.c).start

            def add(rows, at, d=d, first=first):
                own = self.part[pl.ds(pl.multiple_of(first + at, self.strip), self.strip)].astype(f32)
                both = own + self.cx[d, rows].astype(f32)
                if d:
                    self.out[d - 1, rows] = both.astype(bf16)
                else:
                    self.total[rows] = both

            self.strips(add)
            if d:
                self.over(d).start()

    def arrive(self):
        for d in (1, 3, 2):
            self.over(d).wait_recv()

    def sum_of(self, rows):
        return self.total[rows] + self.rx[0, rows].astype(f32) + self.rx[1, rows].astype(f32) + self.rx[2, rows].astype(f32)

    def finish(self):
        for d in range(4):
            self.across(d).wait_send()
        for d in (1, 2, 3):
            self.over(d).wait_send()


def call(body, name_id, outs, out_specs, ins, in_specs, scratch, cost=20_000_000):
    return pl.pallas_call(
        body,
        out_shape=outs,
        in_specs=in_specs,
        out_specs=out_specs,
        scratch_shapes=scratch,
        cost_estimate=pl.CostEstimate(flops=0, bytes_accessed=cost, transcendentals=0),
        compiler_params=pltpu.CompilerParams(
            collective_id=name_id, has_side_effects=True, vmem_limit_bytes=48 * 2**20
        ),
    )(*ins)


def shape(dims, kind):
    return jax.ShapeDtypeStruct(dims, kind)


def exchange_copies(pieces, sems, keep):
    _, p, _ = here()
    away, own = [], []
    for i, (source, width, target, first, led) in enumerate(pieces):
        rows = source.shape[-2]
        spot = target.at[pl.ds(pl.multiple_of(p * rows, 16), rows), pl.ds(first, width)]
        for d in range(G):
            q = ring(p, d)
            taken = source.at[q] if led else source.at[:, pl.ds(pl.multiple_of(q * width, 128), width)]
            if d:
                away.append(rcopy(taken, spot, sems[0].at[d - 1, i], sems[1].at[d - 1, i], p=q))
            else:
                own.append(pltpu.make_async_copy(taken, spot, keep.at[i]))
    return away, own


def exchange_a_body(z_ref, x_ref, q_ref, small_ref, out_ref, send, recv, keep):
    _, p, c = here()
    greet(*[{"p": ring(p, d)} for d in range(1, G)])
    zw, xw, qw, sw = (r.shape[1] // G for r in (z_ref, x_ref, q_ref, q_ref))
    pieces = [
        (z_ref, zw, out_ref, 0, False), (x_ref, xw, out_ref, zw, False),
        (q_ref, qw, out_ref, zw + xw, False), (small_ref, small_ref.shape[2], out_ref, zw + xw + qw, True),
    ]
    away, own = exchange_copies(pieces, (send, recv), keep)
    for copy in away + own:
        copy.start()
    for copy in own + away:
        copy.wait()


def start_body(planes, out_w, o_w, gate_w, up_w, down_w, first, low, wb, wc, wd, n1, ol, *sems):
    z, p, c = here()
    greet(*plane_partners(p, c), *line_partners(z, planes))
    send, recv, keep, rim_s, rim_r = sems[:5]
    rows = first.shape[0]
    a = Spread(first, n1, lambda q, k: slot_at(q, k, rows, RIM), sems[5:10])
    b = Spread(low, ol, lambda q, k: slot_at(q, k, rows), sems[10:15])
    ow, aw, gw, uw, dw = (r.shape[1] // G for r in (out_w, o_w, gate_w, up_w, down_w))
    pieces = [
        (out_w, ow, wb, 0, False), (o_w, aw, wb, ow, False),
        (gate_w, gw, wc, 0, False), (up_w, uw, wc, gw, False), (down_w, dw, wd, 0, False),
    ]
    away, own = exchange_copies(pieces, (send, recv), keep)
    a.start()
    for copy in away + own:
        copy.start()
    b.start()
    a.pass_on()
    a.finish()
    last = n1.at[pl.ds(n1.shape[0] - RIM, RIM)]
    rim = rcopy(last, n1.at[pl.ds(0, RIM)], rim_s, rim_r, z=lax.rem(z + 1, planes))
    rim.start()
    for copy in own + away:
        copy.wait()
    b.pass_on()
    b.finish()
    rim.wait()


def spread_body(block, out, *sems):
    _, p, c = here()
    greet(*plane_partners(p, c))
    rows = block.shape[0]
    s = Spread(block, out, lambda q, k: pl.ds(pl.multiple_of((k * G + q) * rows, 16), rows), sems)
    s.start()
    s.pass_on()
    s.finish()


def line_body(planes, upward, state, factor, states, factors, s1, r1, s2, r2):
    z, _, _ = here()
    greet(*line_partners(z, planes))
    way = 1 if upward else -1

    def pair(d):
        to = lax.rem(z + way * d + planes, planes)
        return (
            rcopy(state, states.at[d - 1], s1.at[d - 1], r1.at[d - 1], z=to),
            rcopy(factor, factors.at[d - 1], s2.at[d - 1], r2.at[d - 1], z=to),
        )

    for d in range(1, planes):
        @pl.when((z + d < planes) if upward else (z - d >= 0))
        def _():
            for copy in pair(d):
                copy.start()

    for d in range(1, planes):
        @pl.when((z - d >= 0) if upward else (z + d < planes))
        def _():
            for copy in pair(d):
                copy.wait_recv()

        @pl.when((z + d < planes) if upward else (z - d >= 0))
        def _():
            for copy in pair(d):
                copy.wait_send()


def hidden_body(part, x_ref, gain, hidden, second, *scratch):
    _, p, c = here()
    greet(*plane_partners(p, c))
    rows = x_ref.shape[0]
    at = lambda q, k: slot_at(q, k, rows)
    s = Collect(part, at, scratch[:8])
    stage = scratch[8]
    s.start()
    s.middle()
    s.arrive()

    def one(r, _):
        h = x_ref[r] + s.sum_of(r)
        hidden[r] = h
        scale = lax.rsqrt(jnp.mean(h * h, axis=-1, keepdims=True) + norm_eps)
        stage[r] = (h * scale * gain[...]).astype(bf16)

    s.strips(one)
    g = Spread(stage, second, at, scratch[9:14])
    g.start()
    g.pass_on()
    s.finish()
    g.finish()


def branch_body(part, hidden, cot, gain, d_hidden, gain_grad, branch, *scratch):
    _, p, c = here()
    greet(*plane_partners(p, c))
    rows = hidden.shape[0]
    at = lambda q, k: slot_at(q, k, rows)
    s = Collect(part, at, scratch[:8])
    stage = scratch[8]
    gain_grad[...] = jnp.zeros_like(gain_grad)
    s.start()
    s.middle()
    s.arrive()

    def one(r, _):
        h = hidden[r]
        scale = lax.rsqrt(jnp.mean(h * h, axis=-1, keepdims=True) + norm_eps)
        grad = s.sum_of(r)
        gain_grad[pl.ds(0, 1)] += jnp.sum(grad * h * scale, axis=0, keepdims=True)
        u = grad * gain[...]
        d = cot[r] + scale * u - h * (scale * scale * scale * jnp.mean(u * h, axis=-1, keepdims=True))
        d_hidden[r] = d
        stage[r] = d.astype(bf16)

    s.strips(one)
    g = Spread(stage, branch, at, scratch[9:14])
    g.start()
    g.pass_on()
    s.finish()
    g.finish()


def final_body(planes, part, x_ref, d_hidden, layer, gain, small, grad_in, layer_out, sums, *scratch):
    z, p, c = here()
    greet(*plane_partners(p, c), *line_partners(z, planes))
    rows = x_ref.shape[0]
    at = lambda q, k: slot_at(q, k, rows)
    s = Collect(part, at, scratch[:8])
    stage, mine, others, zs, zr, es, er, ek = scratch[8:16]
    half = pl.ds(pl.multiple_of(c * rows, 16), rows)

    def halves(i, source, target):
        return (
            rcopy(source, target.at[half], es.at[i], er.at[i], head=1 - c),
            pltpu.make_async_copy(source, target.at[half], ek.at[i]),
        )

    s.start()
    first = halves(0, layer, layer_out)
    for copy in first:
        copy.start()
    mine[...] = small[...]
    s.middle()
    s.arrive()

    def one(r, _):
        v = x_ref[r]
        scale = lax.rsqrt(jnp.mean(v * v, axis=-1, keepdims=True) + norm_eps)
        grad = s.sum_of(r)
        mine[pl.ds(3, 1)] += jnp.sum(grad * v * scale, axis=0, keepdims=True)
        u = grad * gain[...]
        stage[r] = d_hidden[r] + scale * u - v * (scale * scale * scale * jnp.mean(u * v, axis=-1, keepdims=True))

    s.strips(one)
    second = halves(1, stage, grad_in)
    for copy in second:
        copy.start()
    lines = [
        rcopy(mine, others.at[d - 1], zs.at[d - 1], zr.at[d - 1], z=lax.rem(z + d, planes)) for d in range(1, planes)
    ]
    for copy in lines:
        copy.start()
    for copy in lines:
        copy.wait()
    total = mine[...]
    for d in range(1, planes):
        total = total + others[d - 1]
    mine[...] = total
    g = Spread(mine, sums, lambda q, k: q * 2 + k, scratch[16:21])
    g.start()
    g.pass_on()
    s.finish()
    for copy in first + second:
        copy.wait()
    g.finish()


def back_body(planes, dbc, dkv, d_silu_bc, gx, g_bc, rim_bc, rim_x, kv_out, *scratch):
    z, p, c = here()
    greet(*plane_partners(p, c), *line_partners(z, planes))
    (cx, bx, rbc, skv, rkv, zkv, acc, xs, xr, bs, br, ks, kr, zs, zr, ms, mr) = scratch
    rows = rbc.shape[1]
    across = rcopy(
        dbc.at[pl.ds(pl.multiple_of((1 - c) * G * rows, 16), G * rows)], cx, xs, xr, head=1 - c
    )
    across.start()
    kv_over = [rcopy(dkv.at[ring(p, d)], rkv.at[d - 1], ks.at[d - 1], kr.at[d - 1], p=ring(p, d)) for d in (1, 2, 3)]
    for copy in kv_over:
        copy.start()
    across.wait_recv()
    bc_over = []
    for d in (1, 2, 3, 0):
        q = ring(p, d)
        own = dbc[pl.ds(pl.multiple_of((c * G + q) * rows, 16), rows)].astype(f32)
        own = own + cx[pl.ds(pl.multiple_of(q * rows, 16), rows)].astype(f32)
        if d:
            bx[d - 1] = own.astype(bf16)
            bc_over.append(rcopy(bx.at[d - 1], rbc.at[d - 1], bs.at[d - 1], br.at[d - 1], p=q))
            bc_over[-1].start()
        else:
            acc[...] = own
    for copy in kv_over:
        copy.wait_recv()

    def add_kv(i, carry):
        v = dkv[p, i].astype(f32)
        for d in range(3):
            v = v + rkv[d, i].astype(f32)
        skv[i] = v.astype(bf16)
        return carry

    lax.fori_loop(0, planes, add_kv, 0)

    def kv_down(d):
        to = lax.rem(z - d + planes, planes)
        return rcopy(skv.at[to], zkv.at[d - 1], zs.at[d - 1], zr.at[d - 1], z=to)

    for d in range(1, planes):
        @pl.when(z - d >= 0)
        def _():
            kv_down(d).start()

    for copy in bc_over:
        copy.wait_recv()
    g = acc[...]
    for d in range(3):
        g = g + rbc[d].astype(f32)
    g_bc[...] = g * d_silu_bc[...]
    before = lax.rem(z - 1 + planes, planes)
    rims = [
        rcopy(g_bc.at[:, pl.ds(0, 128)], rim_bc, ms.at[0], mr.at[0], z=before),
        rcopy(gx, rim_x, ms.at[1], mr.at[1], z=before),
    ]
    for copy in rims:
        copy.start()
    kv_out[...] = skv[z].astype(f32)
    for d in range(1, planes):
        @pl.when(z + d < planes)
        def _():
            kv_down(d).wait_recv()
            kv_out[...] += zkv[d - 1].astype(f32)

        @pl.when(z - d >= 0)
        def _():
            kv_down(d).wait_send()

    for copy in rims:
        copy.wait()
    across.wait_send()
    for copy in kv_over + bc_over:
        copy.wait_send()


def dot(a, b, ca, cb):
    return lax.dot_general(a, b, (((ca,), (cb,)), ((), ())), preferred_element_type=f32)


def exact(text, *operands):
    return jnp.einsum(text, *operands, precision=highest, preferred_element_type=f32)


def d_silu(v):
    s = jax.nn.sigmoid(v)
    return s * (1.0 + v * (1.0 - s))


def shifted(block, axis, distance):
    count = lax.axis_size(axis)
    route = [(i - distance, i) for i in range(count) if 0 <= i - distance < count]
    return lax.ppermute(block, axis, route)


def rope_tables(offsets, first, count):
    half = HD // 2
    index = (first + jnp.arange(count)).astype(f32)
    freqs = rope_base ** (-2.0 * index / HD)
    angles = offsets.astype(f32)[:, None] * freqs[None, :]
    return jnp.cos(angles), jnp.sin(angles)


def turn(v, cosine, sine):
    half = v.shape[-1] // 2
    a, b = v[:, :half], v[:, half:]
    return jnp.concatenate([a * cosine - b * sine, b * cosine + a * sine], axis=-1)


def conv_parts(padded, starts, places):
    length = starts.shape[0]
    parts = []
    for lag in range(K):
        valid = (places - (K - 1 - lag) >= starts)[:, None]
        parts.append(jnp.where(valid, padded[lag : lag + length], 0.0))
    return parts


def conv_back(grad, grad_next, padded, taps, starts, places, starts_next):
    length = starts.shape[0]
    edge = K - 1
    longer = jnp.concatenate([grad, grad_next], axis=0)
    starts_long = jnp.concatenate([starts, starts_next])
    total = jnp.zeros_like(grad)
    tap_grads = []
    for lag in range(K):
        ahead = edge - lag
        seen = (places >= starts_long[ahead : ahead + length])[:, None]
        total = total + jnp.where(seen, longer[ahead : ahead + length], 0.0) * taps[lag][None, :]
        valid = (places - ahead >= starts)[:, None]
        tap_grads.append(jnp.sum(jnp.where(valid, grad, 0.0) * padded[lag : lag + length], axis=0))
    return total, jnp.stack(tap_grads)


def mixer_row(v):
    return v.reshape(1, -1)


def on_device(
    layer_input, doc_start, mixer_gain, ffn_gain,
    z_weight, x_weight, bc_weight, dt_weight, q_weight, k_weight, v_weight,
    o_weight, out_weight, gate_weight, up_weight, down_weight,
    conv_inner, conv_state, decay_log, dt_bias, skip_coef, ssm_gain, cotangent,
):
    tokens, width = layer_input.shape
    rows = z_weight.shape[0]
    planes = lax.axis_size("z")
    cores = lax.axis_size("head")
    zi, pi, hi = (lax.axis_index(a) for a in ("z", "p", "head"))
    T = tokens * G
    total_tokens = T * planes
    offset = zi * T
    places = offset + jnp.arange(T, dtype=jnp.int32)
    all_starts = lax.all_gather(doc_start, ("z", "p"), axis=0, tiled=True)
    starts = lax.dynamic_slice_in_dim(all_starts, offset, T, 0)
    own = tokens // cores
    heads = decay_log.shape[0] // G
    chan = heads * P_SIZE
    bcs = 2 * N // cores // G
    quarter_half = HD // 2 // G

    def my_slice(v, size, index, axis):
        return lax.dynamic_slice_in_dim(v, index * size, size, axis)

    taps_inner = my_slice(conv_inner, chan, pi, 1)
    taps_state = my_slice(conv_state, bcs, hi * G + pi, 1)
    rates = my_slice(decay_log, heads, pi, 0)
    bias = my_slice(dt_bias, heads, pi, 0)
    skip = my_slice(skip_coef, heads, pi, 0)
    gain_s = my_slice(ssm_gain, chan, pi, 0)

    def cut(w):
        return w.reshape(rows, G, -1)

    bc_mine = lax.dynamic_slice_in_dim(bc_weight, hi * (2 * N // cores), 2 * N // cores, 1)
    k_cut = jnp.moveaxis(k_weight.reshape(rows, 2, G, quarter_half), 2, 1).reshape(rows, G, -1)
    a_sizes = [chan, chan, HD, bcs, 2 * quarter_half, 2 * quarter_half, heads]
    a_at = [sum(a_sizes[:i]) for i in range(len(a_sizes))]
    pad = -sum(a_sizes) % 128
    small_w = jnp.concatenate(
        [cut(bc_mine), k_cut, cut(v_weight), cut(dt_weight), jnp.zeros((rows, G, pad), bf16)], axis=2
    )
    small_w = jnp.moveaxis(small_w, 1, 0)
    a_cols = sum(a_sizes) + pad

    def gather(w):
        return lax.all_gather(w, "z", axis=0, tiled=True)

    exchange_sems = lambda n: [DMA((3, n)), DMA((3, n)), DMA((n,))]
    wa = gather(call(
        exchange_a_body, 0, shape((G * rows, a_cols), bf16), HBM,
        (z_weight, x_weight, q_weight, small_w), [HBM] * 4, exchange_sems(4),
    ))

    def half(v):
        return lax.dynamic_slice_in_dim(v, hi * own, own, 0)

    x_own, cot_own = half(layer_input), half(cotangent)
    r1 = lax.rsqrt(jnp.mean(x_own * x_own, axis=-1, keepdims=True) + norm_eps)
    first_own = (x_own * r1 * mixer_gain).astype(bf16)
    wb, wc, wd, first_rim, out_low = call(
        functools.partial(start_body, planes), 1,
        (shape((G * rows, chan + HD), bf16), shape((G * rows, gate_weight.shape[1] * 2 // G), bf16),
         shape((G * rows, down_weight.shape[1] // G), bf16), shape((RIM + T, width), bf16), shape((T, width), bf16)),
        (HBM,) * 5,
        (out_weight, o_weight, gate_weight, up_weight, down_weight, first_own, cot_own.astype(bf16)),
        [HBM] * 5 + [VMEM] * 2,
        exchange_sems(5) + [DMA(()), DMA(())] + Spread.sems * 2, cost=150_000_000,
    )
    wb, wc, wd = gather(wb), gather(wc), gather(wd)
    first = first_rim[RIM:]

    def scatter(grad):
        g = lax.psum_scatter(grad.astype(bf16), "z", scatter_dimension=0, tiled=True)
        g = lax.all_to_all(g.reshape(G, rows, -1), "p", 0, 0, tiled=True)
        return jnp.moveaxis(g, 0, 1).astype(f32)

    edge = K - 1
    pa = dot(first_rim, wa, 1, 0)
    rim_seen = jnp.where(zi > 0, pa[RIM - edge : RIM], 0.0)
    z_part, inner_pre, q_proj, bc_pre, k_proj, v_proj, step_raw = (
        pa[RIM:, a : a + s] for a, s in zip(a_at, a_sizes)
    )
    pad_inner = jnp.concatenate([rim_seen[:, a_at[1] : a_at[1] + chan], inner_pre], axis=0)
    pad_bc = jnp.concatenate([rim_seen[:, a_at[3] : a_at[3] + bcs], bc_pre], axis=0)
    cv_x = sum(p * t[None, :] for p, t in zip(conv_parts(pad_inner, starts, places), taps_inner))
    cv_bc = sum(p * t[None, :] for p, t in zip(conv_parts(pad_bc, starts, places), taps_state))
    conv_x = jax.nn.silu(cv_x)
    bc_low = jax.nn.silu(cv_bc).astype(bf16)
    bc_t = call(spread_body, 2, shape((2 * N, T), bf16), HBM, (bc_low.T,), [HBM], Spread.sems)
    bc_all = bc_t.T
    step = jax.nn.softplus(step_raw + bias)
    log_decay = -jnp.exp(rates) * step

    L = CHUNK
    nc = T // L
    lower = (jnp.arange(L)[:, None] >= jnp.arange(L)[None, :]).astype(f32)
    b_rows = bc_all[:, :N].astype(f32).reshape(nc, L, N)
    c_rows = bc_all[:, N:].astype(f32).reshape(nc, L, N)

    def by_head(v):
        return v.reshape(nc, L, heads, P_SIZE).transpose(0, 2, 1, 3)

    def by_token(v):
        return v.transpose(0, 2, 1, 3).reshape(T, chan)

    xh = by_head(conv_x)
    step_h = step.reshape(nc, L, heads).transpose(0, 2, 1)
    la_h = log_decay.reshape(nc, L, heads).transpose(0, 2, 1)
    cs = exact("ij,chj->chi", lower, la_h)
    st = starts.reshape(nc, L)
    pl_ = places.reshape(nc, L)
    visible = (st[:, :, None] <= pl_[:, None, :]) & (pl_[:, None, :] <= pl_[:, :, None])
    span = cs[:, :, :, None] - cs[:, :, None, :]
    weights = jnp.where(visible[:, None], jnp.exp(jnp.where(visible[:, None], span, 0.0)), 0.0)
    inter = exact("cin,cjn->cij", c_rows, b_rows)
    mix = weights * inter[:, None]
    driven = xh * step_h[..., None]
    carried = (st < pl_[:, :1]).astype(f32)
    decay_in = jnp.exp(cs) * carried[:, None, :]
    closing = jnp.where((st[:, -1:] <= pl_)[:, None, :], jnp.exp(cs[:, :, -1:] - cs), 0.0)
    dtot = decay_in[:, :, -1]
    local = exact("chjp,cjn->chpn", driven * closing[..., None], b_rows)
    entering = []
    state = jnp.zeros((heads, P_SIZE, N), f32)
    through = jnp.ones((heads,), f32)
    reach = []
    for c in range(nc):
        entering.append(state)
        reach.append(through)
        state = state * dtot[c][:, None, None] + local[c]
        through = through * dtot[c]

    def line(upward, state, name_id):
        flat = jnp.broadcast_to(jnp.pad(through, (0, 8 - heads))[:, None], (8, 128))
        states, factors = call(
            functools.partial(line_body, planes, upward), name_id,
            (shape((planes - 1, chan, N), bf16), shape((planes - 1, 8, 128), f32)), (HBM, HBM),
            (state.reshape(chan, N).astype(bf16), flat), [HBM, HBM],
            [DMA((planes - 1,)) for _ in range(4)],
        )
        total = jnp.zeros((heads, P_SIZE, N), f32)
        for d in reversed(range(1, planes)):
            there = (zi - d >= 0) if upward else (zi + d < planes)
            new = total * factors[d - 1, :heads, :1][:, :, None] + states[d - 1].reshape(heads, P_SIZE, N).astype(f32)
            total = jnp.where(there, new, total)
        return total

    before = line(True, state, 3)
    state_in = jnp.stack([s + before * r[:, None, None] for s, r in zip(entering, reach)])
    y_off = exact("cin,chpn->chip", c_rows, state_in) * decay_in[..., None]
    y_scan = exact("chij,chjp->chip", mix, driven) + y_off
    y_h = y_scan + skip[None, :, None, None] * xh

    ssm = by_token(y_h)
    same_head = (jnp.arange(chan)[:, None] // P_SIZE == jnp.arange(heads)[None, :]).astype(f32)

    def head_mean(v):
        return jnp.repeat(jnp.mean(v.reshape(T, heads, P_SIZE), axis=-1), P_SIZE, axis=1)

    sz = jax.nn.silu(z_part)
    gated = ssm * sz
    r_s = lax.rsqrt(head_mean(gated * gated) + norm_eps)
    ssm_low = (gated * r_s * gain_s).astype(bf16)

    offsets = places - starts
    cos_q, sin_q = rope_tables(offsets, 0, HD // 2)
    cos_k, sin_k = rope_tables(offsets, pi * quarter_half, quarter_half)
    scale = HD ** (-0.5)
    query = (turn(q_proj, cos_q, sin_q) * scale).astype(bf16)
    kv_own = jnp.concatenate([turn(k_proj, cos_k, sin_k).astype(bf16), v_proj.astype(bf16)], axis=1)
    kv_all = lax.all_gather(kv_own.T, ("z", "p"), axis=0).reshape(planes, G, 4, quarter_half, T)
    keys = kv_all[:, :, :2].transpose(0, 4, 2, 1, 3).reshape(total_tokens, HD)
    values = kv_all[:, :, 2:].transpose(0, 4, 1, 2, 3).reshape(total_tokens, HD)
    key_len = min(512, total_tokens)
    first_block = starts[0] // key_len
    last_block = (offset + T - 1) // key_len

    def key_block(index):
        begin = index * key_len
        kb = lax.dynamic_slice_in_dim(keys, begin, key_len, 0)
        vb = lax.dynamic_slice_in_dim(values, begin, key_len, 0)
        at = begin + jnp.arange(key_len, dtype=jnp.int32)
        seen = (at[None, :] >= starts[:, None]) & (at[None, :] <= places[:, None])
        return kb, vb, seen, dot(query, kb, 1, 1)

    def running(index, carry):
        peak, mass = carry
        _, _, seen, scores = key_block(index)
        new = jnp.maximum(peak, jnp.max(jnp.where(seen, scores, -1e30), axis=-1))
        mass = mass * jnp.exp(peak - new) + jnp.sum(jnp.where(seen, jnp.exp(scores - new[:, None]), 0.0), axis=-1)
        return new, mass

    peak, mass = lax.fori_loop(
        first_block, last_block + 1, running, (jnp.full((T,), -1e30, f32), jnp.zeros((T,), f32))
    )
    log_mass = peak + jnp.log(mass)

    def weighted(index, total):
        _, vb, seen, scores = key_block(index)
        probs = jnp.where(seen, jnp.exp(scores - log_mass[:, None]), 0.0).astype(bf16)
        return total + dot(probs, vb, 1, 0)

    attended = lax.fori_loop(first_block, last_block + 1, weighted, jnp.zeros((T, HD), f32))
    att_low = attended.astype(bf16)

    both_low = jnp.concatenate([ssm_low, att_low], axis=1)
    collect = Collect.scratch(own, width) + [pltpu.VMEM((own, width), bf16)] + Spread.sems
    hidden, second = call(
        hidden_body, 4, (shape((own, width), f32), shape((T, width), bf16)), (VMEM, HBM),
        (dot(both_low, wb, 1, 1).astype(bf16), x_own, mixer_row(ffn_gain)), [VMEM] * 3, collect,
    )
    pc = dot(second, wc, 1, 0)
    ff = pc.shape[1] // 2
    gate_pre, up_pre = pc[:, :ff], pc[:, ff:]
    s_gate = jax.nn.silu(gate_pre)
    act_low = (s_gate * up_pre).astype(bf16)
    layer_own = hidden + lax.psum_scatter(
        dot(act_low, wd, 1, 1).astype(bf16), ("p", "head"), scatter_dimension=0, tiled=True
    ).astype(f32)

    grad_d = dot(out_low, act_low, 0, 0)
    d_act = dot(out_low, wd, 1, 0)
    gu_low = jnp.concatenate([d_act * up_pre * d_silu(gate_pre), d_act * s_gate], axis=1).astype(bf16)
    grad_c = dot(second, gu_low, 0, 0)
    d_hidden, grad_ffn, branch = call(
        branch_body, 5, (shape((own, width), f32), shape((8, width), f32), shape((T, width), bf16)), (VMEM, VMEM, HBM),
        (dot(gu_low, wc, 1, 1).astype(bf16), hidden, cot_own, mixer_row(ffn_gain)), [VMEM] * 4, collect,
    )
    grad_b = dot(branch, both_low, 0, 0)
    d_both = dot(branch, wb, 1, 0)
    d_norm_s, d_att = d_both[:, :chan], d_both[:, chan:].astype(bf16)

    grad_gain_s = jnp.sum(d_norm_s * gated * r_s, axis=0)
    u_s = d_norm_s * gain_s
    d_gated = r_s * u_s - gated * r_s**3 * head_mean(u_s * gated)
    d_z = d_gated * ssm * d_silu(z_part)
    dy = by_head(d_gated * sz)
    dy_in = dy * decay_in[..., None]
    from_chunk = exact("chip,cin->chpn", dy_in, c_rows)
    zero_state = jnp.zeros((heads, P_SIZE, N), f32)
    g = zero_state
    leaving = [None] * nc
    for c in reversed(range(nc)):
        leaving[c] = g
        g = g * dtot[c][:, None, None] + from_chunk[c]
    after = line(False, g, 6)
    scale_c = jnp.ones((heads,), f32)
    d_state = [None] * nc
    for c in reversed(range(nc)):
        d_state[c] = leaving[c] + after * scale_c[:, None, None]
        scale_c = scale_c * dtot[c]
    d_state = jnp.stack(d_state)
    d_mix = exact("chip,chjp->chij", dy, driven)
    d_inter = jnp.sum(weights * d_mix, axis=1)
    d_c = exact("cij,cjn->cin", d_inter, b_rows) + exact("chip,chpn->cin", dy_in, state_in)
    closed = driven * closing[..., None]
    d_b = exact("cij,cin->cjn", d_inter, c_rows) + exact("chpn,chjp->cjn", d_state, closed)
    d_driven = exact("chij,chip->chjp", mix, dy) + closing[..., None] * exact("chpn,cjn->chjp", d_state, b_rows)
    d_closing = jnp.sum(closed * exact("chpn,cjn->chjp", d_state, b_rows), axis=-1)
    d_cs = jnp.sum(dy * y_scan, axis=-1) - jnp.sum(driven * d_driven, axis=-1)
    d_total = jnp.sum(d_closing, axis=-1) + dtot * jnp.sum(d_state * state_in, axis=(2, 3))
    d_la = exact("ji,chj->chi", lower, d_cs) + d_total[:, :, None]
    d_step = jnp.sum(d_driven * xh, axis=-1)
    dx = by_token(d_driven * step_h[..., None] + skip[None, :, None, None] * dy)
    grad_skip = jnp.sum(dy * xh, axis=(0, 2, 3))
    d_raw = (d_step - jnp.exp(rates)[None, :, None] * d_la).transpose(0, 2, 1).reshape(T, heads)
    d_raw = d_raw * jax.nn.sigmoid(step_raw + bias)
    grad_bias = jnp.sum(d_raw, axis=0)
    grad_rates = jnp.sum(d_la * la_h, axis=(0, 2))
    d_bc_all = jnp.concatenate([d_b.reshape(T, N), d_c.reshape(T, N)], axis=1).astype(bf16)
    gx = dx * d_silu(cv_x)
    balance = jnp.sum(d_att.astype(f32) * attended, axis=-1, keepdims=True)

    def grads(index, carry):
        d_query, d_keys, d_values = carry
        kb, vb, seen, scores = key_block(index)
        probs = jnp.where(seen, jnp.exp(scores - log_mass[:, None]), 0.0)
        d_scores = (probs * (dot(d_att, vb, 1, 1) - balance)).astype(bf16)
        d_query = d_query + dot(d_scores, kb, 1, 0)
        d_keys = lax.dynamic_update_slice_in_dim(d_keys, dot(d_scores, query, 0, 0), index * key_len, 0)
        d_values = lax.dynamic_update_slice_in_dim(d_values, dot(probs.astype(bf16), d_att, 0, 0), index * key_len, 0)
        return d_query, d_keys, d_values

    zero_keys = jnp.zeros((total_tokens, HD), f32)
    d_query, d_keys, d_values = lax.fori_loop(
        first_block, last_block + 1, grads, (jnp.zeros((T, HD), f32), zero_keys, zero_keys)
    )
    dk_cut = d_keys.astype(bf16).reshape(planes, T, 2, G, quarter_half).transpose(3, 0, 2, 4, 1)
    dv_cut = d_values.astype(bf16).reshape(planes, T, G, 2, quarter_half).transpose(2, 0, 3, 4, 1)
    dkv = jnp.concatenate([dk_cut, dv_cut], axis=2).reshape(G, planes, 4 * quarter_half, T)
    kvr = 4 * quarter_half
    gx_first = gx[:RIM]
    g_bc, rim_bc, rim_x, dkv = call(
        functools.partial(back_body, planes), 7,
        (shape((bcs, T), f32), shape((bcs, 128), f32), shape((RIM, chan), f32), shape((kvr, T), f32)), (VMEM,) * 4,
        (d_bc_all.T, dkv, d_silu(cv_bc).T, gx_first), [VMEM] * 4,
        [pltpu.VMEM((G * bcs, T), bf16), pltpu.VMEM((3, bcs, T), bf16), pltpu.VMEM((3, bcs, T), bf16),
         pltpu.VMEM((planes, kvr, T), bf16), pltpu.VMEM((3, planes, kvr, T), bf16), pltpu.VMEM((planes - 1, kvr, T), bf16),
         pltpu.VMEM((bcs, T), f32), DMA(()), DMA(()), DMA((3,)), DMA((3,)), DMA((3,)), DMA((3,)),
         DMA((planes - 1,)), DMA((planes - 1,)), DMA((2,)), DMA((2,))],
    )
    dkv = dkv.T
    later = zi < planes - 1
    gx_next = jnp.where(later, rim_x[:edge], 0.0)
    gb_next = jnp.where(later, rim_bc[:, :edge].T, 0.0)
    ends = jnp.minimum(offset + T + jnp.arange(edge), total_tokens - 1)
    starts_next = jnp.where(later, all_starts[ends], total_tokens)
    d_inner_pre, grad_conv_inner = conv_back(gx, gx_next, pad_inner, taps_inner, starts, places, starts_next)
    d_bc_pre, grad_conv_state = conv_back(g_bc.T, gb_next, pad_bc, taps_state, starts, places, starts_next)
    d_q = turn(d_query, cos_q, -sin_q) * scale
    d_k = turn(dkv[:, : 2 * quarter_half], cos_k, -sin_k)
    d_v = dkv[:, 2 * quarter_half :]

    da_low = jnp.concatenate(
        [d_z, d_inner_pre, d_q, d_bc_pre, d_k, d_v, d_raw, jnp.zeros((T, pad), f32)], axis=1
    ).astype(bf16)
    grad_a = dot(first, da_low, 0, 0)
    small = [grad_conv_inner, grad_conv_state, grad_rates, grad_bias, grad_skip, grad_gain_s]
    at = [0]
    for s in small:
        at.append(at[-1] + s.size)
    flat = jnp.concatenate([s.reshape(-1) for s in small] + [jnp.zeros((2 * width - at[-1],), f32)]).reshape(2, width)
    flat = jnp.concatenate([flat, grad_ffn[:1], jnp.zeros((5, width), f32)], axis=0)
    grad_input, layer_out, sums = call(
        functools.partial(final_body, planes), 8,
        (shape((tokens, width), f32), shape((tokens, width), f32), shape((2 * G, 8, width), f32)), (HBM, HBM, VMEM),
        (dot(da_low, wa, 1, 1).astype(bf16), x_own, d_hidden, layer_own, mixer_row(mixer_gain), flat), [VMEM] * 6,
        Collect.scratch(own, width)
        + [pltpu.VMEM((own, width), f32), pltpu.VMEM((8, width), f32), pltpu.VMEM((planes - 1, 8, width), f32),
           DMA((planes - 1,)), DMA((planes - 1,)), DMA((2,)), DMA((2,)), DMA((2,))]
        + Spread.sems,
    )

    ga, gb, gc, gd = (scatter(g) for g in (grad_a, grad_b, grad_c, grad_d))
    g_z, g_x, g_q, g_bc, g_k, g_v, g_dt = (ga[:, :, a : a + s] for a, s in zip(a_at, a_sizes))
    g_k = jnp.moveaxis(g_k.reshape(rows, G, 2, quarter_half), 1, 2)
    g_bc = lax.all_gather(g_bc.reshape(rows, -1).astype(bf16), "head", axis=1, tiled=True).astype(f32)

    sums = sums.reshape(G, cores, 8, width)
    every = sums[:, :, :2].reshape(G, cores, 2 * width)
    mine = lax.dynamic_index_in_dim(every, hi, 1, False)
    pieces = [mine[:, a:b] for a, b in zip(at, at[1:])]
    o_conv_inner = jnp.moveaxis(pieces[0].reshape(G, K, chan), 0, 1).reshape(K, G * chan)
    o_conv_state = every[:, :, at[1] : at[2]].reshape(G, cores, K, bcs).transpose(2, 1, 0, 3).reshape(K, 2 * N)
    per = width // (planes * G)
    gains = lax.dynamic_slice_in_dim(jnp.sum(sums[:, :, 2:4], axis=(0, 1)), (zi * G + pi) * per, per, 1)
    gains = (gains[1], gains[0])

    def whole(g):
        return g.reshape(rows, -1)

    return (
        layer_out, grad_input, gains[0], gains[1],
        whole(g_z), whole(g_x), g_bc, whole(g_dt), whole(g_q), whole(g_k), whole(g_v),
        whole(gb[:, :, chan:]), whole(gb[:, :, :chan]),
        whole(gc[:, :, :ff]), whole(gc[:, :, ff:]), whole(gd),
        o_conv_inner, o_conv_state,
        pieces[2].reshape(-1), pieces[3].reshape(-1), pieces[4].reshape(-1), pieces[5].reshape(-1),
    )


def solution(mesh):
    seq, cores = mesh.shape["seq"], mesh.shape["head"]
    planes = Mesh(mesh.devices.reshape(seq // G, G, cores), ("z", "p", "head"))
    s = ("z", "p")
    both, row, head, whole = P(s, "head"), P(s, None), P("head"), P()
    placed = (
        row, P(s), whole, whole, both, both, row, both, both, both, both, both, both, both, both, both,
        P(None, "head"), whole, head, head, head, head, row,
    )
    return jax.shard_map(
        on_device,
        mesh=planes,
        in_specs=placed,
        out_specs=(
            row, row, P(s), P(s), both, both, row, both, both, both, both, both, both, both, both, both,
            P(None, "head"), whole, head, head, head, head,
        ),
        check_vma=False,
    )
```

```python
import functools

import jax
import jax.numpy as jnp
from jax import lax
from jax.experimental import pallas as pl
from jax.experimental.pallas import tpu as pltpu
from jax.sharding import Mesh, PartitionSpec as P

P_SIZE = 64
N = 256
HD = 128
K = 4
G = 4
CHUNK = 128
RIM = 16

highest = lax.Precision.HIGHEST
rope_base = 10000.0
norm_eps = 1e-05
bf16 = jnp.bfloat16
f32 = jnp.float32
MESH = pl.DeviceIdType.MESH
HBM = pl.BlockSpec(memory_space=pl.ANY)
VMEM = pl.BlockSpec(memory_space=pltpu.VMEM)
DMA = pltpu.SemaphoreType.DMA


def rcopy(src, dst, send, recv, **where):
    return pltpu.make_async_remote_copy(
        src_ref=src, dst_ref=dst, send_sem=send, recv_sem=recv, device_id=where, device_id_type=MESH
    )


def here():
    return lax.axis_index("z"), lax.axis_index("p"), lax.axis_index("head")


def ring(p, d):
    return lax.rem(p + d + G, G)


def greet(*partners):
    barrier = pltpu.get_barrier_semaphore()
    for where in partners:
        pl.semaphore_signal(barrier, inc=1, device_id=where, device_id_type=MESH)
    pl.semaphore_wait(barrier, len(partners))


def plane_partners(p, c):
    return [{"p": ring(p, d)} for d in range(1, G)] + [{"head": 1 - c}]


def line_partners(z, planes):
    return [{"z": lax.rem(z + d, planes)} for d in range(1, planes)]


def beside(p):
    return p + 1 - 2 * lax.rem(p, 2), lax.rem(p + 2, G), G - 1 - p


class Spread:
    sems = [DMA((2,)), DMA((2,)), DMA((2,)), DMA((2,)), DMA((4,)), DMA((4,)), DMA(())]

    def __init__(self, block, out, start, rows, sems, cores=True):
        self.block, self.out, self.first, self.rows, self.cores = block, out, start, rows, cores
        self.s1, self.r1, self.s2, self.r2, self.s3, self.r3, self.keep = sems
        _, self.p, self.c = here()
        self.around = beside(self.p)

    def spot(self, q, half=None):
        first, rows = self.first(q, self.c), self.rows
        if half is not None:
            first, rows = first + half * (rows // 2), rows // 2
        return self.out.at[pl.ds(first, rows)]

    def over(self, i):
        return rcopy(self.block, self.spot(self.p), self.s1.at[i], self.r1.at[i], p=self.around[i])

    def relay(self, i):
        spot = self.spot(self.around[i], i)
        return rcopy(spot, spot, self.s2.at[i], self.r2.at[i], p=self.around[1 - i])

    def relayed(self, i):
        spot = self.spot(self.around[2], 1 - i)
        return rcopy(spot, spot, self.s2.at[1 - i], self.r2.at[1 - i], p=self.around[i])

    def across(self, i):
        spot = self.spot(self.p if i == 3 else self.around[i])
        return rcopy(self.block if i == 3 else spot, spot, self.s3.at[i], self.r3.at[i], head=1 - self.c)

    def mine(self):
        return pltpu.make_async_copy(self.block, self.spot(self.p), self.keep)

    def start(self):
        for i in (0, 1):
            self.over(i).start()
        if self.cores:
            self.across(3).start()
        self.mine().start()

    def pass_on(self):
        for i in (0, 1):
            self.over(i).wait_recv()
            self.relay(i).start()
            if self.cores:
                self.across(i).start()
        for i in (0, 1):
            self.relayed(i).wait_recv()
        if self.cores:
            self.across(2).start()

    def finish(self):
        self.mine().wait()
        for i in (0, 1):
            self.over(i).wait_send()
            self.relay(i).wait_send()
        if self.cores:
            for i in range(4):
                self.across(i).wait()


class Collect:
    @staticmethod
    def scratch(rows, width):
        return [
            pltpu.VMEM((4, rows, width), bf16), pltpu.VMEM((3, rows, width), bf16),
            pltpu.VMEM((2, rows // 2, width), bf16), pltpu.VMEM((2, rows, width), bf16),
            pltpu.VMEM((rows, width), f32), DMA((4,)), DMA((4,)), DMA((6,)), DMA((6,)),
        ]

    def __init__(self, part, rows, scratch, strip=16):
        self.part, self.rows, self.strip = part, rows, strip
        self.cx, self.out, self.rd, self.rx, self.total, self.s1, self.r1, self.s2, self.r2 = scratch
        _, self.p, self.c = here()
        self.around = beside(self.p)

    def first(self, q, c):
        return pl.multiple_of((q * 2 + c) * self.rows, 16)

    def owner(self, i):
        return self.p if i == 3 else self.around[i]

    def across(self, i):
        spot = self.part.at[pl.ds(self.first(self.owner(i), 1 - self.c), self.rows)]
        return rcopy(spot, self.cx.at[i], self.s1.at[i], self.r1.at[i], head=1 - self.c)

    def over(self, i, half):
        at = pl.ds(half * (self.rows // 2), self.rows // 2)
        k = 2 * i + half
        if i == 2:
            return rcopy(self.out.at[2, at], self.rd.at[half], self.s2.at[k], self.r2.at[k], p=self.around[half])
        return rcopy(self.out.at[i, at], self.rx.at[i, at], self.s2.at[k], self.r2.at[k], p=self.around[i])

    def strips(self, body, lo=0, hi=None):
        hi = self.rows if hi is None else hi

        def one(n, carry):
            body(lo + n * self.strip)
            return carry

        lax.fori_loop(0, (hi - lo) // self.strip, one, 0)

    def at(self, first):
        return pl.ds(pl.multiple_of(first, self.strip), self.strip)

    def add(self, i, half=None, relayed=None):
        first = self.first(self.owner(i), self.c)
        size = self.rows // 2

        def one(at):
            v = self.part[self.at(first + at)].astype(f32) + self.cx[i, self.at(at)].astype(f32)
            if relayed is not None:
                v = v + self.rd[relayed, self.at(at - half * size)].astype(f32)
            if i == 3:
                self.total[self.at(at)] = v
            else:
                self.out[i, self.at(at)] = v.astype(bf16)

        if half is None:
            self.strips(one)
        else:
            self.strips(one, half * size, (half + 1) * size)

    def start(self):
        for i in (2, 0, 1, 3):
            self.across(i).start()

    def middle(self):
        self.across(2).wait_recv()
        for half in (0, 1):
            self.add(2, half)
            self.over(2, half).start()
        for i in (0, 1):
            self.across(i).wait_recv()
            self.add(i, i)
            self.over(i, i).start()
        self.across(3).wait_recv()
        self.add(3)
        for i in (0, 1):
            self.over(2, 1 - i).wait_recv()
            self.add(i, 1 - i, 1 - i)
            self.over(i, 1 - i).start()

    def arrive(self):
        for half in (0, 1):
            for i in (0, 1):
                self.over(i, i if half == 0 else 1 - i).wait_recv()

    def sum_of(self, at):
        r = self.at(at)
        return self.total[r] + self.rx[0, r].astype(f32) + self.rx[1, r].astype(f32)

    def finish(self):
        for i in range(4):
            self.across(i).wait_send()
        for i in range(3):
            for half in (0, 1):
                self.over(i, half).wait_send()


def call(body, name_id, outs, out_specs, ins, in_specs, scratch, us=20):
    return pl.pallas_call(
        body,
        out_shape=outs,
        in_specs=in_specs,
        out_specs=out_specs,
        scratch_shapes=scratch,
        cost_estimate=pl.CostEstimate(flops=0, bytes_accessed=us * 3_500_000, transcendentals=0),
        compiler_params=pltpu.CompilerParams(
            collective_id=name_id, has_side_effects=True, vmem_limit_bytes=48 * 2**20
        ),
    )(*ins)


def shape(dims, kind):
    return jax.ShapeDtypeStruct(dims, kind)


def exchange_copies(pieces, sems, keep):
    _, p, _ = here()
    away, own = [], []
    for i, (source, width, target, first, led) in enumerate(pieces):
        rows = source.shape[-2]
        spot = target.at[pl.ds(pl.multiple_of(p * rows, 16), rows), pl.ds(first, width)]
        for d in range(G):
            q = ring(p, d)
            taken = source.at[q] if led else source.at[:, pl.ds(pl.multiple_of(q * width, 128), width)]
            if d:
                away.append(rcopy(taken, spot, sems[0].at[d - 1, i], sems[1].at[d - 1, i], p=q))
            else:
                own.append(pltpu.make_async_copy(taken, spot, keep.at[i]))
    return away, own


def exchange_a_body(x_ref, q_ref, small_ref, out_ref, send, recv, keep):
    _, p, c = here()
    greet(*[{"p": ring(p, d)} for d in range(1, G)])
    xw, qw = (r.shape[1] // G for r in (x_ref, q_ref))
    pieces = [
        (x_ref, xw, out_ref, 0, False), (q_ref, qw, out_ref, xw, False),
        (small_ref, small_ref.shape[2], out_ref, xw + qw, True),
    ]
    away, own = exchange_copies(pieces, (send, recv), keep)
    for copy in away + own:
        copy.start()
    for copy in own + away:
        copy.wait()


def exchange_b_body(z_ref, out_ref, o_ref, wb, send, recv, keep):
    _, p, c = here()
    greet(*[{"p": ring(p, d)} for d in range(1, G)])
    zw, ow, aw = (r.shape[1] // G for r in (z_ref, out_ref, o_ref))
    pieces = [(z_ref, zw, wb, 0, False), (out_ref, ow, wb, zw, False), (o_ref, aw, wb, zw + ow, False)]
    away, own = exchange_copies(pieces, (send, recv), keep)
    for copy in away + own:
        copy.start()
    for copy in own + away:
        copy.wait()


def start_body(planes, gate_w, up_w, down_w, first, low, docs, wc, wd, n1, ol, all_docs, *sems):
    z, p, c = here()
    greet(*plane_partners(p, c), *line_partners(z, planes))
    send, recv, keep, rim_s, rim_r, ps, pr, zs, zr, dk = sems[:10]
    rows = first.shape[0]
    a = Spread(first, n1, lambda q, k: pl.multiple_of(RIM + (q * 2 + k) * rows, 16), rows, sems[10:17])
    b = Spread(low, ol, lambda q, k: pl.multiple_of((q * 2 + k) * rows, 16), rows, sems[17:24])
    gw, uw, dw = (r.shape[1] // G for r in (gate_w, up_w, down_w))
    pieces = [(gate_w, gw, wc, 0, False), (up_w, uw, wc, gw, False), (down_w, dw, wd, 0, False)]
    away, own = exchange_copies(pieces, (send, recv), keep)
    near = [rcopy(docs, all_docs.at[z, p], ps.at[d - 1], pr.at[d - 1], p=ring(p, d)) for d in (1, 2, 3)]
    own_docs = pltpu.make_async_copy(docs, all_docs.at[z, p], dk)
    a.start()
    for copy in near:
        copy.start()
    own_docs.start()
    for copy in own:
        copy.start()
    a.pass_on()
    for copy in away:
        copy.start()
    b.start()
    a.finish()
    last = n1.at[pl.ds(n1.shape[0] - RIM, RIM)]
    rim = rcopy(last, n1.at[pl.ds(0, RIM)], rim_s, rim_r, z=lax.rem(z + 1, planes))
    rim.start()
    own_docs.wait()
    for copy in near:
        copy.wait()
    far = [
        rcopy(all_docs.at[z], all_docs.at[z], zs.at[d - 1], zr.at[d - 1], z=lax.rem(z + d, planes)) for d in range(1, planes)
    ]
    for copy in far:
        copy.start()
    b.pass_on()
    for copy in own + away:
        copy.wait()
    b.finish()
    rim.wait()
    for copy in far:
        copy.wait()


def spread_body(planes, block, kv, out, lines, zs, zr, zk, *sems):
    z, p, c = here()
    greet(*plane_partners(p, c), *line_partners(z, planes))
    rows = block.shape[0]
    far = [rcopy(kv, lines.at[z], zs.at[d - 1], zr.at[d - 1], z=lax.rem(z + d, planes)) for d in range(1, planes)]
    keep = pltpu.make_async_copy(kv, lines.at[z], zk)
    for copy in far:
        copy.start()
    keep.start()
    s = Spread(block, out, lambda q, k: pl.multiple_of((k * G + q) * rows, 16), rows, sems)
    s.start()
    s.pass_on()
    s.finish()
    keep.wait()
    for copy in far:
        copy.wait()


def state_copies(planes, upward, state, factor, states, factors, sems):
    z, _, _ = here()
    s1, r1, s2, r2 = sems
    way = 1 if upward else -1

    def pair(d):
        to = lax.rem(z + way * d + planes, planes)
        return (
            rcopy(state, states.at[d - 1], s1.at[d - 1], r1.at[d - 1], z=to),
            rcopy(factor, factors.at[d - 1], s2.at[d - 1], r2.at[d - 1], z=to),
        )

    def start():
        for d in range(1, planes):
            @pl.when((z + d < planes) if upward else (z - d >= 0))
            def _():
                for copy in pair(d):
                    copy.start()

    def wait():
        for d in range(1, planes):
            @pl.when((z - d >= 0) if upward else (z + d < planes))
            def _():
                for copy in pair(d):
                    copy.wait_recv()

            @pl.when((z + d < planes) if upward else (z - d >= 0))
            def _():
                for copy in pair(d):
                    copy.wait_send()

    return start, wait


def up_body(planes, state, factor, lines, states, factors, kv, *sems):
    z, p, c = here()
    greet(*plane_partners(p, c), *line_partners(z, planes))
    start, wait = state_copies(planes, True, state, factor, states, factors, sems[:4])
    start()
    s = Spread(lines, kv, lambda q, k: q * planes, planes, sems[4:], cores=False)
    s.start()
    s.pass_on()
    s.finish()
    wait()


def down_body(planes, state, factor, dkv, states, factors, kv, *sems):
    z, p, c = here()
    greet(*plane_partners(p, c), *line_partners(z, planes))
    start, wait = state_copies(planes, False, state, factor, states, factors, sems[:4])
    start()
    ks, kr, kk = sems[4:]
    over = [rcopy(dkv.at[ring(p, d)], kv.at[d], ks.at[d - 1], kr.at[d - 1], p=ring(p, d)) for d in (1, 2, 3)]
    keep = pltpu.make_async_copy(dkv.at[p], kv.at[0], kk)
    for copy in over:
        copy.start()
    keep.start()
    keep.wait()
    for copy in over:
        copy.wait()
    wait()


def hidden_body(part, x_ref, gain, hidden, second, *scratch):
    _, p, c = here()
    greet(*plane_partners(p, c))
    rows = x_ref.shape[0]
    s = Collect(part, rows, scratch[:9])
    stage = scratch[9]
    s.start()
    s.middle()
    s.arrive()

    def one(at):
        r = s.at(at)
        h = x_ref[r] + s.sum_of(at)
        hidden[r] = h
        scale = lax.rsqrt(jnp.mean(h * h, axis=-1, keepdims=True) + norm_eps)
        stage[r] = (h * scale * gain[...]).astype(bf16)

    s.strips(one)
    g = Spread(stage, second, s.first, rows, scratch[10:17])
    g.start()
    g.pass_on()
    s.finish()
    g.finish()


def branch_body(part, hidden, cot, gain, d_hidden, gain_grad, branch, *scratch):
    _, p, c = here()
    greet(*plane_partners(p, c))
    rows = hidden.shape[0]
    s = Collect(part, rows, scratch[:9])
    stage = scratch[9]
    gain_grad[...] = jnp.zeros_like(gain_grad)
    s.start()
    s.middle()
    s.arrive()

    def one(at):
        r = s.at(at)
        h = hidden[r]
        scale = lax.rsqrt(jnp.mean(h * h, axis=-1, keepdims=True) + norm_eps)
        grad = s.sum_of(at)
        gain_grad[pl.ds(0, 1)] += jnp.sum(grad * h * scale, axis=0, keepdims=True)
        u = grad * gain[...]
        d = cot[r] + scale * u - h * (scale * scale * scale * jnp.mean(u * h, axis=-1, keepdims=True))
        d_hidden[r] = d
        stage[r] = d.astype(bf16)

    s.strips(one)
    g = Spread(stage, branch, s.first, rows, scratch[10:17])
    g.start()
    g.pass_on()
    s.finish()
    g.finish()


def final_body(planes, part, x_ref, d_hidden, layer, gain, small, grad_in, layer_out, sums, *scratch):
    z, p, c = here()
    greet(*plane_partners(p, c), *line_partners(z, planes))
    rows = x_ref.shape[0]
    s = Collect(part, rows, scratch[:9])
    stage, mine, others, zs, zr, es, er, ek = scratch[9:17]
    half = pl.ds(pl.multiple_of(c * rows, 16), rows)

    def halves(i, source, target):
        return (
            rcopy(source, target.at[half], es.at[i], er.at[i], head=1 - c),
            pltpu.make_async_copy(source, target.at[half], ek.at[i]),
        )

    s.start()
    first = halves(0, layer, layer_out)
    for copy in first:
        copy.start()
    mine[...] = small[...]
    s.middle()
    s.arrive()

    def one(at):
        r = s.at(at)
        v = x_ref[r]
        scale = lax.rsqrt(jnp.mean(v * v, axis=-1, keepdims=True) + norm_eps)
        grad = s.sum_of(at)
        mine[pl.ds(3, 1)] += jnp.sum(grad * v * scale, axis=0, keepdims=True)
        u = grad * gain[...]
        stage[r] = d_hidden[r] + scale * u - v * (scale * scale * scale * jnp.mean(u * v, axis=-1, keepdims=True))

    s.strips(one)
    second = halves(1, stage, grad_in)
    for copy in second:
        copy.start()
    lines = [
        rcopy(mine, others.at[d - 1], zs.at[d - 1], zr.at[d - 1], z=lax.rem(z + d, planes)) for d in range(1, planes)
    ]
    for copy in lines:
        copy.start()
    for copy in lines:
        copy.wait()
    total = mine[...]
    for d in range(1, planes):
        total = total + others[d - 1]
    mine[...] = total
    g = Spread(mine, sums, lambda q, k: pl.multiple_of((q * 2 + k) * RIM, RIM), RIM, scratch[17:24])
    g.start()
    g.pass_on()
    s.finish()
    for copy in first + second:
        copy.wait()
    g.finish()


def back_body(planes, dbc, dkv, d_silu_bc, gx, g_bc, rim_bc, rim_x, kv_out, *scratch):
    z, p, c = here()
    greet(*plane_partners(p, c), *line_partners(z, planes))
    (cx, bx, rbc, skv, zkv, acc, xs, xr, bs, br, zs, zr, ms, mr) = scratch
    rows = rbc.shape[1]
    across = rcopy(
        dbc.at[pl.ds(pl.multiple_of((1 - c) * G * rows, 16), G * rows)], cx, xs, xr, head=1 - c
    )
    across.start()

    def add_kv(i, carry):
        v = dkv[0, i].astype(f32)
        for d in (1, 2, 3):
            v = v + dkv[d, i].astype(f32)
        skv[i] = v.astype(bf16)
        return carry

    lax.fori_loop(0, planes, add_kv, 0)

    def kv_down(d):
        to = lax.rem(z - d + planes, planes)
        return rcopy(skv.at[to], zkv.at[d - 1], zs.at[d - 1], zr.at[d - 1], z=to)

    for d in range(1, planes):
        @pl.when(z - d >= 0)
        def _():
            kv_down(d).start()

    across.wait_recv()
    bc_over = []
    for d in (1, 2, 3, 0):
        q = ring(p, d)
        own = dbc[pl.ds(pl.multiple_of((c * G + q) * rows, 16), rows)].astype(f32)
        own = own + cx[pl.ds(pl.multiple_of(q * rows, 16), rows)].astype(f32)
        if d:
            bx[d - 1] = own.astype(bf16)
            bc_over.append(rcopy(bx.at[d - 1], rbc.at[d - 1], bs.at[d - 1], br.at[d - 1], p=q))
            bc_over[-1].start()
        else:
            acc[...] = own
    for copy in bc_over:
        copy.wait_recv()
    g = acc[...]
    for d in range(3):
        g = g + rbc[d].astype(f32)
    g_bc[...] = g * d_silu_bc[...]
    before = lax.rem(z - 1 + planes, planes)
    rims = [
        rcopy(g_bc.at[:, pl.ds(0, 128)], rim_bc, ms.at[0], mr.at[0], z=before),
        rcopy(gx, rim_x, ms.at[1], mr.at[1], z=before),
    ]
    for copy in rims:
        copy.start()
    kv_out[...] = skv[z].astype(f32)
    for d in range(1, planes):
        @pl.when(z + d < planes)
        def _():
            kv_down(d).wait_recv()
            kv_out[...] += zkv[d - 1].astype(f32)

        @pl.when(z - d >= 0)
        def _():
            kv_down(d).wait_send()

    for copy in rims:
        copy.wait()
    across.wait_send()
    for copy in bc_over:
        copy.wait_send()


def mm(a, b, ca, cb):
    return lax.dot_general(a.astype(bf16), b.astype(bf16), (((ca,), (cb,)), ((), ())), preferred_element_type=f32)


def mm_exact(a, b, ca, cb):
    return lax.dot_general(a, b, (((ca,), (cb,)), ((), ())), precision=highest, preferred_element_type=f32)


def iota(dims, axis):
    return lax.broadcasted_iota(jnp.int32, dims, axis)


def soft(v):
    return jnp.maximum(v, 0.0) + jnp.log1p(jnp.exp(-jnp.abs(v)))


def sig(v):
    return 1.0 / (1.0 + jnp.exp(-v))


def rates_of(raw, bias, rates, heads):
    lane = iota((CHUNK, 128), 1)
    step = jnp.where(lane < heads, soft(raw + bias), 0.0)
    log_decay = -jnp.exp(rates) * step
    lower = (iota((CHUNK, CHUNK), 0) >= iota((CHUNK, CHUNK), 1)).astype(f32)
    return step, log_decay, mm_exact(lower, log_decay, 1, 0)


def pair_of(v, pair):
    left = iota((CHUNK, 128), 1) < P_SIZE
    return jnp.where(left, v[:, 2 * pair : 2 * pair + 1], v[:, 2 * pair + 1 : 2 * pair + 2])


def lanes(v, pair):
    return v[:, pair * 128 : (pair + 1) * 128]


def halves_of(a, b):
    return jnp.where(iota(a.shape, 1) < P_SIZE, a, b)


def head_means(v):
    same = (iota((128, 128), 0) // P_SIZE == iota((128, 128), 1) // P_SIZE).astype(f32) / P_SIZE
    return jnp.concatenate([mm_exact(lanes(v, k), same, 1, 0) for k in range(v.shape[1] // 128)], axis=1)


def head_sums(v, heads):
    chan = v.shape[1]
    pick = (iota((chan, 128), 0) // P_SIZE == iota((chan, 128), 1)).astype(f32)
    return mm_exact(v, pick, 1, 0)


def scale_rows(v, factor, heads):
    return jnp.concatenate(
        [v[h * P_SIZE : (h + 1) * P_SIZE] * factor[h : h + 1, :1] for h in range(heads)], axis=0
    )


def conv_of(pa_ref, taps_ref, starts, place, c, chan, first):
    block = pa_ref[pl.ds(pl.multiple_of(c * CHUNK + RIM - 8, 8), CHUNK + 8), first : first + chan]
    total = jnp.zeros((CHUNK, chan), f32)
    for lag in range(K):
        back = K - 1 - lag
        total = total + jnp.where(place - back >= starts, block[8 - back : 8 - back + CHUNK] * taps_ref[lag : lag + 1], 0.0)
    return total


def places_of(base_ref, c):
    return base_ref[0] + c * CHUNK + iota((CHUNK, 1), 0)


def weights_of(h, cs, cs_t, visible):
    span = cs[:, h : h + 1] - cs_t[h : h + 1]
    return jnp.where(visible, jnp.exp(jnp.where(visible, span, 0.0)), 0.0)


def visible_of(base_ref, c, starts, place):
    across = base_ref[0] + c * CHUNK + iota((CHUNK, CHUNK), 1)
    return (starts <= across) & (across <= place)


def decays_of(cs, starts, place):
    first = place[:1]
    decay_in = jnp.where(starts < first, jnp.exp(cs), 0.0)
    closing = jnp.where(starts[CHUNK - 1 :] <= place, jnp.exp(cs[CHUNK - 1 :] - cs), 0.0)
    return decay_in, closing


def scan_body(heads, base_ref, pa_ref, bc_ref, starts_ref, taps_ref, bias_ref, rates_ref,
              y_ref, cv_ref, enter_ref, reach_ref, state_out, through_out, state, through):
    c = pl.program_id(0)
    chan = heads * P_SIZE

    @pl.when(c == 0)
    def _():
        state[...] = jnp.zeros_like(state)
        through[...] = jnp.ones_like(through)

    starts, place = starts_ref[...], places_of(base_ref, c)
    raw = pa_ref[pl.ds(pl.multiple_of(c * CHUNK + RIM, 16), CHUNK), chan + 2 * HD :]
    step, _, cs = rates_of(raw, bias_ref[...], rates_ref[...], heads)
    cs_t = cs.T
    cv = conv_of(pa_ref, taps_ref, starts, place, c, chan, 0)
    cv_ref[...] = cv
    x = cv * sig(cv)
    b_rows, c_rows = bc_ref[:, :N], bc_ref[:, N:]
    inter = mm(c_rows, b_rows, 1, 1)
    visible = visible_of(base_ref, c, starts, place)
    decay_in, closing = decays_of(cs, starts, place)
    ends = decay_in.T
    for k in range(heads // 2):
        driven = lanes(x, k) * pair_of(step, k)
        mixed = [mm(weights_of(2 * k + i, cs, cs_t, visible) * inter, driven, 1, 0) for i in (0, 1)]
        y_ref[:, k * 128 : (k + 1) * 128] = halves_of(*mixed)
        local = mm(driven * pair_of(closing, k), b_rows, 0, 0)
        at = pl.ds(k * 128, 128)
        old = state[at]
        enter_ref[0, at] = old
        both = jnp.concatenate(
            [old[i * P_SIZE : (i + 1) * P_SIZE] * ends[2 * k + i : 2 * k + i + 1, CHUNK - 1 :] for i in (0, 1)], axis=0
        )
        state[at] = both + local
    factor = jnp.broadcast_to(ends[:8, CHUNK - 1 :], (8, 128))
    reach_ref[0, :8] = through[...]
    reach_ref[0, 8:] = factor
    through[...] = through[...] * factor
    state_out[...] = state[...].astype(bf16)
    through_out[...] = through[...]


def gate_parts(y_scan, cv, z, skip, gain):
    x = cv * sig(cv)
    ssm = y_scan + skip * x
    s = sig(z)
    gated = ssm * (z * s)
    r = lax.rsqrt(head_means(gated * gated) + norm_eps)
    return x, ssm, s, gated, r


def gate_body(heads, base_ref, pa_ref, bc_ref, starts_ref, bias_ref, rates_ref, y_ref, cv_ref, enter_ref, reach_ref,
              before_ref, z_ref, skip_ref, gain_ref, low_ref, scan_ref):
    c = pl.program_id(0)
    chan = heads * P_SIZE
    starts, place = starts_ref[...], places_of(base_ref, c)
    raw = pa_ref[pl.ds(pl.multiple_of(c * CHUNK + RIM, 16), CHUNK), chan + 2 * HD :]
    _, _, cs = rates_of(raw, bias_ref[...], rates_ref[...], heads)
    decay_in, _ = decays_of(cs, starts, place)
    state_in = enter_ref[0] + scale_rows(before_ref[...], reach_ref[0], heads)
    c_rows = bc_ref[:, N:]
    off = [mm(c_rows, state_in[k * 128 : (k + 1) * 128], 1, 1) * pair_of(decay_in, k) for k in range(heads // 2)]
    y_scan = y_ref[...] + jnp.concatenate(off, axis=1)
    scan_ref[...] = y_scan
    _, _, _, gated, r = gate_parts(y_scan, cv_ref[...], z_ref[...], skip_ref[...], gain_ref[...])
    low_ref[...] = (gated * r * gain_ref[...]).astype(bf16)


def gate_back_body(heads, chunks, base_ref, pa_ref, bc_ref, starts_ref, bias_ref, rates_ref, d_ref, scan_ref, cv_ref,
                   reach_ref, z_ref, skip_ref, gain_ref, dz_ref, dy_ref, leave_ref, tail_ref, state_out, gain_out, state, tail):
    c = chunks - 1 - pl.program_id(0)
    chan = heads * P_SIZE

    @pl.when(c == chunks - 1)
    def _():
        state[...] = jnp.zeros_like(state)
        tail[...] = jnp.ones_like(tail)
        gain_out[...] = jnp.zeros_like(gain_out)

    starts, place = starts_ref[...], places_of(base_ref, c)
    raw = pa_ref[pl.ds(pl.multiple_of(c * CHUNK + RIM, 16), CHUNK), chan + 2 * HD :]
    _, _, cs = rates_of(raw, bias_ref[...], rates_ref[...], heads)
    decay_in, _ = decays_of(cs, starts, place)
    z = z_ref[...]
    x, ssm, s, gated, r = gate_parts(scan_ref[...], cv_ref[...], z, skip_ref[...], gain_ref[...])
    d = d_ref[...]
    gain_out[:1] += jnp.sum(d * gated * r, axis=0, keepdims=True)
    u = d * gain_ref[...]
    d_gated = r * u - gated * (r * r * r * head_means(u * gated))
    dz_ref[...] = (d_gated * ssm * (s * (1.0 + z * (1.0 - s)))).astype(bf16)
    dy = d_gated * (z * s)
    dy_ref[...] = dy
    c_rows = bc_ref[:, N:]
    leave_ref[0] = state[...]
    tail_ref[0] = tail[...]
    factor = reach_ref[0, 8:]
    local = [mm(lanes(dy, k) * pair_of(decay_in, k), c_rows, 0, 0) for k in range(heads // 2)]
    state[...] = scale_rows(state[...], factor, heads) + jnp.concatenate(local, axis=0)
    tail[...] = tail[...] * factor
    state_out[...] = state[...].astype(bf16)


def scan_back_body(heads, base_ref, pa_ref, bc_ref, starts_ref, bias_ref, rates_ref, dy_ref, cv_ref,
                   enter_ref, reach_ref, before_ref, leave_ref, tail_ref, after_ref, skip_ref,
                   gx_ref, dbc_ref, raw_out, rows_out, skip_out):
    c = pl.program_id(0)
    chan = heads * P_SIZE

    @pl.when(c == 0)
    def _():
        rows_out[...] = jnp.zeros_like(rows_out)
        skip_out[...] = jnp.zeros_like(skip_out)

    starts, place = starts_ref[...], places_of(base_ref, c)
    raw = pa_ref[pl.ds(pl.multiple_of(c * CHUNK + RIM, 16), CHUNK), chan + 2 * HD :]
    step, log_decay, cs = rates_of(raw, bias_ref[...], rates_ref[...], heads)
    cs_t = cs.T
    visible = visible_of(base_ref, c, starts, place)
    decay_in, closing = decays_of(cs, starts, place)
    b_rows, c_rows = bc_ref[:, :N], bc_ref[:, N:]
    inter = mm(c_rows, b_rows, 1, 1)
    cv = cv_ref[...]
    s = sig(cv)
    x = cv * s
    dy = dy_ref[...]
    state_in = enter_ref[0] + scale_rows(before_ref[...], reach_ref[0], heads)
    d_state = leave_ref[0] + scale_rows(after_ref[...], tail_ref[0], heads)
    left = iota((CHUNK, 128), 1) < P_SIZE
    d_inter = jnp.zeros((CHUNK, CHUNK), f32)
    d_b = jnp.zeros((CHUNK, N), f32)
    d_c = jnp.zeros((CHUNK, N), f32)
    inside, outside, closes, drives = [], [], [], []
    for k in range(heads // 2):
        at = slice(k * 128, (k + 1) * 128)
        driven = (lanes(x, k) * pair_of(step, k)).astype(bf16)
        dyk = lanes(dy, k)
        dyb = dyk.astype(bf16)
        d_mixed, y_mixed = [], []
        for i in (0, 1):
            w = weights_of(2 * k + i, cs, cs_t, visible)
            mix = (w * inter).astype(bf16)
            half = jnp.where(left if i == 0 else ~left, dyb, jnp.zeros_like(dyb))
            d_inter = d_inter + w * mm(half, driven, 1, 1)
            d_mixed.append(mm(mix, dyb, 0, 0))
            y_mixed.append(mm(mix, driven, 1, 0))
        d_mix = halves_of(*d_mixed)
        close = pair_of(closing, k)
        d_close = mm(b_rows, d_state[at], 1, 1)
        closed = driven.astype(f32) * close
        enter = pair_of(decay_in, k)
        y_off = mm(c_rows, state_in[at], 1, 1) * enter
        d_c = d_c + mm(dyk * enter, state_in[at], 1, 0)
        d_b = d_b + mm(closed, d_state[at], 1, 0)
        inside.append(dyb.astype(f32) * halves_of(*y_mixed) - driven.astype(f32) * d_mix)
        outside.append(dyk * y_off)
        closes.append(closed * d_close)
        drives.append(d_mix + close * d_close)
    d_c = d_c + mm(d_inter, b_rows, 1, 0)
    d_b = d_b + mm(d_inter, c_rows, 0, 0)
    dbc_ref[:, :N] = d_b.astype(bf16)
    dbc_ref[:, N:] = d_c.astype(bf16)
    d_driven = jnp.concatenate(drives, axis=1)
    closes = head_sums(jnp.concatenate(closes, axis=1), heads)
    d_cs = head_sums(jnp.concatenate(inside, axis=1) + jnp.concatenate(outside, axis=1), heads) - closes
    kept = head_sums_t(d_state * state_in, heads)
    whole = decay_in[CHUNK - 1 :] * kept + jnp.sum(closes, axis=0, keepdims=True)
    upper = (iota((CHUNK, CHUNK), 0) <= iota((CHUNK, CHUNK), 1)).astype(f32)
    d_la = mm_exact(upper, d_cs, 1, 0) + whole
    d_step = head_sums(d_driven * x, heads)
    d_raw = (d_step - jnp.exp(rates_ref[...]) * d_la) * sig(raw + bias_ref[...])
    d_raw = jnp.where(iota((CHUNK, 128), 1) < heads, d_raw, 0.0)
    raw_out[...] = d_raw.astype(bf16)
    rows_out[:1] += jnp.sum(d_raw, axis=0, keepdims=True)
    rows_out[1:2] += jnp.sum(d_la * log_decay, axis=0, keepdims=True)
    skip_out[:1] += jnp.sum(dy * x, axis=0, keepdims=True)
    wide = jnp.concatenate([pair_of(step, k) for k in range(heads // 2)], axis=1)
    gx_ref[...] = (d_driven * wide + skip_ref[...] * dy) * (s * (1.0 + cv * (1.0 - s)))


def head_sums_t(v, heads):
    column = jnp.sum(v, axis=1, keepdims=True)
    pick = (iota((v.shape[0], 128), 0) // P_SIZE == iota((v.shape[0], 128), 1)).astype(f32)
    return jnp.sum(column * pick, axis=0, keepdims=True)


def chunked(body, chunks, outs, out_specs, ins, in_specs, scratch=()):
    return pl.pallas_call(
        body,
        grid=(chunks,),
        out_shape=outs,
        in_specs=in_specs,
        out_specs=out_specs,
        scratch_shapes=list(scratch),
        cost_estimate=pl.CostEstimate(flops=2_000_000_000, bytes_accessed=40_000_000, transcendentals=0),
        compiler_params=pltpu.CompilerParams(vmem_limit_bytes=48 * 2**20),
    )(*ins)


def dot(a, b, ca, cb):
    return lax.dot_general(a, b, (((ca,), (cb,)), ((), ())), preferred_element_type=f32)


def exact(text, *operands):
    return jnp.einsum(text, *operands, precision=highest, preferred_element_type=f32)


def d_silu(v):
    s = jax.nn.sigmoid(v)
    return s * (1.0 + v * (1.0 - s))


def shifted(block, axis, distance):
    count = lax.axis_size(axis)
    route = [(i - distance, i) for i in range(count) if 0 <= i - distance < count]
    return lax.ppermute(block, axis, route)


def rope_tables(offsets, first, count):
    half = HD // 2
    index = (first + jnp.arange(count)).astype(f32)
    freqs = rope_base ** (-2.0 * index / HD)
    angles = offsets.astype(f32)[:, None] * freqs[None, :]
    return jnp.cos(angles), jnp.sin(angles)


def turn(v, cosine, sine):
    half = v.shape[-1] // 2
    a, b = v[:, :half], v[:, half:]
    return jnp.concatenate([a * cosine - b * sine, b * cosine + a * sine], axis=-1)


def conv_rows(padded, taps, starts, places):
    length = starts.shape[0]
    total = jnp.zeros((length, padded.shape[1]), f32)
    for lag in range(K):
        back = K - 1 - lag
        valid = (places - back >= starts)[:, None]
        total = total + jnp.where(valid, padded[RIM - back : RIM - back + length] * taps[lag][None, :], 0.0)
    return total


def conv_back(grad, grad_next, padded, taps, starts, places, starts_next):
    length = starts.shape[0]
    edge = K - 1
    longer = jnp.concatenate([grad, grad_next], axis=0)
    starts_long = jnp.concatenate([starts, starts_next])
    total = jnp.zeros_like(grad)
    tap_grads = []
    for lag in range(K):
        ahead = edge - lag
        seen = (places >= starts_long[ahead : ahead + length])[:, None]
        total = total + jnp.where(seen, longer[ahead : ahead + length], 0.0) * taps[lag][None, :]
        valid = (places - ahead >= starts)[:, None]
        tap_grads.append(jnp.sum(jnp.where(valid, grad * padded[RIM - ahead : RIM - ahead + length], 0.0), axis=0))
    return total, jnp.stack(tap_grads)


def mixer_row(v):
    return v.reshape(1, -1)


def on_device(
    layer_input, doc_start, mixer_gain, ffn_gain,
    z_weight, x_weight, bc_weight, dt_weight, q_weight, k_weight, v_weight,
    o_weight, out_weight, gate_weight, up_weight, down_weight,
    conv_inner, conv_state, decay_log, dt_bias, skip_coef, ssm_gain, cotangent,
):
    tokens, width = layer_input.shape
    rows = z_weight.shape[0]
    planes = lax.axis_size("z")
    cores = lax.axis_size("head")
    zi, pi, hi = (lax.axis_index(a) for a in ("z", "p", "head"))
    T = tokens * G
    total_tokens = T * planes
    offset = zi * T
    places = offset + jnp.arange(T, dtype=jnp.int32)
    own = tokens // cores
    heads = decay_log.shape[0] // G
    chan = heads * P_SIZE
    bcs = 2 * N // cores // G
    quarter_half = HD // 2 // G

    def my_slice(v, size, index, axis):
        return lax.dynamic_slice_in_dim(v, index * size, size, axis)

    taps_inner = my_slice(conv_inner, chan, pi, 1)
    taps_state = my_slice(conv_state, bcs, hi * G + pi, 1)
    rates = my_slice(decay_log, heads, pi, 0)
    bias = my_slice(dt_bias, heads, pi, 0)
    skip = my_slice(skip_coef, heads, pi, 0)
    gain_s = my_slice(ssm_gain, chan, pi, 0)

    def cut(w):
        return w.reshape(rows, G, -1)

    bc_mine = lax.dynamic_slice_in_dim(bc_weight, hi * (2 * N // cores), 2 * N // cores, 1)
    k_cut = jnp.moveaxis(k_weight.reshape(rows, 2, G, quarter_half), 2, 1).reshape(rows, G, -1)
    a_sizes = [chan, HD, bcs, 2 * quarter_half, 2 * quarter_half, heads]
    a_at = [sum(a_sizes[:i]) for i in range(len(a_sizes))]
    pad = -sum(a_sizes) % 128
    small_w = jnp.concatenate(
        [cut(bc_mine), k_cut, cut(v_weight), cut(dt_weight), jnp.zeros((rows, G, pad), bf16)], axis=2
    )
    small_w = jnp.moveaxis(small_w, 1, 0)
    a_cols = sum(a_sizes) + pad

    def gather(w):
        return lax.all_gather(w, "z", axis=0, tiled=True)

    exchange_sems = lambda n: [DMA((3, n)), DMA((3, n)), DMA((n,))]
    wa = gather(call(
        exchange_a_body, 0, shape((G * rows, a_cols), bf16), HBM,
        (x_weight, q_weight, small_w), [HBM] * 3, exchange_sems(3),
    ))

    def half(v):
        return lax.dynamic_slice_in_dim(v, hi * own, own, 0)

    x_own, cot_own = half(layer_input), half(cotangent)
    r1 = lax.rsqrt(jnp.mean(x_own * x_own, axis=-1, keepdims=True) + norm_eps)
    first_own = (x_own * r1 * mixer_gain).astype(bf16)
    wb = gather(call(
        exchange_b_body, 9, shape((G * rows, 2 * chan + HD), bf16), HBM,
        (z_weight, out_weight, o_weight), [HBM] * 3, exchange_sems(3),
    ))
    wc, wd, first_rim, out_low, docs = call(
        functools.partial(start_body, planes), 1,
        (shape((G * rows, gate_weight.shape[1] * 2 // G), bf16),
         shape((G * rows, down_weight.shape[1] // G), bf16), shape((RIM + T, width), bf16), shape((T, width), bf16),
         shape((planes, G, 8, tokens), jnp.int32)),
        (HBM,) * 5,
        (gate_weight, up_weight, down_weight, first_own, cot_own.astype(bf16), jnp.broadcast_to(doc_start[None], (8, tokens))),
        [HBM] * 3 + [VMEM] * 3,
        exchange_sems(3) + [DMA(()), DMA(()), DMA((3,)), DMA((3,)), DMA((planes - 1,)), DMA((planes - 1,)), DMA(())]
        + Spread.sems * 2, us=55,
    )
    wc, wd = gather(wc), gather(wd)
    wz, wb = wb[:, :chan], wb[:, chan:]
    first = first_rim[RIM:]
    all_starts = docs[:, :, 0].reshape(-1)
    starts = lax.dynamic_slice_in_dim(all_starts, offset, T, 0)

    def line_sum(grad):
        return lax.psum_scatter(grad, "z", scatter_dimension=0, tiled=True)

    def scatter(g):
        g = lax.all_to_all(g.reshape(G, rows, -1), "p", 0, 0, tiled=True)
        return jnp.moveaxis(g, 0, 1).astype(f32)

    edge = K - 1
    pa = dot(first_rim, wa, 1, 0)
    z_part = dot(first, wz, 1, 0)
    q_proj, bc_pre, k_proj, v_proj = (pa[RIM:, a : a + s] for a, s in zip(a_at[1:5], a_sizes[1:5]))
    bc_ext = pa[:, a_at[2] : a_at[2] + bcs]
    cv_bc = conv_rows(bc_ext, taps_state, starts, places)
    bc_low = jax.nn.silu(cv_bc).astype(bf16)
    offsets = places - starts
    cos_q, sin_q = rope_tables(offsets, 0, HD // 2)
    cos_k, sin_k = rope_tables(offsets, pi * quarter_half, quarter_half)
    scale = HD ** (-0.5)
    kvr = 4 * quarter_half
    query = (turn(q_proj, cos_q, sin_q) * scale).astype(bf16)
    kv_own = jnp.concatenate([turn(k_proj, cos_k, sin_k).astype(bf16), v_proj.astype(bf16)], axis=1)
    line_sems = [DMA((planes - 1,)), DMA((planes - 1,))]
    bc_t, kv_line = call(
        functools.partial(spread_body, planes), 2, (shape((2 * N, T), bf16), shape((planes, kvr, T), bf16)), (HBM, HBM),
        (bc_low.T, kv_own.T), [HBM, HBM], line_sems + [DMA(())] + Spread.sems,
    )
    bc_all = bc_t.T

    L = CHUNK
    nc = T // L
    base = jnp.full((1,), offset, jnp.int32)
    starts_col = starts[:, None]

    def row128(v):
        return jnp.pad(v, (0, 128 - v.shape[0]))[None]

    bias_row, rates_row = row128(bias), row128(rates)
    skip_row, gain_row = jnp.repeat(skip, P_SIZE)[None], gain_s[None]
    smem = pl.BlockSpec(memory_space=pltpu.SMEM)

    def specs(turned=False):
        at = (lambda c: nc - 1 - c) if turned else (lambda c: c)
        return (
            lambda cols: pl.BlockSpec((L, cols), lambda c: (at(c), 0)),
            lambda *dims: pl.BlockSpec(dims, lambda c: (0,) * len(dims)),
            lambda rows, cols: pl.BlockSpec((1, rows, cols), lambda c: (at(c), 0, 0)),
        )

    tile, fixed, stack = specs()
    pa_spec = fixed(*pa.shape)
    y_diag, cv_x, enter, reach, state, through = chunked(
        functools.partial(scan_body, heads), nc,
        (shape((T, chan), f32), shape((T, chan), f32), shape((nc, chan, N), f32), shape((nc, 16, 128), f32),
         shape((chan, N), bf16), shape((8, 128), f32)),
        (tile(chan), tile(chan), stack(chan, N), stack(16, 128), fixed(chan, N), fixed(8, 128)),
        (base, pa, bc_all, starts_col, taps_inner, bias_row, rates_row),
        [smem, pa_spec, tile(2 * N), tile(1), fixed(K, chan), fixed(1, 128), fixed(1, 128)],
        [pltpu.VMEM((chan, N), f32), pltpu.VMEM((8, 128), f32)],
    )

    def entering(upward, states, factors):
        total = jnp.zeros((chan, N), f32)
        for d in reversed(range(1, planes)):
            there = (zi - d >= 0) if upward else (zi + d < planes)
            factor = jnp.repeat(factors[d - 1, :heads, :1], P_SIZE, axis=0)
            total = jnp.where(there, total * factor + states[d - 1].astype(f32), total)
        return total

    state_shapes = (shape((planes - 1, chan, N), bf16), shape((planes - 1, 8, 128), f32))
    states, factors, kv_all = call(
        functools.partial(up_body, planes), 3, state_shapes + (shape((G * planes, kvr, T), bf16),), (HBM,) * 3,
        (state, through, kv_line), [HBM] * 3, line_sems * 2 + Spread.sems, us=28,
    )
    before = entering(True, states, factors)
    ssm_low, y_scan = chunked(
        functools.partial(gate_body, heads), nc,
        (shape((T, chan), bf16), shape((T, chan), f32)), (tile(chan), tile(chan)),
        (base, pa, bc_all, starts_col, bias_row, rates_row, y_diag, cv_x, enter, reach, before, z_part, skip_row, gain_row),
        [smem, pa_spec, tile(2 * N), tile(1), fixed(1, 128), fixed(1, 128), tile(chan), tile(chan), stack(chan, N),
         stack(16, 128), fixed(chan, N), tile(chan), fixed(1, chan), fixed(1, chan)],
    )

    kv_all = kv_all.reshape(G, planes, 4, quarter_half, T)
    keys = kv_all[:, :, :2].transpose(1, 4, 2, 0, 3).reshape(total_tokens, HD)
    values = kv_all[:, :, 2:].transpose(1, 4, 0, 2, 3).reshape(total_tokens, HD)
    key_len = min(512, total_tokens)
    first_block = starts[0] // key_len
    last_block = (offset + T - 1) // key_len

    def key_block(index):
        begin = index * key_len
        kb = lax.dynamic_slice_in_dim(keys, begin, key_len, 0)
        vb = lax.dynamic_slice_in_dim(values, begin, key_len, 0)
        at = begin + jnp.arange(key_len, dtype=jnp.int32)
        seen = (at[None, :] >= starts[:, None]) & (at[None, :] <= places[:, None])
        return kb, vb, seen, dot(query, kb, 1, 1)

    def running(index, carry):
        peak, mass = carry
        _, _, seen, scores = key_block(index)
        new = jnp.maximum(peak, jnp.max(jnp.where(seen, scores, -1e30), axis=-1))
        mass = mass * jnp.exp(peak - new) + jnp.sum(jnp.where(seen, jnp.exp(scores - new[:, None]), 0.0), axis=-1)
        return new, mass

    peak, mass = lax.fori_loop(
        first_block, last_block + 1, running, (jnp.full((T,), -1e30, f32), jnp.zeros((T,), f32))
    )
    log_mass = peak + jnp.log(mass)

    def weighted(index, total):
        _, vb, seen, scores = key_block(index)
        probs = jnp.where(seen, jnp.exp(scores - log_mass[:, None]), 0.0).astype(bf16)
        return total + dot(probs, vb, 1, 0)

    attended = lax.fori_loop(first_block, last_block + 1, weighted, jnp.zeros((T, HD), f32))
    att_low = attended.astype(bf16)

    both_low = jnp.concatenate([ssm_low, att_low], axis=1)
    collect = Collect.scratch(own, width) + [pltpu.VMEM((own, width), bf16)] + Spread.sems
    hidden, second = call(
        hidden_body, 4, (shape((own, width), f32), shape((T, width), bf16)), (VMEM, HBM),
        (dot(both_low, wb, 1, 1).astype(bf16), x_own, mixer_row(ffn_gain)), [VMEM] * 3, collect, us=50,
    )
    pc = dot(second, wc, 1, 0)
    ff = pc.shape[1] // 2
    gate_pre, up_pre = pc[:, :ff], pc[:, ff:]
    s_gate = jax.nn.silu(gate_pre)
    act_low = (s_gate * up_pre).astype(bf16)
    layer_own = hidden + lax.psum_scatter(
        dot(act_low, wd, 1, 1).astype(bf16), ("p", "head"), scatter_dimension=0, tiled=True
    ).astype(f32)

    grad_d = dot(out_low, act_low, 0, 0)
    d_act = dot(out_low, wd, 1, 0)
    gu_low = jnp.concatenate([d_act * up_pre * d_silu(gate_pre), d_act * s_gate], axis=1).astype(bf16)
    grad_c = dot(second, gu_low, 0, 0)
    part_c = dot(gu_low, wc, 1, 1).astype(bf16)
    grad_c, grad_d, part_c = lax.optimization_barrier((grad_c.astype(bf16), grad_d.astype(bf16), part_c))
    sum_d = line_sum(grad_d)
    sum_c = line_sum(grad_c)
    d_hidden, grad_ffn, branch = call(
        branch_body, 5, (shape((own, width), f32), shape((8, width), f32), shape((T, width), bf16)), (VMEM, VMEM, HBM),
        (part_c, hidden, cot_own, mixer_row(ffn_gain)), [VMEM] * 4, collect, us=50,
    )
    grad_b = dot(branch, both_low, 0, 0)
    d_both = dot(branch, wb, 1, 0)
    d_norm_s, d_att = d_both[:, :chan], d_both[:, chan:].astype(bf16)

    back, _, back_stack = specs(True)
    dz_low, dy, leave, tail, g_state, grad_gain_s = chunked(
        functools.partial(gate_back_body, heads, nc), nc,
        (shape((T, chan), bf16), shape((T, chan), f32), shape((nc, chan, N), f32), shape((nc, 8, 128), f32),
         shape((chan, N), bf16), shape((8, chan), f32)),
        (back(chan), back(chan), back_stack(chan, N), back_stack(8, 128), fixed(chan, N), fixed(8, chan)),
        (base, pa, bc_all, starts_col, bias_row, rates_row, d_norm_s, y_scan, cv_x, reach, z_part, skip_row, gain_row),
        [smem, pa_spec, back(2 * N), back(1), fixed(1, 128), fixed(1, 128), back(chan), back(chan), back(chan),
         back_stack(16, 128), back(chan), fixed(1, chan), fixed(1, chan)],
        [pltpu.VMEM((chan, N), f32), pltpu.VMEM((8, 128), f32)],
    )
    grad_zb = jnp.concatenate([dot(first, dz_low, 0, 0).astype(bf16), grad_b.astype(bf16)], axis=1)
    g_state, sum_d, grad_zb = lax.optimization_barrier((g_state, sum_d, grad_zb))
    sum_zb = line_sum(grad_zb)
    balance = jnp.sum(d_att.astype(f32) * attended, axis=-1, keepdims=True)

    def grads(index, carry):
        d_query, d_keys, d_values = carry
        kb, vb, seen, scores = key_block(index)
        probs = jnp.where(seen, jnp.exp(scores - log_mass[:, None]), 0.0)
        d_scores = (probs * (dot(d_att, vb, 1, 1) - balance)).astype(bf16)
        d_query = d_query + dot(d_scores, kb, 1, 0)
        d_keys = lax.dynamic_update_slice_in_dim(d_keys, dot(d_scores, query, 0, 0), index * key_len, 0)
        d_values = lax.dynamic_update_slice_in_dim(d_values, dot(probs.astype(bf16), d_att, 0, 0), index * key_len, 0)
        return d_query, d_keys, d_values

    zero_keys = jnp.zeros((total_tokens, HD), f32)
    d_query, d_keys, d_values = lax.fori_loop(
        first_block, last_block + 1, grads, (jnp.zeros((T, HD), f32), zero_keys, zero_keys)
    )
    dk_cut = d_keys.astype(bf16).reshape(planes, T, 2, G, quarter_half).transpose(3, 0, 2, 4, 1)
    dv_cut = d_values.astype(bf16).reshape(planes, T, G, 2, quarter_half).transpose(2, 0, 3, 4, 1)
    dkv = jnp.concatenate([dk_cut, dv_cut], axis=2).reshape(G, planes, 4 * quarter_half, T)
    states, factors, dkv = call(
        functools.partial(down_body, planes), 6, state_shapes + (shape((G, planes, kvr, T), bf16),), (HBM,) * 3,
        (g_state, through, dkv), [HBM] * 3, line_sems * 2 + [DMA((3,)), DMA((3,)), DMA(())], us=35,
    )
    after = entering(False, states, factors)
    gx, d_bc_all, d_raw, grad_rows, grad_skip = chunked(
        functools.partial(scan_back_body, heads), nc,
        (shape((T, chan), f32), shape((T, 2 * N), bf16), shape((T, 128), bf16), shape((8, 128), f32), shape((8, chan), f32)),
        (tile(chan), tile(2 * N), tile(128), fixed(8, 128), fixed(8, chan)),
        (base, pa, bc_all, starts_col, bias_row, rates_row, dy, cv_x, enter, reach, before, leave, tail, after, skip_row),
        [smem, pa_spec, tile(2 * N), tile(1), fixed(1, 128), fixed(1, 128), tile(chan), tile(chan),
         stack(chan, N), stack(16, 128), fixed(chan, N), stack(chan, N), stack(8, 128), fixed(chan, N), fixed(1, chan)],
    )
    grad_gain_s = grad_gain_s[0]
    grad_bias, grad_rates = grad_rows[0, :heads], grad_rows[1, :heads]
    grad_skip = jnp.sum(grad_skip[0].reshape(heads, P_SIZE), axis=1)

    gx_first = gx[:RIM]
    d_bc_t, sum_c = lax.optimization_barrier((d_bc_all.T, sum_c))
    g_bc, rim_bc, rim_x, dkv = call(
        functools.partial(back_body, planes), 7,
        (shape((bcs, T), f32), shape((bcs, 128), f32), shape((RIM, chan), f32), shape((kvr, T), f32)), (VMEM,) * 4,
        (d_bc_t, dkv, d_silu(cv_bc).T, gx_first), [VMEM] * 4,
        [pltpu.VMEM((G * bcs, T), bf16), pltpu.VMEM((3, bcs, T), bf16), pltpu.VMEM((3, bcs, T), bf16),
         pltpu.VMEM((planes, kvr, T), bf16), pltpu.VMEM((planes - 1, kvr, T), bf16),
         pltpu.VMEM((bcs, T), f32), DMA(()), DMA(()), DMA((3,)), DMA((3,)),
         DMA((planes - 1,)), DMA((planes - 1,)), DMA((2,)), DMA((2,))],
    )
    dkv = dkv.T
    later = zi < planes - 1
    gx_next = jnp.where(later, rim_x[:edge], 0.0)
    gb_next = jnp.where(later, rim_bc[:, :edge].T, 0.0)
    ends = jnp.minimum(offset + T + jnp.arange(edge), total_tokens - 1)
    starts_next = jnp.where(later, all_starts[ends], total_tokens)
    d_inner_pre, grad_conv_inner = conv_back(gx, gx_next, pa[:, :chan], taps_inner, starts, places, starts_next)
    d_bc_pre, grad_conv_state = conv_back(g_bc.T, gb_next, bc_ext, taps_state, starts, places, starts_next)
    d_q = turn(d_query, cos_q, -sin_q) * scale
    d_k = turn(dkv[:, : 2 * quarter_half], cos_k, -sin_k)
    d_v = dkv[:, 2 * quarter_half :]

    da_low = jnp.concatenate(
        [v.astype(bf16) for v in (d_inner_pre, d_q, d_bc_pre, d_k, d_v)] + [d_raw], axis=1
    )
    grad_a = dot(first, da_low, 0, 0).astype(bf16)
    small = [grad_conv_inner, grad_conv_state, grad_rates, grad_bias, grad_skip, grad_gain_s]
    at = [0]
    for s in small:
        at.append(at[-1] + s.size)
    flat = jnp.concatenate([s.reshape(-1) for s in small] + [jnp.zeros((2 * width - at[-1],), f32)]).reshape(2, width)
    flat = jnp.concatenate([flat, grad_ffn[:1], jnp.zeros((RIM - 3, width), f32)], axis=0)
    gc, gd = scatter(sum_c), scatter(sum_d)
    part_a = (dot(da_low, wa, 1, 1) + dot(dz_low, wz, 1, 1)).astype(bf16)
    part_a, gc, gd = lax.optimization_barrier((part_a, gc, gd))
    sum_a = line_sum(grad_a)
    grad_input, layer_out, sums = call(
        functools.partial(final_body, planes), 8,
        (shape((tokens, width), f32), shape((tokens, width), f32), shape((2 * G * RIM, width), f32)), (HBM, HBM, HBM),
        (part_a, x_own, d_hidden, layer_own, mixer_row(mixer_gain), flat), [VMEM] * 6,
        Collect.scratch(own, width)
        + [pltpu.VMEM((own, width), f32), pltpu.VMEM((RIM, width), f32), pltpu.VMEM((planes - 1, RIM, width), f32),
           DMA((planes - 1,)), DMA((planes - 1,)), DMA((2,)), DMA((2,)), DMA((2,))]
        + Spread.sems, us=45,
    )

    ga, gb = scatter(sum_a), scatter(sum_zb)
    g_z, gb = gb[:, :, :chan], gb[:, :, chan:]
    g_x, g_q, g_bc, g_k, g_v, g_dt = (ga[:, :, a : a + s] for a, s in zip(a_at, a_sizes))
    g_k = jnp.moveaxis(g_k.reshape(rows, G, 2, quarter_half), 1, 2)
    g_bc = lax.all_gather(g_bc.reshape(rows, -1).astype(bf16), "head", axis=1, tiled=True).astype(f32)

    sums = sums.reshape(G, cores, RIM, width)
    every = sums[:, :, :2].reshape(G, cores, 2 * width)
    mine = lax.dynamic_index_in_dim(every, hi, 1, False)
    pieces = [mine[:, a:b] for a, b in zip(at, at[1:])]
    o_conv_inner = jnp.moveaxis(pieces[0].reshape(G, K, chan), 0, 1).reshape(K, G * chan)
    o_conv_state = every[:, :, at[1] : at[2]].reshape(G, cores, K, bcs).transpose(2, 1, 0, 3).reshape(K, 2 * N)
    per = width // (planes * G)
    gains = lax.dynamic_slice_in_dim(jnp.sum(sums[:, :, 2:4], axis=(0, 1)), (zi * G + pi) * per, per, 1)
    gains = (gains[1], gains[0])

    def whole(g):
        return g.reshape(rows, -1)

    return (
        layer_out, grad_input, gains[0], gains[1],
        whole(g_z), whole(g_x), g_bc, whole(g_dt), whole(g_q), whole(g_k), whole(g_v),
        whole(gb[:, :, chan:]), whole(gb[:, :, :chan]),
        whole(gc[:, :, :ff]), whole(gc[:, :, ff:]), whole(gd),
        o_conv_inner, o_conv_state,
        pieces[2].reshape(-1), pieces[3].reshape(-1), pieces[4].reshape(-1), pieces[5].reshape(-1),
    )


def solution(mesh):
    seq, cores = mesh.shape["seq"], mesh.shape["head"]
    planes = Mesh(mesh.devices.reshape(seq // G, G, cores), ("z", "p", "head"))
    s = ("z", "p")
    both, row, head, whole = P(s, "head"), P(s, None), P("head"), P()
    placed = (
        row, P(s), whole, whole, both, both, row, both, both, both, both, both, both, both, both, both,
        P(None, "head"), whole, head, head, head, head, row,
    )
    return jax.shard_map(
        on_device,
        mesh=planes,
        in_specs=placed,
        out_specs=(
            row, row, P(s), P(s), both, both, row, both, both, both, both, both, both, both, both, both,
            P(None, "head"), whole, head, head, head, head,
        ),
        check_vma=False,
    )
```

```python
import functools
import math

import jax
import jax.numpy as jnp
from jax import lax
from jax.experimental import pallas as pl
from jax.experimental.pallas import tpu as pltpu
from jax.sharding import Mesh, PartitionSpec as P

P_SIZE = 64
N = 256
HD = 128
K = 4
G = 4
CHUNK = 128
RIM = 16

highest = lax.Precision.HIGHEST
rope_base = 10000.0
norm_eps = 1e-05
bf16 = jnp.bfloat16
f32 = jnp.float32
MESH = pl.DeviceIdType.MESH
HBM = pl.BlockSpec(memory_space=pl.ANY)
VMEM = pl.BlockSpec(memory_space=pltpu.VMEM)
DMA = pltpu.SemaphoreType.DMA


def rcopy(src, dst, send, recv, **where):
    return pltpu.make_async_remote_copy(
        src_ref=src, dst_ref=dst, send_sem=send, recv_sem=recv, device_id=where, device_id_type=MESH
    )


def here():
    return lax.axis_index("z"), lax.axis_index("p"), lax.axis_index("head")


def ring(p, d):
    return lax.rem(p + d + G, G)


def greet(*partners):
    barrier = pltpu.get_barrier_semaphore()
    for where in partners:
        pl.semaphore_signal(barrier, inc=1, device_id=where, device_id_type=MESH)
    pl.semaphore_wait(barrier, len(partners))


def plane_partners(p, c):
    return [{"p": ring(p, d)} for d in range(1, G)] + [{"head": 1 - c}]


def line_partners(z, planes):
    return [{"z": lax.rem(z + d, planes)} for d in range(1, planes)]


def beside(p):
    return p + 1 - 2 * lax.rem(p, 2), lax.rem(p + 2, G), G - 1 - p


class Spread:
    sems = [DMA((2,)), DMA((2,)), DMA((2,)), DMA((2,)), DMA((4,)), DMA((4,)), DMA(())]

    def __init__(self, block, out, start, rows, sems, cores=True):
        self.block, self.out, self.first, self.rows, self.cores = block, out, start, rows, cores
        self.s1, self.r1, self.s2, self.r2, self.s3, self.r3, self.keep = sems
        _, self.p, self.c = here()
        self.around = beside(self.p)

    def spot(self, q, half=None):
        first, rows = self.first(q, self.c), self.rows
        if half is not None:
            first, rows = first + half * (rows // 2), rows // 2
        return self.out.at[pl.ds(first, rows)]

    def over(self, i):
        return rcopy(self.block, self.spot(self.p), self.s1.at[i], self.r1.at[i], p=self.around[i])

    def relay(self, i):
        spot = self.spot(self.around[i], i)
        return rcopy(spot, spot, self.s2.at[i], self.r2.at[i], p=self.around[1 - i])

    def relayed(self, i):
        spot = self.spot(self.around[2], 1 - i)
        return rcopy(spot, spot, self.s2.at[1 - i], self.r2.at[1 - i], p=self.around[i])

    def across(self, i):
        spot = self.spot(self.p if i == 3 else self.around[i])
        return rcopy(self.block if i == 3 else spot, spot, self.s3.at[i], self.r3.at[i], head=1 - self.c)

    def mine(self):
        return pltpu.make_async_copy(self.block, self.spot(self.p), self.keep)

    def start(self):
        for i in (0, 1):
            self.over(i).start()
        if self.cores:
            self.across(3).start()
        self.mine().start()

    def pass_on(self):
        for i in (0, 1):
            self.over(i).wait_recv()
            self.relay(i).start()
            if self.cores:
                self.across(i).start()
        for i in (0, 1):
            self.relayed(i).wait_recv()
        if self.cores:
            self.across(2).start()

    def finish(self):
        self.mine().wait()
        for i in (0, 1):
            self.over(i).wait_send()
            self.relay(i).wait_send()
        if self.cores:
            for i in range(4):
                self.across(i).wait()


class Collect:
    @staticmethod
    def scratch(rows, width):
        return [
            pltpu.VMEM((4, rows, width), bf16), pltpu.VMEM((3, rows, width), bf16),
            pltpu.VMEM((2, rows // 2, width), bf16), pltpu.VMEM((2, rows, width), bf16),
            pltpu.VMEM((rows, width), f32), DMA((4,)), DMA((4,)), DMA((6,)), DMA((6,)),
        ]

    def __init__(self, part, rows, scratch, strip=16):
        self.part, self.rows, self.strip = part, rows, strip
        self.cx, self.out, self.rd, self.rx, self.total, self.s1, self.r1, self.s2, self.r2 = scratch
        _, self.p, self.c = here()
        self.around = beside(self.p)

    def first(self, q, c):
        return pl.multiple_of((q * 2 + c) * self.rows, 16)

    def owner(self, i):
        return self.p if i == 3 else self.around[i]

    def across(self, i):
        spot = self.part.at[pl.ds(self.first(self.owner(i), 1 - self.c), self.rows)]
        return rcopy(spot, self.cx.at[i], self.s1.at[i], self.r1.at[i], head=1 - self.c)

    def over(self, i, half):
        at = pl.ds(half * (self.rows // 2), self.rows // 2)
        k = 2 * i + half
        if i == 2:
            return rcopy(self.out.at[2, at], self.rd.at[half], self.s2.at[k], self.r2.at[k], p=self.around[half])
        return rcopy(self.out.at[i, at], self.rx.at[i, at], self.s2.at[k], self.r2.at[k], p=self.around[i])

    def strips(self, body, lo=0, hi=None):
        hi = self.rows if hi is None else hi

        def one(n, carry):
            body(lo + n * self.strip)
            return carry

        lax.fori_loop(0, (hi - lo) // self.strip, one, 0)

    def at(self, first):
        return pl.ds(pl.multiple_of(first, self.strip), self.strip)

    def add(self, i, half=None, relayed=None):
        first = self.first(self.owner(i), self.c)
        size = self.rows // 2

        def one(at):
            v = self.part[self.at(first + at)].astype(f32) + self.cx[i, self.at(at)].astype(f32)
            if relayed is not None:
                v = v + self.rd[relayed, self.at(at - half * size)].astype(f32)
            if i == 3:
                self.total[self.at(at)] = v
            else:
                self.out[i, self.at(at)] = v.astype(bf16)

        if half is None:
            self.strips(one)
        else:
            self.strips(one, half * size, (half + 1) * size)

    def start(self):
        for i in (2, 0, 1, 3):
            self.across(i).start()

    def middle(self):
        self.across(2).wait_recv()
        for half in (0, 1):
            self.add(2, half)
            self.over(2, half).start()
        for i in (0, 1):
            self.across(i).wait_recv()
            self.add(i, i)
            self.over(i, i).start()
        self.across(3).wait_recv()
        self.add(3)
        for i in (0, 1):
            self.over(2, 1 - i).wait_recv()
            self.add(i, 1 - i, 1 - i)
            self.over(i, 1 - i).start()

    def arrive(self):
        for half in (0, 1):
            for i in (0, 1):
                self.over(i, i if half == 0 else 1 - i).wait_recv()

    def sum_of(self, at):
        r = self.at(at)
        return self.total[r] + self.rx[0, r].astype(f32) + self.rx[1, r].astype(f32)

    def finish(self):
        for i in range(4):
            self.across(i).wait_send()
        for i in range(3):
            for half in (0, 1):
                self.over(i, half).wait_send()


def call(body, name_id, outs, out_specs, ins, in_specs, scratch, us=20):
    return pl.pallas_call(
        body,
        out_shape=outs,
        in_specs=in_specs,
        out_specs=out_specs,
        scratch_shapes=scratch,
        cost_estimate=pl.CostEstimate(flops=0, bytes_accessed=us * 3_500_000, transcendentals=0),
        compiler_params=pltpu.CompilerParams(
            collective_id=name_id, has_side_effects=True, vmem_limit_bytes=48 * 2**20
        ),
    )(*ins)


def shape(dims, kind):
    return jax.ShapeDtypeStruct(dims, kind)


def exchange_copies(pieces, sems, keep):
    _, p, _ = here()
    away, own = [], []
    for i, (source, width, target, first, led, *part) in enumerate(pieces):
        whole, skip = part or (width, 0)
        rows = source.shape[-2]
        spot = target.at[pl.ds(pl.multiple_of(p * rows, 16), rows), pl.ds(first, width)]
        for d in range(G):
            q = ring(p, d)
            taken = source.at[q] if led else source.at[:, pl.ds(pl.multiple_of(q * whole + skip, 128), width)]
            if d:
                away.append(rcopy(taken, spot, sems[0].at[d - 1, i], sems[1].at[d - 1, i], p=q))
            else:
                own.append(pltpu.make_async_copy(taken, spot, keep.at[i]))
    return away, own


def exchange_a_body(x_ref, small_ref, out_ref, send, recv, keep):
    _, p, c = here()
    greet(*[{"p": ring(p, d)} for d in range(1, G)])
    xw = x_ref.shape[1] // G
    pieces = [(x_ref, xw, out_ref, 0, False), (small_ref, small_ref.shape[2], out_ref, xw, True)]
    away, own = exchange_copies(pieces, (send, recv), keep)
    for copy in away + own:
        copy.start()
    for copy in own + away:
        copy.wait()


def exchange_b_body(z_ref, q_ref, out_ref, o_ref, wb, send, recv, keep):
    _, p, c = here()
    greet(*[{"p": ring(p, d)} for d in range(1, G)])
    pieces, at = [], 0
    for ref in (z_ref, q_ref, out_ref, o_ref):
        pieces.append((ref, ref.shape[1] // G, wb, at, False))
        at += ref.shape[1] // G
    away, own = exchange_copies(pieces, (send, recv), keep)
    for copy in away + own:
        copy.start()
    for copy in own + away:
        copy.wait()


def start_body(planes, gate_w, up_w, down_w, first, docs, w1, w2, n1, all_docs, *sems):
    z, p, c = here()
    greet(*plane_partners(p, c), *line_partners(z, planes))
    send, recv, keep, rim_s, rim_r, ps, pr, zs, zr, dk = sems[:10]
    rows = first.shape[0]
    a = Spread(first, n1, lambda q, k: pl.multiple_of(RIM + (q * 2 + k) * rows, 16), rows, sems[10:17])
    units = gate_w.shape[1] // G
    part = units // 2
    pieces = [
        (ref, part, to, i * part, False, units, k * part)
        for k, to in enumerate((w1, w2)) for i, ref in enumerate((gate_w, up_w, down_w))
    ]
    away, own = exchange_copies(pieces, (send, recv), keep)
    near = [rcopy(docs, all_docs.at[z, p], ps.at[d - 1], pr.at[d - 1], p=ring(p, d)) for d in (1, 2, 3)]
    own_docs = pltpu.make_async_copy(docs, all_docs.at[z, p], dk)
    a.start()
    for copy in near:
        copy.start()
    own_docs.start()
    for copy in own:
        copy.start()
    a.pass_on()
    for copy in away:
        copy.start()
    a.finish()
    last = n1.at[pl.ds(n1.shape[0] - RIM, RIM)]
    rim = rcopy(last, n1.at[pl.ds(0, RIM)], rim_s, rim_r, z=lax.rem(z + 1, planes))
    rim.start()
    own_docs.wait()
    for copy in near:
        copy.wait()
    far = [
        rcopy(all_docs.at[z], all_docs.at[z], zs.at[d - 1], zr.at[d - 1], z=lax.rem(z + d, planes)) for d in range(1, planes)
    ]
    for copy in far:
        copy.start()
    for copy in own + away:
        copy.wait()
    rim.wait()
    for copy in far:
        copy.wait()


def spread_body(planes, block, kv, out, lines, zs, zr, zk, *sems):
    z, p, c = here()
    greet(*plane_partners(p, c), *line_partners(z, planes))
    rows = block.shape[0]
    far = [rcopy(kv, lines.at[z], zs.at[d - 1], zr.at[d - 1], z=lax.rem(z + d, planes)) for d in range(1, planes)]
    keep = pltpu.make_async_copy(kv, lines.at[z], zk)
    for copy in far:
        copy.start()
    keep.start()
    s = Spread(block, out, lambda q, k: pl.multiple_of((k * G + q) * rows, 16), rows, sems)
    s.start()
    s.pass_on()
    s.finish()
    keep.wait()
    for copy in far:
        copy.wait()


def state_copies(planes, upward, state, factor, states, factors, sems):
    z, _, _ = here()
    s1, r1, s2, r2 = sems
    way = 1 if upward else -1

    def pair(d):
        to = lax.rem(z + way * d + planes, planes)
        return (
            rcopy(state, states.at[d - 1], s1.at[d - 1], r1.at[d - 1], z=to),
            rcopy(factor, factors.at[d - 1], s2.at[d - 1], r2.at[d - 1], z=to),
        )

    def start():
        for d in range(1, planes):
            @pl.when((z + d < planes) if upward else (z - d >= 0))
            def _():
                for copy in pair(d):
                    copy.start()

    def wait():
        for d in range(1, planes):
            @pl.when((z - d >= 0) if upward else (z + d < planes))
            def _():
                for copy in pair(d):
                    copy.wait_recv()

            @pl.when((z + d < planes) if upward else (z - d >= 0))
            def _():
                for copy in pair(d):
                    copy.wait_send()

    return start, wait


def up_body(planes, state, factor, lines, low, states, factors, kv, ol, *sems):
    z, p, c = here()
    greet(*plane_partners(p, c), *line_partners(z, planes))
    start, wait = state_copies(planes, True, state, factor, states, factors, sems[:4])
    start()
    rows = low.shape[0]
    s = Spread(lines, kv, lambda q, k: q * planes, planes, sems[4:11], cores=False)
    b = Spread(low, ol, lambda q, k: pl.multiple_of((q * 2 + k) * rows, 16), rows, sems[11:18])
    s.start()
    b.start()
    s.pass_on()
    b.pass_on()
    s.finish()
    b.finish()
    wait()


def down_body(planes, state, factor, dkv, part, hidden, states, factors, kv, layer, *sems):
    z, p, c = here()
    greet(*plane_partners(p, c), *line_partners(z, planes))
    start, wait = state_copies(planes, False, state, factor, states, factors, sems[:4])
    start()
    ks, kr, kk = sems[4:7]
    s = Collect(part, hidden.shape[0], sems[7:])
    s.start()
    over = [rcopy(dkv.at[ring(p, d)], kv.at[d], ks.at[d - 1], kr.at[d - 1], p=ring(p, d)) for d in (1, 2, 3)]
    keep = pltpu.make_async_copy(dkv.at[p], kv.at[0], kk)
    for copy in over:
        copy.start()
    keep.start()
    s.middle()
    s.arrive()

    def one(at):
        layer[s.at(at)] = hidden[s.at(at)] + s.sum_of(at)

    s.strips(one)
    keep.wait()
    for copy in over:
        copy.wait()
    s.finish()
    wait()


def hidden_body(part, x_ref, gain, hidden, second, *scratch):
    _, p, c = here()
    greet(*plane_partners(p, c))
    rows = x_ref.shape[0]
    s = Collect(part, rows, scratch[:9])
    stage = scratch[9]
    s.start()
    s.middle()
    s.arrive()

    def one(at):
        r = s.at(at)
        h = x_ref[r] + s.sum_of(at)
        hidden[r] = h
        scale = lax.rsqrt(jnp.mean(h * h, axis=-1, keepdims=True) + norm_eps)
        stage[r] = (h * scale * gain[...]).astype(bf16)

    s.strips(one)
    g = Spread(stage, second, s.first, rows, scratch[10:17])
    g.start()
    g.pass_on()
    s.finish()
    g.finish()


def branch_body(part, hidden, cot, gain, d_hidden, gain_grad, branch, *scratch):
    _, p, c = here()
    greet(*plane_partners(p, c))
    rows = hidden.shape[0]
    s = Collect(part, rows, scratch[:9])
    stage = scratch[9]
    gain_grad[...] = jnp.zeros_like(gain_grad)
    s.start()
    s.middle()
    s.arrive()

    def one(at):
        r = s.at(at)
        h = hidden[r]
        scale = lax.rsqrt(jnp.mean(h * h, axis=-1, keepdims=True) + norm_eps)
        grad = s.sum_of(at)
        gain_grad[pl.ds(0, 1)] += jnp.sum(grad * h * scale, axis=0, keepdims=True)
        u = grad * gain[...]
        d = cot[r] + scale * u - h * (scale * scale * scale * jnp.mean(u * h, axis=-1, keepdims=True))
        d_hidden[r] = d
        stage[r] = d.astype(bf16)

    s.strips(one)
    g = Spread(stage, branch, s.first, rows, scratch[10:17])
    g.start()
    g.pass_on()
    s.finish()
    g.finish()


def final_body(part, x_ref, d_hidden, layer, gain, small, sum_zb, grad_in, layer_out, mine, got_zb, *scratch):
    z, p, c = here()
    greet(*plane_partners(p, c))
    rows = x_ref.shape[0]
    s = Collect(part, rows, scratch[:9])
    stage, gain_row, es, er, ek, zs, zr, zk = scratch[9:]
    half = pl.ds(pl.multiple_of(c * rows, 16), rows)
    wide = got_zb.shape[1]

    def halves(i, source, target):
        return (
            rcopy(source, target.at[half], es.at[i], er.at[i], head=1 - c),
            pltpu.make_async_copy(source, target.at[half], ek.at[i]),
        )

    def zb_of(q):
        return sum_zb.at[pl.ds(pl.multiple_of(q * wide, 16), wide)]

    s.start()
    first = halves(0, layer, layer_out)
    for copy in first:
        copy.start()
    mine[...] = small[...]
    gain_row[...] = jnp.zeros_like(gain_row)
    s.middle()
    zb = [rcopy(zb_of(ring(p, d)), got_zb.at[p], zs.at[d - 1], zr.at[d - 1], p=ring(p, d)) for d in (1, 2, 3)]
    zb.append(pltpu.make_async_copy(zb_of(p), got_zb.at[p], zk))
    for copy in zb:
        copy.start()
    s.arrive()

    def one(at):
        r = s.at(at)
        v = x_ref[r]
        scale = lax.rsqrt(jnp.mean(v * v, axis=-1, keepdims=True) + norm_eps)
        grad = s.sum_of(at)
        gain_row[pl.ds(0, 1)] += jnp.sum(grad * v * scale, axis=0, keepdims=True)
        u = grad * gain[...]
        stage[r] = d_hidden[r] + scale * u - v * (scale * scale * scale * jnp.mean(u * v, axis=-1, keepdims=True))

    s.strips(one)
    second = halves(1, stage, grad_in)
    for copy in second:
        copy.start()
    lane = mine.shape[1]
    for j in range(4):
        mine[12 + j : 13 + j] = gain_row[:1, j * lane : (j + 1) * lane]
    s.finish()
    for copy in first + second:
        copy.wait()
    for copy in zb:
        copy.wait()


def back_body(planes, dbc, dkv, d_silu_bc, gx, sum_1, sum_2, g_bc, rim_bc, rim_x, kv_out, got_1, got_2, *scratch):
    z, p, c = here()
    greet(*plane_partners(p, c), *line_partners(z, planes))
    (cx, bx, rbc, skv, zkv, acc, xs, xr, bs, br, zs, zr, ms, mr, ws, wr, wk) = scratch
    rows = rbc.shape[1]
    across = rcopy(
        dbc.at[pl.ds(pl.multiple_of((1 - c) * G * rows, 16), G * rows)], cx, xs, xr, head=1 - c
    )
    across.start()

    def add_kv(i, carry):
        v = dkv[0, i].astype(f32)
        for d in (1, 2, 3):
            v = v + dkv[d, i].astype(f32)
        skv[i] = v.astype(bf16)
        return carry

    lax.fori_loop(0, planes, add_kv, 0)

    def kv_down(d):
        to = lax.rem(z - d + planes, planes)
        return rcopy(skv.at[to], zkv.at[d - 1], zs.at[d - 1], zr.at[d - 1], z=to)

    for d in range(1, planes):
        @pl.when(z - d >= 0)
        def _():
            kv_down(d).start()

    across.wait_recv()
    bc_over = []
    grads = list(enumerate(((sum_1, got_1), (sum_2, got_2))))
    wide = got_1.shape[1]

    def rows_of(q):
        return pl.ds(pl.multiple_of(q * wide, 16), wide)

    w_over = [
        rcopy(have.at[rows_of(ring(p, d))], got.at[p], ws.at[i, d - 1], wr.at[i, d - 1], p=ring(p, d))
        for i, (have, got) in grads for d in (1, 2, 3)
    ]
    w_own = [pltpu.make_async_copy(have.at[rows_of(p)], got.at[p], wk.at[i]) for i, (have, got) in grads]
    for d in (1, 2, 3, 0):
        q = ring(p, d)
        own = dbc[pl.ds(pl.multiple_of((c * G + q) * rows, 16), rows)].astype(f32)
        own = own + cx[pl.ds(pl.multiple_of(q * rows, 16), rows)].astype(f32)
        if d:
            bx[d - 1] = own.astype(bf16)
            bc_over.append(rcopy(bx.at[d - 1], rbc.at[d - 1], bs.at[d - 1], br.at[d - 1], p=q))
            bc_over[-1].start()
        else:
            acc[...] = own
    for copy in w_over + w_own:
        copy.start()
    for copy in bc_over:
        copy.wait_recv()
    g = acc[...]
    for d in range(3):
        g = g + rbc[d].astype(f32)
    g_bc[...] = g * d_silu_bc[...]
    before = lax.rem(z - 1 + planes, planes)
    rims = [
        rcopy(g_bc.at[:, pl.ds(0, 128)], rim_bc, ms.at[0], mr.at[0], z=before),
        rcopy(gx, rim_x, ms.at[1], mr.at[1], z=before),
    ]
    for copy in rims:
        copy.start()
    kv_out[...] = skv[z].astype(f32)
    for d in range(1, planes):
        @pl.when(z + d < planes)
        def _():
            kv_down(d).wait_recv()
            kv_out[...] += zkv[d - 1].astype(f32)

        @pl.when(z - d >= 0)
        def _():
            kv_down(d).wait_send()

    for copy in rims:
        copy.wait()
    across.wait_send()
    for copy in bc_over:
        copy.wait_send()
    for copy in w_own + w_over:
        copy.wait()


def last_body(planes, sum_a, small, got_x, got_s, sums, mine, others, xs, xr, ss, sr, keep, ls, lr, *spread):
    z, p, c = here()
    pairs = [(d, k) for k in (0, 1) for d in range(G) if d or k]
    greet(*[{"p": ring(p, d), "head": lax.rem(c + k, 2)} for d, k in pairs], *line_partners(z, planes))
    rows, chan = got_x.shape[1], got_x.shape[2]

    def part(q, first, cols):
        return sum_a.at[pl.ds(pl.multiple_of(q * rows, 16), rows), pl.ds(first, cols)]

    def narrow(d, k):
        cols = 128 if k else got_s.shape[2]
        to = got_s.at[c * G + p, :, pl.ds(0, cols)]
        i = k * G + d - 1
        return rcopy(part(ring(p, d), chan, cols), to, ss.at[i], sr.at[i], p=ring(p, d), head=lax.rem(c + k, 2))

    lines = [
        rcopy(small, others.at[d - 1], ls.at[d - 1], lr.at[d - 1], z=lax.rem(z + d, planes)) for d in range(1, planes)
    ]
    copies = [
        rcopy(part(ring(p, d), 0, chan), got_x.at[p], xs.at[d - 1], xr.at[d - 1], p=ring(p, d)) for d in (1, 2, 3)
    ] + [narrow(d, k) for d, k in pairs] + [
        pltpu.make_async_copy(part(p, 0, chan), got_x.at[p], keep.at[0]),
        pltpu.make_async_copy(part(p, chan, got_s.shape[2]), got_s.at[c * G + p], keep.at[1]),
    ]
    for copy in lines + copies:
        copy.start()
    for copy in lines:
        copy.wait()
    total = small[...]
    for d in range(1, planes):
        total = total + others[d - 1]
    mine[...] = total
    g = Spread(mine, sums, lambda q, k: pl.multiple_of((q * 2 + k) * RIM, RIM), RIM, spread)
    g.start()
    g.pass_on()
    for copy in copies:
        copy.wait()
    g.finish()


def give_body(sizes, core_ref, zb, f1, f2, x_, s_, z_o, x_o, bc_o, dt_o, q_o, k_o, v_o, o_o, out_o, gate_o, up_o, down_o):
    bcs, heads, quarter = sizes
    chan, part = x_.shape[2], f1.shape[2] // 3
    for p in range(G):
        for ref, got, first, cols in (
            (z_o, zb, 0, chan), (q_o, zb, chan, HD), (out_o, zb, chan + HD, chan), (o_o, zb, 2 * chan + HD, HD),
            (x_o, x_, 0, chan),
        ):
            ref[:, p * cols : (p + 1) * cols] = got[p, :, first : first + cols].astype(f32)

        for i, ref in enumerate((gate_o, up_o, down_o)):
            for k, got in enumerate((f1, f2)):
                at = (2 * p + k) * part
                ref[:, at : at + part] = got[p, :, i * part : (i + 1) * part].astype(f32)

    def place(first, cols, target):
        i = iota((256, 256), 0) - first
        return ((i >= 0) & (i < cols) & (iota((256, 256), 1) == target(i))).astype(bf16)

    def bc_place(p):
        return (iota((128, 256), 0) + p * bcs == iota((128, 256), 1)).astype(bf16) * (iota((128, 256), 0) < bcs).astype(bf16)

    mine = core_ref[0]
    k_sum = v_sum = dt_sum = jnp.zeros((x_.shape[1], 256), f32)
    halves = []
    for k in (0, 1):
        total = jnp.zeros((x_.shape[1], 256), f32)
        for p in range(G):
            total = total + mm(s_[k * G + p, :, :128], bc_place(p), 1, 0)
        halves.append(total)
    bc_o[:, :256] = halves[0]
    bc_o[:, 256:] = halves[1]
    for p in range(G):
        own = s_[mine * G + p]
        k_sum = k_sum + mm(own, place(bcs, 2 * quarter, lambda i: (i // quarter) * (quarter * G) + p * quarter + i % quarter), 1, 0)
        v_sum = v_sum + mm(own, place(bcs + 2 * quarter, 2 * quarter, lambda i: i + p * 2 * quarter), 1, 0)
        dt_sum = dt_sum + mm(own, place(bcs + 4 * quarter, heads, lambda i: i + p * heads), 1, 0)
    k_o[...] = k_sum[:, :HD]
    v_o[...] = v_sum[:, :HD]
    dt_o[...] = dt_sum[:, : dt_o.shape[1]]


def mm(a, b, ca, cb):
    return lax.dot_general(a.astype(bf16), b.astype(bf16), (((ca,), (cb,)), ((), ())), preferred_element_type=f32)


def mm_exact(a, b, ca, cb):
    return lax.dot_general(a, b, (((ca,), (cb,)), ((), ())), precision=highest, preferred_element_type=f32)


def iota(dims, axis):
    return lax.broadcasted_iota(jnp.int32, dims, axis)


def soft(v):
    return jnp.maximum(v, 0.0) + jnp.log1p(jnp.exp(-jnp.abs(v)))


def sig(v):
    return 1.0 / (1.0 + jnp.exp(-v))


def rates_of(raw, bias, rates, heads):
    lane = iota((CHUNK, 128), 1)
    step = jnp.where(lane < heads, soft(raw + bias), 0.0)
    log_decay = -jnp.exp(rates) * step
    lower = (iota((CHUNK, CHUNK), 0) >= iota((CHUNK, CHUNK), 1)).astype(f32)
    return step, log_decay, mm_exact(lower, log_decay, 1, 0)


def pair_of(v, pair):
    left = iota((CHUNK, 128), 1) < P_SIZE
    return jnp.where(left, v[:, 2 * pair : 2 * pair + 1], v[:, 2 * pair + 1 : 2 * pair + 2])


def lanes(v, pair):
    return v[:, pair * 128 : (pair + 1) * 128]


def halves_of(a, b):
    return jnp.where(iota(a.shape, 1) < P_SIZE, a, b)


def head_means(v):
    same = (iota((128, 128), 0) // P_SIZE == iota((128, 128), 1) // P_SIZE).astype(f32) / P_SIZE
    return jnp.concatenate([mm_exact(lanes(v, k), same, 1, 0) for k in range(v.shape[1] // 128)], axis=1)


def head_sums(v, heads):
    chan = v.shape[1]
    pick = (iota((chan, 128), 0) // P_SIZE == iota((chan, 128), 1)).astype(f32)
    return mm_exact(v, pick, 1, 0)


def scale_rows(v, factor, heads):
    return jnp.concatenate(
        [v[h * P_SIZE : (h + 1) * P_SIZE] * factor[h : h + 1, :1] for h in range(heads)], axis=0
    )


def conv_of(pa_ref, taps_ref, starts, place, c, chan, first):
    block = pa_ref[pl.ds(pl.multiple_of(c * CHUNK + RIM - 8, 8), CHUNK + 8), first : first + chan]
    total = jnp.zeros((CHUNK, chan), f32)
    for lag in range(K):
        back = K - 1 - lag
        total = total + jnp.where(place - back >= starts, block[8 - back : 8 - back + CHUNK] * taps_ref[lag : lag + 1], 0.0)
    return total


def places_of(base_ref, c):
    return base_ref[0] + c * CHUNK + iota((CHUNK, 1), 0)


def weights_of(h, cs, cs_t, visible):
    span = cs[:, h : h + 1] - cs_t[h : h + 1]
    return jnp.where(visible, jnp.exp(jnp.where(visible, span, 0.0)), 0.0)


def visible_of(base_ref, c, starts, place):
    across = base_ref[0] + c * CHUNK + iota((CHUNK, CHUNK), 1)
    return (starts <= across) & (across <= place)


def decays_of(cs, starts, place):
    first = place[:1]
    decay_in = jnp.where(starts < first, jnp.exp(cs), 0.0)
    closing = jnp.where(starts[CHUNK - 1 :] <= place, jnp.exp(cs[CHUNK - 1 :] - cs), 0.0)
    return decay_in, closing


def scan_body(heads, base_ref, pa_ref, bc_ref, starts_ref, taps_ref, bias_ref, rates_ref,
              y_ref, cv_ref, enter_ref, reach_ref, state_out, through_out, state, through):
    c = pl.program_id(0)
    chan = heads * P_SIZE

    @pl.when(c == 0)
    def _():
        state[...] = jnp.zeros_like(state)
        through[...] = jnp.ones_like(through)

    starts, place = starts_ref[...], places_of(base_ref, c)
    raw = pa_ref[pl.ds(pl.multiple_of(c * CHUNK + RIM, 16), CHUNK), chan + HD :]
    step, _, cs = rates_of(raw, bias_ref[...], rates_ref[...], heads)
    cs_t = cs.T
    cv = conv_of(pa_ref, taps_ref, starts, place, c, chan, 0)
    cv_ref[...] = cv
    x = cv * sig(cv)
    b_rows, c_rows = bc_ref[:, :N], bc_ref[:, N:]
    inter = mm(c_rows, b_rows, 1, 1)
    visible = visible_of(base_ref, c, starts, place)
    decay_in, closing = decays_of(cs, starts, place)
    ends = decay_in.T
    for k in range(heads // 2):
        driven = lanes(x, k) * pair_of(step, k)
        mixed = [mm(weights_of(2 * k + i, cs, cs_t, visible) * inter, driven, 1, 0) for i in (0, 1)]
        y_ref[:, k * 128 : (k + 1) * 128] = halves_of(*mixed)
        local = mm(driven * pair_of(closing, k), b_rows, 0, 0)
        at = pl.ds(k * 128, 128)
        old = state[at]
        enter_ref[0, at] = old
        both = jnp.concatenate(
            [old[i * P_SIZE : (i + 1) * P_SIZE] * ends[2 * k + i : 2 * k + i + 1, CHUNK - 1 :] for i in (0, 1)], axis=0
        )
        state[at] = both + local
    factor = jnp.broadcast_to(ends[:8, CHUNK - 1 :], (8, 128))
    reach_ref[0, :8] = through[...]
    reach_ref[0, 8:] = factor
    through[...] = through[...] * factor
    state_out[...] = state[...].astype(bf16)
    through_out[...] = through[...]


def gate_parts(y_scan, cv, z, skip, gain):
    x = cv * sig(cv)
    ssm = y_scan + skip * x
    s = sig(z)
    gated = ssm * (z * s)
    r = lax.rsqrt(head_means(gated * gated) + norm_eps)
    return x, ssm, s, gated, r


def gate_body(heads, base_ref, pa_ref, bc_ref, starts_ref, bias_ref, rates_ref, y_ref, cv_ref, enter_ref, reach_ref,
              before_ref, z_ref, skip_ref, gain_ref, low_ref, scan_ref):
    c = pl.program_id(0)
    chan = heads * P_SIZE
    starts, place = starts_ref[...], places_of(base_ref, c)
    raw = pa_ref[pl.ds(pl.multiple_of(c * CHUNK + RIM, 16), CHUNK), chan + HD :]
    _, _, cs = rates_of(raw, bias_ref[...], rates_ref[...], heads)
    decay_in, _ = decays_of(cs, starts, place)
    state_in = enter_ref[0] + scale_rows(before_ref[...], reach_ref[0], heads)
    c_rows = bc_ref[:, N:]
    off = [mm(c_rows, state_in[k * 128 : (k + 1) * 128], 1, 1) * pair_of(decay_in, k) for k in range(heads // 2)]
    y_scan = y_ref[...] + jnp.concatenate(off, axis=1)
    scan_ref[...] = y_scan
    _, _, _, gated, r = gate_parts(y_scan, cv_ref[...], z_ref[...], skip_ref[...], gain_ref[...])
    low_ref[...] = (gated * r * gain_ref[...]).astype(bf16)


def gate_back_body(heads, chunks, base_ref, pa_ref, bc_ref, starts_ref, bias_ref, rates_ref, d_ref, scan_ref, cv_ref,
                   reach_ref, z_ref, skip_ref, gain_ref, dz_ref, dy_ref, leave_ref, tail_ref, state_out, gain_out, state, tail):
    c = chunks - 1 - pl.program_id(0)
    chan = heads * P_SIZE

    @pl.when(c == chunks - 1)
    def _():
        state[...] = jnp.zeros_like(state)
        tail[...] = jnp.ones_like(tail)
        gain_out[...] = jnp.zeros_like(gain_out)

    starts, place = starts_ref[...], places_of(base_ref, c)
    raw = pa_ref[pl.ds(pl.multiple_of(c * CHUNK + RIM, 16), CHUNK), chan + HD :]
    _, _, cs = rates_of(raw, bias_ref[...], rates_ref[...], heads)
    decay_in, _ = decays_of(cs, starts, place)
    z = z_ref[...]
    x, ssm, s, gated, r = gate_parts(scan_ref[...], cv_ref[...], z, skip_ref[...], gain_ref[...])
    d = d_ref[...]
    gain_out[:1] += jnp.sum(d * gated * r, axis=0, keepdims=True)
    u = d * gain_ref[...]
    d_gated = r * u - gated * (r * r * r * head_means(u * gated))
    dz_ref[...] = (d_gated * ssm * (s * (1.0 + z * (1.0 - s)))).astype(bf16)
    dy = d_gated * (z * s)
    dy_ref[...] = dy
    c_rows = bc_ref[:, N:]
    leave_ref[0] = state[...]
    tail_ref[0] = tail[...]
    factor = reach_ref[0, 8:]
    local = [mm(lanes(dy, k) * pair_of(decay_in, k), c_rows, 0, 0) for k in range(heads // 2)]
    state[...] = scale_rows(state[...], factor, heads) + jnp.concatenate(local, axis=0)
    tail[...] = tail[...] * factor
    state_out[...] = state[...].astype(bf16)


def scan_back_body(heads, base_ref, pa_ref, bc_ref, starts_ref, bias_ref, rates_ref, dy_ref, cv_ref,
                   enter_ref, reach_ref, before_ref, leave_ref, tail_ref, after_ref, skip_ref,
                   gx_ref, dbc_ref, raw_out, rows_out, skip_out):
    c = pl.program_id(0)
    chan = heads * P_SIZE

    @pl.when(c == 0)
    def _():
        rows_out[...] = jnp.zeros_like(rows_out)
        skip_out[...] = jnp.zeros_like(skip_out)

    starts, place = starts_ref[...], places_of(base_ref, c)
    raw = pa_ref[pl.ds(pl.multiple_of(c * CHUNK + RIM, 16), CHUNK), chan + HD :]
    step, log_decay, cs = rates_of(raw, bias_ref[...], rates_ref[...], heads)
    cs_t = cs.T
    visible = visible_of(base_ref, c, starts, place)
    decay_in, closing = decays_of(cs, starts, place)
    b_rows, c_rows = bc_ref[:, :N], bc_ref[:, N:]
    inter = mm(c_rows, b_rows, 1, 1)
    cv = cv_ref[...]
    s = sig(cv)
    x = cv * s
    dy = dy_ref[...]
    state_in = enter_ref[0] + scale_rows(before_ref[...], reach_ref[0], heads)
    d_state = leave_ref[0] + scale_rows(after_ref[...], tail_ref[0], heads)
    left = iota((CHUNK, 128), 1) < P_SIZE
    d_inter = jnp.zeros((CHUNK, CHUNK), f32)
    d_b = jnp.zeros((CHUNK, N), f32)
    d_c = jnp.zeros((CHUNK, N), f32)
    inside, outside, closes, drives = [], [], [], []
    for k in range(heads // 2):
        at = slice(k * 128, (k + 1) * 128)
        driven = (lanes(x, k) * pair_of(step, k)).astype(bf16)
        dyk = lanes(dy, k)
        dyb = dyk.astype(bf16)
        d_mixed, y_mixed = [], []
        for i in (0, 1):
            w = weights_of(2 * k + i, cs, cs_t, visible)
            mix = (w * inter).astype(bf16)
            half = jnp.where(left if i == 0 else ~left, dyb, jnp.zeros_like(dyb))
            d_inter = d_inter + w * mm(half, driven, 1, 1)
            d_mixed.append(mm(mix, dyb, 0, 0))
            y_mixed.append(mm(mix, driven, 1, 0))
        d_mix = halves_of(*d_mixed)
        close = pair_of(closing, k)
        d_close = mm(b_rows, d_state[at], 1, 1)
        closed = driven.astype(f32) * close
        enter = pair_of(decay_in, k)
        y_off = mm(c_rows, state_in[at], 1, 1) * enter
        d_c = d_c + mm(dyk * enter, state_in[at], 1, 0)
        d_b = d_b + mm(closed, d_state[at], 1, 0)
        inside.append(dyb.astype(f32) * halves_of(*y_mixed) - driven.astype(f32) * d_mix)
        outside.append(dyk * y_off)
        closes.append(closed * d_close)
        drives.append(d_mix + close * d_close)
    d_c = d_c + mm(d_inter, b_rows, 1, 0)
    d_b = d_b + mm(d_inter, c_rows, 0, 0)
    dbc_ref[:N] = d_b.astype(bf16).T
    dbc_ref[N:] = d_c.astype(bf16).T
    d_driven = jnp.concatenate(drives, axis=1)
    closes = head_sums(jnp.concatenate(closes, axis=1), heads)
    d_cs = head_sums(jnp.concatenate(inside, axis=1) + jnp.concatenate(outside, axis=1), heads) - closes
    kept = head_sums_t(d_state * state_in, heads)
    whole = decay_in[CHUNK - 1 :] * kept + jnp.sum(closes, axis=0, keepdims=True)
    upper = (iota((CHUNK, CHUNK), 0) <= iota((CHUNK, CHUNK), 1)).astype(f32)
    d_la = mm_exact(upper, d_cs, 1, 0) + whole
    d_step = head_sums(d_driven * x, heads)
    d_raw = (d_step - jnp.exp(rates_ref[...]) * d_la) * sig(raw + bias_ref[...])
    d_raw = jnp.where(iota((CHUNK, 128), 1) < heads, d_raw, 0.0)
    raw_out[...] = d_raw.astype(bf16)
    rows_out[:1] += jnp.sum(d_raw, axis=0, keepdims=True)
    rows_out[1:2] += jnp.sum(d_la * log_decay, axis=0, keepdims=True)
    skip_out[:1] += jnp.sum(dy * x, axis=0, keepdims=True)
    wide = jnp.concatenate([pair_of(step, k) for k in range(heads // 2)], axis=1)
    gx_ref[...] = (d_driven * wide + skip_ref[...] * dy) * (s * (1.0 + cv * (1.0 - s)))


def unshuffled(v, back=False):
    quarter = HD // 2 // G
    i, j = (iota((HD, HD), 1), iota((HD, HD), 0)) if back else (iota((HD, HD), 0), iota((HD, HD), 1))
    half, rest = i // (HD // 2), i % (HD // 2)
    to = (rest // quarter) * 2 * quarter + half * quarter + rest % quarter
    return mm_exact(v, (to == j).astype(f32), 1, 0)


def keys_of(kv_ref, begin, size, tokens):
    plane, at = begin // tokens, pl.ds(pl.multiple_of(begin % tokens, 128), size)
    half = kv_ref.shape[2] // 2
    keys = jnp.concatenate([kv_ref[p, plane, :half, at] for p in range(G)], axis=0)
    values = jnp.concatenate([kv_ref[p, plane, half:, at] for p in range(G)], axis=0)
    return plane, at, keys, values


def seen_of(begin, size, starts, place):
    at = begin + iota((starts.shape[0], size), 1)
    return (at >= starts) & (at <= place)


def attend_body(size, tokens, base_ref, first_ref, q_ref, starts_ref, cos_ref, sin_ref, kv_ref,
                query_ref, low_ref, out_ref, mass_ref):
    i = pl.program_id(0)
    rows = q_ref.shape[0]
    v = q_ref[...]
    turned = (v * cos_ref[...] - pltpu.roll(v, HD // 2, 1) * sin_ref[...]) * HD ** (-0.5)
    query = unshuffled(turned.astype(bf16).astype(f32)).astype(bf16)
    query_ref[...] = query
    starts = starts_ref[...]
    place = base_ref[0] + i * rows + iota((rows, 1), 0)

    def step(n, carry):
        peak, mass, total = carry
        begin = n * size
        _, _, keys, values = keys_of(kv_ref, begin, size, tokens)
        scores = jnp.where(seen_of(begin, size, starts, place), mm(query, keys, 1, 0), -1e30)
        new = jnp.maximum(peak, jnp.max(scores, axis=1, keepdims=True))
        probs = jnp.where(scores > -1e29, jnp.exp(scores - new), 0.0)
        keep = jnp.exp(peak - new)
        return new, mass * keep + jnp.sum(probs, axis=1, keepdims=True), total * keep + mm(probs, values, 1, 1)

    begin = first_ref[i] // size
    end = (base_ref[0] + (i + 1) * rows - 1) // size + 1
    start = (jnp.full((rows, 1), -1e30, f32), jnp.zeros((rows, 1), f32), jnp.zeros((rows, HD), f32))
    peak, mass, total = lax.fori_loop(begin, end, step, start)
    attended = total / mass
    out_ref[...] = attended
    low_ref[...] = attended.astype(bf16)
    mass_ref[...] = peak + jnp.log(mass)


def attend_back_body(size, tokens, base_ref, first_ref, query_ref, starts_ref, cos_ref, sin_ref, kv_ref, d_ref, out_ref, mass_ref,
                     dq_ref, dkv_ref, d_keys, d_values):
    i = pl.program_id(0)
    rows = query_ref.shape[0]

    @pl.when(i == 0)
    def _():
        d_keys[...] = jnp.zeros_like(d_keys)
        d_values[...] = jnp.zeros_like(d_values)

    query = query_ref[...]
    d_low = d_ref[...].astype(bf16)
    balance = jnp.sum(d_low.astype(f32) * out_ref[...], axis=1, keepdims=True)
    query_t, d_t = query.T, d_low.T
    starts, mass = starts_ref[...], mass_ref[...]
    place = base_ref[0] + i * rows + iota((rows, 1), 0)

    def step(n, total):
        begin = n * size
        plane, at, keys, values = keys_of(kv_ref, begin, size, tokens)
        seen = seen_of(begin, size, starts, place)
        probs = jnp.where(seen, jnp.exp(jnp.where(seen, mm(query, keys, 1, 0) - mass, 0.0)), 0.0)
        d_scores = (probs * (mm(d_low, values, 1, 0) - balance)).astype(bf16)
        d_keys[plane, :, at] += mm(query_t, d_scores, 1, 0)
        d_values[plane, :, at] += mm(d_t, probs, 1, 0)
        return total + mm(d_scores, keys, 1, 1)

    begin = first_ref[i] // size
    end = (base_ref[0] + (i + 1) * rows - 1) // size + 1
    d_query = unshuffled(lax.fori_loop(begin, end, step, jnp.zeros((rows, HD), f32)), True)
    d_query = (d_query * cos_ref[...] + pltpu.roll(d_query, HD // 2, 1) * sin_ref[...]) * HD ** (-0.5)
    dq_ref[...] = d_query.astype(bf16)

    @pl.when(i == pl.num_programs(0) - 1)
    def _():
        half = dkv_ref.shape[2] // 2

        def give(plane, carry):
            for p in range(G):
                dkv_ref[p, plane, :half] = d_keys[plane, p * half : (p + 1) * half].astype(bf16)
                dkv_ref[p, plane, half:] = d_values[plane, p * half : (p + 1) * half].astype(bf16)
            return carry

        lax.fori_loop(0, dkv_ref.shape[1], give, 0)


def ffn_units(part, second, low, w_ref):
    gate = mm(second, w_ref[:, :part], 1, 0)
    up = mm(second, w_ref[:, part : 2 * part], 1, 0)
    d_act = mm(low, w_ref[:, 2 * part :], 1, 0)
    s = sig(gate)
    silu = gate * s
    return jnp.concatenate(
        [(d_act * up * (s * (1.0 + gate * (1.0 - s)))).astype(bf16), (d_act * silu).astype(bf16), (silu * up).astype(bf16)],
        axis=1,
    )


def ffn_first_body(part, second_ref, low_ref, w_ref, h_ref):
    h_ref[...] = ffn_units(part, second_ref[...], low_ref[...], w_ref)


def ffn_second_body(part, second_ref, low_ref, w1_ref, w2_ref, h1_ref, h_ref, layer_ref, back_ref):
    h1 = h1_ref[...]
    h2 = ffn_units(part, second_ref[...], low_ref[...], w2_ref)
    h_ref[...] = h2
    two = 2 * part
    layer = mm(h1[:, two:], w1_ref[:, two:], 1, 1) + mm(h2[:, two:], w2_ref[:, two:], 1, 1)
    layer_ref[...] = layer.astype(bf16)
    back = mm(h1[:, :two], w1_ref[:, :two], 1, 1) + mm(h2[:, :two], w2_ref[:, :two], 1, 1)
    back_ref[...] = back.astype(bf16)


def ffn_grad_body(part, second_ref, low_ref, h_ref, out_ref):
    two = 2 * part
    out_ref[:, :two] = mm(second_ref[...], h_ref[:, :two], 0, 0).astype(bf16)
    out_ref[:, two:] = mm(low_ref[...], h_ref[:, two:], 0, 0).astype(bf16)


def finish_body(chunks, chan, base_ref, pa_ref, gx_ref, rim_x, g_bc, rim_bc, dkv, raw_ref, starts_ref, taps_ref, cos_ref, sin_ref,
                out_ref, taps_out):
    c = pl.program_id(0)
    wide = chan + 128

    @pl.when(c == 0)
    def _():
        taps_out[...] = jnp.zeros_like(taps_out)

    rows = g_bc.shape[0]
    here_ = pl.ds(pl.multiple_of(c * CHUNK, CHUNK), CHUNK)
    last = c == chunks - 1
    ahead_at = jnp.minimum((c + 1) * CHUNK, (chunks - 1) * CHUNK)
    next_ = pl.ds(pl.multiple_of(ahead_at, CHUNK), CHUNK)

    def put(first):
        return (iota((rows, 128), 1) == iota((rows, 128), 0) + first).astype(f32)

    bc_here = mm_exact(g_bc[:, here_], put(0), 0, 0)
    bc_next = mm_exact(jnp.where(last, rim_bc[...], g_bc[:, next_]), put(0), 0, 0)[:8]
    gx_next = jnp.where(last, rim_x[:8], gx_ref[pl.ds(pl.multiple_of(ahead_at, 8), 8)])
    longer = jnp.concatenate([
        jnp.concatenate([gx_ref[here_], bc_here], axis=1), jnp.concatenate([gx_next, bc_next], axis=1)
    ], axis=0)
    starts = starts_ref[pl.ds(pl.multiple_of(c * CHUNK, 8), CHUNK + 8)]
    place = places_of(base_ref, c)
    block = pa_ref[pl.ds(pl.multiple_of(c * CHUNK + RIM - 8, 8), CHUNK + 8), :wide]
    total = jnp.zeros((CHUNK, wide), f32)
    for lag in range(K):
        ahead = K - 1 - lag
        seen = place >= starts[ahead : ahead + CHUNK]
        total = total + jnp.where(seen, longer[ahead : ahead + CHUNK], 0.0) * taps_ref[lag : lag + 1]
        valid = place - ahead >= starts[:CHUNK]
        part = jnp.where(valid, longer[:CHUNK] * block[8 - ahead : 8 - ahead + CHUNK], 0.0)
        taps_out[lag : lag + 1] += jnp.sum(part, axis=0, keepdims=True)
    quarter = cos_ref.shape[0]
    kv = dkv[:, here_]
    a, b = kv[:quarter], kv[quarter : 2 * quarter]
    cosine, sine = cos_ref[:, here_], sin_ref[:, here_]
    kv = jnp.concatenate([a * cosine + b * sine, b * cosine - a * sine, kv[2 * quarter :]], axis=0)
    out_ref[:, :chan] = total[:, :chan].astype(bf16)
    out_ref[:, chan:wide] = (total[:, chan:] + mm(kv, put(rows), 0, 0)).astype(bf16)
    out_ref[:, wide:] = raw_ref[...]


def head_sums_t(v, heads):
    column = jnp.sum(v, axis=1, keepdims=True)
    pick = (iota((v.shape[0], 128), 0) // P_SIZE == iota((v.shape[0], 128), 1)).astype(f32)
    return jnp.sum(column * pick, axis=0, keepdims=True)


def chunked(body, chunks, outs, out_specs, ins, in_specs, scratch=()):
    return pl.pallas_call(
        body,
        grid=(chunks,),
        out_shape=outs,
        in_specs=in_specs,
        out_specs=out_specs,
        scratch_shapes=list(scratch),
        cost_estimate=pl.CostEstimate(flops=2_000_000_000, bytes_accessed=40_000_000, transcendentals=0),
        compiler_params=pltpu.CompilerParams(vmem_limit_bytes=48 * 2**20),
    )(*ins)


def dot(a, b, ca, cb):
    return lax.dot_general(a, b, (((ca,), (cb,)), ((), ())), preferred_element_type=f32)


def exact(text, *operands):
    return jnp.einsum(text, *operands, precision=highest, preferred_element_type=f32)


def d_silu(v):
    s = jax.nn.sigmoid(v)
    return s * (1.0 + v * (1.0 - s))


def shifted(block, axis, distance):
    count = lax.axis_size(axis)
    route = [(i - distance, i) for i in range(count) if 0 <= i - distance < count]
    return lax.ppermute(block, axis, route)


def rope_tables(offsets, first, count):
    half = HD // 2
    index = (first + jnp.arange(count)).astype(f32)
    freqs = rope_base ** (-2.0 * index / HD)
    angles = offsets.astype(f32)[:, None] * freqs[None, :]
    return jnp.cos(angles), jnp.sin(angles)


def turn(v, cosine, sine):
    half = v.shape[-1] // 2
    a, b = v[:, :half], v[:, half:]
    return jnp.concatenate([a * cosine - b * sine, b * cosine + a * sine], axis=-1)


def conv_rows(padded, taps, starts, places):
    length = starts.shape[0]
    total = jnp.zeros((length, padded.shape[1]), f32)
    for lag in range(K):
        back = K - 1 - lag
        valid = (places - back >= starts)[:, None]
        total = total + jnp.where(valid, padded[RIM - back : RIM - back + length] * taps[lag][None, :], 0.0)
    return total


def mixer_row(v):
    return v.reshape(1, -1)


def on_device(
    layer_input, doc_start, mixer_gain, ffn_gain,
    z_weight, x_weight, bc_weight, dt_weight, q_weight, k_weight, v_weight,
    o_weight, out_weight, gate_weight, up_weight, down_weight,
    conv_inner, conv_state, decay_log, dt_bias, skip_coef, ssm_gain, cotangent,
):
    tokens, width = layer_input.shape
    rows = z_weight.shape[0]
    planes = lax.axis_size("z")
    cores = lax.axis_size("head")
    zi, pi, hi = (lax.axis_index(a) for a in ("z", "p", "head"))
    T = tokens * G
    total_tokens = T * planes
    offset = zi * T
    places = offset + jnp.arange(T, dtype=jnp.int32)
    own = tokens // cores
    heads = decay_log.shape[0] // G
    chan = heads * P_SIZE
    bcs = 2 * N // cores // G
    quarter_half = HD // 2 // G

    def my_slice(v, size, index, axis):
        return lax.dynamic_slice_in_dim(v, index * size, size, axis)

    taps_inner = my_slice(conv_inner, chan, pi, 1)
    taps_state = my_slice(conv_state, bcs, hi * G + pi, 1)
    rates = my_slice(decay_log, heads, pi, 0)
    bias = my_slice(dt_bias, heads, pi, 0)
    skip = my_slice(skip_coef, heads, pi, 0)
    gain_s = my_slice(ssm_gain, chan, pi, 0)

    def cut(w):
        return w.reshape(rows, G, -1)

    bc_mine = lax.dynamic_slice_in_dim(bc_weight, hi * (2 * N // cores), 2 * N // cores, 1)
    k_cut = jnp.moveaxis(k_weight.reshape(rows, 2, G, quarter_half), 2, 1).reshape(rows, G, -1)
    a_sizes = [chan, bcs, 2 * quarter_half, 2 * quarter_half, heads]
    a_at = [sum(a_sizes[:i]) for i in range(len(a_sizes))]
    pad = -sum(a_sizes) % 128
    small_w = jnp.concatenate(
        [cut(bc_mine), k_cut, cut(v_weight), cut(dt_weight), jnp.zeros((rows, G, pad), bf16)], axis=2
    )
    small_w = jnp.moveaxis(small_w, 1, 0)
    a_cols = sum(a_sizes) + pad

    def gather(w):
        return lax.all_gather(w, "z", axis=0, tiled=True)

    exchange_sems = lambda n: [DMA((3, n)), DMA((3, n)), DMA((n,))]
    wa = gather(call(
        exchange_a_body, 0, shape((G * rows, a_cols), bf16), HBM,
        (x_weight, small_w), [HBM] * 2, exchange_sems(2),
    ))

    def half(v):
        return lax.dynamic_slice_in_dim(v, hi * own, own, 0)

    x_own, cot_own = half(layer_input), half(cotangent)
    r1 = lax.rsqrt(jnp.mean(x_own * x_own, axis=-1, keepdims=True) + norm_eps)
    first_own = (x_own * r1 * mixer_gain).astype(bf16)
    wb = gather(call(
        exchange_b_body, 9, shape((G * rows, 2 * (chan + HD)), bf16), HBM,
        (z_weight, q_weight, out_weight, o_weight), [HBM] * 4, exchange_sems(4),
    ))
    part = gate_weight.shape[1] // G // 2
    w1, w2, first_rim, docs = call(
        functools.partial(start_body, planes), 1,
        (shape((G * rows, 3 * part), bf16), shape((G * rows, 3 * part), bf16), shape((RIM + T, width), bf16),
         shape((planes, G, 8, tokens), jnp.int32)),
        (HBM,) * 4,
        (gate_weight, up_weight, down_weight, first_own, jnp.broadcast_to(doc_start[None], (8, tokens))),
        [HBM] * 3 + [VMEM] * 2,
        exchange_sems(6) + [DMA(()), DMA(()), DMA((3,)), DMA((3,)), DMA((planes - 1,)), DMA((planes - 1,)), DMA(())]
        + Spread.sems, us=40,
    )
    w1, w2 = gather(w1), gather(w2)
    wz, wb = wb[:, : chan + HD], wb[:, chan + HD :]
    first = first_rim[RIM:]
    all_starts = docs[:, :, 0].reshape(-1)
    starts = lax.dynamic_slice_in_dim(all_starts, offset, T, 0)

    def line_sum(grad):
        return lax.psum_scatter(grad, "z", scatter_dimension=0, tiled=True)

    edge = K - 1
    pa = dot(first_rim, wa, 1, 0)
    zq = dot(first, wz, 1, 0)
    bc_pre, k_proj, v_proj = (pa[RIM:, a : a + s] for a, s in zip(a_at[1:4], a_sizes[1:4]))
    bc_ext = pa[:, a_at[1] : a_at[1] + bcs]
    cv_bc = conv_rows(bc_ext, taps_state, starts, places)
    bc_low = jax.nn.silu(cv_bc).astype(bf16)
    offsets = places - starts
    cos_q, sin_q = rope_tables(offsets, 0, HD // 2)
    cos_k, sin_k = rope_tables(offsets, pi * quarter_half, quarter_half)
    cos_row = jnp.concatenate([cos_q, cos_q], axis=1)
    sin_row = jnp.concatenate([sin_q, -sin_q], axis=1)
    kvr = 4 * quarter_half
    kv_own = jnp.concatenate([turn(k_proj, cos_k, sin_k).astype(bf16), v_proj.astype(bf16)], axis=1)
    line_sems = [DMA((planes - 1,)), DMA((planes - 1,))]
    bc_t, kv_line = call(
        functools.partial(spread_body, planes), 2, (shape((2 * N, T), bf16), shape((planes, kvr, T), bf16)), (HBM, HBM),
        (bc_low.T, kv_own.T), [HBM, HBM], line_sems + [DMA(())] + Spread.sems,
    )
    bc_all = bc_t.T

    L = CHUNK
    nc = T // L
    base = jnp.full((1,), offset, jnp.int32)
    starts_col = starts[:, None]

    def row128(v):
        return jnp.pad(v, (0, 128 - v.shape[0]))[None]

    bias_row, rates_row = row128(bias), row128(rates)
    skip_row, gain_row = jnp.repeat(skip, P_SIZE)[None], gain_s[None]
    smem = pl.BlockSpec(memory_space=pltpu.SMEM)

    def specs(turned=False):
        at = (lambda c: nc - 1 - c) if turned else (lambda c: c)
        return (
            lambda cols: pl.BlockSpec((L, cols), lambda c: (at(c), 0)),
            lambda *dims: pl.BlockSpec(dims, lambda c: (0,) * len(dims)),
            lambda rows, cols: pl.BlockSpec((1, rows, cols), lambda c: (at(c), 0, 0)),
        )

    tile, fixed, stack = specs()
    pa_spec = fixed(*pa.shape)
    y_diag, cv_x, enter, reach, state, through = chunked(
        functools.partial(scan_body, heads), nc,
        (shape((T, chan), f32), shape((T, chan), f32), shape((nc, chan, N), f32), shape((nc, 16, 128), f32),
         shape((chan, N), bf16), shape((8, 128), f32)),
        (tile(chan), tile(chan), stack(chan, N), stack(16, 128), fixed(chan, N), fixed(8, 128)),
        (base, pa, bc_all, starts_col, taps_inner, bias_row, rates_row),
        [smem, pa_spec, tile(2 * N), tile(1), fixed(K, chan), fixed(1, 128), fixed(1, 128)],
        [pltpu.VMEM((chan, N), f32), pltpu.VMEM((8, 128), f32)],
    )

    def entering(upward, states, factors):
        total = jnp.zeros((chan, N), f32)
        for d in reversed(range(1, planes)):
            there = (zi - d >= 0) if upward else (zi + d < planes)
            factor = jnp.repeat(factors[d - 1, :heads, :1], P_SIZE, axis=0)
            total = jnp.where(there, total * factor + states[d - 1].astype(f32), total)
        return total

    state_shapes = (shape((planes - 1, chan, N), bf16), shape((planes - 1, 8, 128), f32))
    states, factors, kv_all, out_low = call(
        functools.partial(up_body, planes), 3, state_shapes + (shape((G * planes, kvr, T), bf16), shape((T, width), bf16)), (HBM,) * 4,
        (state, through, kv_line, cot_own.astype(bf16)), [HBM] * 4, line_sems * 2 + Spread.sems * 2, us=38,
    )
    before = entering(True, states, factors)
    ssm_low, y_scan = chunked(
        functools.partial(gate_body, heads), nc,
        (shape((T, chan), bf16), shape((T, chan), f32)), (tile(chan), tile(chan)),
        (base, pa, bc_all, starts_col, bias_row, rates_row, y_diag, cv_x, enter, reach, before, zq, skip_row, gain_row),
        [smem, pa_spec, tile(2 * N), tile(1), fixed(1, 128), fixed(1, 128), tile(chan), tile(chan), stack(chan, N),
         stack(16, 128), fixed(chan, N), tile(chan), fixed(1, chan), fixed(1, chan)],
    )

    size = math.gcd(512, T)
    qrows = math.gcd(256, T)
    kv_all = kv_all.reshape(G, planes, kvr, T)
    firsts = starts.reshape(-1, qrows)[:, 0]

    def column(at, cols):
        return pl.BlockSpec((qrows, cols), lambda i: (i, at))

    kv_spec = pl.BlockSpec((G, planes, kvr, T), lambda i: (0, 0, 0, 0))
    at_q = chan // HD
    query, att_low, attended, log_mass = chunked(
        functools.partial(attend_body, size, T), T // qrows,
        (shape((T, HD), bf16), shape((T, HD), bf16), shape((T, HD), f32), shape((T, 1), f32)),
        (column(0, HD), column(0, HD), column(0, HD), column(0, 1)),
        (base, firsts, zq, starts_col, cos_row, sin_row, kv_all),
        [smem, smem, column(at_q, HD), column(0, 1), column(0, HD), column(0, HD), kv_spec],
    )

    both_low = jnp.concatenate([ssm_low, att_low], axis=1)
    collect = Collect.scratch(own, width) + [pltpu.VMEM((own, width), bf16)] + Spread.sems
    hidden, second = call(
        hidden_body, 4, (shape((own, width), f32), shape((T, width), bf16)), (VMEM, HBM),
        (dot(both_low, wb, 1, 1).astype(bf16), x_own, mixer_row(ffn_gain)), [VMEM] * 3, collect, us=50,
    )
    ftile = math.gcd(256, T)
    wide = 3 * part

    def rows_spec(cols):
        return pl.BlockSpec((ftile, cols), lambda i: (i, 0))

    def all_spec(v):
        return pl.BlockSpec(v.shape, lambda i: (0,) * len(v.shape))

    h1 = chunked(
        functools.partial(ffn_first_body, part), T // ftile, shape((T, wide), bf16), rows_spec(wide),
        (second, out_low, w1), [rows_spec(width), rows_spec(width), all_spec(w1)],
    )

    def ffn_grads(h):
        tile_d = math.gcd(256, width)
        columns = pl.BlockSpec((T, tile_d), lambda i: (0, i))
        return chunked(
            functools.partial(ffn_grad_body, part), width // tile_d, shape((width, wide), bf16),
            pl.BlockSpec((tile_d, wide), lambda i: (i, 0)), (second, out_low, h), [columns, columns, all_spec(h)],
        )

    grad_1 = ffn_grads(h1)
    w2, grad_1 = lax.optimization_barrier((w2, grad_1))
    sum_1 = line_sum(grad_1)
    h2, part_l, part_c = chunked(
        functools.partial(ffn_second_body, part), T // ftile,
        (shape((T, wide), bf16), shape((T, width), bf16), shape((T, width), bf16)),
        (rows_spec(wide), rows_spec(width), rows_spec(width)),
        (second, out_low, w1, w2, h1), [rows_spec(width), rows_spec(width), all_spec(w1), all_spec(w2), rows_spec(wide)],
    )
    d_hidden, grad_ffn, branch = call(
        branch_body, 5, (shape((own, width), f32), shape((8, width), f32), shape((T, width), bf16)), (VMEM, VMEM, HBM),
        (part_c, hidden, cot_own, mixer_row(ffn_gain)), [VMEM] * 4, collect, us=50,
    )
    h2, branch = lax.optimization_barrier((h2, branch))
    sum_2 = line_sum(ffn_grads(h2))
    grad_b = dot(branch, both_low, 0, 0)
    d_both = dot(branch, wb, 1, 0)

    back, _, back_stack = specs(True)
    dz_low, dy, leave, tail, g_state, grad_gain_s = chunked(
        functools.partial(gate_back_body, heads, nc), nc,
        (shape((T, chan), bf16), shape((T, chan), f32), shape((nc, chan, N), f32), shape((nc, 8, 128), f32),
         shape((chan, N), bf16), shape((8, chan), f32)),
        (back(chan), back(chan), back_stack(chan, N), back_stack(8, 128), fixed(chan, N), fixed(8, chan)),
        (base, pa, bc_all, starts_col, bias_row, rates_row, d_both, y_scan, cv_x, reach, zq, skip_row, gain_row),
        [smem, pa_spec, back(2 * N), back(1), fixed(1, 128), fixed(1, 128), back(chan), back(chan), back(chan),
         back_stack(16, 128), back(chan), fixed(1, chan), fixed(1, chan)],
        [pltpu.VMEM((chan, N), f32), pltpu.VMEM((8, 128), f32)],
    )
    dq_low, dkv = chunked(
        functools.partial(attend_back_body, size, T), T // qrows,
        (shape((T, HD), bf16), shape((G, planes, kvr, T), bf16)), (column(0, HD), kv_spec),
        (base, firsts, query, starts_col, cos_row, sin_row, kv_all, d_both, attended, log_mass),
        [smem, smem, column(0, HD), column(0, 1), column(0, HD), column(0, HD), kv_spec, column(at_q, HD), column(0, HD),
         column(0, 1)],
        [pltpu.VMEM((planes, HD, T), f32), pltpu.VMEM((planes, HD, T), f32)],
    )
    dzq_low = jnp.concatenate([dz_low, dq_low], axis=1)
    grad_zb = jnp.concatenate([dot(first, dzq_low, 0, 0).astype(bf16), grad_b.astype(bf16)], axis=1)
    g_state, sum_1, grad_zb = lax.optimization_barrier((g_state, sum_1, grad_zb))
    states, factors, dkv, layer_own = call(
        functools.partial(down_body, planes), 6, state_shapes + (shape((G, planes, kvr, T), bf16), shape((own, width), f32)),
        (HBM,) * 3 + (VMEM,), (g_state, through, dkv, part_l, hidden), [HBM] * 3 + [VMEM] * 2,
        line_sems * 2 + [DMA((3,)), DMA((3,)), DMA(())] + Collect.scratch(own, width), us=45,
    )
    states, grad_zb = lax.optimization_barrier((states, grad_zb))
    sum_zb = line_sum(grad_zb)
    after = entering(False, states, factors)
    gx, d_bc_all, d_raw, grad_rows, grad_skip = chunked(
        functools.partial(scan_back_body, heads), nc,
        (shape((T, chan), f32), shape((2 * N, T), bf16), shape((T, 128), bf16), shape((8, 128), f32), shape((8, chan), f32)),
        (tile(chan), pl.BlockSpec((2 * N, L), lambda c: (0, c)), tile(128), fixed(8, 128), fixed(8, chan)),
        (base, pa, bc_all, starts_col, bias_row, rates_row, dy, cv_x, enter, reach, before, leave, tail, after, skip_row),
        [smem, pa_spec, tile(2 * N), tile(1), fixed(1, 128), fixed(1, 128), tile(chan), tile(chan),
         stack(chan, N), stack(16, 128), fixed(chan, N), stack(chan, N), stack(8, 128), fixed(chan, N), fixed(1, chan)],
    )
    grad_gain_s = grad_gain_s[0]
    grad_bias, grad_rates = grad_rows[0, :heads], grad_rows[1, :heads]
    grad_skip = jnp.sum(grad_skip[0].reshape(heads, P_SIZE), axis=1)

    gx_first = gx[:RIM]
    d_bc_t, sum_2 = lax.optimization_barrier((d_bc_all, sum_2))
    g_bc, rim_bc, rim_x, dkv, got_1, got_2 = call(
        functools.partial(back_body, planes), 7,
        (shape((bcs, T), f32), shape((bcs, 128), f32), shape((RIM, chan), f32), shape((kvr, T), f32))
        + tuple(shape((G, rows, v.shape[1]), bf16) for v in (sum_1, sum_2)), (VMEM,) * 4 + (HBM,) * 2,
        (d_bc_t, dkv, d_silu(cv_bc).T, gx_first, sum_1, sum_2), [VMEM] * 4 + [HBM] * 2,
        [pltpu.VMEM((G * bcs, T), bf16), pltpu.VMEM((3, bcs, T), bf16), pltpu.VMEM((3, bcs, T), bf16),
         pltpu.VMEM((planes, kvr, T), bf16), pltpu.VMEM((planes - 1, kvr, T), bf16),
         pltpu.VMEM((bcs, T), f32), DMA(()), DMA(()), DMA((3,)), DMA((3,)),
         DMA((planes - 1,)), DMA((planes - 1,)), DMA((2,)), DMA((2,)), DMA((2, 3)), DMA((2, 3)), DMA((2,))], us=30,
    )
    starts_long = jnp.concatenate([all_starts, jnp.full((8,), total_tokens, jnp.int32)])
    starts_long = lax.dynamic_slice_in_dim(starts_long, offset, T + 8, 0)[:, None]
    taps_both = jnp.concatenate([taps_inner, taps_state, jnp.zeros((K, 128 - bcs), f32)], axis=1)
    da_low, grad_taps = chunked(
        functools.partial(finish_body, nc, chan), nc,
        (shape((T, a_cols), bf16), shape((8, chan + 128), f32)), (tile(a_cols), fixed(8, chan + 128)),
        (base, pa, gx, rim_x, g_bc, rim_bc, dkv, d_raw, starts_long, taps_both, cos_k.T, sin_k.T),
        [smem, pa_spec, fixed(T, chan), fixed(RIM, chan), fixed(bcs, T), fixed(bcs, 128), fixed(kvr, T), tile(128),
         fixed(T + 8, 1), fixed(K, chan + 128), fixed(quarter_half, T), fixed(quarter_half, T)],
    )
    grad_a = dot(first, da_low, 0, 0).astype(bf16)
    grad_a, sum_zb = lax.optimization_barrier((grad_a, sum_zb))
    sum_a = line_sum(grad_a)
    lane = width // 4

    def lines_of(*parts):
        both = jnp.concatenate(parts, axis=1)
        return jnp.pad(both, ((0, 0), (0, lane - both.shape[1])))

    flat = jnp.concatenate(
        [grad_taps[:K], lines_of(grad_gain_s[None]),
         lines_of(row128(grad_rates), row128(grad_bias), row128(grad_skip)), jnp.zeros((2, lane), f32),
         grad_ffn[:1].reshape(4, lane), jnp.zeros((4, lane), f32)], axis=0,
    )
    part_a = (dot(da_low, wa, 1, 1) + dot(dzq_low, wz, 1, 1)).astype(bf16)
    grad_input, layer_out, mine, got_zb = call(
        final_body, 8,
        (shape((tokens, width), f32), shape((tokens, width), f32), shape((RIM, lane), f32),
         shape((G, rows, sum_zb.shape[1]), bf16)), (HBM, HBM, VMEM, HBM),
        (part_a, x_own, d_hidden, layer_own, mixer_row(mixer_gain), flat, sum_zb), [VMEM] * 6 + [HBM],
        Collect.scratch(own, width)
        + [pltpu.VMEM((own, width), f32), pltpu.VMEM((8, width), f32), DMA((2,)), DMA((2,)), DMA((2,)),
           DMA((3,)), DMA((3,)), DMA(())], us=40,
    )

    got_x, got_s, sums = call(
        functools.partial(last_body, planes), 10,
        (shape((G, rows, chan), bf16), shape((2 * G, rows, a_cols - chan), bf16), shape((2 * G * RIM, lane), f32)),
        (HBM,) * 3, (sum_a, mine), [HBM, VMEM],
        [pltpu.VMEM((RIM, lane), f32), pltpu.VMEM((planes - 1, RIM, lane), f32), DMA((3,)), DMA((3,)), DMA((2 * G,)), DMA((2 * G,)),
         DMA((2,)), DMA((planes - 1,)), DMA((planes - 1,))] + Spread.sems,
    )
    strip = min(32, rows)

    def got(v):
        return pl.BlockSpec((v.shape[0], strip, v.shape[2]), lambda c: (0, c, 0))

    def given(cols):
        return pl.BlockSpec((strip, cols), lambda c: (c, 0))

    widths = [w.shape[1] for w in (
        z_weight, x_weight, bc_weight, dt_weight, q_weight, k_weight, v_weight, o_weight, out_weight,
        gate_weight, up_weight, down_weight,
    )]
    gathered = (got_zb, got_1, got_2, got_x, got_s)
    weights = chunked(
        functools.partial(give_body, (bcs, heads, quarter_half)), rows // strip,
        tuple(shape((rows, w), f32) for w in widths), tuple(given(w) for w in widths),
        (jnp.full((1,), hi, jnp.int32),) + gathered, [smem] + [got(v) for v in gathered],
    )

    sums = sums.reshape(G, cores, RIM, lane)
    mine = lax.dynamic_index_in_dim(sums, hi, 1, False)
    o_conv_inner = mine[:, :K, :chan].transpose(1, 0, 2).reshape(K, G * chan)
    o_conv_state = sums[:, :, :K, chan : chan + bcs].transpose(2, 1, 0, 3).reshape(K, 2 * N)
    per = width // (planes * G)
    gains = jnp.sum(sums[:, :, 8:], axis=(0, 1)).reshape(2, width)
    gains = lax.dynamic_slice_in_dim(gains, (zi * G + pi) * per, per, 1)

    return (
        layer_out, grad_input, gains[1], gains[0], *weights,
        o_conv_inner, o_conv_state,
        mine[:, 5, :heads].reshape(-1), mine[:, 5, 128 : 128 + heads].reshape(-1),
        mine[:, 5, 256 : 256 + heads].reshape(-1), mine[:, 4, :chan].reshape(-1),
    )


def solution(mesh):
    seq, cores = mesh.shape["seq"], mesh.shape["head"]
    planes = Mesh(mesh.devices.reshape(seq // G, G, cores), ("z", "p", "head"))
    s = ("z", "p")
    both, row, head, whole = P(s, "head"), P(s, None), P("head"), P()
    placed = (
        row, P(s), whole, whole, both, both, row, both, both, both, both, both, both, both, both, both,
        P(None, "head"), whole, head, head, head, head, row,
    )
    return jax.shard_map(
        on_device,
        mesh=planes,
        in_specs=placed,
        out_specs=(
            row, row, P(s), P(s), both, both, row, both, both, both, both, both, both, both, both, both,
            P(None, "head"), whole, head, head, head, head,
        ),
        check_vma=False,
    )
```

```python
import functools
import math

import jax
import jax.numpy as jnp
from jax import lax
from jax.experimental import pallas as pl
from jax.experimental.pallas import tpu as pltpu
from jax.sharding import Mesh, PartitionSpec as P

P_SIZE = 64
N = 256
HD = 128
K = 4
G = 4
CHUNK = 128
RIM = 16

highest = lax.Precision.HIGHEST
rope_base = 10000.0
norm_eps = 1e-05
bf16 = jnp.bfloat16
f32 = jnp.float32
MESH = pl.DeviceIdType.MESH
HBM = pl.BlockSpec(memory_space=pl.ANY)
VMEM = pl.BlockSpec(memory_space=pltpu.VMEM)
DMA = pltpu.SemaphoreType.DMA


def rcopy(src, dst, send, recv, **where):
    return pltpu.make_async_remote_copy(
        src_ref=src, dst_ref=dst, send_sem=send, recv_sem=recv, device_id=where, device_id_type=MESH
    )


def here():
    return lax.axis_index("z"), lax.axis_index("p"), lax.axis_index("head")


def ring(p, d):
    return lax.rem(p + d + G, G)


def greet(*partners):
    barrier = pltpu.get_barrier_semaphore()
    for where in partners:
        pl.semaphore_signal(barrier, inc=1, device_id=where, device_id_type=MESH)
    pl.semaphore_wait(barrier, len(partners))


def plane_partners(p, c):
    return [{"p": ring(p, d)} for d in range(1, G)] + [{"head": 1 - c}]


def line_partners(z, planes):
    return [{"z": lax.rem(z + d, planes)} for d in range(1, planes)]


def beside(p):
    return p + 1 - 2 * lax.rem(p, 2), lax.rem(p + 2, G), G - 1 - p


class Spread:
    sems = [DMA((2,)), DMA((2,)), DMA((2,)), DMA((2,)), DMA((4,)), DMA((4,)), DMA(())]

    def __init__(self, block, out, start, rows, sems, cores=True):
        self.block, self.out, self.first, self.rows, self.cores = block, out, start, rows, cores
        self.s1, self.r1, self.s2, self.r2, self.s3, self.r3, self.keep = sems
        _, self.p, self.c = here()
        self.around = beside(self.p)

    def spot(self, q, half=None):
        first, rows = self.first(q, self.c), self.rows
        if half is not None:
            first, rows = first + half * (rows // 2), rows // 2
        return self.out.at[pl.ds(first, rows)]

    def over(self, i):
        return rcopy(self.block, self.spot(self.p), self.s1.at[i], self.r1.at[i], p=self.around[i])

    def relay(self, i):
        spot = self.spot(self.around[i], i)
        return rcopy(spot, spot, self.s2.at[i], self.r2.at[i], p=self.around[1 - i])

    def relayed(self, i):
        spot = self.spot(self.around[2], 1 - i)
        return rcopy(spot, spot, self.s2.at[1 - i], self.r2.at[1 - i], p=self.around[i])

    def across(self, i):
        spot = self.spot(self.p if i == 3 else self.around[i])
        return rcopy(self.block if i == 3 else spot, spot, self.s3.at[i], self.r3.at[i], head=1 - self.c)

    def mine(self):
        return pltpu.make_async_copy(self.block, self.spot(self.p), self.keep)

    def start(self):
        for i in (0, 1):
            self.over(i).start()
        if self.cores:
            self.across(3).start()
        self.mine().start()

    def pass_on(self):
        for i in (0, 1):
            self.over(i).wait_recv()
            self.relay(i).start()
            if self.cores:
                self.across(i).start()
        for i in (0, 1):
            self.relayed(i).wait_recv()
        if self.cores:
            self.across(2).start()

    def finish(self):
        self.mine().wait()
        for i in (0, 1):
            self.over(i).wait_send()
            self.relay(i).wait_send()
        if self.cores:
            for i in range(4):
                self.across(i).wait()


class Collect:
    @staticmethod
    def scratch(rows, width, cores=True):
        return [
            pltpu.VMEM((4, rows, width) if cores else (1, 16, 128), bf16), pltpu.VMEM((3, rows, width), bf16),
            pltpu.VMEM((2, rows // 2, width), bf16), pltpu.VMEM((2, rows, width), bf16),
            pltpu.VMEM((rows, width), f32), DMA((4,)), DMA((4,)), DMA((6,)), DMA((6,)),
        ]

    def __init__(self, part, rows, scratch, strip=16, cores=True):
        self.part, self.rows, self.strip, self.cores = part, rows, strip, cores
        self.cx, self.out, self.rd, self.rx, self.total, self.s1, self.r1, self.s2, self.r2 = scratch
        _, self.p, self.c = here()
        self.around = beside(self.p)

    def first(self, q, c):
        return pl.multiple_of(((q * 2 + c) if self.cores else q) * self.rows, 16)

    def owner(self, i):
        return self.p if i == 3 else self.around[i]

    def across(self, i):
        spot = self.part.at[pl.ds(self.first(self.owner(i), 1 - self.c), self.rows)]
        return rcopy(spot, self.cx.at[i], self.s1.at[i], self.r1.at[i], head=1 - self.c)

    def over(self, i, half):
        at = pl.ds(half * (self.rows // 2), self.rows // 2)
        k = 2 * i + half
        if i == 2:
            return rcopy(self.out.at[2, at], self.rd.at[half], self.s2.at[k], self.r2.at[k], p=self.around[half])
        return rcopy(self.out.at[i, at], self.rx.at[i, at], self.s2.at[k], self.r2.at[k], p=self.around[i])

    def strips(self, body, lo=0, hi=None):
        hi = self.rows if hi is None else hi

        def one(n, carry):
            body(lo + n * self.strip)
            return carry

        lax.fori_loop(0, (hi - lo) // self.strip, one, 0)

    def at(self, first):
        return pl.ds(pl.multiple_of(first, self.strip), self.strip)

    def add(self, i, half=None, relayed=None):
        first = self.first(self.owner(i), self.c)
        size = self.rows // 2

        def one(at):
            v = self.part[self.at(first + at)].astype(f32)
            if self.cores:
                v = v + self.cx[i, self.at(at)].astype(f32)
            if relayed is not None:
                v = v + self.rd[relayed, self.at(at - half * size)].astype(f32)
            if i == 3:
                self.total[self.at(at)] = v
            else:
                self.out[i, self.at(at)] = v.astype(bf16)

        if half is None:
            self.strips(one)
        else:
            self.strips(one, half * size, (half + 1) * size)

    def start(self):
        if self.cores:
            for i in (2, 0, 1, 3):
                self.across(i).start()

    def crossed(self, i):
        if self.cores:
            self.across(i).wait_recv()

    def begin(self):
        self.crossed(2)
        for half in (0, 1):
            self.add(2, half)
            self.over(2, half).start()
        for i in (0, 1):
            self.crossed(i)
            self.add(i, i)
            self.over(i, i).start()
        self.crossed(3)
        self.add(3)

    def relay(self):
        for i in (0, 1):
            self.over(2, 1 - i).wait_recv()
            self.add(i, 1 - i, 1 - i)
            self.over(i, 1 - i).start()

    def middle(self):
        self.begin()
        self.relay()

    def arrive(self):
        for half in (0, 1):
            for i in (0, 1):
                self.over(i, i if half == 0 else 1 - i).wait_recv()

    def sum_of(self, at):
        r = self.at(at)
        return self.total[r] + self.rx[0, r].astype(f32) + self.rx[1, r].astype(f32)

    def finish(self):
        if self.cores:
            for i in range(4):
                self.across(i).wait_send()
        for i in range(3):
            for half in (0, 1):
                self.over(i, half).wait_send()


def call(body, name_id, outs, out_specs, ins, in_specs, scratch, us=20, mib=12):
    return pl.pallas_call(
        body,
        out_shape=outs,
        in_specs=in_specs,
        out_specs=out_specs,
        scratch_shapes=scratch,
        cost_estimate=pl.CostEstimate(flops=0, bytes_accessed=us * 3_500_000, transcendentals=0),
        compiler_params=pltpu.CompilerParams(
            collective_id=name_id, has_side_effects=True, vmem_limit_bytes=mib * 2**20
        ),
    )(*ins)


def shape(dims, kind):
    return jax.ShapeDtypeStruct(dims, kind)


def exchange_copies(pieces, sems, keep):
    _, p, _ = here()
    away, own = [], []
    for i, (source, width, target, first, led, *part) in enumerate(pieces):
        whole, skip = part or (width, 0)
        rows = source.shape[-2]
        spot = target.at[pl.ds(pl.multiple_of(p * rows, 16), rows), pl.ds(first, width)]
        for d in range(G):
            q = ring(p, d)
            taken = source.at[q] if led else source.at[:, pl.ds(pl.multiple_of(q * whole + skip, 128), width)]
            if d:
                away.append(rcopy(taken, spot, sems[0].at[d - 1, i], sems[1].at[d - 1, i], p=q))
            else:
                own.append(pltpu.make_async_copy(taken, spot, keep.at[i]))
    return away, own


def exchange_a_body(x_ref, small_ref, out_ref, send, recv, keep):
    _, p, c = here()
    greet(*[{"p": ring(p, d)} for d in range(1, G)])
    xw = x_ref.shape[1] // G
    pieces = [(x_ref, xw, out_ref, 0, False), (small_ref, small_ref.shape[2], out_ref, xw, True)]
    away, own = exchange_copies(pieces, (send, recv), keep)
    for copy in away + own:
        copy.start()
    for copy in own + away:
        copy.wait()


def exchange_b_body(z_ref, q_ref, out_ref, o_ref, wb, send, recv, keep):
    _, p, c = here()
    greet(*[{"p": ring(p, d)} for d in range(1, G)])
    pieces, at = [], 0
    for ref in (z_ref, q_ref, out_ref, o_ref):
        pieces.append((ref, ref.shape[1] // G, wb, at, False))
        at += ref.shape[1] // G
    away, own = exchange_copies(pieces, (send, recv), keep)
    for copy in away + own:
        copy.start()
    for copy in own + away:
        copy.wait()


def start_body(planes, first, docs, steps, n1, all_docs, all_steps, *sems):
    z, p, c = here()
    greet(*plane_partners(p, c), *line_partners(z, planes))
    rim_s, rim_r, ps, pr, zs, zr, dk = sems[:7]
    rows = first.shape[0]
    a = Spread(first, n1, lambda q, k: pl.multiple_of(RIM + (q * 2 + k) * rows, 16), rows, sems[7:])
    near = [
        rcopy(have(ring(p, d)), every.at[z, p], ps.at[i, d - 1], pr.at[i, d - 1], p=ring(p, d))
        for i, (have, every) in enumerate(((lambda q: docs, all_docs), (lambda q: steps.at[q], all_steps))) for d in (1, 2, 3)
    ]
    own = [
        pltpu.make_async_copy(docs, all_docs.at[z, p], dk.at[0]), pltpu.make_async_copy(steps.at[p], all_steps.at[z, p], dk.at[1])
    ]
    a.start()
    for copy in near + own:
        copy.start()
    for copy in own + near:
        copy.wait()
    far = [
        rcopy(every.at[z], every.at[z], zs.at[i, d - 1], zr.at[i, d - 1], z=lax.rem(z + d, planes))
        for i, every in enumerate((all_docs, all_steps)) for d in range(1, planes)
    ]
    for copy in far:
        copy.start()
    a.pass_on()
    a.finish()
    last = n1.at[pl.ds(n1.shape[0] - RIM, RIM)]
    rim = rcopy(last, n1.at[pl.ds(0, RIM)], rim_s, rim_r, z=lax.rem(z + 1, planes))
    rim.start()
    for copy in far:
        copy.wait()
    rim.wait()


def spread_body(planes, block, kv, gate_w, up_w, down_w, out, lines, w1, w2, zs, zr, zk, send, recv, hold, *sems):
    z, p, c = here()
    greet(*plane_partners(p, c), *line_partners(z, planes))
    rows = block.shape[0]
    far = [rcopy(kv, lines.at[z], zs.at[d - 1], zr.at[d - 1], z=lax.rem(z + d, planes)) for d in range(1, planes)]
    keep = pltpu.make_async_copy(kv, lines.at[z], zk)
    for copy in far:
        copy.start()
    keep.start()
    s = Spread(block, out, lambda q, k: pl.multiple_of((k * G + q) * rows, 16), rows, sems)
    units = gate_w.shape[1] // G
    pieces = [
        (ref, part, to, i * part, False, units, skip)
        for to, part, skip in ((w1, w1.shape[1] // 3, 0), (w2, w2.shape[1] // 3, w1.shape[1] // 3))
        for i, ref in enumerate((gate_w, up_w, down_w))
    ]
    away, own = exchange_copies(pieces, (send, recv), hold)
    s.start()
    for copy in away + own:
        copy.start()
    s.pass_on()
    s.finish()
    for copy in own + away:
        copy.wait()
    keep.wait()
    for copy in far:
        copy.wait()


def state_copies(planes, upward, state, factor, states, factors, sems):
    z, _, _ = here()
    s1, r1, s2, r2 = sems
    way = 1 if upward else -1

    def pair(d):
        to = lax.rem(z + way * d + planes, planes)
        return (
            rcopy(state, states.at[d - 1], s1.at[d - 1], r1.at[d - 1], z=to),
            rcopy(factor, factors.at[d - 1], s2.at[d - 1], r2.at[d - 1], z=to),
        )

    def start():
        for d in range(1, planes):
            @pl.when((z + d < planes) if upward else (z - d >= 0))
            def _():
                for copy in pair(d):
                    copy.start()

    def wait():
        for d in range(1, planes):
            @pl.when((z - d >= 0) if upward else (z + d < planes))
            def _():
                for copy in pair(d):
                    copy.wait_recv()

            @pl.when((z + d < planes) if upward else (z - d >= 0))
            def _():
                for copy in pair(d):
                    copy.wait_send()

    return start, wait


def up_body(planes, state, factor, lines, low, states, factors, kv, ol, *sems):
    z, p, c = here()
    greet(*plane_partners(p, c), *line_partners(z, planes))
    start, wait = state_copies(planes, True, state, factor, states, factors, sems[:4])
    start()
    rows = low.shape[0]
    s = Spread(lines, kv, lambda q, k: q * planes, planes, sems[4:11], cores=False)
    b = Spread(low, ol, lambda q, k: pl.multiple_of((q * 2 + k) * rows, 16), rows, sems[11:18])
    s.start()
    b.start()
    s.pass_on()
    b.pass_on()
    s.finish()
    b.finish()
    wait()


def down_body(planes, state, factor, dkv, part, hidden, states, factors, kv, layer, *sems):
    z, p, c = here()
    greet(*plane_partners(p, c), *line_partners(z, planes))
    start, wait = state_copies(planes, False, state, factor, states, factors, sems[:4])
    start()
    k = Collect(dkv, kv.shape[0], sems[4:13], cores=False)
    s = Collect(part, hidden.shape[0], sems[13:])
    s.start()
    k.begin()
    s.begin()
    k.relay()
    s.relay()
    k.arrive()

    def sum_kv(at):
        kv[k.at(at)] = k.sum_of(at).astype(bf16)

    k.strips(sum_kv)
    s.arrive()

    def one(at):
        layer[s.at(at)] = hidden[s.at(at)] + s.sum_of(at)

    s.strips(one)
    k.finish()
    s.finish()
    wait()


def hidden_body(part, x_ref, gain, hidden, second, *scratch):
    _, p, c = here()
    greet(*plane_partners(p, c))
    rows = x_ref.shape[0]
    s = Collect(part, rows, scratch[:9])
    stage = scratch[9]
    s.start()
    s.middle()
    s.arrive()

    def one(at):
        r = s.at(at)
        h = x_ref[r] + s.sum_of(at)
        hidden[r] = h
        scale = lax.rsqrt(jnp.mean(h * h, axis=-1, keepdims=True) + norm_eps)
        stage[r] = (h * scale * gain[...]).astype(bf16)

    s.strips(one)
    g = Spread(stage, second, s.first, rows, scratch[10:17])
    g.start()
    g.pass_on()
    s.finish()
    g.finish()


def branch_body(part, hidden, cot, gain, d_hidden, gain_grad, branch, *scratch):
    _, p, c = here()
    greet(*plane_partners(p, c))
    rows = hidden.shape[0]
    s = Collect(part, rows, scratch[:9])
    stage = scratch[9]
    gain_grad[...] = jnp.zeros_like(gain_grad)
    s.start()
    s.middle()
    s.arrive()

    def one(at):
        r = s.at(at)
        h = hidden[r]
        scale = lax.rsqrt(jnp.mean(h * h, axis=-1, keepdims=True) + norm_eps)
        grad = s.sum_of(at)
        gain_grad[pl.ds(0, 1)] += jnp.sum(grad * h * scale, axis=0, keepdims=True)
        u = grad * gain[...]
        d = cot[r] + scale * u - h * (scale * scale * scale * jnp.mean(u * h, axis=-1, keepdims=True))
        d_hidden[r] = d
        stage[r] = d.astype(bf16)

    s.strips(one)
    g = Spread(stage, branch, s.first, rows, scratch[10:17])
    g.start()
    g.pass_on()
    s.finish()
    g.finish()


def final_body(part, x_ref, d_hidden, layer, gain, taps, norm, rows_ref, ffn, sum_z, sum_b, grad_in, layer_out, mine, got_z, got_b, *scratch):
    z, p, c = here()
    greet(*plane_partners(p, c))
    rows = x_ref.shape[0]
    s = Collect(part, rows, scratch[:9])
    stage, gain_row, es, er, ek, zs, zr, zk = scratch[9:]
    half = pl.ds(pl.multiple_of(c * rows, 16), rows)
    wide = got_z.shape[1]

    def halves(i, source, target):
        return (
            rcopy(source, target.at[half], es.at[i], er.at[i], head=1 - c),
            pltpu.make_async_copy(source, target.at[half], ek.at[i]),
        )

    def rows_of(v, q):
        cols = got_z.shape[2]
        return v.at[pl.ds(pl.multiple_of(q * wide, 16), wide), pl.ds(v.shape[1] - cols, cols)]

    s.start()
    first = halves(0, layer, layer_out)
    for copy in first:
        copy.start()
    lane = mine.shape[1]
    mine[...] = jnp.zeros_like(mine)
    mine[:K, : taps.shape[1]] = taps[:K]
    mine[4:5, : norm.shape[1]] = norm[:1]
    for j in range(3):
        mine[5:6, j * 128 : (j + 1) * 128] = rows_ref[j : j + 1]
    for j in range(4):
        mine[8 + j : 9 + j] = ffn[:1, j * lane : (j + 1) * lane]
    gain_row[...] = jnp.zeros_like(gain_row)
    s.middle()
    zb = []
    for i, (have, got) in enumerate(((sum_z, got_z), (sum_b, got_b))):
        for d in (1, 2, 3):
            zb.append(rcopy(rows_of(have, ring(p, d)), got.at[p], zs.at[i, d - 1], zr.at[i, d - 1], p=ring(p, d)))
        zb.append(pltpu.make_async_copy(rows_of(have, p), got.at[p], zk.at[i]))
    for copy in zb:
        copy.start()
    s.arrive()

    def one(at):
        r = s.at(at)
        v = x_ref[r]
        scale = lax.rsqrt(jnp.mean(v * v, axis=-1, keepdims=True) + norm_eps)
        grad = s.sum_of(at)
        gain_row[pl.ds(0, 1)] += jnp.sum(grad * v * scale, axis=0, keepdims=True)
        u = grad * gain[...]
        stage[r] = d_hidden[r] + scale * u - v * (scale * scale * scale * jnp.mean(u * v, axis=-1, keepdims=True))

    s.strips(one)
    second = halves(1, stage, grad_in)
    for copy in second:
        copy.start()
    for j in range(4):
        mine[12 + j : 13 + j] = gain_row[:1, j * lane : (j + 1) * lane]
    s.finish()
    for copy in first + second:
        copy.wait()
    for copy in zb:
        copy.wait()


def back_body(planes, dbc, dkv, d_silu_bc, gx, sum_1, sum_2, g_bc, rim_bc, rim_x, kv_out, got_1, got_2, *scratch):
    z, p, c = here()
    greet(*plane_partners(p, c), *line_partners(z, planes))
    (cx, bx, rbc, zkv, acc, xs, xr, bs, br, zs, zr, ms, mr, ws, wr, wk) = scratch
    rows = rbc.shape[1]
    across = rcopy(
        dbc.at[pl.ds(pl.multiple_of((1 - c) * G * rows, 16), G * rows)], cx, xs, xr, head=1 - c
    )
    across.start()

    def kv_down(d):
        to = lax.rem(z - d + planes, planes)
        return rcopy(dkv.at[to], zkv.at[d - 1], zs.at[d - 1], zr.at[d - 1], z=to)

    for d in range(1, planes):
        @pl.when(z - d >= 0)
        def _():
            kv_down(d).start()

    across.wait_recv()
    bc_over = []
    grads = list(enumerate(((sum_1, got_1), (sum_2, got_2))))
    wide = got_1.shape[1]

    def rows_of(q):
        return pl.ds(pl.multiple_of(q * wide, 16), wide)

    w_over = [
        rcopy(have.at[rows_of(ring(p, d)), pl.ds(0, got.shape[2])], got.at[p], ws.at[i, d - 1], wr.at[i, d - 1], p=ring(p, d))
        for i, (have, got) in grads for d in (1, 2, 3)
    ]
    w_own = [pltpu.make_async_copy(have.at[rows_of(p), pl.ds(0, got.shape[2])], got.at[p], wk.at[i]) for i, (have, got) in grads]
    for d in (1, 2, 3, 0):
        q = ring(p, d)
        own = dbc[pl.ds(pl.multiple_of((c * G + q) * rows, 16), rows)].astype(f32)
        own = own + cx[pl.ds(pl.multiple_of(q * rows, 16), rows)].astype(f32)
        if d:
            bx[d - 1] = own.astype(bf16)
            bc_over.append(rcopy(bx.at[d - 1], rbc.at[d - 1], bs.at[d - 1], br.at[d - 1], p=q))
            bc_over[-1].start()
        else:
            acc[...] = own
    for copy in w_over + w_own:
        copy.start()
    for copy in bc_over:
        copy.wait_recv()
    g = acc[...]
    for d in range(3):
        g = g + rbc[d].astype(f32)
    g_bc[...] = g * d_silu_bc[...]
    before = lax.rem(z - 1 + planes, planes)
    rims = [
        rcopy(g_bc.at[:, pl.ds(0, 128)], rim_bc, ms.at[0], mr.at[0], z=before),
        rcopy(gx.at[pl.ds(0, RIM)], rim_x, ms.at[1], mr.at[1], z=before),
    ]
    for copy in rims:
        copy.start()
    kv_out[...] = dkv[z].astype(f32)
    for d in range(1, planes):
        @pl.when(z + d < planes)
        def _():
            kv_down(d).wait_recv()
            kv_out[...] += zkv[d - 1].astype(f32)

        @pl.when(z - d >= 0)
        def _():
            kv_down(d).wait_send()

    for copy in rims:
        copy.wait()
    across.wait_send()
    for copy in bc_over:
        copy.wait_send()
    for copy in w_own + w_over:
        copy.wait()


def last_body(planes, sum_a, small, steps, got_x, got_s, sums, got_t, mine, others, t_own, t_far, xs, xr, ss, sr, keep, ls, lr,
              ts, tr, qs, qr, tk, *spread):
    z, p, c = here()
    pairs = [(d, k) for k in (0, 1) for d in range(G) if d or k]
    greet(*[{"p": ring(p, d), "head": lax.rem(c + k, 2)} for d, k in pairs], *line_partners(z, planes))
    rows, chan = got_x.shape[1], got_x.shape[2]

    def part(q, first, cols):
        return sum_a.at[pl.ds(pl.multiple_of(q * rows, 16), rows), pl.ds(first, cols)]

    def narrow(d, k):
        cols, to = got_s.shape[2], got_s.at[c * G + p]
        i = k * G + d - 1
        return rcopy(part(ring(p, d), chan, cols), to, ss.at[i], sr.at[i], p=ring(p, d), head=lax.rem(c + k, 2))

    lines = [
        rcopy(small, others.at[d - 1], ls.at[d - 1], lr.at[d - 1], z=lax.rem(z + d, planes)) for d in range(1, planes)
    ] + [
        rcopy(steps.at[lax.rem(z + d, planes)], t_far.at[d - 1], ts.at[d - 1], tr.at[d - 1], z=lax.rem(z + d, planes))
        for d in range(1, planes)
    ]
    copies = [
        rcopy(part(ring(p, d), 0, chan), got_x.at[p], xs.at[d - 1], xr.at[d - 1], p=ring(p, d)) for d in (1, 2, 3)
    ] + [narrow(d, k) for d, k in pairs] + [
        pltpu.make_async_copy(part(p, 0, chan), got_x.at[p], keep.at[0]),
        pltpu.make_async_copy(part(p, chan, got_s.shape[2]), got_s.at[c * G + p], keep.at[1]),
    ]
    for copy in lines + copies:
        copy.start()
    for copy in lines:
        copy.wait()
    total = small[...]
    for d in range(1, planes):
        total = total + others[d - 1]
    mine[...] = total
    g = Spread(mine, sums, lambda q, k: pl.multiple_of((q * 2 + k) * RIM, RIM), RIM, spread)
    g.start()
    total = steps[z]
    for d in range(1, planes):
        total = total + t_far[d - 1]
    t_own[...] = total
    back = [rcopy(t_own.at[ring(p, d)], got_t.at[p], qs.at[d - 1], qr.at[d - 1], p=ring(p, d)) for d in (1, 2, 3)]
    back.append(pltpu.make_async_copy(t_own.at[p], got_t.at[p], tk))
    for copy in back:
        copy.start()
    g.pass_on()
    for copy in copies + back:
        copy.wait()
    g.finish()


def give_body(sizes, core_ref, zq, ob, f1, f2, x_, s_, layer, grad, z_o, x_o, bc_o, q_o, k_o, v_o, o_o, out_o, gate_o, up_o, down_o,
              layer_o, grad_o):
    bcs, quarter = sizes
    layer_o[...] = layer[...]
    grad_o[...] = grad[...]
    chan, units = x_.shape[2], (f1.shape[2] + f2.shape[2]) // 3
    for p in range(G):
        for ref, got, first, cols in (
            (z_o, zq, 0, chan), (q_o, zq, chan, HD), (out_o, ob, 0, chan), (o_o, ob, chan, HD),
            (x_o, x_, 0, chan),
        ):
            ref[:, p * cols : (p + 1) * cols] = got[p, :, first : first + cols].astype(f32)

        for i, ref in enumerate((gate_o, up_o, down_o)):
            for got, skip in ((f1, 0), (f2, f1.shape[2] // 3)):
                part = got.shape[2] // 3
                at = p * units + skip
                ref[:, at : at + part] = got[p, :, i * part : (i + 1) * part].astype(f32)

    def place(first, cols, target):
        i = iota((128, 128), 0) - first
        return ((i >= 0) & (i < cols) & (iota((128, 128), 1) == target(i))).astype(bf16)

    def bc_place(p):
        return (iota((128, 256), 0) + p * bcs == iota((128, 256), 1)).astype(bf16) * (iota((128, 256), 0) < bcs).astype(bf16)

    mine = core_ref[0]
    k_sum = v_sum = jnp.zeros((x_.shape[1], 128), f32)
    halves = []
    for k in (0, 1):
        total = jnp.zeros((x_.shape[1], 256), f32)
        for p in range(G):
            total = total + mm(s_[k * G + p], bc_place(p), 1, 0)
        halves.append(total)
    bc_o[:, :256] = halves[0]
    bc_o[:, 256:] = halves[1]
    for p in range(G):
        own = s_[mine * G + p]
        k_sum = k_sum + mm(own, place(bcs, 2 * quarter, lambda i: (i // quarter) * (quarter * G) + p * quarter + i % quarter), 1, 0)
        v_sum = v_sum + mm(own, place(bcs + 2 * quarter, 2 * quarter, lambda i: i + p * 2 * quarter), 1, 0)
    k_o[...] = k_sum
    v_o[...] = v_sum


def mm(a, b, ca, cb):
    return lax.dot_general(a.astype(bf16), b.astype(bf16), (((ca,), (cb,)), ((), ())), preferred_element_type=f32)


def mm_exact(a, b, ca, cb):
    return lax.dot_general(a, b, (((ca,), (cb,)), ((), ())), precision=highest, preferred_element_type=f32)


def iota(dims, axis):
    return lax.broadcasted_iota(jnp.int32, dims, axis)


def soft(v):
    return jnp.maximum(v, 0.0) + jnp.log1p(jnp.exp(-jnp.abs(v)))


def sig(v):
    return 1.0 / (1.0 + jnp.exp(-v))


def rates_of(raw, bias, rates, heads):
    lane = iota((CHUNK, 128), 1)
    step = jnp.where(lane < heads, soft(raw + bias), 0.0)
    log_decay = -jnp.exp(rates) * step
    lower = (iota((CHUNK, CHUNK), 0) >= iota((CHUNK, CHUNK), 1)).astype(f32)
    return step, log_decay, mm_exact(lower, log_decay, 1, 0)


def pair_of(v, pair):
    left = iota((CHUNK, 128), 1) < P_SIZE
    return jnp.where(left, v[:, 2 * pair : 2 * pair + 1], v[:, 2 * pair + 1 : 2 * pair + 2])


def lanes(v, pair):
    return v[:, pair * 128 : (pair + 1) * 128]


def halves_of(a, b):
    return jnp.where(iota(a.shape, 1) < P_SIZE, a, b)


def head_means(v):
    same = (iota((128, 128), 0) // P_SIZE == iota((128, 128), 1) // P_SIZE).astype(f32) / P_SIZE
    return jnp.concatenate([mm_exact(lanes(v, k), same, 1, 0) for k in range(v.shape[1] // 128)], axis=1)


def head_sums(v, heads):
    chan = v.shape[1]
    pick = (iota((chan, 128), 0) // P_SIZE == iota((chan, 128), 1)).astype(f32)
    return mm_exact(v, pick, 1, 0)


def scale_rows(v, factor, heads):
    return jnp.concatenate(
        [v[h * P_SIZE : (h + 1) * P_SIZE] * factor[h : h + 1, :1] for h in range(heads)], axis=0
    )


def conv_of(pa_ref, taps_ref, starts, place, c, chan, first):
    block = pa_ref[pl.ds(pl.multiple_of(c * CHUNK + RIM - 8, 8), CHUNK + 8), first : first + chan]
    total = jnp.zeros((CHUNK, chan), f32)
    for lag in range(K):
        back = K - 1 - lag
        total = total + jnp.where(place - back >= starts, block[8 - back : 8 - back + CHUNK] * taps_ref[lag : lag + 1], 0.0)
    return total


def places_of(base_ref, c):
    return base_ref[0] + c * CHUNK + iota((CHUNK, 1), 0)


def weights_of(h, cs, cs_t, visible):
    span = cs[:, h : h + 1] - cs_t[h : h + 1]
    return jnp.where(visible, jnp.exp(jnp.where(visible, span, 0.0)), 0.0)


def visible_of(base_ref, c, starts, place):
    across = base_ref[0] + c * CHUNK + iota((CHUNK, CHUNK), 1)
    return (starts <= across) & (across <= place)


def decays_of(cs, starts, place):
    first = place[:1]
    decay_in = jnp.where(starts < first, jnp.exp(cs), 0.0)
    closing = jnp.where(starts[CHUNK - 1 :] <= place, jnp.exp(cs[CHUNK - 1 :] - cs), 0.0)
    return decay_in, closing


def scan_body(heads, base_ref, raw_ref, pa_ref, bc_ref, starts_ref, taps_ref, bias_ref, rates_ref,
              y_ref, cv_ref, enter_ref, reach_ref, state_out, through_out, state, through):
    c = pl.program_id(0)
    chan = heads * P_SIZE

    @pl.when(c == 0)
    def _():
        state[...] = jnp.zeros_like(state)
        through[...] = jnp.ones_like(through)

    starts, place = starts_ref[...], places_of(base_ref, c)
    raw = raw_ref[...]
    step, _, cs = rates_of(raw, bias_ref[...], rates_ref[...], heads)
    cs_t = cs.T
    cv = conv_of(pa_ref, taps_ref, starts, place, c, chan, 0)
    cv_ref[...] = cv
    x = cv * sig(cv)
    b_rows, c_rows = bc_ref[:, :N], bc_ref[:, N:]
    inter = mm(c_rows, b_rows, 1, 1)
    visible = visible_of(base_ref, c, starts, place)
    decay_in, closing = decays_of(cs, starts, place)
    ends = decay_in.T
    for k in range(heads // 2):
        driven = lanes(x, k) * pair_of(step, k)
        mixed = [mm(weights_of(2 * k + i, cs, cs_t, visible) * inter, driven, 1, 0) for i in (0, 1)]
        y_ref[:, k * 128 : (k + 1) * 128] = halves_of(*mixed)
        local = mm(driven * pair_of(closing, k), b_rows, 0, 0)
        at = pl.ds(k * 128, 128)
        old = state[at]
        enter_ref[0, at] = old
        both = jnp.concatenate(
            [old[i * P_SIZE : (i + 1) * P_SIZE] * ends[2 * k + i : 2 * k + i + 1, CHUNK - 1 :] for i in (0, 1)], axis=0
        )
        state[at] = both + local
    factor = jnp.broadcast_to(ends[:8, CHUNK - 1 :], (8, 128))
    reach_ref[0, :8] = through[...]
    reach_ref[0, 8:] = factor
    through[...] = through[...] * factor
    state_out[...] = state[...].astype(bf16)
    through_out[...] = through[...]


def gate_parts(y_scan, cv, z, skip, gain):
    x = cv * sig(cv)
    ssm = y_scan + skip * x
    s = sig(z)
    gated = ssm * (z * s)
    r = lax.rsqrt(head_means(gated * gated) + norm_eps)
    return x, ssm, s, gated, r


def gate_body(heads, base_ref, raw_ref, bc_ref, starts_ref, bias_ref, rates_ref, y_ref, cv_ref, enter_ref, reach_ref,
              before_ref, z_ref, skip_ref, gain_ref, low_ref, scan_ref):
    c = pl.program_id(0)
    chan = heads * P_SIZE
    starts, place = starts_ref[...], places_of(base_ref, c)
    raw = raw_ref[...]
    _, _, cs = rates_of(raw, bias_ref[...], rates_ref[...], heads)
    decay_in, _ = decays_of(cs, starts, place)
    state_in = enter_ref[0] + scale_rows(before_ref[...], reach_ref[0], heads)
    c_rows = bc_ref[:, N:]
    off = [mm(c_rows, state_in[k * 128 : (k + 1) * 128], 1, 1) * pair_of(decay_in, k) for k in range(heads // 2)]
    y_scan = y_ref[...] + jnp.concatenate(off, axis=1)
    scan_ref[...] = y_scan
    _, _, _, gated, r = gate_parts(y_scan, cv_ref[...], z_ref[...], skip_ref[...], gain_ref[...])
    low_ref[...] = (gated * r * gain_ref[...]).astype(bf16)


def gate_back_body(heads, chunks, base_ref, raw_ref, bc_ref, starts_ref, bias_ref, rates_ref, d_ref, scan_ref, cv_ref,
                   reach_ref, z_ref, skip_ref, gain_ref, dz_ref, dy_ref, leave_ref, tail_ref, state_out, gain_out, state, tail):
    c = chunks - 1 - pl.program_id(0)
    chan = heads * P_SIZE

    @pl.when(c == chunks - 1)
    def _():
        state[...] = jnp.zeros_like(state)
        tail[...] = jnp.ones_like(tail)
        gain_out[...] = jnp.zeros_like(gain_out)

    starts, place = starts_ref[...], places_of(base_ref, c)
    raw = raw_ref[...]
    _, _, cs = rates_of(raw, bias_ref[...], rates_ref[...], heads)
    decay_in, _ = decays_of(cs, starts, place)
    z = z_ref[...]
    x, ssm, s, gated, r = gate_parts(scan_ref[...], cv_ref[...], z, skip_ref[...], gain_ref[...])
    d = d_ref[...]
    gain_out[:1] += jnp.sum(d * gated * r, axis=0, keepdims=True)
    u = d * gain_ref[...]
    d_gated = r * u - gated * (r * r * r * head_means(u * gated))
    dz_ref[...] = (d_gated * ssm * (s * (1.0 + z * (1.0 - s)))).astype(bf16)
    dy = d_gated * (z * s)
    dy_ref[...] = dy
    c_rows = bc_ref[:, N:]
    leave_ref[0] = state[...]
    tail_ref[0] = tail[...]
    factor = reach_ref[0, 8:]
    local = [mm(lanes(dy, k) * pair_of(decay_in, k), c_rows, 0, 0) for k in range(heads // 2)]
    state[...] = scale_rows(state[...], factor, heads) + jnp.concatenate(local, axis=0)
    tail[...] = tail[...] * factor
    state_out[...] = state[...].astype(bf16)


def scan_back_body(heads, base_ref, raw_ref, bc_ref, starts_ref, bias_ref, rates_ref, dy_ref, cv_ref,
                   enter_ref, reach_ref, before_ref, leave_ref, tail_ref, after_ref, skip_ref,
                   gx_ref, dbc_ref, raw_out, rows_out):
    c = pl.program_id(0)
    chan = heads * P_SIZE

    @pl.when(c == 0)
    def _():
        rows_out[...] = jnp.zeros_like(rows_out)

    starts, place = starts_ref[...], places_of(base_ref, c)
    raw = raw_ref[...]
    step, log_decay, cs = rates_of(raw, bias_ref[...], rates_ref[...], heads)
    cs_t = cs.T
    visible = visible_of(base_ref, c, starts, place)
    decay_in, closing = decays_of(cs, starts, place)
    b_rows, c_rows = bc_ref[:, :N], bc_ref[:, N:]
    inter = mm(c_rows, b_rows, 1, 1)
    cv = cv_ref[...]
    s = sig(cv)
    x = cv * s
    dy = dy_ref[...]
    state_in = enter_ref[0] + scale_rows(before_ref[...], reach_ref[0], heads)
    d_state = leave_ref[0] + scale_rows(after_ref[...], tail_ref[0], heads)
    left = iota((CHUNK, 128), 1) < P_SIZE
    d_inter = jnp.zeros((CHUNK, CHUNK), f32)
    d_b = jnp.zeros((CHUNK, N), f32)
    d_c = jnp.zeros((CHUNK, N), f32)
    inside, outside, closes, drives = [], [], [], []
    for k in range(heads // 2):
        at = slice(k * 128, (k + 1) * 128)
        driven = (lanes(x, k) * pair_of(step, k)).astype(bf16)
        dyk = lanes(dy, k)
        dyb = dyk.astype(bf16)
        d_mixed, y_mixed = [], []
        for i in (0, 1):
            w = weights_of(2 * k + i, cs, cs_t, visible)
            mix = (w * inter).astype(bf16)
            half = jnp.where(left if i == 0 else ~left, dyb, jnp.zeros_like(dyb))
            d_inter = d_inter + w * mm(half, driven, 1, 1)
            d_mixed.append(mm(mix, dyb, 0, 0))
            y_mixed.append(mm(mix, driven, 1, 0))
        d_mix = halves_of(*d_mixed)
        close = pair_of(closing, k)
        d_close = mm(b_rows, d_state[at], 1, 1)
        closed = driven.astype(f32) * close
        enter = pair_of(decay_in, k)
        y_off = mm(c_rows, state_in[at], 1, 1) * enter
        d_c = d_c + mm(dyk * enter, state_in[at], 1, 0)
        d_b = d_b + mm(closed, d_state[at], 1, 0)
        inside.append(dyb.astype(f32) * halves_of(*y_mixed) - driven.astype(f32) * d_mix)
        outside.append(dyk * y_off)
        closes.append(closed * d_close)
        drives.append(d_mix + close * d_close)
    d_c = d_c + mm(d_inter, b_rows, 1, 0)
    d_b = d_b + mm(d_inter, c_rows, 0, 0)
    dbc_ref[:N] = d_b.astype(bf16).T
    dbc_ref[N:] = d_c.astype(bf16).T
    d_driven = jnp.concatenate(drives, axis=1)
    closes = head_sums(jnp.concatenate(closes, axis=1), heads)
    d_cs = head_sums(jnp.concatenate(inside, axis=1) + jnp.concatenate(outside, axis=1), heads) - closes
    kept = head_sums_t(d_state * state_in, heads)
    whole = decay_in[CHUNK - 1 :] * kept + jnp.sum(closes, axis=0, keepdims=True)
    upper = (iota((CHUNK, CHUNK), 0) <= iota((CHUNK, CHUNK), 1)).astype(f32)
    d_la = mm_exact(upper, d_cs, 1, 0) + whole
    d_step = head_sums(d_driven * x, heads)
    d_raw = (d_step - jnp.exp(rates_ref[...]) * d_la) * sig(raw + bias_ref[...])
    d_raw = jnp.where(iota((CHUNK, 128), 1) < heads, d_raw, 0.0)
    raw_out[...] = d_raw.astype(bf16)
    rows_out[:1] += jnp.sum(d_la * log_decay, axis=0, keepdims=True)
    rows_out[1:2] += jnp.sum(d_raw, axis=0, keepdims=True)
    rows_out[2:3] += jnp.sum(head_sums(dy * x, heads), axis=0, keepdims=True)
    wide = jnp.concatenate([pair_of(step, k) for k in range(heads // 2)], axis=1)
    gx_ref[...] = (d_driven * wide + skip_ref[...] * dy) * (s * (1.0 + cv * (1.0 - s)))


def unshuffled(v, back=False):
    quarter = HD // 2 // G
    i, j = (iota((HD, HD), 1), iota((HD, HD), 0)) if back else (iota((HD, HD), 0), iota((HD, HD), 1))
    half, rest = i // (HD // 2), i % (HD // 2)
    to = (rest // quarter) * 2 * quarter + half * quarter + rest % quarter
    return mm_exact(v, (to == j).astype(f32), 1, 0)


def keys_of(kv_ref, begin, size, tokens):
    plane, at = begin // tokens, pl.ds(pl.multiple_of(begin % tokens, 128), size)
    half = kv_ref.shape[2] // 2
    keys = jnp.concatenate([kv_ref[p, plane, :half, at] for p in range(G)], axis=0)
    values = jnp.concatenate([kv_ref[p, plane, half:, at] for p in range(G)], axis=0)
    return plane, at, keys, values


def seen_of(begin, size, starts, place):
    at = begin + iota((starts.shape[0], size), 1)
    return (at >= starts) & (at <= place)


def attend_body(size, tokens, base_ref, first_ref, q_ref, starts_ref, cos_ref, sin_ref, kv_ref,
                query_ref, low_ref, out_ref, mass_ref):
    i = pl.program_id(0)
    rows = q_ref.shape[0]
    v = q_ref[...]
    turned = (v * cos_ref[...] - pltpu.roll(v, HD // 2, 1) * sin_ref[...]) * HD ** (-0.5)
    query = unshuffled(turned.astype(bf16).astype(f32)).astype(bf16)
    query_ref[...] = query
    starts = starts_ref[...]
    place = base_ref[0] + i * rows + iota((rows, 1), 0)

    def step(n, carry):
        peak, mass, total = carry
        begin = n * size
        _, _, keys, values = keys_of(kv_ref, begin, size, tokens)
        scores = jnp.where(seen_of(begin, size, starts, place), mm(query, keys, 1, 0), -1e30)
        new = jnp.maximum(peak, jnp.max(scores, axis=1, keepdims=True))
        probs = jnp.where(scores > -1e29, jnp.exp(scores - new), 0.0)
        keep = jnp.exp(peak - new)
        return new, mass * keep + jnp.sum(probs, axis=1, keepdims=True), total * keep + mm(probs, values, 1, 1)

    begin = first_ref[i] // size
    end = (base_ref[0] + (i + 1) * rows - 1) // size + 1
    start = (jnp.full((rows, 1), -1e30, f32), jnp.zeros((rows, 1), f32), jnp.zeros((rows, HD), f32))
    peak, mass, total = lax.fori_loop(begin, end, step, start)
    attended = total / mass
    out_ref[...] = attended
    low_ref[...] = attended.astype(bf16)
    mass_ref[...] = peak + jnp.log(mass)


def attend_back_body(size, tokens, base_ref, first_ref, query_ref, starts_ref, cos_ref, sin_ref, kv_ref, d_ref, out_ref, mass_ref,
                     dq_ref, dkv_ref, d_keys, d_values):
    i = pl.program_id(0)
    rows = query_ref.shape[0]

    @pl.when(i == 0)
    def _():
        d_keys[...] = jnp.zeros_like(d_keys)
        d_values[...] = jnp.zeros_like(d_values)

    query = query_ref[...]
    d_low = d_ref[...].astype(bf16)
    balance = jnp.sum(d_low.astype(f32) * out_ref[...], axis=1, keepdims=True)
    query_t, d_t = query.T, d_low.T
    starts, mass = starts_ref[...], mass_ref[...]
    place = base_ref[0] + i * rows + iota((rows, 1), 0)

    def step(n, total):
        begin = n * size
        plane, at, keys, values = keys_of(kv_ref, begin, size, tokens)
        seen = seen_of(begin, size, starts, place)
        probs = jnp.where(seen, jnp.exp(jnp.where(seen, mm(query, keys, 1, 0) - mass, 0.0)), 0.0)
        d_scores = (probs * (mm(d_low, values, 1, 0) - balance)).astype(bf16)
        d_keys[plane, :, at] += mm(query_t, d_scores, 1, 0)
        d_values[plane, :, at] += mm(d_t, probs, 1, 0)
        return total + mm(d_scores, keys, 1, 1)

    begin = first_ref[i] // size
    end = (base_ref[0] + (i + 1) * rows - 1) // size + 1
    d_query = unshuffled(lax.fori_loop(begin, end, step, jnp.zeros((rows, HD), f32)), True)
    d_query = (d_query * cos_ref[...] + pltpu.roll(d_query, HD // 2, 1) * sin_ref[...]) * HD ** (-0.5)
    dq_ref[...] = d_query.astype(bf16)

    @pl.when(i == pl.num_programs(0) - 1)
    def _():
        half = dkv_ref.shape[2] // 2

        def give(plane, carry):
            for p in range(G):
                dkv_ref[p, plane, :half] = d_keys[plane, p * half : (p + 1) * half].astype(bf16)
                dkv_ref[p, plane, half:] = d_values[plane, p * half : (p + 1) * half].astype(bf16)
            return carry

        lax.fori_loop(0, dkv_ref.shape[1], give, 0)


def ffn_units(part, second, low, w_ref):
    gate = mm(second, w_ref[:, :part], 1, 0)
    up = mm(second, w_ref[:, part : 2 * part], 1, 0)
    d_act = mm(low, w_ref[:, 2 * part :], 1, 0)
    s = sig(gate)
    silu = gate * s
    return jnp.concatenate(
        [(d_act * up * (s * (1.0 + gate * (1.0 - s)))).astype(bf16), (d_act * silu).astype(bf16), (silu * up).astype(bf16)],
        axis=1,
    )


def ffn_body(part, second_ref, low_ref, w_ref, *refs):
    *done, h_ref, layer_ref, back_ref = refs
    h = ffn_units(part, second_ref[...], low_ref[...], w_ref)
    h_ref[...] = h
    two = 2 * part
    layer = mm(h[:, two:], w_ref[:, two:], 1, 1)
    back = mm(h[:, :two], w_ref[:, :two], 1, 1)
    if done:
        layer = layer + done[0][...].astype(f32)
        back = back + done[1][...].astype(f32)
    layer_ref[...] = layer.astype(bf16)
    back_ref[...] = back.astype(bf16)


def ffn_grad_body(part, second_ref, low_ref, h_ref, out_ref):
    two = 2 * part
    out_ref[:, :two] = mm(second_ref[...], h_ref[:, :two], 0, 0).astype(bf16)
    out_ref[:, two:] = mm(low_ref[...], h_ref[:, two:], 0, 0).astype(bf16)


def finish_body(chunks, chan, base_ref, pa_ref, gx_ref, rim_x, g_bc, rim_bc, dkv, starts_ref, taps_ref, cos_ref, sin_ref,
                out_ref, taps_out):
    c = pl.program_id(0)
    wide = chan + 128

    @pl.when(c == 0)
    def _():
        taps_out[...] = jnp.zeros_like(taps_out)

    rows = g_bc.shape[0]
    here_ = pl.ds(pl.multiple_of(c * CHUNK, CHUNK), CHUNK)
    last = c == chunks - 1
    ahead_at = jnp.minimum((c + 1) * CHUNK, (chunks - 1) * CHUNK)
    next_ = pl.ds(pl.multiple_of(ahead_at, CHUNK), CHUNK)

    def put(first):
        return (iota((rows, 128), 1) == iota((rows, 128), 0) + first).astype(f32)

    bc_here = mm_exact(g_bc[:, here_], put(0), 0, 0)
    bc_next = mm_exact(jnp.where(last, rim_bc[...], g_bc[:, next_]), put(0), 0, 0)[:8]
    gx_next = jnp.where(last, rim_x[:8], gx_ref[pl.ds(pl.multiple_of(ahead_at, 8), 8)])
    longer = jnp.concatenate([
        jnp.concatenate([gx_ref[here_], bc_here], axis=1), jnp.concatenate([gx_next, bc_next], axis=1)
    ], axis=0)
    starts = starts_ref[pl.ds(pl.multiple_of(c * CHUNK, 8), CHUNK + 8)]
    place = places_of(base_ref, c)
    block = pa_ref[pl.ds(pl.multiple_of(c * CHUNK + RIM - 8, 8), CHUNK + 8), :wide]
    total = jnp.zeros((CHUNK, wide), f32)
    for lag in range(K):
        ahead = K - 1 - lag
        seen = place >= starts[ahead : ahead + CHUNK]
        total = total + jnp.where(seen, longer[ahead : ahead + CHUNK], 0.0) * taps_ref[lag : lag + 1]
        valid = place - ahead >= starts[:CHUNK]
        part = jnp.where(valid, longer[:CHUNK] * block[8 - ahead : 8 - ahead + CHUNK], 0.0)
        taps_out[lag : lag + 1] += jnp.sum(part, axis=0, keepdims=True)
    quarter = cos_ref.shape[0]
    kv = dkv[:, here_]
    a, b = kv[:quarter], kv[quarter : 2 * quarter]
    cosine, sine = cos_ref[:, here_], sin_ref[:, here_]
    kv = jnp.concatenate([a * cosine + b * sine, b * cosine - a * sine, kv[2 * quarter :]], axis=0)
    out_ref[:, :chan] = total[:, :chan].astype(bf16)
    out_ref[:, chan:wide] = (total[:, chan:] + mm(kv, put(rows), 0, 0)).astype(bf16)


def prepare_body(chan, base_ref, pa_ref, starts_ref, taps_ref, cos_ref, sin_ref, bc_ref, slope_ref, kv_ref):
    c = pl.program_id(0)
    cv = conv_of(pa_ref, taps_ref, starts_ref[...], places_of(base_ref, c), c, 128, chan).T
    rows, quarter = bc_ref.shape[0], cos_ref.shape[0]
    cv = cv[:rows]
    s = sig(cv)
    bc_ref[...] = (cv * s).astype(bf16)
    slope_ref[...] = s * (1.0 + cv * (1.0 - s))
    kv = pa_ref[pl.ds(pl.multiple_of(c * CHUNK + RIM, 16), CHUNK), chan : chan + 128].T[rows:]
    a, b = kv[:quarter], kv[quarter : 2 * quarter]
    cosine, sine = cos_ref[...], sin_ref[...]
    kv_ref[:quarter] = (a * cosine - b * sine).astype(bf16)
    kv_ref[quarter : 2 * quarter] = (b * cosine + a * sine).astype(bf16)
    kv_ref[2 * quarter :] = kv[2 * quarter :].astype(bf16)


def back_part_body(da_ref, dz_ref, raw_ref, wa_ref, wz_ref, ws_ref, out_ref):
    total = mm(da_ref[...], wa_ref[...], 1, 1) + mm(dz_ref[...], wz_ref[...], 1, 1) + mm(raw_ref[...], ws_ref[...], 1, 0)
    out_ref[...] = total.astype(bf16)


def head_sums_t(v, heads):
    column = jnp.sum(v, axis=1, keepdims=True)
    pick = (iota((v.shape[0], 128), 0) // P_SIZE == iota((v.shape[0], 128), 1)).astype(f32)
    return jnp.sum(column * pick, axis=0, keepdims=True)


def chunked(body, chunks, outs, out_specs, ins, in_specs, scratch=(), mib=16, near=(), keep=()):
    ins = [
        pltpu.with_memory_space_constraint(v, pltpu.HBM) if s.memory_space is None and v.size > 20000 and i not in near else v
        for i, (v, s) in enumerate(zip(ins, in_specs))
    ]
    if isinstance(outs, tuple):
        outs = tuple(
            (pltpu.VMEM if i in keep else pltpu.HBM)(v.shape, v.dtype) if v.size > 20000 else v for i, v in enumerate(outs)
        )
    else:
        outs = (pltpu.VMEM if keep else pltpu.HBM)(outs.shape, outs.dtype)
    return pl.pallas_call(
        body,
        grid=(chunks,),
        out_shape=outs,
        in_specs=in_specs,
        out_specs=out_specs,
        scratch_shapes=list(scratch),
        cost_estimate=pl.CostEstimate(flops=2_000_000_000, bytes_accessed=40_000_000, transcendentals=0),
        compiler_params=pltpu.CompilerParams(vmem_limit_bytes=mib * 2**20),
    )(*ins)


def dot(a, b, ca, cb):
    return lax.dot_general(a, b, (((ca,), (cb,)), ((), ())), preferred_element_type=f32)


def exact(text, *operands):
    return jnp.einsum(text, *operands, precision=highest, preferred_element_type=f32)


def d_silu(v):
    s = jax.nn.sigmoid(v)
    return s * (1.0 + v * (1.0 - s))


def shifted(block, axis, distance):
    count = lax.axis_size(axis)
    route = [(i - distance, i) for i in range(count) if 0 <= i - distance < count]
    return lax.ppermute(block, axis, route)


def rope_tables(offsets, first, count):
    half = HD // 2
    index = (first + jnp.arange(count)).astype(f32)
    freqs = rope_base ** (-2.0 * index / HD)
    angles = offsets.astype(f32)[:, None] * freqs[None, :]
    return jnp.cos(angles), jnp.sin(angles)


def turn(v, cosine, sine):
    half = v.shape[-1] // 2
    a, b = v[:, :half], v[:, half:]
    return jnp.concatenate([a * cosine - b * sine, b * cosine + a * sine], axis=-1)


def conv_rows(padded, taps, starts, places):
    length = starts.shape[0]
    total = jnp.zeros((length, padded.shape[1]), f32)
    for lag in range(K):
        back = K - 1 - lag
        valid = (places - back >= starts)[:, None]
        total = total + jnp.where(valid, padded[RIM - back : RIM - back + length] * taps[lag][None, :], 0.0)
    return total


def mixer_row(v):
    return v.reshape(1, -1)


def on_device(
    layer_input, doc_start, mixer_gain, ffn_gain,
    z_weight, x_weight, bc_weight, dt_weight, q_weight, k_weight, v_weight,
    o_weight, out_weight, gate_weight, up_weight, down_weight,
    conv_inner, conv_state, decay_log, dt_bias, skip_coef, ssm_gain, cotangent,
):
    tokens, width = layer_input.shape
    rows = z_weight.shape[0]
    planes = lax.axis_size("z")
    cores = lax.axis_size("head")
    zi, pi, hi = (lax.axis_index(a) for a in ("z", "p", "head"))
    T = tokens * G
    total_tokens = T * planes
    offset = zi * T
    places = offset + jnp.arange(T, dtype=jnp.int32)
    own = tokens // cores
    heads = decay_log.shape[0] // G
    chan = heads * P_SIZE
    bcs = 2 * N // cores // G
    quarter_half = HD // 2 // G

    def my_slice(v, size, index, axis):
        return lax.dynamic_slice_in_dim(v, index * size, size, axis)

    taps_inner = my_slice(conv_inner, chan, pi, 1)
    taps_state = my_slice(conv_state, bcs, hi * G + pi, 1)
    rates = my_slice(decay_log, heads, pi, 0)
    bias = my_slice(dt_bias, heads, pi, 0)
    skip = my_slice(skip_coef, heads, pi, 0)
    gain_s = my_slice(ssm_gain, chan, pi, 0)

    def cut(w):
        return w.reshape(rows, G, -1)

    bc_mine = lax.dynamic_slice_in_dim(bc_weight, hi * (2 * N // cores), 2 * N // cores, 1)
    k_cut = jnp.moveaxis(k_weight.reshape(rows, 2, G, quarter_half), 2, 1).reshape(rows, G, -1)
    small_w = jnp.concatenate([cut(bc_mine), k_cut, cut(v_weight)], axis=2)
    small_w = jnp.moveaxis(small_w, 1, 0)
    a_cols = chan + 128
    own_steps = jnp.pad(dt_weight.T.reshape(G, heads, rows), ((0, 0), (0, 16 - heads), (0, 0)))

    def gather(w):
        return lax.all_gather(w, "z", axis=0, tiled=True)

    exchange_sems = lambda n: [DMA((3, n)), DMA((3, n)), DMA((n,))]
    wa = gather(call(
        exchange_a_body, 0, shape((G * rows, a_cols), bf16), HBM,
        (x_weight, small_w), [HBM] * 2, exchange_sems(2),
    ))

    def half(v):
        return lax.dynamic_slice_in_dim(v, hi * own, own, 0)

    x_own, cot_own = half(layer_input), half(cotangent)
    r1 = lax.rsqrt(jnp.mean(x_own * x_own, axis=-1, keepdims=True) + norm_eps)
    first_own = (x_own * r1 * mixer_gain).astype(bf16)
    wb = gather(call(
        exchange_b_body, 9, shape((G * rows, 2 * (chan + HD)), bf16), HBM,
        (z_weight, q_weight, out_weight, o_weight), [HBM] * 4, exchange_sems(4),
    ))
    first_rim, docs, steps = call(
        functools.partial(start_body, planes), 1,
        (shape((RIM + T, width), bf16), shape((planes, G, 8, tokens), jnp.int32), shape((planes, G, 16, rows), bf16)), (HBM,) * 3,
        (first_own, jnp.broadcast_to(doc_start[None], (8, tokens)), own_steps), [VMEM] * 3,
        [DMA(()), DMA(()), DMA((2, 3)), DMA((2, 3)), DMA((2, planes - 1)), DMA((2, planes - 1)), DMA((2,))] + Spread.sems, us=25,
    )
    w_step = jnp.pad(steps.transpose(2, 0, 1, 3).reshape(16, width), ((0, 112), (0, 0)))
    w_zqob = wb
    wz, wb = wb[:, : chan + HD], wb[:, chan + HD :]
    first = first_rim[RIM:]
    all_starts = docs[:, :, 0].reshape(-1)
    starts = lax.dynamic_slice_in_dim(all_starts, offset, T, 0)

    def line_sum(grad):
        return lax.psum_scatter(grad, "z", scatter_dimension=0, tiled=True)

    raw = dot(first, w_step, 1, 1)
    pa = dot(first_rim, wa, 1, 0)
    zq = dot(first, wz, 1, 0)
    offsets = places - starts
    cos_q, sin_q = rope_tables(offsets, 0, HD // 2)
    cos_row = jnp.concatenate([cos_q, cos_q], axis=1)
    sin_row = jnp.concatenate([sin_q, -sin_q], axis=1)
    cos_k, sin_k = (v.T for v in rope_tables(offsets, pi * quarter_half, quarter_half))
    kvr = 4 * quarter_half
    L = CHUNK
    nc = T // L
    base = jnp.full((1,), offset, jnp.int32)
    starts_col = starts[:, None]
    smem = pl.BlockSpec(memory_space=pltpu.SMEM)
    taps_pair = jnp.concatenate([taps_state, jnp.zeros((K, 128 - bcs), f32)], axis=1)
    along = lambda rows_: pl.BlockSpec((rows_, L), lambda c: (0, c))
    bc_low, slope_bc, kv_own = chunked(
        functools.partial(prepare_body, chan), nc,
        (shape((bcs, T), bf16), shape((bcs, T), f32), shape((kvr, T), bf16)), (along(bcs), along(bcs), along(kvr)),
        (base, pa, starts_col, taps_pair, cos_k, sin_k),
        [smem, pl.BlockSpec(pa.shape, lambda c: (0, 0)), pl.BlockSpec((L, 1), lambda c: (c, 0)), pl.BlockSpec((K, 128), lambda c: (0, 0)),
         along(quarter_half), along(quarter_half)],
    )
    line_sems = [DMA((planes - 1,)), DMA((planes - 1,))]
    units = gate_weight.shape[1] // G
    parts = (units - 128, 128)
    bc_t, kv_line, w1, w2 = call(
        functools.partial(spread_body, planes), 2,
        (shape((2 * N, T), bf16), shape((planes, kvr, T), bf16)) + tuple(shape((G * rows, 3 * n), bf16) for n in parts), (HBM,) * 4,
        (bc_low, kv_own, gate_weight, up_weight, down_weight), [HBM] * 5,
        line_sems + [DMA(())] + exchange_sems(6) + Spread.sems, us=28,
    )
    w1, w2 = gather(w1), gather(w2)
    bc_all = bc_t.T


    def row128(v):
        return jnp.pad(v, (0, 128 - v.shape[0]))[None]

    bias_row, rates_row = row128(bias), row128(rates)
    skip_row, gain_row = jnp.repeat(skip, P_SIZE)[None], gain_s[None]

    def specs(turned=False):
        at = (lambda c: nc - 1 - c) if turned else (lambda c: c)
        return (
            lambda cols: pl.BlockSpec((L, cols), lambda c: (at(c), 0)),
            lambda *dims: pl.BlockSpec(dims, lambda c: (0,) * len(dims)),
            lambda rows, cols: pl.BlockSpec((1, rows, cols), lambda c: (at(c), 0, 0)),
        )

    tile, fixed, stack = specs()
    pa_spec = fixed(*pa.shape)
    y_diag, cv_x, enter, reach, state, through = chunked(
        functools.partial(scan_body, heads), nc,
        (shape((T, chan), f32), shape((T, chan), f32), shape((nc, chan, N), f32), shape((nc, 16, 128), f32),
         shape((chan, N), bf16), shape((8, 128), f32)),
        (tile(chan), tile(chan), stack(chan, N), stack(16, 128), fixed(chan, N), fixed(8, 128)),
        (base, raw, pa, bc_all, starts_col, taps_inner, bias_row, rates_row),
        [smem, tile(128), pa_spec, tile(2 * N), tile(1), fixed(K, chan), fixed(1, 128), fixed(1, 128)],
        [pltpu.VMEM((chan, N), f32), pltpu.VMEM((8, 128), f32)],
    )

    def entering(upward, states, factors):
        total = jnp.zeros((chan, N), f32)
        for d in reversed(range(1, planes)):
            there = (zi - d >= 0) if upward else (zi + d < planes)
            factor = jnp.repeat(factors[d - 1, :heads, :1], P_SIZE, axis=0)
            total = jnp.where(there, total * factor + states[d - 1].astype(f32), total)
        return total

    state_shapes = (shape((planes - 1, chan, N), bf16), shape((planes - 1, 8, 128), f32))
    states, factors, kv_all, out_low = call(
        functools.partial(up_body, planes), 3, state_shapes + (shape((G * planes, kvr, T), bf16), shape((T, width), bf16)), (HBM,) * 4,
        (state, through, kv_line, cot_own.astype(bf16)), [HBM] * 4, line_sems * 2 + Spread.sems * 2, us=38,
    )
    before = entering(True, states, factors)
    ssm_low, y_scan = chunked(
        functools.partial(gate_body, heads), nc,
        (shape((T, chan), bf16), shape((T, chan), f32)), (tile(chan), tile(chan)),
        (base, raw, bc_all, starts_col, bias_row, rates_row, y_diag, cv_x, enter, reach, before, zq, skip_row, gain_row),
        [smem, tile(128), tile(2 * N), tile(1), fixed(1, 128), fixed(1, 128), tile(chan), tile(chan), stack(chan, N),
         stack(16, 128), fixed(chan, N), tile(chan), fixed(1, chan), fixed(1, chan)],
    )

    size = math.gcd(512, T)
    qrows = math.gcd(256, T)
    kv_all = kv_all.reshape(G, planes, kvr, T)
    firsts = starts.reshape(-1, qrows)[:, 0]

    def column(at, cols):
        return pl.BlockSpec((qrows, cols), lambda i: (i, at))

    kv_spec = pl.BlockSpec((G, planes, kvr, T), lambda i: (0, 0, 0, 0))
    at_q = chan // HD
    query, att_low, attended, log_mass = chunked(
        functools.partial(attend_body, size, T), T // qrows,
        (shape((T, HD), bf16), shape((T, HD), bf16), shape((T, HD), f32), shape((T, 1), f32)),
        (column(0, HD), column(0, HD), column(0, HD), column(0, 1)),
        (base, firsts, zq, starts_col, cos_row, sin_row, kv_all),
        [smem, smem, column(at_q, HD), column(0, 1), column(0, HD), column(0, HD), kv_spec], mib=12 + 2 * planes,
    )

    both_low = jnp.concatenate([ssm_low, att_low], axis=1)
    collect = Collect.scratch(own, width) + [pltpu.VMEM((own, width), bf16)] + Spread.sems
    hidden, second = call(
        hidden_body, 4, (shape((own, width), f32), shape((T, width), bf16)), (VMEM, HBM),
        (dot(both_low, wb, 1, 1).astype(bf16), x_own, mixer_row(ffn_gain)), [VMEM] * 3, collect, us=50,
    )
    ftile = math.gcd(256, T)

    def rows_spec(cols):
        return pl.BlockSpec((ftile, cols), lambda i: (i, 0))

    def all_spec(v):
        return pl.BlockSpec(v.shape, lambda i: (0,) * len(v.shape))

    def ffn(w, *done):
        wide = w.shape[1]
        return chunked(
            functools.partial(ffn_body, wide // 3), T // ftile,
            (shape((T, wide), bf16), shape((T, width), bf16), shape((T, width), bf16)),
            (rows_spec(wide), rows_spec(width), rows_spec(width)),
            (second, out_low, w) + done, [rows_spec(width), rows_spec(width), all_spec(w)] + [rows_spec(width)] * len(done), mib=36, keep=(2,) if done else (),
        )

    def ffn_grads(h):
        wide = h.shape[1]
        tile_d = math.gcd(256, width)
        columns = pl.BlockSpec((T, tile_d), lambda i: (0, i))
        return chunked(
            functools.partial(ffn_grad_body, wide // 3), width // tile_d, shape((width, wide), bf16),
            pl.BlockSpec((tile_d, wide), lambda i: (i, 0)), (second, out_low, h), [columns, columns, all_spec(h)], mib=24,
        )

    h1, part_l, part_c = ffn(w1)
    grad_1 = ffn_grads(h1)
    w2, grad_1 = lax.optimization_barrier((w2, grad_1))
    sum_1 = line_sum(grad_1)
    h2, part_l, part_c = ffn(w2, part_l, part_c)
    d_hidden, grad_ffn, branch = call(
        branch_body, 5, (shape((own, width), f32), shape((8, width), f32), shape((T, width), bf16)), (VMEM, VMEM, HBM),
        (part_c, hidden, cot_own, mixer_row(ffn_gain)), [VMEM] * 4, collect, us=50,
    )
    h2, branch = lax.optimization_barrier((h2, branch))
    grad_2 = ffn_grads(h2)
    grad_2b = jnp.concatenate([grad_2, dot(branch, both_low, 0, 0).astype(bf16)], axis=1)
    d_both = dot(branch, wb, 1, 0)

    back, _, back_stack = specs(True)
    dz_low, dy, leave, tail, g_state, grad_gain_s = chunked(
        functools.partial(gate_back_body, heads, nc), nc,
        (shape((T, chan), bf16), shape((T, chan), f32), shape((nc, chan, N), f32), shape((nc, 8, 128), f32),
         shape((chan, N), bf16), shape((8, chan), f32)),
        (back(chan), back(chan), back_stack(chan, N), back_stack(8, 128), fixed(chan, N), fixed(8, chan)),
        (base, raw, bc_all, starts_col, bias_row, rates_row, d_both, y_scan, cv_x, reach, zq, skip_row, gain_row),
        [smem, back(128), back(2 * N), back(1), fixed(1, 128), fixed(1, 128), back(chan), back(chan), back(chan),
         back_stack(16, 128), back(chan), fixed(1, chan), fixed(1, chan)],
        [pltpu.VMEM((chan, N), f32), pltpu.VMEM((8, 128), f32)],
    )
    grad_2b, sum_1, dz_low = lax.optimization_barrier((grad_2b, sum_1, dz_low))
    sum_2 = line_sum(grad_2b)

    dq_low, dkv = chunked(
        functools.partial(attend_back_body, size, T), T // qrows,
        (shape((T, HD), bf16), shape((G, planes, kvr, T), bf16)), (column(0, HD), kv_spec),
        (base, firsts, query, starts_col, cos_row, sin_row, kv_all, d_both, attended, log_mass),
        [smem, smem, column(0, HD), column(0, 1), column(0, HD), column(0, HD), kv_spec, column(at_q, HD), column(0, HD),
         column(0, 1)],
        [pltpu.VMEM((planes, HD, T), f32), pltpu.VMEM((planes, HD, T), f32)], mib=14 + 3 * planes,
    )
    dzq_low = jnp.concatenate([dz_low, dq_low], axis=1)
    grad_z = dot(first, dzq_low, 0, 0).astype(bf16)
    g_state, sum_1, grad_z = lax.optimization_barrier((g_state, sum_1, grad_z))
    states, factors, dkv, layer_own = call(
        functools.partial(down_body, planes), 6, state_shapes + (shape((planes * kvr, T), bf16), shape((own, width), f32)),
        (HBM,) * 2 + (VMEM,) * 2, (g_state, through, dkv.reshape(-1, T), part_l, hidden), [HBM] * 2 + [VMEM] * 3,
        line_sems * 2 + Collect.scratch(planes * kvr, T, False) + Collect.scratch(own, width), us=45, mib=14 + 2 * planes,
    )
    states, grad_z = lax.optimization_barrier((states, grad_z))
    sum_z = line_sum(grad_z)
    after = entering(False, states, factors)
    gx, d_bc_all, d_raw, grad_rows = chunked(
        functools.partial(scan_back_body, heads), nc,
        (shape((T, chan), f32), shape((2 * N, T), bf16), shape((T, 128), bf16), shape((8, 128), f32)),
        (tile(chan), pl.BlockSpec((2 * N, L), lambda c: (0, c)), tile(128), fixed(8, 128)),
        (base, raw, bc_all, starts_col, bias_row, rates_row, dy, cv_x, enter, reach, before, leave, tail, after, skip_row),
        [smem, tile(128), tile(2 * N), tile(1), fixed(1, 128), fixed(1, 128), tile(chan), tile(chan),
         stack(chan, N), stack(16, 128), fixed(chan, N), stack(chan, N), stack(8, 128), fixed(chan, N), fixed(1, chan)],
    )

    d_bc_t, sum_2 = lax.optimization_barrier((d_bc_all, sum_2))
    g_bc, rim_bc, rim_x, dkv, got_1, got_2 = call(
        functools.partial(back_body, planes), 7,
        (shape((bcs, T), f32), shape((bcs, 128), f32), shape((RIM, chan), f32), shape((kvr, T), f32))
        + tuple(shape((G, rows, v.shape[1]), bf16) for v in (h1, h2)), (VMEM,) * 4 + (HBM,) * 2,
        (d_bc_t, dkv.reshape(planes, kvr, T), slope_bc, gx, sum_1, sum_2), [VMEM] * 3 + [HBM] * 3,
        [pltpu.VMEM((G * bcs, T), bf16), pltpu.VMEM((3, bcs, T), bf16), pltpu.VMEM((3, bcs, T), bf16),
         pltpu.VMEM((planes - 1, kvr, T), bf16), pltpu.VMEM((bcs, T), f32), DMA(()), DMA(()), DMA((3,)), DMA((3,)),
         DMA((planes - 1,)), DMA((planes - 1,)), DMA((2,)), DMA((2,)), DMA((2, 3)), DMA((2, 3)), DMA((2,))], us=30,
    )
    starts_long = jnp.concatenate([all_starts, jnp.full((8,), total_tokens, jnp.int32)])
    starts_long = lax.dynamic_slice_in_dim(starts_long, offset, T + 8, 0)[:, None]
    taps_both = jnp.concatenate([taps_inner, taps_pair], axis=1)
    da_low, grad_taps = chunked(
        functools.partial(finish_body, nc, chan), nc,
        (shape((T, a_cols), bf16), shape((8, chan + 128), f32)), (tile(a_cols), fixed(8, chan + 128)),
        (base, pa, gx, rim_x, g_bc, rim_bc, dkv, starts_long, taps_both, cos_k, sin_k),
        [smem, pa_spec, fixed(T, chan), fixed(RIM, chan), fixed(bcs, T), fixed(bcs, 128), fixed(kvr, T),
         fixed(T + 8, 1), fixed(K, chan + 128), fixed(quarter_half, T), fixed(quarter_half, T)], near=(3, 4, 5, 6),
    )
    grad_a = dot(first, da_low, 0, 0).astype(bf16)
    grad_a, sum_z = lax.optimization_barrier((grad_a, sum_z))
    sum_a = line_sum(grad_a)
    lane = width // 4
    part_a = chunked(
        back_part_body, T // ftile, shape((T, width), bf16), rows_spec(width), (da_low, dzq_low, d_raw, wa, w_zqob, w_step),
        [rows_spec(v.shape[1]) for v in (da_low, dzq_low, d_raw)] + [all_spec(v) for v in (wa, wz, w_step)], mib=28, keep=(0,),
    )
    grad_step = dot(d_raw, first, 0, 0)[:16].reshape(16, planes, G, rows).transpose(1, 2, 0, 3)
    groups = (shape((G, rows, chan + HD), bf16),) * 2
    grad_input, layer_out, mine, got_z, got_b = call(
        final_body, 8,
        (shape((tokens, width), f32), shape((tokens, width), f32), shape((RIM, lane), f32)) + groups, (HBM, HBM, VMEM, HBM, HBM),
        (part_a, x_own, d_hidden, layer_own, mixer_row(mixer_gain), grad_taps, grad_gain_s, grad_rows, grad_ffn, sum_z, sum_2),
        [VMEM] * 9 + [HBM] * 2,
        Collect.scratch(own, width)
        + [pltpu.VMEM((own, width), f32), pltpu.VMEM((8, width), f32), DMA((2,)), DMA((2,)), DMA((2,)),
           DMA((2, 3)), DMA((2, 3)), DMA((2,))], us=40,
    )

    got_x, got_s, sums, got_t = call(
        functools.partial(last_body, planes), 10,
        (shape((G, rows, chan), bf16), shape((2 * G, rows, a_cols - chan), bf16), shape((2 * G * RIM, lane), f32),
         shape((G, 16, rows), f32)), (HBM,) * 4, (sum_a, mine, grad_step), [HBM, VMEM, VMEM],
        [pltpu.VMEM((RIM, lane), f32), pltpu.VMEM((planes - 1, RIM, lane), f32), pltpu.VMEM((G, 16, rows), f32),
         pltpu.VMEM((planes - 1, G, 16, rows), f32), DMA((3,)), DMA((3,)), DMA((2 * G,)), DMA((2 * G,)),
         DMA((2,)), DMA((planes - 1,)), DMA((planes - 1,)), DMA((planes - 1,)), DMA((planes - 1,)), DMA((3,)), DMA((3,)), DMA(())]
        + Spread.sems,
    )
    strip = min(32, rows)

    def got(v):
        return pl.BlockSpec((v.shape[0], strip, v.shape[2]), lambda c: (0, c, 0))

    def given(cols):
        return pl.BlockSpec((strip, cols), lambda c: (c, 0))

    widths = [w.shape[1] for w in (
        z_weight, x_weight, bc_weight, q_weight, k_weight, v_weight, o_weight, out_weight,
        gate_weight, up_weight, down_weight,
    )]
    gathered = (got_z, got_b, got_1, got_2, got_x, got_s)
    steps_ = rows // strip
    moved = pl.BlockSpec((tokens // steps_, width), lambda c: (c, 0))
    *weights, layer_out, grad_input = chunked(
        functools.partial(give_body, (bcs, quarter_half)), steps_,
        tuple(shape((rows, w), f32) for w in widths) + (shape((tokens, width), f32),) * 2,
        tuple(given(w) for w in widths) + (moved, moved),
        (jnp.full((1,), hi, jnp.int32),) + gathered + (layer_out, grad_input), [smem] + [got(v) for v in gathered] + [moved, moved], mib=40,
    )
    weights.insert(3, got_t[:, :heads].reshape(G * heads, rows).T)

    sums = sums.reshape(G, cores, RIM, lane)
    mine = lax.dynamic_index_in_dim(sums, hi, 1, False)
    o_conv_inner = mine[:, :K, :chan].transpose(1, 0, 2).reshape(K, G * chan)
    o_conv_state = sums[:, :, :K, chan : chan + bcs].transpose(2, 1, 0, 3).reshape(K, 2 * N)
    per = width // (planes * G)
    gains = jnp.sum(sums[:, :, 8:], axis=(0, 1)).reshape(2, width)
    gains = lax.dynamic_slice_in_dim(gains, (zi * G + pi) * per, per, 1)

    return (
        layer_out, grad_input, gains[1], gains[0], *weights,
        o_conv_inner, o_conv_state,
        mine[:, 5, :heads].reshape(-1), mine[:, 5, 128 : 128 + heads].reshape(-1),
        mine[:, 5, 256 : 256 + heads].reshape(-1), mine[:, 4, :chan].reshape(-1),
    )


def solution(mesh):
    seq, cores = mesh.shape["seq"], mesh.shape["head"]
    planes = Mesh(mesh.devices.reshape(seq // G, G, cores), ("z", "p", "head"))
    s = ("z", "p")
    both, row, head, whole = P(s, "head"), P(s, None), P("head"), P()
    placed = (
        row, P(s), whole, whole, both, both, row, both, both, both, both, both, both, both, both, both,
        P(None, "head"), whole, head, head, head, head, row,
    )
    return jax.shard_map(
        on_device,
        mesh=planes,
        in_specs=placed,
        out_specs=(
            row, row, P(s), P(s), both, both, row, both, both, both, both, both, both, both, both, both,
            P(None, "head"), whole, head, head, head, head,
        ),
        check_vma=False,
    )
```

```python
import functools
import math

import jax
import jax.numpy as jnp
from jax import lax
from jax.experimental import pallas as pl
from jax.experimental.pallas import tpu as pltpu
from jax.sharding import Mesh, PartitionSpec as P

P_SIZE = 64
N = 256
HD = 128
K = 4
G = 4
CHUNK = 128
RIM = 16

highest = lax.Precision.HIGHEST
rope_base = 10000.0
norm_eps = 1e-05
bf16 = jnp.bfloat16
f32 = jnp.float32
MESH = pl.DeviceIdType.MESH
HBM = pl.BlockSpec(memory_space=pl.ANY)
VMEM = pl.BlockSpec(memory_space=pltpu.VMEM)
DMA = pltpu.SemaphoreType.DMA


def rcopy(src, dst, send, recv, **where):
    return pltpu.make_async_remote_copy(
        src_ref=src, dst_ref=dst, send_sem=send, recv_sem=recv, device_id=where, device_id_type=MESH
    )


def here():
    return lax.axis_index("z"), lax.axis_index("p"), lax.axis_index("head")


def ring(p, d):
    return lax.rem(p + d + G, G)


def greet(*partners):
    barrier = pltpu.get_barrier_semaphore()
    for where in partners:
        pl.semaphore_signal(barrier, inc=1, device_id=where, device_id_type=MESH)
    pl.semaphore_wait(barrier, len(partners))


def plane_partners(p, c):
    return [{"p": ring(p, d)} for d in range(1, G)] + [{"head": 1 - c}]


def line_partners(z, planes):
    return [{"z": lax.rem(z + d, planes)} for d in range(1, planes)]


def beside(p):
    return p + 1 - 2 * lax.rem(p, 2), lax.rem(p + 2, G), G - 1 - p


class Spread:
    sems = [DMA((2,)), DMA((2,)), DMA((2,)), DMA((2,)), DMA((4,)), DMA((4,)), DMA(())]

    def __init__(self, block, out, start, rows, sems, cores=True):
        self.block, self.out, self.first, self.rows, self.cores = block, out, start, rows, cores
        self.s1, self.r1, self.s2, self.r2, self.s3, self.r3, self.keep = sems
        _, self.p, self.c = here()
        self.around = beside(self.p)

    def spot(self, q, half=None):
        first, rows = self.first(q, self.c), self.rows
        if half is not None:
            first, rows = first + half * (rows // 2), rows // 2
        return self.out.at[pl.ds(first, rows)]

    def over(self, i):
        return rcopy(self.block, self.spot(self.p), self.s1.at[i], self.r1.at[i], p=self.around[i])

    def relay(self, i):
        spot = self.spot(self.around[i], i)
        return rcopy(spot, spot, self.s2.at[i], self.r2.at[i], p=self.around[1 - i])

    def relayed(self, i):
        spot = self.spot(self.around[2], 1 - i)
        return rcopy(spot, spot, self.s2.at[1 - i], self.r2.at[1 - i], p=self.around[i])

    def across(self, i):
        spot = self.spot(self.p if i == 3 else self.around[i])
        return rcopy(self.block if i == 3 else spot, spot, self.s3.at[i], self.r3.at[i], head=1 - self.c)

    def mine(self):
        return pltpu.make_async_copy(self.block, self.spot(self.p), self.keep)

    def start(self):
        for i in (0, 1):
            self.over(i).start()
        if self.cores:
            self.across(3).start()
        self.mine().start()

    def pass_on(self):
        for i in (0, 1):
            self.over(i).wait_recv()
            self.relay(i).start()
            if self.cores:
                self.across(i).start()
        for i in (0, 1):
            self.relayed(i).wait_recv()
        if self.cores:
            self.across(2).start()

    def finish(self):
        self.mine().wait()
        for i in (0, 1):
            self.over(i).wait_send()
            self.relay(i).wait_send()
        if self.cores:
            for i in range(4):
                self.across(i).wait()


class Collect:
    @staticmethod
    def scratch(rows, width, cores=True):
        return [
            pltpu.VMEM((4, rows, width) if cores else (1, 16, 128), bf16), pltpu.VMEM((3, rows, width), bf16),
            pltpu.VMEM((2, rows // 2, width), bf16), pltpu.VMEM((2, rows, width), bf16),
            pltpu.VMEM((rows, width), f32), DMA((4,)), DMA((4,)), DMA((6,)), DMA((6,)),
        ]

    def __init__(self, part, rows, scratch, strip=16, cores=True):
        self.part, self.rows, self.strip, self.cores = part, rows, strip, cores
        self.cx, self.out, self.rd, self.rx, self.total, self.s1, self.r1, self.s2, self.r2 = scratch
        _, self.p, self.c = here()
        self.around = beside(self.p)

    def first(self, q, c):
        return pl.multiple_of(((q * 2 + c) if self.cores else q) * self.rows, 16)

    def owner(self, i):
        return self.p if i == 3 else self.around[i]

    def across(self, i):
        spot = self.part.at[pl.ds(self.first(self.owner(i), 1 - self.c), self.rows)]
        return rcopy(spot, self.cx.at[i], self.s1.at[i], self.r1.at[i], head=1 - self.c)

    def over(self, i, half):
        at = pl.ds(half * (self.rows // 2), self.rows // 2)
        k = 2 * i + half
        if i == 2:
            return rcopy(self.out.at[2, at], self.rd.at[half], self.s2.at[k], self.r2.at[k], p=self.around[half])
        return rcopy(self.out.at[i, at], self.rx.at[i, at], self.s2.at[k], self.r2.at[k], p=self.around[i])

    def strips(self, body, lo=0, hi=None):
        hi = self.rows if hi is None else hi

        def one(n, carry):
            body(lo + n * self.strip)
            return carry

        lax.fori_loop(0, (hi - lo) // self.strip, one, 0)

    def at(self, first):
        return pl.ds(pl.multiple_of(first, self.strip), self.strip)

    def add(self, i, half=None, relayed=None):
        first = self.first(self.owner(i), self.c)
        size = self.rows // 2

        def one(at):
            v = self.part[self.at(first + at)].astype(f32)
            if self.cores:
                v = v + self.cx[i, self.at(at)].astype(f32)
            if relayed is not None:
                v = v + self.rd[relayed, self.at(at - half * size)].astype(f32)
            if i == 3:
                self.total[self.at(at)] = v
            else:
                self.out[i, self.at(at)] = v.astype(bf16)

        if half is None:
            self.strips(one)
        else:
            self.strips(one, half * size, (half + 1) * size)

    def start(self):
        if self.cores:
            for i in (2, 0, 1, 3):
                self.across(i).start()

    def crossed(self, i):
        if self.cores:
            self.across(i).wait_recv()

    def begin(self):
        self.crossed(2)
        for half in (0, 1):
            self.add(2, half)
            self.over(2, half).start()
        for i in (0, 1):
            self.crossed(i)
            self.add(i, i)
            self.over(i, i).start()
        self.crossed(3)
        self.add(3)

    def relay(self):
        for i in (0, 1):
            self.over(2, 1 - i).wait_recv()
            self.add(i, 1 - i, 1 - i)
            self.over(i, 1 - i).start()

    def middle(self):
        self.begin()
        self.relay()

    def arrive(self):
        for half in (0, 1):
            for i in (0, 1):
                self.over(i, i if half == 0 else 1 - i).wait_recv()

    def sum_of(self, at):
        r = self.at(at)
        return self.total[r] + self.rx[0, r].astype(f32) + self.rx[1, r].astype(f32)

    def finish(self):
        if self.cores:
            for i in range(4):
                self.across(i).wait_send()
        for i in range(3):
            for half in (0, 1):
                self.over(i, half).wait_send()


def call(body, name_id, outs, out_specs, ins, in_specs, scratch, us=20, mib=12):
    ins = [pltpu.with_memory_space_constraint(v, pltpu.HBM) if s is HBM and v.size > 20000 else v for v, s in zip(ins, in_specs)]
    if isinstance(outs, tuple):
        outs = tuple(pltpu.HBM(v.shape, v.dtype) if s is HBM else v for v, s in zip(outs, out_specs))
    elif out_specs is HBM:
        outs = pltpu.HBM(outs.shape, outs.dtype)
    return pl.pallas_call(
        body,
        out_shape=outs,
        in_specs=in_specs,
        out_specs=out_specs,
        scratch_shapes=scratch,
        cost_estimate=pl.CostEstimate(flops=0, bytes_accessed=us * 3_500_000, transcendentals=0),
        compiler_params=pltpu.CompilerParams(
            collective_id=name_id, has_side_effects=True, vmem_limit_bytes=mib * 2**20
        ),
    )(*ins)


def shape(dims, kind):
    return jax.ShapeDtypeStruct(dims, kind)


def exchange_copies(pieces, sems, keep):
    _, p, _ = here()
    away, own = [], []
    for i, (source, width, target, first, led, *part) in enumerate(pieces):
        whole, skip = part or (width, 0)
        rows = source.shape[-2]
        spot = target.at[pl.ds(pl.multiple_of(p * rows, 16), rows), pl.ds(first, width)]
        for d in range(G):
            q = ring(p, d)
            taken = source.at[q] if led else source.at[:, pl.ds(pl.multiple_of(q * whole + skip, 128), width)]
            if d:
                away.append(rcopy(taken, spot, sems[0].at[d - 1, i], sems[1].at[d - 1, i], p=q))
            else:
                own.append(pltpu.make_async_copy(taken, spot, keep.at[i]))
    return away, own


def exchange_a_body(x_ref, small_ref, out_ref, send, recv, keep):
    _, p, c = here()
    greet(*[{"p": ring(p, d)} for d in range(1, G)])
    xw = x_ref.shape[1] // G
    pieces = [(x_ref, xw, out_ref, 0, False), (small_ref, small_ref.shape[2], out_ref, xw, True)]
    away, own = exchange_copies(pieces, (send, recv), keep)
    for copy in away + own:
        copy.start()
    for copy in own + away:
        copy.wait()


def exchange_b_body(z_ref, q_ref, out_ref, o_ref, wb, send, recv, keep):
    _, p, c = here()
    greet(*[{"p": ring(p, d)} for d in range(1, G)])
    pieces, at = [], 0
    for ref in (z_ref, q_ref, out_ref, o_ref):
        pieces.append((ref, ref.shape[1] // G, wb, at, False))
        at += ref.shape[1] // G
    away, own = exchange_copies(pieces, (send, recv), keep)
    for copy in away + own:
        copy.start()
    for copy in own + away:
        copy.wait()


def start_body(planes, first, docs, steps, n1, all_docs, all_steps, *sems):
    z, p, c = here()
    greet(*plane_partners(p, c), *line_partners(z, planes))
    rim_s, rim_r, ps, pr, zs, zr, dk = sems[:7]
    rows = first.shape[0]
    a = Spread(first, n1, lambda q, k: pl.multiple_of(RIM + (q * 2 + k) * rows, 16), rows, sems[7:])
    near = [
        rcopy(have(ring(p, d)), every.at[z, p], ps.at[i, d - 1], pr.at[i, d - 1], p=ring(p, d))
        for i, (have, every) in enumerate(((lambda q: docs, all_docs), (lambda q: steps.at[q], all_steps))) for d in (1, 2, 3)
    ]
    own = [
        pltpu.make_async_copy(docs, all_docs.at[z, p], dk.at[0]), pltpu.make_async_copy(steps.at[p], all_steps.at[z, p], dk.at[1])
    ]
    a.start()
    for copy in near + own:
        copy.start()
    for copy in own + near:
        copy.wait()
    far = [
        rcopy(every.at[z], every.at[z], zs.at[i, d - 1], zr.at[i, d - 1], z=lax.rem(z + d, planes))
        for i, every in enumerate((all_docs, all_steps)) for d in range(1, planes)
    ]
    for copy in far:
        copy.start()
    a.pass_on()
    a.finish()
    last = n1.at[pl.ds(n1.shape[0] - RIM, RIM)]
    rim = rcopy(last, n1.at[pl.ds(0, RIM)], rim_s, rim_r, z=lax.rem(z + 1, planes))
    rim.start()
    for copy in far:
        copy.wait()
    rim.wait()


def spread_body(planes, block, kv, gate_w, up_w, down_w, out, lines, w1, w2, zs, zr, zk, send, recv, hold, *sems):
    z, p, c = here()
    greet(*plane_partners(p, c), *line_partners(z, planes))
    rows = block.shape[0]
    far = [rcopy(kv, lines.at[z], zs.at[d - 1], zr.at[d - 1], z=lax.rem(z + d, planes)) for d in range(1, planes)]
    keep = pltpu.make_async_copy(kv, lines.at[z], zk)
    for copy in far:
        copy.start()
    keep.start()
    s = Spread(block, out, lambda q, k: pl.multiple_of((k * G + q) * rows, 16), rows, sems)
    units = gate_w.shape[1] // G
    pieces = [
        (ref, part, to, i * part, False, units, skip)
        for to, part, skip in ((w1, w1.shape[1] // 3, 0), (w2, w2.shape[1] // 3, w1.shape[1] // 3))
        for i, ref in enumerate((gate_w, up_w, down_w))
    ]
    away, own = exchange_copies(pieces, (send, recv), hold)
    s.start()
    for copy in away + own:
        copy.start()
    s.pass_on()
    s.finish()
    for copy in own + away:
        copy.wait()
    keep.wait()
    for copy in far:
        copy.wait()


def state_copies(planes, upward, state, factor, states, factors, sems):
    z, _, _ = here()
    s1, r1, s2, r2 = sems
    way = 1 if upward else -1

    def pair(d):
        to = lax.rem(z + way * d + planes, planes)
        return (
            rcopy(state, states.at[d - 1], s1.at[d - 1], r1.at[d - 1], z=to),
            rcopy(factor, factors.at[d - 1], s2.at[d - 1], r2.at[d - 1], z=to),
        )

    def start():
        for d in range(1, planes):
            @pl.when((z + d < planes) if upward else (z - d >= 0))
            def _():
                for copy in pair(d):
                    copy.start()

    def wait():
        for d in range(1, planes):
            @pl.when((z - d >= 0) if upward else (z + d < planes))
            def _():
                for copy in pair(d):
                    copy.wait_recv()

            @pl.when((z + d < planes) if upward else (z - d >= 0))
            def _():
                for copy in pair(d):
                    copy.wait_send()

    return start, wait


def up_body(planes, state, factor, lines, low, states, factors, kv, ol, *sems):
    z, p, c = here()
    greet(*plane_partners(p, c), *line_partners(z, planes))
    start, wait = state_copies(planes, True, state, factor, states, factors, sems[:4])
    start()
    rows = low.shape[0]
    s = Spread(lines, kv, lambda q, k: q * planes, planes, sems[4:11], cores=False)
    b = Spread(low, ol, lambda q, k: pl.multiple_of((q * 2 + k) * rows, 16), rows, sems[11:18])
    s.start()
    b.start()
    s.pass_on()
    b.pass_on()
    s.finish()
    b.finish()
    wait()


def down_body(planes, state, factor, dkv, part, hidden, states, factors, kv, layer, *sems):
    z, p, c = here()
    greet(*plane_partners(p, c), *line_partners(z, planes))
    start, wait = state_copies(planes, False, state, factor, states, factors, sems[:4])
    start()
    k = Collect(dkv, kv.shape[0], sems[4:13], cores=False)
    s = Collect(part, hidden.shape[0], sems[13:])
    s.start()
    k.begin()
    s.begin()
    k.relay()
    s.relay()
    k.arrive()

    def sum_kv(at):
        kv[k.at(at)] = k.sum_of(at).astype(bf16)

    k.strips(sum_kv)
    s.arrive()

    def one(at):
        layer[s.at(at)] = hidden[s.at(at)] + s.sum_of(at)

    s.strips(one)
    k.finish()
    s.finish()
    wait()


def hidden_body(part, x_ref, gain, hidden, second, *scratch):
    _, p, c = here()
    greet(*plane_partners(p, c))
    rows = x_ref.shape[0]
    s = Collect(part, rows, scratch[:9])
    stage = scratch[9]
    s.start()
    s.middle()
    s.arrive()

    def one(at):
        r = s.at(at)
        h = x_ref[r] + s.sum_of(at)
        hidden[r] = h
        scale = lax.rsqrt(jnp.mean(h * h, axis=-1, keepdims=True) + norm_eps)
        stage[r] = (h * scale * gain[...]).astype(bf16)

    s.strips(one)
    g = Spread(stage, second, s.first, rows, scratch[10:17])
    g.start()
    g.pass_on()
    s.finish()
    g.finish()


def branch_body(part, hidden, cot, gain, d_hidden, gain_grad, branch, *scratch):
    _, p, c = here()
    greet(*plane_partners(p, c))
    rows = hidden.shape[0]
    s = Collect(part, rows, scratch[:9])
    stage = scratch[9]
    gain_grad[...] = jnp.zeros_like(gain_grad)
    s.start()
    s.middle()
    s.arrive()

    def one(at):
        r = s.at(at)
        h = hidden[r]
        scale = lax.rsqrt(jnp.mean(h * h, axis=-1, keepdims=True) + norm_eps)
        grad = s.sum_of(at)
        gain_grad[pl.ds(0, 1)] += jnp.sum(grad * h * scale, axis=0, keepdims=True)
        u = grad * gain[...]
        d = cot[r] + scale * u - h * (scale * scale * scale * jnp.mean(u * h, axis=-1, keepdims=True))
        d_hidden[r] = d
        stage[r] = d.astype(bf16)

    s.strips(one)
    g = Spread(stage, branch, s.first, rows, scratch[10:17])
    g.start()
    g.pass_on()
    s.finish()
    g.finish()


def final_body(part, x_ref, d_hidden, layer, gain, taps, norm, rows_ref, ffn, sum_z, sum_b, grad_in, layer_out, mine, got_z, got_b, *scratch):
    z, p, c = here()
    greet(*plane_partners(p, c))
    rows = x_ref.shape[0]
    s = Collect(part, rows, scratch[:9])
    stage, gain_row, es, er, ek, zs, zr, zk = scratch[9:]
    half = pl.ds(pl.multiple_of(c * rows, 16), rows)
    wide = got_z.shape[1]

    def halves(i, source, target):
        return (
            rcopy(source, target.at[half], es.at[i], er.at[i], head=1 - c),
            pltpu.make_async_copy(source, target.at[half], ek.at[i]),
        )

    def rows_of(v, q):
        cols = got_z.shape[2]
        return v.at[pl.ds(pl.multiple_of(q * wide, 16), wide), pl.ds(v.shape[1] - cols, cols)]

    s.start()
    first = halves(0, layer, layer_out)
    for copy in first:
        copy.start()
    lane = mine.shape[1]
    mine[...] = jnp.zeros_like(mine)
    mine[:K, : taps.shape[1]] = taps[:K]
    mine[4:5, : norm.shape[1]] = norm[:1]
    for j in range(3):
        mine[5:6, j * 128 : (j + 1) * 128] = rows_ref[j : j + 1]
    for j in range(4):
        mine[8 + j : 9 + j] = ffn[:1, j * lane : (j + 1) * lane]
    gain_row[...] = jnp.zeros_like(gain_row)
    s.middle()
    zb = []
    for i, (have, got) in enumerate(((sum_z, got_z), (sum_b, got_b))):
        for d in (1, 2, 3):
            zb.append(rcopy(rows_of(have, ring(p, d)), got.at[p], zs.at[i, d - 1], zr.at[i, d - 1], p=ring(p, d)))
        zb.append(pltpu.make_async_copy(rows_of(have, p), got.at[p], zk.at[i]))
    for copy in zb:
        copy.start()
    s.arrive()

    def one(at):
        r = s.at(at)
        v = x_ref[r]
        scale = lax.rsqrt(jnp.mean(v * v, axis=-1, keepdims=True) + norm_eps)
        grad = s.sum_of(at)
        gain_row[pl.ds(0, 1)] += jnp.sum(grad * v * scale, axis=0, keepdims=True)
        u = grad * gain[...]
        stage[r] = d_hidden[r] + scale * u - v * (scale * scale * scale * jnp.mean(u * v, axis=-1, keepdims=True))

    s.strips(one)
    second = halves(1, stage, grad_in)
    for copy in second:
        copy.start()
    for j in range(4):
        mine[12 + j : 13 + j] = gain_row[:1, j * lane : (j + 1) * lane]
    s.finish()
    for copy in first + second:
        copy.wait()
    for copy in zb:
        copy.wait()


def back_body(planes, dbc, dkv, d_silu_bc, gx, sum_1, sum_2, g_bc, rim_bc, rim_x, kv_out, got_1, got_2, *scratch):
    z, p, c = here()
    greet(*plane_partners(p, c), *line_partners(z, planes))
    (cx, bx, rbc, zkv, acc, xs, xr, bs, br, zs, zr, ms, mr, ws, wr, wk) = scratch
    rows = rbc.shape[1]
    across = rcopy(
        dbc.at[pl.ds(pl.multiple_of((1 - c) * G * rows, 16), G * rows)], cx, xs, xr, head=1 - c
    )
    across.start()

    def kv_down(d):
        to = lax.rem(z - d + planes, planes)
        return rcopy(dkv.at[to], zkv.at[d - 1], zs.at[d - 1], zr.at[d - 1], z=to)

    for d in range(1, planes):
        @pl.when(z - d >= 0)
        def _():
            kv_down(d).start()

    across.wait_recv()
    bc_over = []
    grads = list(enumerate(((sum_1, got_1), (sum_2, got_2))))
    wide = got_1.shape[1]

    def rows_of(q):
        return pl.ds(pl.multiple_of(q * wide, 16), wide)

    w_over = [
        rcopy(have.at[rows_of(ring(p, d)), pl.ds(0, got.shape[2])], got.at[p], ws.at[i, d - 1], wr.at[i, d - 1], p=ring(p, d))
        for i, (have, got) in grads for d in (1, 2, 3)
    ]
    w_own = [pltpu.make_async_copy(have.at[rows_of(p), pl.ds(0, got.shape[2])], got.at[p], wk.at[i]) for i, (have, got) in grads]
    for d in (1, 2, 3, 0):
        q = ring(p, d)
        own = dbc[pl.ds(pl.multiple_of((c * G + q) * rows, 16), rows)].astype(f32)
        own = own + cx[pl.ds(pl.multiple_of(q * rows, 16), rows)].astype(f32)
        if d:
            bx[d - 1] = own.astype(bf16)
            bc_over.append(rcopy(bx.at[d - 1], rbc.at[d - 1], bs.at[d - 1], br.at[d - 1], p=q))
            bc_over[-1].start()
        else:
            acc[...] = own
    for copy in w_over + w_own:
        copy.start()
    for copy in bc_over:
        copy.wait_recv()
    g = acc[...]
    for d in range(3):
        g = g + rbc[d].astype(f32)
    g_bc[...] = g * d_silu_bc[...]
    before = lax.rem(z - 1 + planes, planes)
    rims = [
        rcopy(g_bc.at[:, pl.ds(0, 128)], rim_bc, ms.at[0], mr.at[0], z=before),
        rcopy(gx.at[pl.ds(0, RIM)], rim_x, ms.at[1], mr.at[1], z=before),
    ]
    for copy in rims:
        copy.start()
    kv_out[...] = dkv[z].astype(f32)
    for d in range(1, planes):
        @pl.when(z + d < planes)
        def _():
            kv_down(d).wait_recv()
            kv_out[...] += zkv[d - 1].astype(f32)

        @pl.when(z - d >= 0)
        def _():
            kv_down(d).wait_send()

    for copy in rims:
        copy.wait()
    across.wait_send()
    for copy in bc_over:
        copy.wait_send()
    for copy in w_own + w_over:
        copy.wait()


def last_body(planes, sum_a, small, steps, got_x, got_s, sums, got_t, mine, others, t_own, t_far, xs, xr, ss, sr, keep, ls, lr,
              ts, tr, qs, qr, tk, gs, gr, gk):
    z, p, c = here()
    pairs = [(d, k) for k in (0, 1) for d in range(G) if d or k]
    greet(*[{"p": ring(p, d), "head": lax.rem(c + k, 2)} for d, k in pairs], *line_partners(z, planes))
    rows, chan = got_x.shape[1], got_x.shape[2]

    def part(q, first, cols):
        return sum_a.at[pl.ds(pl.multiple_of(q * rows, 16), rows), pl.ds(first, cols)]

    def narrow(d, k):
        cols, to = got_s.shape[2], got_s.at[c * G + p]
        i = k * G + d - 1
        return rcopy(part(ring(p, d), chan, cols), to, ss.at[i], sr.at[i], p=ring(p, d), head=lax.rem(c + k, 2))

    lines = [
        rcopy(small, others.at[d - 1], ls.at[d - 1], lr.at[d - 1], z=lax.rem(z + d, planes)) for d in range(1, planes)
    ] + [
        rcopy(steps.at[lax.rem(z + d, planes)], t_far.at[d - 1], ts.at[d - 1], tr.at[d - 1], z=lax.rem(z + d, planes))
        for d in range(1, planes)
    ]
    copies = [
        rcopy(part(ring(p, d), 0, chan), got_x.at[p], xs.at[d - 1], xr.at[d - 1], p=ring(p, d)) for d in (1, 2, 3)
    ] + [narrow(d, k) for d, k in pairs] + [
        pltpu.make_async_copy(part(p, 0, chan), got_x.at[p], keep.at[0]),
        pltpu.make_async_copy(part(p, chan, got_s.shape[2]), got_s.at[c * G + p], keep.at[1]),
    ]
    for copy in lines + copies:
        copy.start()
    for copy in lines:
        copy.wait()
    total = small[...]
    for d in range(1, planes):
        total = total + others[d - 1]
    mine[...] = total
    place = sums.at[pl.ds(pl.multiple_of((p * 2 + c) * RIM, RIM), RIM)]
    shares = [
        rcopy(mine, place, gs.at[k * G + d - 1], gr.at[k * G + d - 1], p=ring(p, d), head=lax.rem(c + k, 2)) for d, k in pairs
    ]
    shares.append(pltpu.make_async_copy(mine, place, gk))
    for copy in shares:
        copy.start()
    total = steps[z]
    for d in range(1, planes):
        total = total + t_far[d - 1]
    t_own[...] = total
    back = [rcopy(t_own.at[ring(p, d)], got_t.at[p], qs.at[d - 1], qr.at[d - 1], p=ring(p, d)) for d in (1, 2, 3)]
    back.append(pltpu.make_async_copy(t_own.at[p], got_t.at[p], tk))
    for copy in back:
        copy.start()
    for copy in copies + back + shares:
        copy.wait()


def give_body(sizes, core_ref, zq, ob, f1, f2, x_, s_, layer, grad, z_o, x_o, bc_o, q_o, k_o, v_o, o_o, out_o, gate_o, up_o, down_o,
              layer_o, grad_o):
    bcs, quarter = sizes
    layer_o[...] = layer[...]
    grad_o[...] = grad[...]
    chan, units = x_.shape[2], (f1.shape[2] + f2.shape[2]) // 3
    for p in range(G):
        for ref, got, first, cols in (
            (z_o, zq, 0, chan), (q_o, zq, chan, HD), (out_o, ob, 0, chan), (o_o, ob, chan, HD),
            (x_o, x_, 0, chan),
        ):
            ref[:, p * cols : (p + 1) * cols] = got[p, :, first : first + cols].astype(f32)

        for i, ref in enumerate((gate_o, up_o, down_o)):
            for got, skip in ((f1, 0), (f2, f1.shape[2] // 3)):
                part = got.shape[2] // 3
                at = p * units + skip
                ref[:, at : at + part] = got[p, :, i * part : (i + 1) * part].astype(f32)

    def place(first, cols, target):
        i = iota((128, 128), 0) - first
        return ((i >= 0) & (i < cols) & (iota((128, 128), 1) == target(i))).astype(bf16)

    def bc_place(p):
        return (iota((128, 256), 0) + p * bcs == iota((128, 256), 1)).astype(bf16) * (iota((128, 256), 0) < bcs).astype(bf16)

    mine = core_ref[0]
    k_sum = v_sum = jnp.zeros((x_.shape[1], 128), f32)
    halves = []
    for k in (0, 1):
        total = jnp.zeros((x_.shape[1], 256), f32)
        for p in range(G):
            total = total + mm(s_[k * G + p], bc_place(p), 1, 0)
        halves.append(total)
    bc_o[:, :256] = halves[0]
    bc_o[:, 256:] = halves[1]
    for p in range(G):
        own = s_[mine * G + p]
        k_sum = k_sum + mm(own, place(bcs, 2 * quarter, lambda i: (i // quarter) * (quarter * G) + p * quarter + i % quarter), 1, 0)
        v_sum = v_sum + mm(own, place(bcs + 2 * quarter, 2 * quarter, lambda i: i + p * 2 * quarter), 1, 0)
    k_o[...] = k_sum
    v_o[...] = v_sum


def mm(a, b, ca, cb):
    return lax.dot_general(a.astype(bf16), b.astype(bf16), (((ca,), (cb,)), ((), ())), preferred_element_type=f32)


def mm_exact(a, b, ca, cb):
    return lax.dot_general(a, b, (((ca,), (cb,)), ((), ())), precision=highest, preferred_element_type=f32)


def iota(dims, axis):
    return lax.broadcasted_iota(jnp.int32, dims, axis)


def soft(v):
    return jnp.maximum(v, 0.0) + jnp.log1p(jnp.exp(-jnp.abs(v)))


def sig(v):
    return 1.0 / (1.0 + jnp.exp(-v))


def rates_of(raw, bias, rates, heads):
    lane = iota((CHUNK, 128), 1)
    step = jnp.where(lane < heads, soft(raw + bias), 0.0)
    log_decay = -jnp.exp(rates) * step
    lower = (iota((CHUNK, CHUNK), 0) >= iota((CHUNK, CHUNK), 1)).astype(f32)
    return step, log_decay, mm_exact(lower, log_decay, 1, 0)


def pair_of(v, pair):
    left = iota((CHUNK, 128), 1) < P_SIZE
    return jnp.where(left, v[:, 2 * pair : 2 * pair + 1], v[:, 2 * pair + 1 : 2 * pair + 2])


def lanes(v, pair):
    return v[:, pair * 128 : (pair + 1) * 128]


def halves_of(a, b):
    return jnp.where(iota(a.shape, 1) < P_SIZE, a, b)


def head_means(v):
    same = (iota((128, 128), 0) // P_SIZE == iota((128, 128), 1) // P_SIZE).astype(f32) / P_SIZE
    return jnp.concatenate([mm_exact(lanes(v, k), same, 1, 0) for k in range(v.shape[1] // 128)], axis=1)


def head_sums(v, heads):
    chan = v.shape[1]
    pick = (iota((chan, 128), 0) // P_SIZE == iota((chan, 128), 1)).astype(f32)
    return mm_exact(v, pick, 1, 0)


def scale_rows(v, factor, heads):
    return jnp.concatenate(
        [v[h * P_SIZE : (h + 1) * P_SIZE] * factor[h : h + 1, :1] for h in range(heads)], axis=0
    )


def conv_of(pa_ref, taps_ref, starts, place, c, chan, first):
    block = pa_ref[pl.ds(pl.multiple_of(c * CHUNK + RIM - 8, 8), CHUNK + 8), first : first + chan]
    total = jnp.zeros((CHUNK, chan), f32)
    for lag in range(K):
        back = K - 1 - lag
        total = total + jnp.where(place - back >= starts, block[8 - back : 8 - back + CHUNK] * taps_ref[lag : lag + 1], 0.0)
    return total


def places_of(base_ref, c):
    return base_ref[0] + c * CHUNK + iota((CHUNK, 1), 0)


def weights_of(h, cs, cs_t, visible):
    span = cs[:, h : h + 1] - cs_t[h : h + 1]
    return jnp.where(visible, jnp.exp(jnp.where(visible, span, 0.0)), 0.0)


def visible_of(base_ref, c, starts, place):
    across = base_ref[0] + c * CHUNK + iota((CHUNK, CHUNK), 1)
    return (starts <= across) & (across <= place)


def decays_of(cs, starts, place):
    first = place[:1]
    decay_in = jnp.where(starts < first, jnp.exp(cs), 0.0)
    closing = jnp.where(starts[CHUNK - 1 :] <= place, jnp.exp(cs[CHUNK - 1 :] - cs), 0.0)
    return decay_in, closing


def scan_body(heads, base_ref, raw_ref, pa_ref, bc_ref, starts_ref, taps_ref, bias_ref, rates_ref,
              y_ref, cv_ref, enter_ref, reach_ref, state_out, through_out, state, through):
    c = pl.program_id(0)
    chan = heads * P_SIZE

    @pl.when(c == 0)
    def _():
        state[...] = jnp.zeros_like(state)
        through[...] = jnp.ones_like(through)

    starts, place = starts_ref[...], places_of(base_ref, c)
    raw = raw_ref[...]
    step, _, cs = rates_of(raw, bias_ref[...], rates_ref[...], heads)
    cs_t = cs.T
    cv = conv_of(pa_ref, taps_ref, starts, place, c, chan, 0)
    cv_ref[...] = cv
    x = cv * sig(cv)
    b_rows, c_rows = bc_ref[:, :N], bc_ref[:, N:]
    inter = mm(c_rows, b_rows, 1, 1)
    visible = visible_of(base_ref, c, starts, place)
    decay_in, closing = decays_of(cs, starts, place)
    ends = decay_in.T
    for k in range(heads // 2):
        driven = lanes(x, k) * pair_of(step, k)
        mixed = [mm(weights_of(2 * k + i, cs, cs_t, visible) * inter, driven, 1, 0) for i in (0, 1)]
        y_ref[:, k * 128 : (k + 1) * 128] = halves_of(*mixed)
        local = mm(driven * pair_of(closing, k), b_rows, 0, 0)
        at = pl.ds(k * 128, 128)
        old = state[at]
        enter_ref[0, at] = old
        both = jnp.concatenate(
            [old[i * P_SIZE : (i + 1) * P_SIZE] * ends[2 * k + i : 2 * k + i + 1, CHUNK - 1 :] for i in (0, 1)], axis=0
        )
        state[at] = both + local
    factor = jnp.broadcast_to(ends[:8, CHUNK - 1 :], (8, 128))
    reach_ref[0, :8] = through[...]
    reach_ref[0, 8:] = factor
    through[...] = through[...] * factor
    state_out[...] = state[...].astype(bf16)
    through_out[...] = through[...]


def gate_parts(y_scan, cv, z, skip, gain):
    x = cv * sig(cv)
    ssm = y_scan + skip * x
    s = sig(z)
    gated = ssm * (z * s)
    r = lax.rsqrt(head_means(gated * gated) + norm_eps)
    return x, ssm, s, gated, r


def gate_body(heads, base_ref, raw_ref, bc_ref, starts_ref, bias_ref, rates_ref, y_ref, cv_ref, enter_ref, reach_ref,
              before_ref, z_ref, skip_ref, gain_ref, low_ref, scan_ref):
    c = pl.program_id(0)
    chan = heads * P_SIZE
    starts, place = starts_ref[...], places_of(base_ref, c)
    raw = raw_ref[...]
    _, _, cs = rates_of(raw, bias_ref[...], rates_ref[...], heads)
    decay_in, _ = decays_of(cs, starts, place)
    state_in = enter_ref[0] + scale_rows(before_ref[...], reach_ref[0], heads)
    c_rows = bc_ref[:, N:]
    off = [mm(c_rows, state_in[k * 128 : (k + 1) * 128], 1, 1) * pair_of(decay_in, k) for k in range(heads // 2)]
    y_scan = y_ref[...] + jnp.concatenate(off, axis=1)
    scan_ref[...] = y_scan
    _, _, _, gated, r = gate_parts(y_scan, cv_ref[...], z_ref[...], skip_ref[...], gain_ref[...])
    low_ref[...] = (gated * r * gain_ref[...]).astype(bf16)


def gate_back_body(heads, chunks, base_ref, raw_ref, bc_ref, starts_ref, bias_ref, rates_ref, d_ref, scan_ref, cv_ref,
                   reach_ref, z_ref, skip_ref, gain_ref, dz_ref, dy_ref, leave_ref, tail_ref, state_out, gain_out, state, tail):
    c = chunks - 1 - pl.program_id(0)
    chan = heads * P_SIZE

    @pl.when(c == chunks - 1)
    def _():
        state[...] = jnp.zeros_like(state)
        tail[...] = jnp.ones_like(tail)
        gain_out[...] = jnp.zeros_like(gain_out)

    starts, place = starts_ref[...], places_of(base_ref, c)
    raw = raw_ref[...]
    _, _, cs = rates_of(raw, bias_ref[...], rates_ref[...], heads)
    decay_in, _ = decays_of(cs, starts, place)
    z = z_ref[...]
    x, ssm, s, gated, r = gate_parts(scan_ref[...], cv_ref[...], z, skip_ref[...], gain_ref[...])
    d = d_ref[...]
    gain_out[:1] += jnp.sum(d * gated * r, axis=0, keepdims=True)
    u = d * gain_ref[...]
    d_gated = r * u - gated * (r * r * r * head_means(u * gated))
    dz_ref[...] = (d_gated * ssm * (s * (1.0 + z * (1.0 - s)))).astype(bf16)
    dy = d_gated * (z * s)
    dy_ref[...] = dy
    c_rows = bc_ref[:, N:]
    leave_ref[0] = state[...]
    tail_ref[0] = tail[...]
    factor = reach_ref[0, 8:]
    local = [mm(lanes(dy, k) * pair_of(decay_in, k), c_rows, 0, 0) for k in range(heads // 2)]
    state[...] = scale_rows(state[...], factor, heads) + jnp.concatenate(local, axis=0)
    tail[...] = tail[...] * factor
    state_out[...] = state[...].astype(bf16)


def scan_back_body(heads, base_ref, raw_ref, bc_ref, starts_ref, bias_ref, rates_ref, dy_ref, cv_ref,
                   enter_ref, reach_ref, before_ref, leave_ref, tail_ref, after_ref, skip_ref,
                   gx_ref, dbc_ref, raw_out, rows_out):
    c = pl.program_id(0)
    chan = heads * P_SIZE

    @pl.when(c == 0)
    def _():
        rows_out[...] = jnp.zeros_like(rows_out)

    starts, place = starts_ref[...], places_of(base_ref, c)
    raw = raw_ref[...]
    step, log_decay, cs = rates_of(raw, bias_ref[...], rates_ref[...], heads)
    cs_t = cs.T
    visible = visible_of(base_ref, c, starts, place)
    decay_in, closing = decays_of(cs, starts, place)
    b_rows, c_rows = bc_ref[:, :N], bc_ref[:, N:]
    inter = mm(c_rows, b_rows, 1, 1)
    cv = cv_ref[...]
    s = sig(cv)
    x = cv * s
    dy = dy_ref[...]
    state_in = enter_ref[0] + scale_rows(before_ref[...], reach_ref[0], heads)
    d_state = leave_ref[0] + scale_rows(after_ref[...], tail_ref[0], heads)
    left = iota((CHUNK, 128), 1) < P_SIZE
    d_inter = jnp.zeros((CHUNK, CHUNK), f32)
    d_b = jnp.zeros((CHUNK, N), f32)
    d_c = jnp.zeros((CHUNK, N), f32)
    inside, outside, closes, drives = [], [], [], []
    for k in range(heads // 2):
        at = slice(k * 128, (k + 1) * 128)
        driven = (lanes(x, k) * pair_of(step, k)).astype(bf16)
        dyk = lanes(dy, k)
        dyb = dyk.astype(bf16)
        d_mixed, y_mixed = [], []
        for i in (0, 1):
            w = weights_of(2 * k + i, cs, cs_t, visible)
            mix = (w * inter).astype(bf16)
            half = jnp.where(left if i == 0 else ~left, dyb, jnp.zeros_like(dyb))
            d_inter = d_inter + w * mm(half, driven, 1, 1)
            d_mixed.append(mm(mix, dyb, 0, 0))
            y_mixed.append(mm(mix, driven, 1, 0))
        d_mix = halves_of(*d_mixed)
        close = pair_of(closing, k)
        d_close = mm(b_rows, d_state[at], 1, 1)
        closed = driven.astype(f32) * close
        enter = pair_of(decay_in, k)
        y_off = mm(c_rows, state_in[at], 1, 1) * enter
        d_c = d_c + mm(dyk * enter, state_in[at], 1, 0)
        d_b = d_b + mm(closed, d_state[at], 1, 0)
        inside.append(dyb.astype(f32) * halves_of(*y_mixed) - driven.astype(f32) * d_mix)
        outside.append(dyk * y_off)
        closes.append(closed * d_close)
        drives.append(d_mix + close * d_close)
    d_c = d_c + mm(d_inter, b_rows, 1, 0)
    d_b = d_b + mm(d_inter, c_rows, 0, 0)
    dbc_ref[:N] = d_b.astype(bf16).T
    dbc_ref[N:] = d_c.astype(bf16).T
    d_driven = jnp.concatenate(drives, axis=1)
    closes = head_sums(jnp.concatenate(closes, axis=1), heads)
    d_cs = head_sums(jnp.concatenate(inside, axis=1) + jnp.concatenate(outside, axis=1), heads) - closes
    kept = head_sums_t(d_state * state_in, heads)
    whole = decay_in[CHUNK - 1 :] * kept + jnp.sum(closes, axis=0, keepdims=True)
    upper = (iota((CHUNK, CHUNK), 0) <= iota((CHUNK, CHUNK), 1)).astype(f32)
    d_la = mm_exact(upper, d_cs, 1, 0) + whole
    d_step = head_sums(d_driven * x, heads)
    d_raw = (d_step - jnp.exp(rates_ref[...]) * d_la) * sig(raw + bias_ref[...])
    d_raw = jnp.where(iota((CHUNK, 128), 1) < heads, d_raw, 0.0)
    raw_out[...] = d_raw.astype(bf16)
    rows_out[:1] += jnp.sum(d_la * log_decay, axis=0, keepdims=True)
    rows_out[1:2] += jnp.sum(d_raw, axis=0, keepdims=True)
    rows_out[2:3] += jnp.sum(head_sums(dy * x, heads), axis=0, keepdims=True)
    wide = jnp.concatenate([pair_of(step, k) for k in range(heads // 2)], axis=1)
    gx_ref[...] = (d_driven * wide + skip_ref[...] * dy) * (s * (1.0 + cv * (1.0 - s)))


def unshuffled(v, back=False):
    quarter = HD // 2 // G
    i, j = (iota((HD, HD), 1), iota((HD, HD), 0)) if back else (iota((HD, HD), 0), iota((HD, HD), 1))
    half, rest = i // (HD // 2), i % (HD // 2)
    to = (rest // quarter) * 2 * quarter + half * quarter + rest % quarter
    return mm_exact(v, (to == j).astype(f32), 1, 0)


def keys_of(kv_ref, begin, size, tokens):
    plane, at = begin // tokens, pl.ds(pl.multiple_of(begin % tokens, 128), size)
    half = kv_ref.shape[2] // 2
    keys = jnp.concatenate([kv_ref[p, plane, :half, at] for p in range(G)], axis=0)
    values = jnp.concatenate([kv_ref[p, plane, half:, at] for p in range(G)], axis=0)
    return plane, at, keys, values


def seen_of(begin, size, starts, place):
    at = begin + iota((starts.shape[0], size), 1)
    return (at >= starts) & (at <= place)


def attend_body(size, tokens, base_ref, first_ref, q_ref, starts_ref, cos_ref, sin_ref, kv_ref,
                query_ref, low_ref, out_ref, mass_ref):
    i = pl.program_id(0)
    rows = q_ref.shape[0]
    v = q_ref[...]
    turned = (v * cos_ref[...] - pltpu.roll(v, HD // 2, 1) * sin_ref[...]) * HD ** (-0.5)
    query = unshuffled(turned.astype(bf16).astype(f32)).astype(bf16)
    query_ref[...] = query
    starts = starts_ref[...]
    place = base_ref[0] + i * rows + iota((rows, 1), 0)

    def step(n, carry):
        peak, mass, total = carry
        begin = n * size
        _, _, keys, values = keys_of(kv_ref, begin, size, tokens)
        scores = jnp.where(seen_of(begin, size, starts, place), mm(query, keys, 1, 0), -1e30)
        new = jnp.maximum(peak, jnp.max(scores, axis=1, keepdims=True))
        probs = jnp.where(scores > -1e29, jnp.exp(scores - new), 0.0)
        keep = jnp.exp(peak - new)
        return new, mass * keep + jnp.sum(probs, axis=1, keepdims=True), total * keep + mm(probs, values, 1, 1)

    begin = first_ref[i] // size
    end = (base_ref[0] + (i + 1) * rows - 1) // size + 1
    start = (jnp.full((rows, 1), -1e30, f32), jnp.zeros((rows, 1), f32), jnp.zeros((rows, HD), f32))
    peak, mass, total = lax.fori_loop(begin, end, step, start)
    attended = total / mass
    out_ref[...] = attended
    low_ref[...] = attended.astype(bf16)
    mass_ref[...] = peak + jnp.log(mass)


def attend_back_body(size, tokens, base_ref, first_ref, query_ref, starts_ref, cos_ref, sin_ref, kv_ref, d_ref, out_ref, mass_ref,
                     dq_ref, dkv_ref, d_keys, d_values):
    i = pl.program_id(0)
    rows = query_ref.shape[0]

    @pl.when(i == 0)
    def _():
        d_keys[...] = jnp.zeros_like(d_keys)
        d_values[...] = jnp.zeros_like(d_values)

    query = query_ref[...]
    d_low = d_ref[...].astype(bf16)
    balance = jnp.sum(d_low.astype(f32) * out_ref[...], axis=1, keepdims=True)
    query_t, d_t = query.T, d_low.T
    starts, mass = starts_ref[...], mass_ref[...]
    place = base_ref[0] + i * rows + iota((rows, 1), 0)

    def step(n, total):
        begin = n * size
        plane, at, keys, values = keys_of(kv_ref, begin, size, tokens)
        seen = seen_of(begin, size, starts, place)
        probs = jnp.where(seen, jnp.exp(jnp.where(seen, mm(query, keys, 1, 0) - mass, 0.0)), 0.0)
        d_scores = (probs * (mm(d_low, values, 1, 0) - balance)).astype(bf16)
        d_keys[plane, :, at] += mm(query_t, d_scores, 1, 0)
        d_values[plane, :, at] += mm(d_t, probs, 1, 0)
        return total + mm(d_scores, keys, 1, 1)

    begin = first_ref[i] // size
    end = (base_ref[0] + (i + 1) * rows - 1) // size + 1
    d_query = unshuffled(lax.fori_loop(begin, end, step, jnp.zeros((rows, HD), f32)), True)
    d_query = (d_query * cos_ref[...] + pltpu.roll(d_query, HD // 2, 1) * sin_ref[...]) * HD ** (-0.5)
    dq_ref[...] = d_query.astype(bf16)

    @pl.when(i == pl.num_programs(0) - 1)
    def _():
        half = dkv_ref.shape[2] // 2

        def give(plane, carry):
            for p in range(G):
                dkv_ref[p, plane, :half] = d_keys[plane, p * half : (p + 1) * half].astype(bf16)
                dkv_ref[p, plane, half:] = d_values[plane, p * half : (p + 1) * half].astype(bf16)
            return carry

        lax.fori_loop(0, dkv_ref.shape[1], give, 0)


def ffn_units(part, second, low, w_ref):
    gate = mm(second, w_ref[:, :part], 1, 0)
    up = mm(second, w_ref[:, part : 2 * part], 1, 0)
    d_act = mm(low, w_ref[:, 2 * part :], 1, 0)
    s = sig(gate)
    silu = gate * s
    return jnp.concatenate(
        [(d_act * up * (s * (1.0 + gate * (1.0 - s)))).astype(bf16), (d_act * silu).astype(bf16), (silu * up).astype(bf16)],
        axis=1,
    )


def ffn_body(part, second_ref, low_ref, w_ref, *refs):
    *done, h_ref, layer_ref, back_ref = refs
    h = ffn_units(part, second_ref[...], low_ref[...], w_ref)
    h_ref[...] = h
    two = 2 * part
    layer = mm(h[:, two:], w_ref[:, two:], 1, 1)
    back = mm(h[:, :two], w_ref[:, :two], 1, 1)
    if done:
        layer = layer + done[0][...].astype(f32)
        back = back + done[1][...].astype(f32)
    layer_ref[...] = layer.astype(bf16)
    back_ref[...] = back.astype(bf16)


def ffn_grad_body(part, second_ref, low_ref, h_ref, out_ref, turned):
    two = 2 * part

    @pl.when(pl.program_id(0) == 0)
    def _():
        turned[...] = h_ref[...].T

    out_ref[:, :two] = mm(turned[:two], second_ref[...], 1, 0).astype(bf16).T
    out_ref[:, two:] = mm(turned[two:], low_ref[...], 1, 0).astype(bf16).T


def finish_body(chunks, chan, base_ref, pa_ref, gx_ref, rim_x, g_bc, rim_bc, dkv, starts_ref, taps_ref, cos_ref, sin_ref,
                out_ref, taps_out):
    c = pl.program_id(0)
    wide = chan + 128

    @pl.when(c == 0)
    def _():
        taps_out[...] = jnp.zeros_like(taps_out)

    rows = g_bc.shape[0]
    here_ = pl.ds(pl.multiple_of(c * CHUNK, CHUNK), CHUNK)
    last = c == chunks - 1
    ahead_at = jnp.minimum((c + 1) * CHUNK, (chunks - 1) * CHUNK)
    next_ = pl.ds(pl.multiple_of(ahead_at, CHUNK), CHUNK)

    def put(first):
        return (iota((rows, 128), 1) == iota((rows, 128), 0) + first).astype(f32)

    bc_here = mm_exact(g_bc[:, here_], put(0), 0, 0)
    bc_next = mm_exact(jnp.where(last, rim_bc[...], g_bc[:, next_]), put(0), 0, 0)[:8]
    gx_next = jnp.where(last, rim_x[:8], gx_ref[pl.ds(pl.multiple_of(ahead_at, 8), 8)])
    longer = jnp.concatenate([
        jnp.concatenate([gx_ref[here_], bc_here], axis=1), jnp.concatenate([gx_next, bc_next], axis=1)
    ], axis=0)
    starts = starts_ref[pl.ds(pl.multiple_of(c * CHUNK, 8), CHUNK + 8)]
    place = places_of(base_ref, c)
    block = pa_ref[pl.ds(pl.multiple_of(c * CHUNK + RIM - 8, 8), CHUNK + 8), :wide]
    total = jnp.zeros((CHUNK, wide), f32)
    for lag in range(K):
        ahead = K - 1 - lag
        seen = place >= starts[ahead : ahead + CHUNK]
        total = total + jnp.where(seen, longer[ahead : ahead + CHUNK], 0.0) * taps_ref[lag : lag + 1]
        valid = place - ahead >= starts[:CHUNK]
        part = jnp.where(valid, longer[:CHUNK] * block[8 - ahead : 8 - ahead + CHUNK], 0.0)
        taps_out[lag : lag + 1] += jnp.sum(part, axis=0, keepdims=True)
    quarter = cos_ref.shape[0]
    kv = dkv[:, here_]
    a, b = kv[:quarter], kv[quarter : 2 * quarter]
    cosine, sine = cos_ref[:, here_], sin_ref[:, here_]
    kv = jnp.concatenate([a * cosine + b * sine, b * cosine - a * sine, kv[2 * quarter :]], axis=0)
    out_ref[:, :chan] = total[:, :chan].astype(bf16)
    out_ref[:, chan:wide] = (total[:, chan:] + mm(kv, put(rows), 0, 0)).astype(bf16)


def prepare_body(chan, base_ref, pa_ref, starts_ref, taps_ref, cos_ref, sin_ref, bc_ref, slope_ref, kv_ref):
    c = pl.program_id(0)
    cv = conv_of(pa_ref, taps_ref, starts_ref[...], places_of(base_ref, c), c, 128, chan).T
    rows, quarter = bc_ref.shape[0], cos_ref.shape[0]
    cv = cv[:rows]
    s = sig(cv)
    bc_ref[...] = (cv * s).astype(bf16)
    slope_ref[...] = s * (1.0 + cv * (1.0 - s))
    kv = pa_ref[pl.ds(pl.multiple_of(c * CHUNK + RIM, 16), CHUNK), chan : chan + 128].T[rows:]
    a, b = kv[:quarter], kv[quarter : 2 * quarter]
    cosine, sine = cos_ref[...], sin_ref[...]
    kv_ref[:quarter] = (a * cosine - b * sine).astype(bf16)
    kv_ref[quarter : 2 * quarter] = (b * cosine + a * sine).astype(bf16)
    kv_ref[2 * quarter :] = kv[2 * quarter :].astype(bf16)


def back_part_body(da_ref, dz_ref, raw_ref, wa_ref, wz_ref, ws_ref, out_ref):
    total = mm(da_ref[...], wa_ref[...], 1, 1) + mm(dz_ref[...], wz_ref[...], 1, 1) + mm(raw_ref[...], ws_ref[...], 1, 0)
    out_ref[...] = total.astype(bf16)


def head_sums_t(v, heads):
    column = jnp.sum(v, axis=1, keepdims=True)
    pick = (iota((v.shape[0], 128), 0) // P_SIZE == iota((v.shape[0], 128), 1)).astype(f32)
    return jnp.sum(column * pick, axis=0, keepdims=True)


def chunked(body, chunks, outs, out_specs, ins, in_specs, scratch=(), mib=16, near=(), keep=()):
    ins = [
        pltpu.with_memory_space_constraint(v, pltpu.HBM) if s.memory_space is None and v.size > 20000 and i not in near else v
        for i, (v, s) in enumerate(zip(ins, in_specs))
    ]
    if isinstance(outs, tuple):
        outs = tuple(
            (pltpu.VMEM if i in keep else pltpu.HBM)(v.shape, v.dtype) if v.size > 20000 else v for i, v in enumerate(outs)
        )
    else:
        outs = (pltpu.VMEM if keep else pltpu.HBM)(outs.shape, outs.dtype)
    return pl.pallas_call(
        body,
        grid=(chunks,),
        out_shape=outs,
        in_specs=in_specs,
        out_specs=out_specs,
        scratch_shapes=list(scratch),
        cost_estimate=pl.CostEstimate(flops=2_000_000_000, bytes_accessed=40_000_000, transcendentals=0),
        compiler_params=pltpu.CompilerParams(vmem_limit_bytes=mib * 2**20),
    )(*ins)


def dot(a, b, ca, cb):
    return lax.dot_general(a, b, (((ca,), (cb,)), ((), ())), preferred_element_type=f32)


def exact(text, *operands):
    return jnp.einsum(text, *operands, precision=highest, preferred_element_type=f32)


def d_silu(v):
    s = jax.nn.sigmoid(v)
    return s * (1.0 + v * (1.0 - s))


def shifted(block, axis, distance):
    count = lax.axis_size(axis)
    route = [(i - distance, i) for i in range(count) if 0 <= i - distance < count]
    return lax.ppermute(block, axis, route)


def rope_tables(offsets, first, count):
    half = HD // 2
    index = (first + jnp.arange(count)).astype(f32)
    freqs = rope_base ** (-2.0 * index / HD)
    angles = offsets.astype(f32)[:, None] * freqs[None, :]
    return jnp.cos(angles), jnp.sin(angles)


def turn(v, cosine, sine):
    half = v.shape[-1] // 2
    a, b = v[:, :half], v[:, half:]
    return jnp.concatenate([a * cosine - b * sine, b * cosine + a * sine], axis=-1)


def conv_rows(padded, taps, starts, places):
    length = starts.shape[0]
    total = jnp.zeros((length, padded.shape[1]), f32)
    for lag in range(K):
        back = K - 1 - lag
        valid = (places - back >= starts)[:, None]
        total = total + jnp.where(valid, padded[RIM - back : RIM - back + length] * taps[lag][None, :], 0.0)
    return total


def mixer_row(v):
    return v.reshape(1, -1)


def on_device(
    layer_input, doc_start, mixer_gain, ffn_gain,
    z_weight, x_weight, bc_weight, dt_weight, q_weight, k_weight, v_weight,
    o_weight, out_weight, gate_weight, up_weight, down_weight,
    conv_inner, conv_state, decay_log, dt_bias, skip_coef, ssm_gain, cotangent,
):
    tokens, width = layer_input.shape
    rows = z_weight.shape[0]
    planes = lax.axis_size("z")
    cores = lax.axis_size("head")
    zi, pi, hi = (lax.axis_index(a) for a in ("z", "p", "head"))
    T = tokens * G
    total_tokens = T * planes
    offset = zi * T
    places = offset + jnp.arange(T, dtype=jnp.int32)
    own = tokens // cores
    heads = decay_log.shape[0] // G
    chan = heads * P_SIZE
    bcs = 2 * N // cores // G
    quarter_half = HD // 2 // G

    def my_slice(v, size, index, axis):
        return lax.dynamic_slice_in_dim(v, index * size, size, axis)

    taps_inner = my_slice(conv_inner, chan, pi, 1)
    taps_state = my_slice(conv_state, bcs, hi * G + pi, 1)
    rates = my_slice(decay_log, heads, pi, 0)
    bias = my_slice(dt_bias, heads, pi, 0)
    skip = my_slice(skip_coef, heads, pi, 0)
    gain_s = my_slice(ssm_gain, chan, pi, 0)

    def cut(w):
        return w.reshape(rows, G, -1)

    bc_mine = lax.dynamic_slice_in_dim(bc_weight, hi * (2 * N // cores), 2 * N // cores, 1)
    k_cut = jnp.moveaxis(k_weight.reshape(rows, 2, G, quarter_half), 2, 1).reshape(rows, G, -1)
    small_w = jnp.concatenate([cut(bc_mine), k_cut, cut(v_weight)], axis=2)
    small_w = jnp.moveaxis(small_w, 1, 0)
    a_cols = chan + 128
    own_steps = jnp.pad(dt_weight.T.reshape(G, heads, rows), ((0, 0), (0, 16 - heads), (0, 0)))

    def gather(w):
        return lax.all_gather(w, "z", axis=0, tiled=True)

    exchange_sems = lambda n: [DMA((3, n)), DMA((3, n)), DMA((n,))]
    wa = gather(call(
        exchange_a_body, 0, shape((G * rows, a_cols), bf16), HBM,
        (x_weight, small_w), [HBM] * 2, exchange_sems(2),
    ))

    def half(v):
        return lax.dynamic_slice_in_dim(v, hi * own, own, 0)

    x_own, cot_own = half(layer_input), half(cotangent)
    r1 = lax.rsqrt(jnp.mean(x_own * x_own, axis=-1, keepdims=True) + norm_eps)
    first_own = (x_own * r1 * mixer_gain).astype(bf16)
    wb = gather(call(
        exchange_b_body, 9, shape((G * rows, 2 * (chan + HD)), bf16), HBM,
        (z_weight, q_weight, out_weight, o_weight), [HBM] * 4, exchange_sems(4),
    ))
    first_rim, docs, steps = call(
        functools.partial(start_body, planes), 1,
        (shape((RIM + T, width), bf16), shape((planes, G, 8, tokens), jnp.int32), shape((planes, G, 16, rows), bf16)), (HBM,) * 3,
        (first_own, jnp.broadcast_to(doc_start[None], (8, tokens)), own_steps), [VMEM] * 3,
        [DMA(()), DMA(()), DMA((2, 3)), DMA((2, 3)), DMA((2, planes - 1)), DMA((2, planes - 1)), DMA((2,))] + Spread.sems, us=25,
    )
    w_step = jnp.pad(steps.transpose(2, 0, 1, 3).reshape(16, width), ((0, 112), (0, 0)))
    w_zqob = wb
    wz, wb = wb[:, : chan + HD], wb[:, chan + HD :]
    first = first_rim[RIM:]
    all_starts = docs[:, :, 0].reshape(-1)
    starts = lax.dynamic_slice_in_dim(all_starts, offset, T, 0)

    def line_sum(grad):
        return lax.psum_scatter(grad, "z", scatter_dimension=0, tiled=True)

    raw = dot(first, w_step, 1, 1)
    pa = dot(first_rim, wa, 1, 0)
    zq = dot(first, wz, 1, 0)
    offsets = places - starts
    cos_q, sin_q = rope_tables(offsets, 0, HD // 2)
    cos_row = jnp.concatenate([cos_q, cos_q], axis=1)
    sin_row = jnp.concatenate([sin_q, -sin_q], axis=1)
    cos_k, sin_k = (v.T for v in rope_tables(offsets, pi * quarter_half, quarter_half))
    kvr = 4 * quarter_half
    L = CHUNK
    nc = T // L
    base = jnp.full((1,), offset, jnp.int32)
    starts_col = starts[:, None]
    smem = pl.BlockSpec(memory_space=pltpu.SMEM)
    taps_pair = jnp.concatenate([taps_state, jnp.zeros((K, 128 - bcs), f32)], axis=1)
    along = lambda rows_: pl.BlockSpec((rows_, L), lambda c: (0, c))
    bc_low, slope_bc, kv_own = chunked(
        functools.partial(prepare_body, chan), nc,
        (shape((bcs, T), bf16), shape((bcs, T), f32), shape((kvr, T), bf16)), (along(bcs), along(bcs), along(kvr)),
        (base, pa, starts_col, taps_pair, cos_k, sin_k),
        [smem, pl.BlockSpec(pa.shape, lambda c: (0, 0)), pl.BlockSpec((L, 1), lambda c: (c, 0)), pl.BlockSpec((K, 128), lambda c: (0, 0)),
         along(quarter_half), along(quarter_half)],
    )
    line_sems = [DMA((planes - 1,)), DMA((planes - 1,))]
    units = gate_weight.shape[1] // G
    parts = (units - 128, 128)
    bc_t, kv_line, w1, w2 = call(
        functools.partial(spread_body, planes), 2,
        (shape((2 * N, T), bf16), shape((planes, kvr, T), bf16)) + tuple(shape((G * rows, 3 * n), bf16) for n in parts), (HBM,) * 4,
        (bc_low, kv_own, gate_weight, up_weight, down_weight), [HBM] * 5,
        line_sems + [DMA(())] + exchange_sems(6) + Spread.sems, us=28,
    )
    w1, w2 = gather(w1), gather(w2)
    bc_all = bc_t.T


    def row128(v):
        return jnp.pad(v, (0, 128 - v.shape[0]))[None]

    bias_row, rates_row = row128(bias), row128(rates)
    skip_row, gain_row = jnp.repeat(skip, P_SIZE)[None], gain_s[None]

    def specs(turned=False):
        at = (lambda c: nc - 1 - c) if turned else (lambda c: c)
        return (
            lambda cols: pl.BlockSpec((L, cols), lambda c: (at(c), 0)),
            lambda *dims: pl.BlockSpec(dims, lambda c: (0,) * len(dims)),
            lambda rows, cols: pl.BlockSpec((1, rows, cols), lambda c: (at(c), 0, 0)),
        )

    tile, fixed, stack = specs()
    pa_spec = fixed(*pa.shape)
    y_diag, cv_x, enter, reach, state, through = chunked(
        functools.partial(scan_body, heads), nc,
        (shape((T, chan), f32), shape((T, chan), f32), shape((nc, chan, N), f32), shape((nc, 16, 128), f32),
         shape((chan, N), bf16), shape((8, 128), f32)),
        (tile(chan), tile(chan), stack(chan, N), stack(16, 128), fixed(chan, N), fixed(8, 128)),
        (base, raw, pa, bc_all, starts_col, taps_inner, bias_row, rates_row),
        [smem, tile(128), pa_spec, tile(2 * N), tile(1), fixed(K, chan), fixed(1, 128), fixed(1, 128)],
        [pltpu.VMEM((chan, N), f32), pltpu.VMEM((8, 128), f32)],
    )

    def entering(upward, states, factors):
        total = jnp.zeros((chan, N), f32)
        for d in reversed(range(1, planes)):
            there = (zi - d >= 0) if upward else (zi + d < planes)
            factor = jnp.repeat(factors[d - 1, :heads, :1], P_SIZE, axis=0)
            total = jnp.where(there, total * factor + states[d - 1].astype(f32), total)
        return total

    state_shapes = (shape((planes - 1, chan, N), bf16), shape((planes - 1, 8, 128), f32))
    states, factors, kv_all, out_low = call(
        functools.partial(up_body, planes), 3, state_shapes + (shape((G * planes, kvr, T), bf16), shape((T, width), bf16)), (HBM,) * 4,
        (state, through, kv_line, cot_own.astype(bf16)), [HBM] * 4, line_sems * 2 + Spread.sems * 2, us=38,
    )
    before = entering(True, states, factors)
    ssm_low, y_scan = chunked(
        functools.partial(gate_body, heads), nc,
        (shape((T, chan), bf16), shape((T, chan), f32)), (tile(chan), tile(chan)),
        (base, raw, bc_all, starts_col, bias_row, rates_row, y_diag, cv_x, enter, reach, before, zq, skip_row, gain_row),
        [smem, tile(128), tile(2 * N), tile(1), fixed(1, 128), fixed(1, 128), tile(chan), tile(chan), stack(chan, N),
         stack(16, 128), fixed(chan, N), tile(chan), fixed(1, chan), fixed(1, chan)],
    )

    size = math.gcd(512, T)
    qrows = math.gcd(256, T)
    kv_all = kv_all.reshape(G, planes, kvr, T)
    firsts = starts.reshape(-1, qrows)[:, 0]

    def column(at, cols):
        return pl.BlockSpec((qrows, cols), lambda i: (i, at))

    kv_spec = pl.BlockSpec((G, planes, kvr, T), lambda i: (0, 0, 0, 0))
    at_q = chan // HD
    query, att_low, attended, log_mass = chunked(
        functools.partial(attend_body, size, T), T // qrows,
        (shape((T, HD), bf16), shape((T, HD), bf16), shape((T, HD), f32), shape((T, 1), f32)),
        (column(0, HD), column(0, HD), column(0, HD), column(0, 1)),
        (base, firsts, zq, starts_col, cos_row, sin_row, kv_all),
        [smem, smem, column(at_q, HD), column(0, 1), column(0, HD), column(0, HD), kv_spec], mib=12 + 2 * planes,
    )

    both_low = jnp.concatenate([ssm_low, att_low], axis=1)
    collect = Collect.scratch(own, width) + [pltpu.VMEM((own, width), bf16)] + Spread.sems
    hidden, second = call(
        hidden_body, 4, (shape((own, width), f32), shape((T, width), bf16)), (VMEM, HBM),
        (dot(both_low, wb, 1, 1).astype(bf16), x_own, mixer_row(ffn_gain)), [VMEM] * 3, collect, us=50,
    )
    ftile = math.gcd(256, T)

    def rows_spec(cols):
        return pl.BlockSpec((ftile, cols), lambda i: (i, 0))

    def all_spec(v):
        return pl.BlockSpec(v.shape, lambda i: (0,) * len(v.shape))

    def ffn(w, *done):
        wide = w.shape[1]
        return chunked(
            functools.partial(ffn_body, wide // 3), T // ftile,
            (shape((T, wide), bf16), shape((T, width), bf16), shape((T, width), bf16)),
            (rows_spec(wide), rows_spec(width), rows_spec(width)),
            (second, out_low, w) + done, [rows_spec(width), rows_spec(width), all_spec(w)] + [rows_spec(width)] * len(done), mib=36, keep=(1, 2) if done else (),
        )

    def ffn_grads(h):
        wide = h.shape[1]
        tile_d = math.gcd(256, width)
        columns = pl.BlockSpec((T, tile_d), lambda i: (0, i))
        return chunked(
            functools.partial(ffn_grad_body, wide // 3), width // tile_d, shape((width, wide), bf16),
            pl.BlockSpec((tile_d, wide), lambda i: (i, 0)), (second, out_low, h), [columns, columns, all_spec(h)],
            [pltpu.VMEM((wide, T), bf16)], mib=24,
        )

    h1, part_l, part_c = ffn(w1)
    grad_1 = ffn_grads(h1)
    w2, grad_1 = lax.optimization_barrier((w2, grad_1))
    sum_1 = line_sum(grad_1)
    h2, part_l, part_c = ffn(w2, part_l, part_c)
    d_hidden, grad_ffn, branch = call(
        branch_body, 5, (shape((own, width), f32), shape((8, width), f32), shape((T, width), bf16)), (VMEM, VMEM, HBM),
        (part_c, hidden, cot_own, mixer_row(ffn_gain)), [VMEM] * 4, collect, us=50,
    )
    h2, branch = lax.optimization_barrier((h2, branch))
    grad_2 = ffn_grads(h2)
    grad_2b = jnp.concatenate([grad_2, dot(branch, both_low, 0, 0).astype(bf16)], axis=1)
    d_both = dot(branch, wb, 1, 0)

    back, _, back_stack = specs(True)
    dz_low, dy, leave, tail, g_state, grad_gain_s = chunked(
        functools.partial(gate_back_body, heads, nc), nc,
        (shape((T, chan), bf16), shape((T, chan), f32), shape((nc, chan, N), f32), shape((nc, 8, 128), f32),
         shape((chan, N), bf16), shape((8, chan), f32)),
        (back(chan), back(chan), back_stack(chan, N), back_stack(8, 128), fixed(chan, N), fixed(8, chan)),
        (base, raw, bc_all, starts_col, bias_row, rates_row, d_both, y_scan, cv_x, reach, zq, skip_row, gain_row),
        [smem, back(128), back(2 * N), back(1), fixed(1, 128), fixed(1, 128), back(chan), back(chan), back(chan),
         back_stack(16, 128), back(chan), fixed(1, chan), fixed(1, chan)],
        [pltpu.VMEM((chan, N), f32), pltpu.VMEM((8, 128), f32)],
    )
    grad_2b, sum_1, dz_low = lax.optimization_barrier((grad_2b, sum_1, dz_low))
    sum_2 = line_sum(grad_2b)

    dq_low, dkv = chunked(
        functools.partial(attend_back_body, size, T), T // qrows,
        (shape((T, HD), bf16), shape((G, planes, kvr, T), bf16)), (column(0, HD), kv_spec),
        (base, firsts, query, starts_col, cos_row, sin_row, kv_all, d_both, attended, log_mass),
        [smem, smem, column(0, HD), column(0, 1), column(0, HD), column(0, HD), kv_spec, column(at_q, HD), column(0, HD),
         column(0, 1)],
        [pltpu.VMEM((planes, HD, T), f32), pltpu.VMEM((planes, HD, T), f32)], mib=14 + 3 * planes,
    )
    dzq_low = jnp.concatenate([dz_low, dq_low], axis=1)
    grad_z = dot(first, dzq_low, 0, 0).astype(bf16)
    g_state, sum_1, grad_z = lax.optimization_barrier((g_state, sum_1, grad_z))
    states, factors, dkv, layer_own = call(
        functools.partial(down_body, planes), 6, state_shapes + (shape((planes * kvr, T), bf16), shape((own, width), f32)),
        (HBM,) * 2 + (VMEM,) * 2, (g_state, through, dkv.reshape(-1, T), part_l, hidden), [HBM] * 2 + [VMEM] * 3,
        line_sems * 2 + Collect.scratch(planes * kvr, T, False) + Collect.scratch(own, width), us=45, mib=14 + 2 * planes,
    )
    states, grad_z = lax.optimization_barrier((states, grad_z))
    sum_z = line_sum(grad_z)
    after = entering(False, states, factors)
    gx, d_bc_all, d_raw, grad_rows = chunked(
        functools.partial(scan_back_body, heads), nc,
        (shape((T, chan), f32), shape((2 * N, T), bf16), shape((T, 128), bf16), shape((8, 128), f32)),
        (tile(chan), pl.BlockSpec((2 * N, L), lambda c: (0, c)), tile(128), fixed(8, 128)),
        (base, raw, bc_all, starts_col, bias_row, rates_row, dy, cv_x, enter, reach, before, leave, tail, after, skip_row),
        [smem, tile(128), tile(2 * N), tile(1), fixed(1, 128), fixed(1, 128), tile(chan), tile(chan),
         stack(chan, N), stack(16, 128), fixed(chan, N), stack(chan, N), stack(8, 128), fixed(chan, N), fixed(1, chan)],
    )

    d_bc_t, sum_2 = lax.optimization_barrier((d_bc_all, sum_2))
    g_bc, rim_bc, rim_x, dkv, got_1, got_2 = call(
        functools.partial(back_body, planes), 7,
        (shape((bcs, T), f32), shape((bcs, 128), f32), shape((RIM, chan), f32), shape((kvr, T), f32))
        + tuple(shape((G, rows, v.shape[1]), bf16) for v in (h1, h2)), (VMEM,) * 4 + (HBM,) * 2,
        (d_bc_t, dkv.reshape(planes, kvr, T), slope_bc, gx, sum_1, sum_2), [VMEM] * 3 + [HBM] * 3,
        [pltpu.VMEM((G * bcs, T), bf16), pltpu.VMEM((3, bcs, T), bf16), pltpu.VMEM((3, bcs, T), bf16),
         pltpu.VMEM((planes - 1, kvr, T), bf16), pltpu.VMEM((bcs, T), f32), DMA(()), DMA(()), DMA((3,)), DMA((3,)),
         DMA((planes - 1,)), DMA((planes - 1,)), DMA((2,)), DMA((2,)), DMA((2, 3)), DMA((2, 3)), DMA((2,))], us=30,
    )
    starts_long = jnp.concatenate([all_starts, jnp.full((8,), total_tokens, jnp.int32)])
    starts_long = lax.dynamic_slice_in_dim(starts_long, offset, T + 8, 0)[:, None]
    taps_both = jnp.concatenate([taps_inner, taps_pair], axis=1)
    da_low, grad_taps = chunked(
        functools.partial(finish_body, nc, chan), nc,
        (shape((T, a_cols), bf16), shape((8, chan + 128), f32)), (tile(a_cols), fixed(8, chan + 128)),
        (base, pa, gx, rim_x, g_bc, rim_bc, dkv, starts_long, taps_both, cos_k, sin_k),
        [smem, pa_spec, fixed(T, chan), fixed(RIM, chan), fixed(bcs, T), fixed(bcs, 128), fixed(kvr, T),
         fixed(T + 8, 1), fixed(K, chan + 128), fixed(quarter_half, T), fixed(quarter_half, T)], near=(3, 4, 5, 6),
    )
    grad_a = dot(first, da_low, 0, 0).astype(bf16)
    grad_a, sum_z = lax.optimization_barrier((grad_a, sum_z))
    sum_a = line_sum(grad_a)
    lane = width // 4
    part_a = chunked(
        back_part_body, T // ftile, shape((T, width), bf16), rows_spec(width), (da_low, dzq_low, d_raw, wa, w_zqob, w_step),
        [rows_spec(v.shape[1]) for v in (da_low, dzq_low, d_raw)] + [all_spec(v) for v in (wa, wz, w_step)], mib=28, keep=(0,),
    )
    grad_step = dot(d_raw, first, 0, 0)[:16].reshape(16, planes, G, rows).transpose(1, 2, 0, 3)
    groups = (shape((G, rows, chan + HD), bf16),) * 2
    grad_input, layer_out, mine, got_z, got_b = call(
        final_body, 8,
        (shape((tokens, width), f32), shape((tokens, width), f32), shape((RIM, lane), f32)) + groups, (HBM, HBM, VMEM, HBM, HBM),
        (part_a, x_own, d_hidden, layer_own, mixer_row(mixer_gain), grad_taps, grad_gain_s, grad_rows, grad_ffn, sum_z, sum_2),
        [VMEM] * 9 + [HBM] * 2,
        Collect.scratch(own, width)
        + [pltpu.VMEM((own, width), f32), pltpu.VMEM((8, width), f32), DMA((2,)), DMA((2,)), DMA((2,)),
           DMA((2, 3)), DMA((2, 3)), DMA((2,))], us=40,
    )

    got_x, got_s, sums, got_t = call(
        functools.partial(last_body, planes), 10,
        (shape((G, rows, chan), bf16), shape((2 * G, rows, a_cols - chan), bf16), shape((2 * G * RIM, lane), f32),
         shape((G, 16, rows), f32)), (HBM,) * 4, (sum_a, mine, grad_step), [HBM, VMEM, VMEM],
        [pltpu.VMEM((RIM, lane), f32), pltpu.VMEM((planes - 1, RIM, lane), f32), pltpu.VMEM((G, 16, rows), f32),
         pltpu.VMEM((planes - 1, G, 16, rows), f32), DMA((3,)), DMA((3,)), DMA((2 * G,)), DMA((2 * G,)),
         DMA((2,)), DMA((planes - 1,)), DMA((planes - 1,)), DMA((planes - 1,)), DMA((planes - 1,)), DMA((3,)), DMA((3,)), DMA(()),
         DMA((2 * G,)), DMA((2 * G,)), DMA(())],
    )
    strip = min(32, rows)

    def got(v):
        return pl.BlockSpec((v.shape[0], strip, v.shape[2]), lambda c: (0, c, 0))

    def given(cols):
        return pl.BlockSpec((strip, cols), lambda c: (c, 0))

    widths = [w.shape[1] for w in (
        z_weight, x_weight, bc_weight, q_weight, k_weight, v_weight, o_weight, out_weight,
        gate_weight, up_weight, down_weight,
    )]
    gathered = (got_z, got_b, got_1, got_2, got_x, got_s)
    steps_ = rows // strip
    moved = pl.BlockSpec((tokens // steps_, width), lambda c: (c, 0))
    *weights, layer_out, grad_input = chunked(
        functools.partial(give_body, (bcs, quarter_half)), steps_,
        tuple(shape((rows, w), f32) for w in widths) + (shape((tokens, width), f32),) * 2,
        tuple(given(w) for w in widths) + (moved, moved),
        (jnp.full((1,), hi, jnp.int32),) + gathered + (layer_out, grad_input), [smem] + [got(v) for v in gathered] + [moved, moved], mib=40,
    )
    weights.insert(3, got_t[:, :heads].reshape(G * heads, rows).T)

    sums = sums.reshape(G, cores, RIM, lane)
    mine = lax.dynamic_index_in_dim(sums, hi, 1, False)
    o_conv_inner = mine[:, :K, :chan].transpose(1, 0, 2).reshape(K, G * chan)
    o_conv_state = sums[:, :, :K, chan : chan + bcs].transpose(2, 1, 0, 3).reshape(K, 2 * N)
    per = width // (planes * G)
    gains = jnp.sum(sums[:, :, 8:], axis=(0, 1)).reshape(2, width)
    gains = lax.dynamic_slice_in_dim(gains, (zi * G + pi) * per, per, 1)

    return (
        layer_out, grad_input, gains[1], gains[0], *weights,
        o_conv_inner, o_conv_state,
        mine[:, 5, :heads].reshape(-1), mine[:, 5, 128 : 128 + heads].reshape(-1),
        mine[:, 5, 256 : 256 + heads].reshape(-1), mine[:, 4, :chan].reshape(-1),
    )


def solution(mesh):
    seq, cores = mesh.shape["seq"], mesh.shape["head"]
    planes = Mesh(mesh.devices.reshape(seq // G, G, cores), ("z", "p", "head"))
    s = ("z", "p")
    both, row, head, whole = P(s, "head"), P(s, None), P("head"), P()
    placed = (
        row, P(s), whole, whole, both, both, row, both, both, both, both, both, both, both, both, both,
        P(None, "head"), whole, head, head, head, head, row,
    )
    return jax.shard_map(
        on_device,
        mesh=planes,
        in_specs=placed,
        out_specs=(
            row, row, P(s), P(s), both, both, row, both, both, both, both, both, both, both, both, both,
            P(None, "head"), whole, head, head, head, head,
        ),
        check_vma=False,
    )
```

```python
import functools
import math

import jax
import jax.numpy as jnp
from jax import lax
from jax.experimental import pallas as pl
from jax.experimental.pallas import tpu as pltpu
from jax.sharding import Mesh, PartitionSpec as P

P_SIZE = 64
N = 256
HD = 128
K = 4
G = 4
CHUNK = 128
RIM = 16

highest = lax.Precision.HIGHEST
rope_base = 10000.0
norm_eps = 1e-05
bf16 = jnp.bfloat16
f32 = jnp.float32
MESH = pl.DeviceIdType.MESH
HBM = pl.BlockSpec(memory_space=pl.ANY)
VMEM = pl.BlockSpec(memory_space=pltpu.VMEM)
DMA = pltpu.SemaphoreType.DMA


def rcopy(src, dst, send, recv, **where):
    return pltpu.make_async_remote_copy(
        src_ref=src, dst_ref=dst, send_sem=send, recv_sem=recv, device_id=where, device_id_type=MESH
    )


def here():
    return lax.axis_index("z"), lax.axis_index("p"), lax.axis_index("head")


def ring(p, d):
    return lax.rem(p + d + G, G)


def greet(*partners):
    barrier = pltpu.get_barrier_semaphore()
    for where in partners:
        pl.semaphore_signal(barrier, inc=1, device_id=where, device_id_type=MESH)
    pl.semaphore_wait(barrier, len(partners))


def plane_partners(p, c):
    return [{"p": ring(p, d)} for d in range(1, G)] + [{"head": 1 - c}]


def line_partners(z, planes):
    return [{"z": lax.rem(z + d, planes)} for d in range(1, planes)]


def beside(p):
    return p + 1 - 2 * lax.rem(p, 2), lax.rem(p + 2, G), G - 1 - p


class Spread:
    sems = [DMA((2,)), DMA((2,)), DMA((2,)), DMA((2,)), DMA((4,)), DMA((4,)), DMA(())]

    def __init__(self, block, out, start, rows, sems, cores=True):
        self.block, self.out, self.first, self.rows, self.cores = block, out, start, rows, cores
        self.s1, self.r1, self.s2, self.r2, self.s3, self.r3, self.keep = sems
        _, self.p, self.c = here()
        self.around = beside(self.p)

    def spot(self, q, half=None):
        first, rows = self.first(q, self.c), self.rows
        if half is not None:
            first, rows = first + half * (rows // 2), rows // 2
        return self.out.at[pl.ds(first, rows)]

    def over(self, i):
        return rcopy(self.block, self.spot(self.p), self.s1.at[i], self.r1.at[i], p=self.around[i])

    def relay(self, i):
        spot = self.spot(self.around[i], i)
        return rcopy(spot, spot, self.s2.at[i], self.r2.at[i], p=self.around[1 - i])

    def relayed(self, i):
        spot = self.spot(self.around[2], 1 - i)
        return rcopy(spot, spot, self.s2.at[1 - i], self.r2.at[1 - i], p=self.around[i])

    def across(self, i):
        spot = self.spot(self.p if i == 3 else self.around[i])
        return rcopy(self.block if i == 3 else spot, spot, self.s3.at[i], self.r3.at[i], head=1 - self.c)

    def mine(self):
        return pltpu.make_async_copy(self.block, self.spot(self.p), self.keep)

    def start(self):
        for i in (0, 1):
            self.over(i).start()
        if self.cores:
            self.across(3).start()
        self.mine().start()

    def pass_on(self):
        for i in (0, 1):
            self.over(i).wait_recv()
            self.relay(i).start()
            if self.cores:
                self.across(i).start()
        for i in (0, 1):
            self.relayed(i).wait_recv()
        if self.cores:
            self.across(2).start()

    def finish(self):
        self.mine().wait()
        for i in (0, 1):
            self.over(i).wait_send()
            self.relay(i).wait_send()
        if self.cores:
            for i in range(4):
                self.across(i).wait()


class Collect:
    @staticmethod
    def scratch(rows, width, cores=True):
        return [
            pltpu.VMEM((4, rows, width) if cores else (1, 16, 128), bf16), pltpu.VMEM((3, rows, width), bf16),
            pltpu.VMEM((2, rows // 2, width), bf16), pltpu.VMEM((2, rows, width), bf16),
            pltpu.VMEM((rows, width), f32), DMA((4,)), DMA((4,)), DMA((6,)), DMA((6,)),
        ]

    def __init__(self, part, rows, scratch, strip=16, cores=True):
        self.part, self.rows, self.strip, self.cores = part, rows, strip, cores
        self.cx, self.out, self.rd, self.rx, self.total, self.s1, self.r1, self.s2, self.r2 = scratch
        _, self.p, self.c = here()
        self.around = beside(self.p)

    def first(self, q, c):
        return pl.multiple_of(((q * 2 + c) if self.cores else q) * self.rows, 16)

    def owner(self, i):
        return self.p if i == 3 else self.around[i]

    def across(self, i):
        spot = self.part.at[pl.ds(self.first(self.owner(i), 1 - self.c), self.rows)]
        return rcopy(spot, self.cx.at[i], self.s1.at[i], self.r1.at[i], head=1 - self.c)

    def over(self, i, half):
        at = pl.ds(half * (self.rows // 2), self.rows // 2)
        k = 2 * i + half
        if i == 2:
            return rcopy(self.out.at[2, at], self.rd.at[half], self.s2.at[k], self.r2.at[k], p=self.around[half])
        return rcopy(self.out.at[i, at], self.rx.at[i, at], self.s2.at[k], self.r2.at[k], p=self.around[i])

    def strips(self, body, lo=0, hi=None):
        hi = self.rows if hi is None else hi

        def one(n, carry):
            body(lo + n * self.strip)
            return carry

        lax.fori_loop(0, (hi - lo) // self.strip, one, 0)

    def at(self, first):
        return pl.ds(pl.multiple_of(first, self.strip), self.strip)

    def add(self, i, half=None, relayed=None):
        first = self.first(self.owner(i), self.c)
        size = self.rows // 2

        def one(at):
            v = self.part[self.at(first + at)].astype(f32)
            if self.cores:
                v = v + self.cx[i, self.at(at)].astype(f32)
            if relayed is not None:
                v = v + self.rd[relayed, self.at(at - half * size)].astype(f32)
            if i == 3:
                self.total[self.at(at)] = v
            else:
                self.out[i, self.at(at)] = v.astype(bf16)

        if half is None:
            self.strips(one)
        else:
            self.strips(one, half * size, (half + 1) * size)

    def start(self):
        if self.cores:
            for i in (2, 0, 1, 3):
                self.across(i).start()

    def crossed(self, i):
        if self.cores:
            self.across(i).wait_recv()

    def begin(self):
        self.crossed(2)
        for half in (0, 1):
            self.add(2, half)
            self.over(2, half).start()
        for i in (0, 1):
            self.crossed(i)
            self.add(i, i)
            self.over(i, i).start()
        self.crossed(3)
        self.add(3)

    def relay(self):
        for i in (0, 1):
            self.over(2, 1 - i).wait_recv()
            self.add(i, 1 - i, 1 - i)
            self.over(i, 1 - i).start()

    def middle(self):
        self.begin()
        self.relay()

    def arrive(self):
        for half in (0, 1):
            for i in (0, 1):
                self.over(i, i if half == 0 else 1 - i).wait_recv()

    def sum_of(self, at):
        r = self.at(at)
        return self.total[r] + self.rx[0, r].astype(f32) + self.rx[1, r].astype(f32)

    def finish(self):
        if self.cores:
            for i in range(4):
                self.across(i).wait_send()
        for i in range(3):
            for half in (0, 1):
                self.over(i, half).wait_send()


def call(body, name_id, outs, out_specs, ins, in_specs, scratch, us=20, mib=12):
    ins = [pltpu.with_memory_space_constraint(v, pltpu.HBM) if s is HBM and v.size > 20000 else v for v, s in zip(ins, in_specs)]
    if isinstance(outs, tuple):
        outs = tuple(pltpu.HBM(v.shape, v.dtype) if s is HBM else v for v, s in zip(outs, out_specs))
    elif out_specs is HBM:
        outs = pltpu.HBM(outs.shape, outs.dtype)
    return pl.pallas_call(
        body,
        out_shape=outs,
        in_specs=in_specs,
        out_specs=out_specs,
        scratch_shapes=scratch,
        cost_estimate=pl.CostEstimate(flops=0, bytes_accessed=us * 3_500_000, transcendentals=0),
        compiler_params=pltpu.CompilerParams(
            collective_id=name_id, has_side_effects=True, vmem_limit_bytes=mib * 2**20
        ),
    )(*ins)


def shape(dims, kind):
    return jax.ShapeDtypeStruct(dims, kind)


def exchange_copies(pieces, sems, keep):
    _, p, _ = here()
    away, own = [], []
    for i, (source, width, target, first, led, *part) in enumerate(pieces):
        whole, skip = part or (width, 0)
        rows = source.shape[-2]
        spot = target.at[pl.ds(pl.multiple_of(p * rows, 16), rows), pl.ds(first, width)]
        for d in range(G):
            q = ring(p, d)
            taken = source.at[q] if led else source.at[:, pl.ds(pl.multiple_of(q * whole + skip, 128), width)]
            if d:
                away.append(rcopy(taken, spot, sems[0].at[d - 1, i], sems[1].at[d - 1, i], p=q))
            else:
                own.append(pltpu.make_async_copy(taken, spot, keep.at[i]))
    return away, own


def exchange_a_body(x_ref, small_ref, out_ref, send, recv, keep):
    _, p, c = here()
    greet(*[{"p": ring(p, d)} for d in range(1, G)])
    xw = x_ref.shape[1] // G
    pieces = [(x_ref, xw, out_ref, 0, False), (small_ref, small_ref.shape[2], out_ref, xw, True)]
    away, own = exchange_copies(pieces, (send, recv), keep)
    for copy in away + own:
        copy.start()
    for copy in own + away:
        copy.wait()


def exchange_b_body(z_ref, q_ref, out_ref, o_ref, wb, send, recv, keep):
    _, p, c = here()
    greet(*[{"p": ring(p, d)} for d in range(1, G)])
    pieces, at = [], 0
    for ref in (z_ref, q_ref, out_ref, o_ref):
        pieces.append((ref, ref.shape[1] // G, wb, at, False))
        at += ref.shape[1] // G
    away, own = exchange_copies(pieces, (send, recv), keep)
    for copy in away + own:
        copy.start()
    for copy in own + away:
        copy.wait()


def start_body(planes, first, docs, steps, n1, all_docs, all_steps, *sems):
    z, p, c = here()
    greet(*plane_partners(p, c), *line_partners(z, planes))
    rim_s, rim_r, ps, pr, zs, zr, dk = sems[:7]
    rows = first.shape[0]
    a = Spread(first, n1, lambda q, k: pl.multiple_of(RIM + (q * 2 + k) * rows, 16), rows, sems[7:])
    near = [
        rcopy(have(ring(p, d)), every.at[z, p], ps.at[i, d - 1], pr.at[i, d - 1], p=ring(p, d))
        for i, (have, every) in enumerate(((lambda q: docs, all_docs), (lambda q: steps.at[q], all_steps))) for d in (1, 2, 3)
    ]
    own = [
        pltpu.make_async_copy(docs, all_docs.at[z, p], dk.at[0]), pltpu.make_async_copy(steps.at[p], all_steps.at[z, p], dk.at[1])
    ]
    a.start()
    for copy in near + own:
        copy.start()
    for copy in own + near:
        copy.wait()
    far = [
        rcopy(every.at[z], every.at[z], zs.at[i, d - 1], zr.at[i, d - 1], z=lax.rem(z + d, planes))
        for i, every in enumerate((all_docs, all_steps)) for d in range(1, planes)
    ]
    for copy in far:
        copy.start()
    a.pass_on()
    a.finish()
    last = n1.at[pl.ds(n1.shape[0] - RIM, RIM)]
    rim = rcopy(last, n1.at[pl.ds(0, RIM)], rim_s, rim_r, z=lax.rem(z + 1, planes))
    rim.start()
    for copy in far:
        copy.wait()
    rim.wait()


def spread_body(planes, block, kv, gate_w, up_w, down_w, out, lines, w1, w2, zs, zr, zk, send, recv, hold, *sems):
    z, p, c = here()
    greet(*plane_partners(p, c), *line_partners(z, planes))
    rows = block.shape[0]
    far = [rcopy(kv, lines.at[z], zs.at[d - 1], zr.at[d - 1], z=lax.rem(z + d, planes)) for d in range(1, planes)]
    keep = pltpu.make_async_copy(kv, lines.at[z], zk)
    for copy in far:
        copy.start()
    keep.start()
    s = Spread(block, out, lambda q, k: pl.multiple_of((k * G + q) * rows, 16), rows, sems)
    units = gate_w.shape[1] // G
    pieces = [
        (ref, part, to, i * part, False, units, skip)
        for to, part, skip in ((w1, w1.shape[1] // 3, 0), (w2, w2.shape[1] // 3, w1.shape[1] // 3))
        for i, ref in enumerate((gate_w, up_w, down_w))
    ]
    away, own = exchange_copies(pieces, (send, recv), hold)
    s.start()
    for copy in away + own:
        copy.start()
    s.pass_on()
    s.finish()
    for copy in own + away:
        copy.wait()
    keep.wait()
    for copy in far:
        copy.wait()


def state_copies(planes, upward, state, factor, states, factors, sems):
    z, _, _ = here()
    s1, r1, s2, r2 = sems
    way = 1 if upward else -1

    def pair(d):
        to = lax.rem(z + way * d + planes, planes)
        return (
            rcopy(state, states.at[d - 1], s1.at[d - 1], r1.at[d - 1], z=to),
            rcopy(factor, factors.at[d - 1], s2.at[d - 1], r2.at[d - 1], z=to),
        )

    def start():
        for d in range(1, planes):
            @pl.when((z + d < planes) if upward else (z - d >= 0))
            def _():
                for copy in pair(d):
                    copy.start()

    def wait():
        for d in range(1, planes):
            @pl.when((z - d >= 0) if upward else (z + d < planes))
            def _():
                for copy in pair(d):
                    copy.wait_recv()

            @pl.when((z + d < planes) if upward else (z - d >= 0))
            def _():
                for copy in pair(d):
                    copy.wait_send()

    return start, wait


def up_body(planes, state, factor, lines, low, states, factors, kv, ol, *sems):
    z, p, c = here()
    greet(*plane_partners(p, c), *line_partners(z, planes))
    start, wait = state_copies(planes, True, state, factor, states, factors, sems[:4])
    start()
    rows = low.shape[0]
    s = Spread(lines, kv, lambda q, k: q * planes, planes, sems[4:11], cores=False)
    b = Spread(low, ol, lambda q, k: pl.multiple_of((q * 2 + k) * rows, 16), rows, sems[11:18])
    s.start()
    b.start()
    s.pass_on()
    b.pass_on()
    s.finish()
    b.finish()
    wait()


def down_body(planes, state, factor, dkv, part, hidden, states, factors, kv, layer, *sems):
    z, p, c = here()
    greet(*plane_partners(p, c), *line_partners(z, planes))
    start, wait = state_copies(planes, False, state, factor, states, factors, sems[:4])
    start()
    k = Collect(dkv, kv.shape[0], sems[4:13], cores=False)
    s = Collect(part, hidden.shape[0], sems[13:])
    s.start()
    k.begin()
    s.begin()
    k.relay()
    s.relay()
    k.arrive()

    def sum_kv(at):
        kv[k.at(at)] = k.sum_of(at).astype(bf16)

    k.strips(sum_kv)
    s.arrive()

    def one(at):
        layer[s.at(at)] = hidden[s.at(at)] + s.sum_of(at)

    s.strips(one)
    k.finish()
    s.finish()
    wait()


def hidden_body(part, x_ref, gain, hidden, second, *scratch):
    _, p, c = here()
    greet(*plane_partners(p, c))
    rows = x_ref.shape[0]
    s = Collect(part, rows, scratch[:9])
    stage = scratch[9]
    s.start()
    s.middle()
    s.arrive()

    def one(at):
        r = s.at(at)
        h = x_ref[r] + s.sum_of(at)
        hidden[r] = h
        scale = lax.rsqrt(jnp.mean(h * h, axis=-1, keepdims=True) + norm_eps)
        stage[r] = (h * scale * gain[...]).astype(bf16)

    s.strips(one)
    g = Spread(stage, second, s.first, rows, scratch[10:17])
    g.start()
    g.pass_on()
    s.finish()
    g.finish()


def branch_body(part, hidden, cot, gain, d_hidden, gain_grad, branch, *scratch):
    _, p, c = here()
    greet(*plane_partners(p, c))
    rows = hidden.shape[0]
    s = Collect(part, rows, scratch[:9])
    stage = scratch[9]
    gain_grad[...] = jnp.zeros_like(gain_grad)
    s.start()
    s.middle()
    s.arrive()

    def one(at):
        r = s.at(at)
        h = hidden[r]
        scale = lax.rsqrt(jnp.mean(h * h, axis=-1, keepdims=True) + norm_eps)
        grad = s.sum_of(at)
        gain_grad[pl.ds(0, 1)] += jnp.sum(grad * h * scale, axis=0, keepdims=True)
        u = grad * gain[...]
        d = cot[r] + scale * u - h * (scale * scale * scale * jnp.mean(u * h, axis=-1, keepdims=True))
        d_hidden[r] = d
        stage[r] = d.astype(bf16)

    s.strips(one)
    g = Spread(stage, branch, s.first, rows, scratch[10:17])
    g.start()
    g.pass_on()
    s.finish()
    g.finish()


def final_body(part, x_ref, d_hidden, layer, gain, taps, norm, rows_ref, ffn, sum_z, sum_b, grad_in, layer_out, mine, got_z, got_b, *scratch):
    z, p, c = here()
    greet(*plane_partners(p, c))
    rows = x_ref.shape[0]
    s = Collect(part, rows, scratch[:9])
    stage, gain_row, es, er, ek, zs, zr, zk = scratch[9:]
    half = pl.ds(pl.multiple_of(c * rows, 16), rows)
    wide = got_z.shape[1]

    def halves(i, source, target):
        return (
            rcopy(source, target.at[half], es.at[i], er.at[i], head=1 - c),
            pltpu.make_async_copy(source, target.at[half], ek.at[i]),
        )

    def rows_of(v, q):
        cols = got_z.shape[2]
        return v.at[pl.ds(pl.multiple_of(q * wide, 16), wide), pl.ds(v.shape[1] - cols, cols)]

    s.start()
    first = halves(0, layer, layer_out)
    for copy in first:
        copy.start()
    lane = mine.shape[1]
    mine[...] = jnp.zeros_like(mine)
    mine[:K, : taps.shape[1]] = taps[:K]
    mine[4:5, : norm.shape[1]] = norm[:1]
    for j in range(3):
        mine[5:6, j * 128 : (j + 1) * 128] = rows_ref[j : j + 1]
    for j in range(4):
        mine[8 + j : 9 + j] = ffn[:1, j * lane : (j + 1) * lane]
    gain_row[...] = jnp.zeros_like(gain_row)
    s.middle()
    zb = []
    for i, (have, got) in enumerate(((sum_z, got_z), (sum_b, got_b))):
        for d in (1, 2, 3):
            zb.append(rcopy(rows_of(have, ring(p, d)), got.at[p], zs.at[i, d - 1], zr.at[i, d - 1], p=ring(p, d)))
        zb.append(pltpu.make_async_copy(rows_of(have, p), got.at[p], zk.at[i]))
    for copy in zb:
        copy.start()
    s.arrive()

    def one(at):
        r = s.at(at)
        v = x_ref[r]
        scale = lax.rsqrt(jnp.mean(v * v, axis=-1, keepdims=True) + norm_eps)
        grad = s.sum_of(at)
        gain_row[pl.ds(0, 1)] += jnp.sum(grad * v * scale, axis=0, keepdims=True)
        u = grad * gain[...]
        stage[r] = d_hidden[r] + scale * u - v * (scale * scale * scale * jnp.mean(u * v, axis=-1, keepdims=True))

    s.strips(one)
    second = halves(1, stage, grad_in)
    for copy in second:
        copy.start()
    for j in range(4):
        mine[12 + j : 13 + j] = gain_row[:1, j * lane : (j + 1) * lane]
    s.finish()
    for copy in first + second:
        copy.wait()
    for copy in zb:
        copy.wait()


def back_body(planes, dbc, dkv, d_silu_bc, gx, sum_1, sum_2, g_bc, rim_bc, rim_x, kv_out, got_1, got_2, *scratch):
    z, p, c = here()
    greet(*plane_partners(p, c), *line_partners(z, planes))
    (cx, bx, rbc, zkv, acc, xs, xr, bs, br, zs, zr, ms, mr, ws, wr, wk) = scratch
    rows = rbc.shape[1]
    across = rcopy(
        dbc.at[pl.ds(pl.multiple_of((1 - c) * G * rows, 16), G * rows)], cx, xs, xr, head=1 - c
    )
    across.start()
    grads = list(enumerate(((sum_1, got_1), (sum_2, got_2))))
    wide = got_1.shape[1]

    def rows_of(q):
        return pl.ds(pl.multiple_of(q * wide, 16), wide)

    w_over = [
        rcopy(have.at[rows_of(ring(p, d)), pl.ds(0, got.shape[2])], got.at[p], ws.at[i, d - 1], wr.at[i, d - 1], p=ring(p, d))
        for i, (have, got) in grads for d in (1, 2, 3)
    ]
    w_own = [
        pltpu.make_async_copy(have.at[rows_of(p), pl.ds(0, got.shape[2])], got.at[p], wk.at[i]) for i, (have, got) in grads
    ]
    for copy in w_over[3:] + w_own:
        copy.start()

    def kv_down(d):
        to = lax.rem(z - d + planes, planes)
        return rcopy(dkv.at[to], zkv.at[d - 1], zs.at[d - 1], zr.at[d - 1], z=to)

    for d in range(1, planes):
        @pl.when(z - d >= 0)
        def _():
            kv_down(d).start()

    across.wait_recv()
    bc_over = []
    for d in (1, 2, 3, 0):
        q = ring(p, d)
        own = dbc[pl.ds(pl.multiple_of((c * G + q) * rows, 16), rows)].astype(f32)
        own = own + cx[pl.ds(pl.multiple_of(q * rows, 16), rows)].astype(f32)
        if d:
            bx[d - 1] = own.astype(bf16)
            bc_over.append(rcopy(bx.at[d - 1], rbc.at[d - 1], bs.at[d - 1], br.at[d - 1], p=q))
            bc_over[-1].start()
        else:
            acc[...] = own
    for copy in w_over[:3]:
        copy.start()
    for copy in bc_over:
        copy.wait_recv()
    g = acc[...]
    for d in range(3):
        g = g + rbc[d].astype(f32)
    g_bc[...] = g * d_silu_bc[...]
    before = lax.rem(z - 1 + planes, planes)
    rims = [
        rcopy(g_bc.at[:, pl.ds(0, 128)], rim_bc, ms.at[0], mr.at[0], z=before),
        rcopy(gx.at[pl.ds(0, RIM)], rim_x, ms.at[1], mr.at[1], z=before),
    ]
    for copy in rims:
        copy.start()
    kv_out[...] = dkv[z].astype(f32)
    for d in range(1, planes):
        @pl.when(z + d < planes)
        def _():
            kv_down(d).wait_recv()
            kv_out[...] += zkv[d - 1].astype(f32)

        @pl.when(z - d >= 0)
        def _():
            kv_down(d).wait_send()

    for copy in rims:
        copy.wait()
    across.wait_send()
    for copy in bc_over:
        copy.wait_send()
    for copy in w_own + w_over:
        copy.wait()


def last_body(planes, sum_a, small, steps, got_x, got_s, sums, got_t, mine, others, t_own, t_far, xs, xr, ss, sr, keep, ls, lr,
              ts, tr, qs, qr, tk, gs, gr, gk):
    z, p, c = here()
    pairs = [(d, k) for k in (0, 1) for d in range(G) if d or k]
    greet(*[{"p": ring(p, d), "head": lax.rem(c + k, 2)} for d, k in pairs], *line_partners(z, planes))
    rows, chan = got_x.shape[1], got_x.shape[2]

    def part(q, first, cols):
        return sum_a.at[pl.ds(pl.multiple_of(q * rows, 16), rows), pl.ds(first, cols)]

    def narrow(d, k):
        cols, to = got_s.shape[2], got_s.at[c * G + p]
        i = k * G + d - 1
        return rcopy(part(ring(p, d), chan, cols), to, ss.at[i], sr.at[i], p=ring(p, d), head=lax.rem(c + k, 2))

    lines = [
        rcopy(small, others.at[d - 1], ls.at[d - 1], lr.at[d - 1], z=lax.rem(z + d, planes)) for d in range(1, planes)
    ] + [
        rcopy(steps.at[lax.rem(z + d, planes)], t_far.at[d - 1], ts.at[d - 1], tr.at[d - 1], z=lax.rem(z + d, planes))
        for d in range(1, planes)
    ]
    copies = [
        rcopy(part(ring(p, d), 0, chan), got_x.at[p], xs.at[d - 1], xr.at[d - 1], p=ring(p, d)) for d in (1, 2, 3)
    ] + [narrow(d, k) for d, k in pairs] + [
        pltpu.make_async_copy(part(p, 0, chan), got_x.at[p], keep.at[0]),
        pltpu.make_async_copy(part(p, chan, got_s.shape[2]), got_s.at[c * G + p], keep.at[1]),
    ]
    for copy in lines + copies:
        copy.start()
    for copy in lines:
        copy.wait()
    total = small[...]
    for d in range(1, planes):
        total = total + others[d - 1]
    mine[...] = total
    place = sums.at[pl.ds(pl.multiple_of((p * 2 + c) * RIM, RIM), RIM)]
    shares = [
        rcopy(mine, place, gs.at[k * G + d - 1], gr.at[k * G + d - 1], p=ring(p, d), head=lax.rem(c + k, 2)) for d, k in pairs
    ]
    shares.append(pltpu.make_async_copy(mine, place, gk))
    for copy in shares:
        copy.start()
    total = steps[z]
    for d in range(1, planes):
        total = total + t_far[d - 1]
    t_own[...] = total
    back = [rcopy(t_own.at[ring(p, d)], got_t.at[p], qs.at[d - 1], qr.at[d - 1], p=ring(p, d)) for d in (1, 2, 3)]
    back.append(pltpu.make_async_copy(t_own.at[p], got_t.at[p], tk))
    for copy in back:
        copy.start()
    for copy in copies + back + shares:
        copy.wait()


def give_ffn_body(f1, f2, *outs):
    units = (f1.shape[2] + f2.shape[2]) // 3
    for p in range(G):
        for i, ref in enumerate(outs):
            for got, skip in ((f1, 0), (f2, f1.shape[2] // 3)):
                part = got.shape[2] // 3
                at = p * units + skip
                ref[:, at : at + part] = got[p, :, i * part : (i + 1) * part].astype(f32)


def give_body(sizes, core_ref, zq, ob, x_, s_, layer, grad, z_o, x_o, bc_o, q_o, k_o, v_o, o_o, out_o, layer_o, grad_o):
    bcs, quarter = sizes
    layer_o[...] = layer[...]
    grad_o[...] = grad[...]
    chan = x_.shape[2]
    for p in range(G):
        for ref, got, first, cols in (
            (z_o, zq, 0, chan), (q_o, zq, chan, HD), (out_o, ob, 0, chan), (o_o, ob, chan, HD),
            (x_o, x_, 0, chan),
        ):
            ref[:, p * cols : (p + 1) * cols] = got[p, :, first : first + cols].astype(f32)

    def place(first, cols, target):
        i = iota((128, 128), 0) - first
        return ((i >= 0) & (i < cols) & (iota((128, 128), 1) == target(i))).astype(bf16)

    def bc_place(p):
        return (iota((128, 256), 0) + p * bcs == iota((128, 256), 1)).astype(bf16) * (iota((128, 256), 0) < bcs).astype(bf16)

    mine = core_ref[0]
    k_sum = v_sum = jnp.zeros((x_.shape[1], 128), f32)
    halves = []
    for k in (0, 1):
        total = jnp.zeros((x_.shape[1], 256), f32)
        for p in range(G):
            total = total + mm(s_[k * G + p], bc_place(p), 1, 0)
        halves.append(total)
    bc_o[:, :256] = halves[0]
    bc_o[:, 256:] = halves[1]
    for p in range(G):
        own = s_[mine * G + p]
        k_sum = k_sum + mm(own, place(bcs, 2 * quarter, lambda i: (i // quarter) * (quarter * G) + p * quarter + i % quarter), 1, 0)
        v_sum = v_sum + mm(own, place(bcs + 2 * quarter, 2 * quarter, lambda i: i + p * 2 * quarter), 1, 0)
    k_o[...] = k_sum
    v_o[...] = v_sum


def mm(a, b, ca, cb):
    return lax.dot_general(a.astype(bf16), b.astype(bf16), (((ca,), (cb,)), ((), ())), preferred_element_type=f32)


def mm_pieces(a, b, ca, cb, pieces, right=False):
    rest, total = (b if right else a), None
    for _ in range(pieces):
        piece = rest.astype(bf16)
        rest = rest - piece.astype(f32)
        part = mm(a, piece, ca, cb) if right else mm(piece, b, ca, cb)
        total = part if total is None else total + part
    return total


def iota(dims, axis):
    return lax.broadcasted_iota(jnp.int32, dims, axis)


def soft(v):
    return jnp.maximum(v, 0.0) + jnp.log1p(jnp.exp(-jnp.abs(v)))


def sig(v):
    return 1.0 / (1.0 + jnp.exp(-v))


def rates_of(raw, bias, rates, heads):
    lane = iota((CHUNK, 128), 1)
    step = jnp.where(lane < heads, soft(raw + bias), 0.0)
    log_decay = -jnp.exp(rates) * step
    lower = (iota((CHUNK, CHUNK), 0) >= iota((CHUNK, CHUNK), 1)).astype(f32)
    return step, log_decay, mm_pieces(lower, log_decay, 1, 0, 3, True)


def pair_of(v, pair):
    left = iota((CHUNK, 128), 1) < P_SIZE
    return jnp.where(left, v[:, 2 * pair : 2 * pair + 1], v[:, 2 * pair + 1 : 2 * pair + 2])


def lanes(v, pair):
    return v[:, pair * 128 : (pair + 1) * 128]


def halves_of(a, b):
    return jnp.where(iota(a.shape, 1) < P_SIZE, a, b)


def head_means(v):
    same = (iota((128, 128), 0) // P_SIZE == iota((128, 128), 1) // P_SIZE).astype(f32) / P_SIZE
    return jnp.concatenate([mm_pieces(lanes(v, k), same, 1, 0, 2) for k in range(v.shape[1] // 128)], axis=1)


def head_sums(v, heads):
    chan = v.shape[1]
    pick = (iota((chan, 128), 0) // P_SIZE == iota((chan, 128), 1)).astype(f32)
    return mm_pieces(v, pick, 1, 0, 3)


def scale_rows(v, factor, heads):
    return jnp.concatenate(
        [v[h * P_SIZE : (h + 1) * P_SIZE] * factor[h : h + 1, :1] for h in range(heads)], axis=0
    )


def conv_of(pa_ref, taps_ref, starts, place, c, chan, first):
    block = pa_ref[pl.ds(pl.multiple_of(c * CHUNK + RIM - 8, 8), CHUNK + 8), first : first + chan]
    total = jnp.zeros((CHUNK, chan), f32)
    for lag in range(K):
        back = K - 1 - lag
        total = total + jnp.where(place - back >= starts, block[8 - back : 8 - back + CHUNK] * taps_ref[lag : lag + 1], 0.0)
    return total


def places_of(base_ref, c):
    return base_ref[0] + c * CHUNK + iota((CHUNK, 1), 0)


def weights_of(h, cs, cs_t, visible):
    span = cs[:, h : h + 1] - cs_t[h : h + 1]
    return jnp.where(visible, jnp.exp(jnp.where(visible, span, 0.0)), 0.0)


def visible_of(base_ref, c, starts, place):
    across = base_ref[0] + c * CHUNK + iota((CHUNK, CHUNK), 1)
    return (starts <= across) & (across <= place)


def decays_of(cs, starts, place):
    first = place[:1]
    decay_in = jnp.where(starts < first, jnp.exp(cs), 0.0)
    closing = jnp.where(starts[CHUNK - 1 :] <= place, jnp.exp(cs[CHUNK - 1 :] - cs), 0.0)
    return decay_in, closing


def scan_body(heads, base_ref, raw_ref, pa_ref, bc_ref, starts_ref, taps_ref, bias_ref, rates_ref,
              y_ref, cv_ref, enter_ref, reach_ref, state_out, through_out, state, through):
    c = pl.program_id(0)
    chan = heads * P_SIZE

    @pl.when(c == 0)
    def _():
        state[...] = jnp.zeros_like(state)
        through[...] = jnp.ones_like(through)

    starts, place = starts_ref[...], places_of(base_ref, c)
    raw = raw_ref[...]
    step, _, cs = rates_of(raw, bias_ref[...], rates_ref[...], heads)
    cs_t = cs.T
    cv = conv_of(pa_ref, taps_ref, starts, place, c, chan, 0)
    cv_ref[...] = cv
    x = cv * sig(cv)
    b_rows, c_rows = bc_ref[:, :N], bc_ref[:, N:]
    inter = mm(c_rows, b_rows, 1, 1)
    visible = visible_of(base_ref, c, starts, place)
    decay_in, closing = decays_of(cs, starts, place)
    ends = decay_in.T
    for k in range(heads // 2):
        driven = lanes(x, k) * pair_of(step, k)
        mixed = [mm(weights_of(2 * k + i, cs, cs_t, visible) * inter, driven, 1, 0) for i in (0, 1)]
        y_ref[:, k * 128 : (k + 1) * 128] = halves_of(*mixed)
        local = mm(driven * pair_of(closing, k), b_rows, 0, 0)
        at = pl.ds(k * 128, 128)
        old = state[at]
        enter_ref[0, at] = old
        both = jnp.concatenate(
            [old[i * P_SIZE : (i + 1) * P_SIZE] * ends[2 * k + i : 2 * k + i + 1, CHUNK - 1 :] for i in (0, 1)], axis=0
        )
        state[at] = both + local
    factor = jnp.broadcast_to(ends[:8, CHUNK - 1 :], (8, 128))
    reach_ref[0, :8] = through[...]
    reach_ref[0, 8:] = factor
    through[...] = through[...] * factor
    state_out[...] = state[...].astype(bf16)
    through_out[...] = through[...]


def gate_parts(y_scan, cv, z, skip, gain):
    x = cv * sig(cv)
    ssm = y_scan + skip * x
    s = sig(z)
    gated = ssm * (z * s)
    r = lax.rsqrt(head_means(gated * gated) + norm_eps)
    return x, ssm, s, gated, r


def gate_body(heads, base_ref, raw_ref, bc_ref, starts_ref, bias_ref, rates_ref, y_ref, cv_ref, enter_ref, reach_ref,
              before_ref, z_ref, skip_ref, gain_ref, low_ref, scan_ref):
    c = pl.program_id(0)
    chan = heads * P_SIZE
    starts, place = starts_ref[...], places_of(base_ref, c)
    raw = raw_ref[...]
    _, _, cs = rates_of(raw, bias_ref[...], rates_ref[...], heads)
    decay_in, _ = decays_of(cs, starts, place)
    state_in = enter_ref[0] + scale_rows(before_ref[...], reach_ref[0], heads)
    c_rows = bc_ref[:, N:]
    off = [mm(c_rows, state_in[k * 128 : (k + 1) * 128], 1, 1) * pair_of(decay_in, k) for k in range(heads // 2)]
    y_scan = y_ref[...] + jnp.concatenate(off, axis=1)
    scan_ref[...] = y_scan
    _, _, _, gated, r = gate_parts(y_scan, cv_ref[...], z_ref[...], skip_ref[...], gain_ref[...])
    low_ref[...] = (gated * r * gain_ref[...]).astype(bf16)


def gate_back_body(heads, chunks, base_ref, raw_ref, bc_ref, starts_ref, bias_ref, rates_ref, d_ref, scan_ref, cv_ref,
                   reach_ref, z_ref, skip_ref, gain_ref, dz_ref, dy_ref, leave_ref, tail_ref, state_out, gain_out, state, tail):
    c = chunks - 1 - pl.program_id(0)
    chan = heads * P_SIZE

    @pl.when(c == chunks - 1)
    def _():
        state[...] = jnp.zeros_like(state)
        tail[...] = jnp.ones_like(tail)
        gain_out[...] = jnp.zeros_like(gain_out)

    starts, place = starts_ref[...], places_of(base_ref, c)
    raw = raw_ref[...]
    _, _, cs = rates_of(raw, bias_ref[...], rates_ref[...], heads)
    decay_in, _ = decays_of(cs, starts, place)
    z = z_ref[...]
    x, ssm, s, gated, r = gate_parts(scan_ref[...], cv_ref[...], z, skip_ref[...], gain_ref[...])
    d = d_ref[...]
    gain_out[:1] += jnp.sum(d * gated * r, axis=0, keepdims=True)
    u = d * gain_ref[...]
    d_gated = r * u - gated * (r * r * r * head_means(u * gated))
    dz_ref[...] = (d_gated * ssm * (s * (1.0 + z * (1.0 - s)))).astype(bf16)
    dy = d_gated * (z * s)
    dy_ref[...] = dy
    c_rows = bc_ref[:, N:]
    leave_ref[0] = state[...]
    tail_ref[0] = tail[...]
    factor = reach_ref[0, 8:]
    local = [mm(lanes(dy, k) * pair_of(decay_in, k), c_rows, 0, 0) for k in range(heads // 2)]
    state[...] = scale_rows(state[...], factor, heads) + jnp.concatenate(local, axis=0)
    tail[...] = tail[...] * factor
    state_out[...] = state[...].astype(bf16)


def scan_back_body(heads, base_ref, raw_ref, bc_ref, starts_ref, bias_ref, rates_ref, dy_ref, cv_ref,
                   enter_ref, reach_ref, before_ref, leave_ref, tail_ref, after_ref, skip_ref,
                   gx_ref, dbc_ref, raw_out, rows_out):
    c = pl.program_id(0)
    chan = heads * P_SIZE

    @pl.when(c == 0)
    def _():
        rows_out[...] = jnp.zeros_like(rows_out)

    starts, place = starts_ref[...], places_of(base_ref, c)
    raw = raw_ref[...]
    step, log_decay, cs = rates_of(raw, bias_ref[...], rates_ref[...], heads)
    cs_t = cs.T
    visible = visible_of(base_ref, c, starts, place)
    decay_in, closing = decays_of(cs, starts, place)
    b_rows, c_rows = bc_ref[:, :N], bc_ref[:, N:]
    inter = mm(c_rows, b_rows, 1, 1)
    cv = cv_ref[...]
    s = sig(cv)
    x = cv * s
    dy = dy_ref[...]
    state_in = enter_ref[0] + scale_rows(before_ref[...], reach_ref[0], heads)
    d_state = leave_ref[0] + scale_rows(after_ref[...], tail_ref[0], heads)
    left = iota((CHUNK, 128), 1) < P_SIZE
    d_inter = jnp.zeros((CHUNK, CHUNK), f32)
    d_b = jnp.zeros((CHUNK, N), f32)
    d_c = jnp.zeros((CHUNK, N), f32)
    inside, outside, closes, drives = [], [], [], []
    for k in range(heads // 2):
        at = slice(k * 128, (k + 1) * 128)
        driven = (lanes(x, k) * pair_of(step, k)).astype(bf16)
        dyk = lanes(dy, k)
        dyb = dyk.astype(bf16)
        d_mixed, y_mixed = [], []
        for i in (0, 1):
            w = weights_of(2 * k + i, cs, cs_t, visible)
            mix = (w * inter).astype(bf16)
            half = jnp.where(left if i == 0 else ~left, dyb, jnp.zeros_like(dyb))
            d_inter = d_inter + w * mm(half, driven, 1, 1)
            d_mixed.append(mm(mix, dyb, 0, 0))
            y_mixed.append(mm(mix, driven, 1, 0))
        d_mix = halves_of(*d_mixed)
        close = pair_of(closing, k)
        d_close = mm(b_rows, d_state[at], 1, 1)
        closed = driven.astype(f32) * close
        enter = pair_of(decay_in, k)
        y_off = mm(c_rows, state_in[at], 1, 1) * enter
        d_c = d_c + mm(dyk * enter, state_in[at], 1, 0)
        d_b = d_b + mm(closed, d_state[at], 1, 0)
        inside.append(dyb.astype(f32) * halves_of(*y_mixed) - driven.astype(f32) * d_mix)
        outside.append(dyk * y_off)
        closes.append(closed * d_close)
        drives.append(d_mix + close * d_close)
    d_c = d_c + mm(d_inter, b_rows, 1, 0)
    d_b = d_b + mm(d_inter, c_rows, 0, 0)
    dbc_ref[:N] = d_b.astype(bf16).T
    dbc_ref[N:] = d_c.astype(bf16).T
    d_driven = jnp.concatenate(drives, axis=1)
    closes = head_sums(jnp.concatenate(closes, axis=1), heads)
    d_cs = head_sums(jnp.concatenate(inside, axis=1) + jnp.concatenate(outside, axis=1), heads) - closes
    kept = head_sums_t(d_state * state_in, heads)
    whole = decay_in[CHUNK - 1 :] * kept + jnp.sum(closes, axis=0, keepdims=True)
    upper = (iota((CHUNK, CHUNK), 0) <= iota((CHUNK, CHUNK), 1)).astype(f32)
    d_la = mm_pieces(upper, d_cs, 1, 0, 3, True) + whole
    d_step = head_sums(d_driven * x, heads)
    d_raw = (d_step - jnp.exp(rates_ref[...]) * d_la) * sig(raw + bias_ref[...])
    d_raw = jnp.where(iota((CHUNK, 128), 1) < heads, d_raw, 0.0)
    raw_out[...] = d_raw.astype(bf16)
    rows_out[:1] += jnp.sum(d_la * log_decay, axis=0, keepdims=True)
    rows_out[1:2] += jnp.sum(d_raw, axis=0, keepdims=True)
    rows_out[2:3] += jnp.sum(head_sums(dy * x, heads), axis=0, keepdims=True)
    wide = jnp.concatenate([pair_of(step, k) for k in range(heads // 2)], axis=1)
    gx_ref[...] = (d_driven * wide + skip_ref[...] * dy) * (s * (1.0 + cv * (1.0 - s)))


def unshuffled(v, back=False):
    quarter = HD // 2 // G
    i, j = (iota((HD, HD), 1), iota((HD, HD), 0)) if back else (iota((HD, HD), 0), iota((HD, HD), 1))
    half, rest = i // (HD // 2), i % (HD // 2)
    to = (rest // quarter) * 2 * quarter + half * quarter + rest % quarter
    return mm_pieces(v, (to == j).astype(f32), 1, 0, 2 if back else 1)


def keys_of(kv_ref, begin, size, tokens):
    plane, at = begin // tokens, pl.ds(pl.multiple_of(begin % tokens, 128), size)
    half = kv_ref.shape[2] // 2
    keys = jnp.concatenate([kv_ref[p, plane, :half, at] for p in range(G)], axis=0)
    values = jnp.concatenate([kv_ref[p, plane, half:, at] for p in range(G)], axis=0)
    return plane, at, keys, values


def seen_of(begin, size, starts, place):
    at = begin + iota((starts.shape[0], size), 1)
    return (at >= starts) & (at <= place)


def attend_body(size, tokens, base_ref, first_ref, q_ref, starts_ref, cos_ref, sin_ref, kv_ref,
                query_ref, low_ref, out_ref, mass_ref):
    i = pl.program_id(0)
    rows = q_ref.shape[0]
    v = q_ref[...]
    turned = (v * cos_ref[...] - pltpu.roll(v, HD // 2, 1) * sin_ref[...]) * HD ** (-0.5)
    query = unshuffled(turned.astype(bf16).astype(f32)).astype(bf16)
    query_ref[...] = query
    starts = starts_ref[...]
    place = base_ref[0] + i * rows + iota((rows, 1), 0)

    def step(n, carry):
        peak, mass, total = carry
        begin = n * size
        _, _, keys, values = keys_of(kv_ref, begin, size, tokens)
        scores = jnp.where(seen_of(begin, size, starts, place), mm(query, keys, 1, 0), -1e30)
        new = jnp.maximum(peak, jnp.max(scores, axis=1, keepdims=True))
        probs = jnp.where(scores > -1e29, jnp.exp(scores - new), 0.0)
        keep = jnp.exp(peak - new)
        return new, mass * keep + jnp.sum(probs, axis=1, keepdims=True), total * keep + mm(probs, values, 1, 1)

    begin = first_ref[i] // size
    end = (base_ref[0] + (i + 1) * rows - 1) // size + 1
    start = (jnp.full((rows, 1), -1e30, f32), jnp.zeros((rows, 1), f32), jnp.zeros((rows, HD), f32))
    peak, mass, total = lax.fori_loop(begin, end, step, start)
    attended = total / mass
    out_ref[...] = attended
    low_ref[...] = attended.astype(bf16)
    mass_ref[...] = peak + jnp.log(mass)


def attend_back_body(size, tokens, base_ref, first_ref, query_ref, starts_ref, cos_ref, sin_ref, kv_ref, d_ref, out_ref, mass_ref,
                     dq_ref, dkv_ref, d_keys, d_values):
    i = pl.program_id(0)
    rows = query_ref.shape[0]

    @pl.when(i == 0)
    def _():
        d_keys[...] = jnp.zeros_like(d_keys)
        d_values[...] = jnp.zeros_like(d_values)

    query = query_ref[...]
    d_low = d_ref[...].astype(bf16)
    balance = jnp.sum(d_low.astype(f32) * out_ref[...], axis=1, keepdims=True)
    query_t, d_t = query.T, d_low.T
    starts, mass = starts_ref[...], mass_ref[...]
    place = base_ref[0] + i * rows + iota((rows, 1), 0)

    def step(n, total):
        begin = n * size
        plane, at, keys, values = keys_of(kv_ref, begin, size, tokens)
        seen = seen_of(begin, size, starts, place)
        probs = jnp.where(seen, jnp.exp(jnp.where(seen, mm(query, keys, 1, 0) - mass, 0.0)), 0.0)
        d_scores = (probs * (mm(d_low, values, 1, 0) - balance)).astype(bf16)
        d_keys[plane, :, at] += mm(query_t, d_scores, 1, 0)
        d_values[plane, :, at] += mm(d_t, probs, 1, 0)
        return total + mm(d_scores, keys, 1, 1)

    begin = first_ref[i] // size
    end = (base_ref[0] + (i + 1) * rows - 1) // size + 1
    d_query = unshuffled(lax.fori_loop(begin, end, step, jnp.zeros((rows, HD), f32)), True)
    d_query = (d_query * cos_ref[...] + pltpu.roll(d_query, HD // 2, 1) * sin_ref[...]) * HD ** (-0.5)
    dq_ref[...] = d_query.astype(bf16)

    @pl.when(i == pl.num_programs(0) - 1)
    def _():
        half = dkv_ref.shape[2] // 2

        def give(plane, carry):
            for p in range(G):
                dkv_ref[p, plane, :half] = d_keys[plane, p * half : (p + 1) * half].astype(bf16)
                dkv_ref[p, plane, half:] = d_values[plane, p * half : (p + 1) * half].astype(bf16)
            return carry

        lax.fori_loop(0, dkv_ref.shape[1], give, 0)


def ffn_units(part, second, low, w_ref):
    gate = mm(second, w_ref[:, :part], 1, 0)
    up = mm(second, w_ref[:, part : 2 * part], 1, 0)
    d_act = mm(low, w_ref[:, 2 * part :], 1, 0)
    s = sig(gate)
    silu = gate * s
    return jnp.concatenate(
        [(d_act * up * (s * (1.0 + gate * (1.0 - s)))).astype(bf16), (d_act * silu).astype(bf16), (silu * up).astype(bf16)],
        axis=1,
    )


def ffn_body(part, second_ref, low_ref, w_ref, *refs):
    *done, h_ref, layer_ref, back_ref = refs
    h = ffn_units(part, second_ref[...], low_ref[...], w_ref)
    h_ref[...] = h
    two = 2 * part
    layer = mm(h[:, two:], w_ref[:, two:], 1, 1)
    back = mm(h[:, :two], w_ref[:, :two], 1, 1)
    if done:
        layer = layer + done[0][...].astype(f32)
        back = back + done[1][...].astype(f32)
    layer_ref[...] = layer.astype(bf16)
    back_ref[...] = back.astype(bf16)


def token_grad_body(widths, *refs):
    count = len(widths)
    tokens, narrow, out_ref, turned = refs[:count], refs[count : 2 * count], refs[2 * count], refs[2 * count + 1]
    at = [sum(widths[:i]) for i in range(count)]

    @pl.when(pl.program_id(0) == 0)
    def _():
        for first, n, ref in zip(at, widths, narrow):
            turned[first : first + n] = ref[...].T

    for first, n, ref in zip(at, widths, tokens):
        rows = ref[ref.shape[0] - turned.shape[1] :]
        out_ref[:, first : first + n] = mm(turned[first : first + n], rows, 1, 0).astype(bf16).T


def finish_body(chunks, chan, base_ref, pa_ref, gx_ref, rim_x, g_bc, rim_bc, dkv, starts_ref, taps_ref, cos_ref, sin_ref,
                out_ref, taps_out):
    c = pl.program_id(0)
    wide = chan + 128

    @pl.when(c == 0)
    def _():
        taps_out[...] = jnp.zeros_like(taps_out)

    rows = g_bc.shape[0]
    here_ = pl.ds(pl.multiple_of(c * CHUNK, CHUNK), CHUNK)
    last = c == chunks - 1
    ahead_at = jnp.minimum((c + 1) * CHUNK, (chunks - 1) * CHUNK)
    next_ = pl.ds(pl.multiple_of(ahead_at, CHUNK), CHUNK)

    def put(first):
        return (iota((rows, 128), 1) == iota((rows, 128), 0) + first).astype(f32)

    bc_here = mm_pieces(g_bc[:, here_], put(0), 0, 0, 3)
    bc_next = mm_pieces(jnp.where(last, rim_bc[...], g_bc[:, next_]), put(0), 0, 0, 3)[:8]
    gx_next = jnp.where(last, rim_x[:8], gx_ref[pl.ds(pl.multiple_of(ahead_at, 8), 8)])
    longer = jnp.concatenate([
        jnp.concatenate([gx_ref[here_], bc_here], axis=1), jnp.concatenate([gx_next, bc_next], axis=1)
    ], axis=0)
    starts = starts_ref[pl.ds(pl.multiple_of(c * CHUNK, 8), CHUNK + 8)]
    place = places_of(base_ref, c)
    block = pa_ref[pl.ds(pl.multiple_of(c * CHUNK + RIM - 8, 8), CHUNK + 8), :wide]
    total = jnp.zeros((CHUNK, wide), f32)
    for lag in range(K):
        ahead = K - 1 - lag
        seen = place >= starts[ahead : ahead + CHUNK]
        total = total + jnp.where(seen, longer[ahead : ahead + CHUNK], 0.0) * taps_ref[lag : lag + 1]
        valid = place - ahead >= starts[:CHUNK]
        part = jnp.where(valid, longer[:CHUNK] * block[8 - ahead : 8 - ahead + CHUNK], 0.0)
        taps_out[lag : lag + 1] += jnp.sum(part, axis=0, keepdims=True)
    quarter = cos_ref.shape[0]
    kv = dkv[:, here_]
    a, b = kv[:quarter], kv[quarter : 2 * quarter]
    cosine, sine = cos_ref[:, here_], sin_ref[:, here_]
    kv = jnp.concatenate([a * cosine + b * sine, b * cosine - a * sine, kv[2 * quarter :]], axis=0)
    out_ref[:, :chan] = total[:, :chan].astype(bf16)
    out_ref[:, chan:wide] = (total[:, chan:] + mm(kv, put(rows), 0, 0)).astype(bf16)


def prepare_body(chan, base_ref, pa_ref, starts_ref, taps_ref, cos_ref, sin_ref, bc_ref, slope_ref, kv_ref):
    c = pl.program_id(0)
    cv = conv_of(pa_ref, taps_ref, starts_ref[...], places_of(base_ref, c), c, 128, chan).T
    rows, quarter = bc_ref.shape[0], cos_ref.shape[0]
    cv = cv[:rows]
    s = sig(cv)
    bc_ref[...] = (cv * s).astype(bf16)
    slope_ref[...] = s * (1.0 + cv * (1.0 - s))
    kv = pa_ref[pl.ds(pl.multiple_of(c * CHUNK + RIM, 16), CHUNK), chan : chan + 128].T[rows:]
    a, b = kv[:quarter], kv[quarter : 2 * quarter]
    cosine, sine = cos_ref[...], sin_ref[...]
    kv_ref[:quarter] = (a * cosine - b * sine).astype(bf16)
    kv_ref[quarter : 2 * quarter] = (b * cosine + a * sine).astype(bf16)
    kv_ref[2 * quarter :] = kv[2 * quarter :].astype(bf16)


def back_part_body(da_ref, dz_ref, raw_ref, wa_ref, wz_ref, ws_ref, out_ref):
    total = mm(da_ref[...], wa_ref[...], 1, 1) + mm(dz_ref[...], wz_ref[...], 1, 1) + mm(raw_ref[...], ws_ref[...], 1, 0)
    out_ref[...] = total.astype(bf16)


def head_sums_t(v, heads):
    column = jnp.sum(v, axis=1, keepdims=True)
    pick = (iota((v.shape[0], 128), 0) // P_SIZE == iota((v.shape[0], 128), 1)).astype(f32)
    return jnp.sum(column * pick, axis=0, keepdims=True)


def chunked(body, chunks, outs, out_specs, ins, in_specs, scratch=(), mib=16, near=(), keep=()):
    ins = [
        pltpu.with_memory_space_constraint(v, pltpu.HBM) if s.memory_space is None and v.size > 20000 and i not in near else v
        for i, (v, s) in enumerate(zip(ins, in_specs))
    ]
    if isinstance(outs, tuple):
        outs = tuple(
            (pltpu.VMEM if i in keep else pltpu.HBM)(v.shape, v.dtype) if v.size > 20000 else v for i, v in enumerate(outs)
        )
    else:
        outs = (pltpu.VMEM if keep else pltpu.HBM)(outs.shape, outs.dtype)
    return pl.pallas_call(
        body,
        grid=(chunks,),
        out_shape=outs,
        in_specs=in_specs,
        out_specs=out_specs,
        scratch_shapes=list(scratch),
        cost_estimate=pl.CostEstimate(flops=2_000_000_000, bytes_accessed=40_000_000, transcendentals=0),
        compiler_params=pltpu.CompilerParams(vmem_limit_bytes=mib * 2**20),
    )(*ins)


def dot(a, b, ca, cb):
    return lax.dot_general(a, b, (((ca,), (cb,)), ((), ())), preferred_element_type=f32)


def exact(text, *operands):
    return jnp.einsum(text, *operands, precision=highest, preferred_element_type=f32)


def d_silu(v):
    s = jax.nn.sigmoid(v)
    return s * (1.0 + v * (1.0 - s))


def shifted(block, axis, distance):
    count = lax.axis_size(axis)
    route = [(i - distance, i) for i in range(count) if 0 <= i - distance < count]
    return lax.ppermute(block, axis, route)


def rope_tables(offsets, first, count):
    half = HD // 2
    index = (first + jnp.arange(count)).astype(f32)
    freqs = rope_base ** (-2.0 * index / HD)
    angles = offsets.astype(f32)[:, None] * freqs[None, :]
    return jnp.cos(angles), jnp.sin(angles)


def turn(v, cosine, sine):
    half = v.shape[-1] // 2
    a, b = v[:, :half], v[:, half:]
    return jnp.concatenate([a * cosine - b * sine, b * cosine + a * sine], axis=-1)


def conv_rows(padded, taps, starts, places):
    length = starts.shape[0]
    total = jnp.zeros((length, padded.shape[1]), f32)
    for lag in range(K):
        back = K - 1 - lag
        valid = (places - back >= starts)[:, None]
        total = total + jnp.where(valid, padded[RIM - back : RIM - back + length] * taps[lag][None, :], 0.0)
    return total


def mixer_row(v):
    return v.reshape(1, -1)


def on_device(
    layer_input, doc_start, mixer_gain, ffn_gain,
    z_weight, x_weight, bc_weight, dt_weight, q_weight, k_weight, v_weight,
    o_weight, out_weight, gate_weight, up_weight, down_weight,
    conv_inner, conv_state, decay_log, dt_bias, skip_coef, ssm_gain, cotangent,
):
    tokens, width = layer_input.shape
    rows = z_weight.shape[0]
    planes = lax.axis_size("z")
    cores = lax.axis_size("head")
    zi, pi, hi = (lax.axis_index(a) for a in ("z", "p", "head"))
    T = tokens * G
    total_tokens = T * planes
    offset = zi * T
    places = offset + jnp.arange(T, dtype=jnp.int32)
    own = tokens // cores
    heads = decay_log.shape[0] // G
    chan = heads * P_SIZE
    bcs = 2 * N // cores // G
    quarter_half = HD // 2 // G

    def my_slice(v, size, index, axis):
        return lax.dynamic_slice_in_dim(v, index * size, size, axis)

    taps_inner = my_slice(conv_inner, chan, pi, 1)
    taps_state = my_slice(conv_state, bcs, hi * G + pi, 1)
    rates = my_slice(decay_log, heads, pi, 0)
    bias = my_slice(dt_bias, heads, pi, 0)
    skip = my_slice(skip_coef, heads, pi, 0)
    gain_s = my_slice(ssm_gain, chan, pi, 0)

    def cut(w):
        return w.reshape(rows, G, -1)

    bc_mine = lax.dynamic_slice_in_dim(bc_weight, hi * (2 * N // cores), 2 * N // cores, 1)
    k_cut = jnp.moveaxis(k_weight.reshape(rows, 2, G, quarter_half), 2, 1).reshape(rows, G, -1)
    small_w = jnp.concatenate([cut(bc_mine), k_cut, cut(v_weight)], axis=2)
    small_w = jnp.moveaxis(small_w, 1, 0)
    a_cols = chan + 128
    own_steps = jnp.pad(dt_weight.T.reshape(G, heads, rows), ((0, 0), (0, 16 - heads), (0, 0)))

    def gather(w):
        return lax.all_gather(w, "z", axis=0, tiled=True)

    exchange_sems = lambda n: [DMA((3, n)), DMA((3, n)), DMA((n,))]
    wa = gather(call(
        exchange_a_body, 0, shape((G * rows, a_cols), bf16), HBM,
        (x_weight, small_w), [HBM] * 2, exchange_sems(2),
    ))

    def half(v):
        return lax.dynamic_slice_in_dim(v, hi * own, own, 0)

    x_own, cot_own = half(layer_input), half(cotangent)
    r1 = lax.rsqrt(jnp.mean(x_own * x_own, axis=-1, keepdims=True) + norm_eps)
    first_own = (x_own * r1 * mixer_gain).astype(bf16)
    wb = gather(call(
        exchange_b_body, 9, shape((G * rows, 2 * (chan + HD)), bf16), HBM,
        (z_weight, q_weight, out_weight, o_weight), [HBM] * 4, exchange_sems(4),
    ))
    first_rim, docs, steps = call(
        functools.partial(start_body, planes), 1,
        (shape((RIM + T, width), bf16), shape((planes, G, 8, tokens), jnp.int32), shape((planes, G, 16, rows), bf16)), (HBM,) * 3,
        (first_own, jnp.broadcast_to(doc_start[None], (8, tokens)), own_steps), [VMEM] * 3,
        [DMA(()), DMA(()), DMA((2, 3)), DMA((2, 3)), DMA((2, planes - 1)), DMA((2, planes - 1)), DMA((2,))] + Spread.sems, us=25,
    )
    w_step = jnp.pad(steps.transpose(2, 0, 1, 3).reshape(16, width), ((0, 112), (0, 0)))
    w_zqob = wb
    wz, wb = wb[:, : chan + HD], wb[:, chan + HD :]
    first = first_rim[RIM:]
    all_starts = docs[:, :, 0].reshape(-1)
    starts = lax.dynamic_slice_in_dim(all_starts, offset, T, 0)

    def line_sum(grad):
        return lax.psum_scatter(grad, "z", scatter_dimension=0, tiled=True)

    raw = dot(first, w_step, 1, 1)
    pa = dot(first_rim, wa, 1, 0)
    zq = dot(first, wz, 1, 0)
    offsets = places - starts
    cos_q, sin_q = rope_tables(offsets, 0, HD // 2)
    cos_row = jnp.concatenate([cos_q, cos_q], axis=1)
    sin_row = jnp.concatenate([sin_q, -sin_q], axis=1)
    cos_k, sin_k = (v.T for v in rope_tables(offsets, pi * quarter_half, quarter_half))
    kvr = 4 * quarter_half
    L = CHUNK
    nc = T // L
    base = jnp.full((1,), offset, jnp.int32)
    starts_col = starts[:, None]
    smem = pl.BlockSpec(memory_space=pltpu.SMEM)
    taps_pair = jnp.concatenate([taps_state, jnp.zeros((K, 128 - bcs), f32)], axis=1)
    along = lambda rows_: pl.BlockSpec((rows_, L), lambda c: (0, c))
    bc_low, slope_bc, kv_own = chunked(
        functools.partial(prepare_body, chan), nc,
        (shape((bcs, T), bf16), shape((bcs, T), f32), shape((kvr, T), bf16)), (along(bcs), along(bcs), along(kvr)),
        (base, pa, starts_col, taps_pair, cos_k, sin_k),
        [smem, pl.BlockSpec(pa.shape, lambda c: (0, 0)), pl.BlockSpec((L, 1), lambda c: (c, 0)), pl.BlockSpec((K, 128), lambda c: (0, 0)),
         along(quarter_half), along(quarter_half)],
    )
    line_sems = [DMA((planes - 1,)), DMA((planes - 1,))]
    units = gate_weight.shape[1] // G
    parts = (units - 128, 128)
    bc_t, kv_line, w1, w2 = call(
        functools.partial(spread_body, planes), 2,
        (shape((2 * N, T), bf16), shape((planes, kvr, T), bf16)) + tuple(shape((G * rows, 3 * n), bf16) for n in parts), (HBM,) * 4,
        (bc_low, kv_own, gate_weight, up_weight, down_weight), [HBM] * 5,
        line_sems + [DMA(())] + exchange_sems(6) + Spread.sems, us=28,
    )
    w1, w2 = gather(w1), gather(w2)
    bc_all = bc_t.T


    def row128(v):
        return jnp.pad(v, (0, 128 - v.shape[0]))[None]

    bias_row, rates_row = row128(bias), row128(rates)
    skip_row, gain_row = jnp.repeat(skip, P_SIZE)[None], gain_s[None]

    def specs(turned=False):
        at = (lambda c: nc - 1 - c) if turned else (lambda c: c)
        return (
            lambda cols: pl.BlockSpec((L, cols), lambda c: (at(c), 0)),
            lambda *dims: pl.BlockSpec(dims, lambda c: (0,) * len(dims)),
            lambda rows, cols: pl.BlockSpec((1, rows, cols), lambda c: (at(c), 0, 0)),
        )

    tile, fixed, stack = specs()
    pa_spec = fixed(*pa.shape)
    y_diag, cv_x, enter, reach, state, through = chunked(
        functools.partial(scan_body, heads), nc,
        (shape((T, chan), f32), shape((T, chan), f32), shape((nc, chan, N), f32), shape((nc, 16, 128), f32),
         shape((chan, N), bf16), shape((8, 128), f32)),
        (tile(chan), tile(chan), stack(chan, N), stack(16, 128), fixed(chan, N), fixed(8, 128)),
        (base, raw, pa, bc_all, starts_col, taps_inner, bias_row, rates_row),
        [smem, tile(128), pa_spec, tile(2 * N), tile(1), fixed(K, chan), fixed(1, 128), fixed(1, 128)],
        [pltpu.VMEM((chan, N), f32), pltpu.VMEM((8, 128), f32)],
    )

    def entering(upward, states, factors):
        total = jnp.zeros((chan, N), f32)
        for d in reversed(range(1, planes)):
            there = (zi - d >= 0) if upward else (zi + d < planes)
            factor = jnp.repeat(factors[d - 1, :heads, :1], P_SIZE, axis=0)
            total = jnp.where(there, total * factor + states[d - 1].astype(f32), total)
        return total

    state_shapes = (shape((planes - 1, chan, N), bf16), shape((planes - 1, 8, 128), f32))
    states, factors, kv_all, out_low = call(
        functools.partial(up_body, planes), 3, state_shapes + (shape((G * planes, kvr, T), bf16), shape((T, width), bf16)), (HBM,) * 4,
        (state, through, kv_line, cot_own.astype(bf16)), [HBM] * 4, line_sems * 2 + Spread.sems * 2, us=38,
    )
    before = entering(True, states, factors)
    ssm_low, y_scan = chunked(
        functools.partial(gate_body, heads), nc,
        (shape((T, chan), bf16), shape((T, chan), f32)), (tile(chan), tile(chan)),
        (base, raw, bc_all, starts_col, bias_row, rates_row, y_diag, cv_x, enter, reach, before, zq, skip_row, gain_row),
        [smem, tile(128), tile(2 * N), tile(1), fixed(1, 128), fixed(1, 128), tile(chan), tile(chan), stack(chan, N),
         stack(16, 128), fixed(chan, N), tile(chan), fixed(1, chan), fixed(1, chan)],
    )

    size = math.gcd(512, T)
    qrows = math.gcd(256, T)
    kv_all = kv_all.reshape(G, planes, kvr, T)
    firsts = starts.reshape(-1, qrows)[:, 0]

    def column(at, cols):
        return pl.BlockSpec((qrows, cols), lambda i: (i, at))

    kv_spec = pl.BlockSpec((G, planes, kvr, T), lambda i: (0, 0, 0, 0))
    at_q = chan // HD
    query, att_low, attended, log_mass = chunked(
        functools.partial(attend_body, size, T), T // qrows,
        (shape((T, HD), bf16), shape((T, HD), bf16), shape((T, HD), f32), shape((T, 1), f32)),
        (column(0, HD), column(0, HD), column(0, HD), column(0, 1)),
        (base, firsts, zq, starts_col, cos_row, sin_row, kv_all),
        [smem, smem, column(at_q, HD), column(0, 1), column(0, HD), column(0, HD), kv_spec], mib=12 + 2 * planes,
    )

    both_low = jnp.concatenate([ssm_low, att_low], axis=1)
    collect = Collect.scratch(own, width) + [pltpu.VMEM((own, width), bf16)] + Spread.sems
    hidden, second = call(
        hidden_body, 4, (shape((own, width), f32), shape((T, width), bf16)), (VMEM, HBM),
        (dot(both_low, wb, 1, 1).astype(bf16), x_own, mixer_row(ffn_gain)), [VMEM] * 3, collect, us=50,
    )
    ftile = math.gcd(256, T)

    def rows_spec(cols):
        return pl.BlockSpec((ftile, cols), lambda i: (i, 0))

    def all_spec(v):
        return pl.BlockSpec(v.shape, lambda i: (0,) * len(v.shape))

    def ffn(w, *done):
        wide = w.shape[1]
        return chunked(
            functools.partial(ffn_body, wide // 3), T // ftile,
            (shape((T, wide), bf16), shape((T, width), bf16), shape((T, width), bf16)),
            (rows_spec(wide), rows_spec(width), rows_spec(width)),
            (second, out_low, w) + done, [rows_spec(width), rows_spec(width), all_spec(w)] + [rows_spec(width)] * len(done), mib=36, keep=(1, 2) if done else (),
        )

    def token_grads(*groups):
        tile_d = math.gcd(512, width)
        widths = tuple(n for *_, n in groups)
        return chunked(
            functools.partial(token_grad_body, widths), width // tile_d, shape((width, sum(widths)), bf16),
            pl.BlockSpec((tile_d, sum(widths)), lambda i: (i, 0)),
            tuple(g[0] for g in groups) + tuple(g[1] for g in groups),
            [pl.BlockSpec((g[0].shape[0], tile_d), lambda i: (0, i)) for g in groups]
            + [pl.BlockSpec((T, n), lambda i, at=at: (0, at)) for _, _, at, n in groups],
            [pltpu.VMEM((sum(widths), T), bf16)], mib=32,
        )

    def ffn_grads(h, *more):
        n = h.shape[1] // 3
        return token_grads((second, h, 0, 2 * n), (out_low, h, 2, n), *more)

    h1, part_l, part_c = ffn(w1)
    grad_1 = ffn_grads(h1)
    w2, grad_1 = lax.optimization_barrier((w2, grad_1))
    sum_1 = line_sum(grad_1)
    h2, part_l, part_c = ffn(w2, part_l, part_c)
    d_hidden, grad_ffn, branch = call(
        branch_body, 5, (shape((own, width), f32), shape((8, width), f32), shape((T, width), bf16)), (VMEM, VMEM, HBM),
        (part_c, hidden, cot_own, mixer_row(ffn_gain)), [VMEM] * 4, collect, us=50,
    )
    h2, branch = lax.optimization_barrier((h2, branch))
    grad_2b = ffn_grads(h2, (branch, both_low, 0, chan + HD))
    d_both = dot(branch, wb, 1, 0)

    back, _, back_stack = specs(True)
    dz_low, dy, leave, tail, g_state, grad_gain_s = chunked(
        functools.partial(gate_back_body, heads, nc), nc,
        (shape((T, chan), bf16), shape((T, chan), f32), shape((nc, chan, N), f32), shape((nc, 8, 128), f32),
         shape((chan, N), bf16), shape((8, chan), f32)),
        (back(chan), back(chan), back_stack(chan, N), back_stack(8, 128), fixed(chan, N), fixed(8, chan)),
        (base, raw, bc_all, starts_col, bias_row, rates_row, d_both, y_scan, cv_x, reach, zq, skip_row, gain_row),
        [smem, back(128), back(2 * N), back(1), fixed(1, 128), fixed(1, 128), back(chan), back(chan), back(chan),
         back_stack(16, 128), back(chan), fixed(1, chan), fixed(1, chan)],
        [pltpu.VMEM((chan, N), f32), pltpu.VMEM((8, 128), f32)],
    )
    grad_2b, sum_1, dz_low = lax.optimization_barrier((grad_2b, sum_1, dz_low))
    sum_2 = line_sum(grad_2b)

    dq_low, dkv = chunked(
        functools.partial(attend_back_body, size, T), T // qrows,
        (shape((T, HD), bf16), shape((G, planes, kvr, T), bf16)), (column(0, HD), kv_spec),
        (base, firsts, query, starts_col, cos_row, sin_row, kv_all, d_both, attended, log_mass),
        [smem, smem, column(0, HD), column(0, 1), column(0, HD), column(0, HD), kv_spec, column(at_q, HD), column(0, HD),
         column(0, 1)],
        [pltpu.VMEM((planes, HD, T), f32), pltpu.VMEM((planes, HD, T), f32)], mib=14 + 3 * planes,
    )
    dzq_low = jnp.concatenate([dz_low, dq_low], axis=1)
    grad_z = dot(first, dzq_low, 0, 0).astype(bf16)
    g_state, sum_1, grad_z = lax.optimization_barrier((g_state, sum_1, grad_z))
    states, factors, dkv, layer_own = call(
        functools.partial(down_body, planes), 6, state_shapes + (shape((planes * kvr, T), bf16), shape((own, width), f32)),
        (HBM,) * 2 + (VMEM,) * 2, (g_state, through, dkv.reshape(-1, T), part_l, hidden), [HBM] * 2 + [VMEM] * 3,
        line_sems * 2 + Collect.scratch(planes * kvr, T, False) + Collect.scratch(own, width), us=45, mib=14 + 2 * planes,
    )
    states, grad_z = lax.optimization_barrier((states, grad_z))
    sum_z = line_sum(grad_z)
    after = entering(False, states, factors)
    gx, d_bc_all, d_raw, grad_rows = chunked(
        functools.partial(scan_back_body, heads), nc,
        (shape((T, chan), f32), shape((2 * N, T), bf16), shape((T, 128), bf16), shape((8, 128), f32)),
        (tile(chan), pl.BlockSpec((2 * N, L), lambda c: (0, c)), tile(128), fixed(8, 128)),
        (base, raw, bc_all, starts_col, bias_row, rates_row, dy, cv_x, enter, reach, before, leave, tail, after, skip_row),
        [smem, tile(128), tile(2 * N), tile(1), fixed(1, 128), fixed(1, 128), tile(chan), tile(chan),
         stack(chan, N), stack(16, 128), fixed(chan, N), stack(chan, N), stack(8, 128), fixed(chan, N), fixed(1, chan)],
    )

    d_bc_t, sum_2 = lax.optimization_barrier((d_bc_all, sum_2))
    g_bc, rim_bc, rim_x, dkv, got_1, got_2 = call(
        functools.partial(back_body, planes), 7,
        (shape((bcs, T), f32), shape((bcs, 128), f32), shape((RIM, chan), f32), shape((kvr, T), f32))
        + tuple(shape((G, rows, v.shape[1]), bf16) for v in (h1, h2)), (VMEM,) * 4 + (HBM,) * 2,
        (d_bc_t, dkv.reshape(planes, kvr, T), slope_bc, gx, sum_1, sum_2), [VMEM] * 3 + [HBM] * 3,
        [pltpu.VMEM((G * bcs, T), bf16), pltpu.VMEM((3, bcs, T), bf16), pltpu.VMEM((3, bcs, T), bf16),
         pltpu.VMEM((planes - 1, kvr, T), bf16), pltpu.VMEM((bcs, T), f32), DMA(()), DMA(()), DMA((3,)), DMA((3,)),
         DMA((planes - 1,)), DMA((planes - 1,)), DMA((2,)), DMA((2,)), DMA((2, 3)), DMA((2, 3)), DMA((2,))], us=30,
    )
    strip = min(32, rows)

    def got(v):
        return pl.BlockSpec((v.shape[0], strip, v.shape[2]), lambda c: (0, c, 0))

    def given(cols):
        return pl.BlockSpec((strip, cols), lambda c: (c, 0))

    ffn_out = chunked(
        give_ffn_body, rows // strip, (shape((rows, G * units), f32),) * 3, (given(G * units),) * 3,
        (got_1, got_2), [got(got_1), got(got_2)], mib=24,
    )
    gx, *ffn_out = lax.optimization_barrier((gx, *ffn_out))
    starts_long = jnp.concatenate([all_starts, jnp.full((8,), total_tokens, jnp.int32)])
    starts_long = lax.dynamic_slice_in_dim(starts_long, offset, T + 8, 0)[:, None]
    taps_both = jnp.concatenate([taps_inner, taps_pair], axis=1)
    da_low, grad_taps = chunked(
        functools.partial(finish_body, nc, chan), nc,
        (shape((T, a_cols), bf16), shape((8, chan + 128), f32)), (tile(a_cols), fixed(8, chan + 128)),
        (base, pa, gx, rim_x, g_bc, rim_bc, dkv, starts_long, taps_both, cos_k, sin_k),
        [smem, pa_spec, fixed(T, chan), fixed(RIM, chan), fixed(bcs, T), fixed(bcs, 128), fixed(kvr, T),
         fixed(T + 8, 1), fixed(K, chan + 128), fixed(quarter_half, T), fixed(quarter_half, T)], near=(3, 4, 5, 6),
    )
    grad_a = dot(first, da_low, 0, 0).astype(bf16)
    grad_a, sum_z = lax.optimization_barrier((grad_a, sum_z))
    sum_a = line_sum(grad_a)
    lane = width // 4
    part_a = chunked(
        back_part_body, T // ftile, shape((T, width), bf16), rows_spec(width), (da_low, dzq_low, d_raw, wa, w_zqob, w_step),
        [rows_spec(v.shape[1]) for v in (da_low, dzq_low, d_raw)] + [all_spec(v) for v in (wa, wz, w_step)], mib=28, keep=(0,),
    )
    grad_step = dot(d_raw, first, 0, 0)[:16].reshape(16, planes, G, rows).transpose(1, 2, 0, 3)
    groups = (shape((G, rows, chan + HD), bf16),) * 2
    grad_input, layer_out, mine, got_z, got_b = call(
        final_body, 8,
        (shape((tokens, width), f32), shape((tokens, width), f32), shape((RIM, lane), f32)) + groups, (HBM, HBM, VMEM, HBM, HBM),
        (part_a, x_own, d_hidden, layer_own, mixer_row(mixer_gain), grad_taps, grad_gain_s, grad_rows, grad_ffn, sum_z, sum_2),
        [VMEM] * 9 + [HBM] * 2,
        Collect.scratch(own, width)
        + [pltpu.VMEM((own, width), f32), pltpu.VMEM((8, width), f32), DMA((2,)), DMA((2,)), DMA((2,)),
           DMA((2, 3)), DMA((2, 3)), DMA((2,))], us=40,
    )

    got_x, got_s, sums, got_t = call(
        functools.partial(last_body, planes), 10,
        (shape((G, rows, chan), bf16), shape((2 * G, rows, a_cols - chan), bf16), shape((2 * G * RIM, lane), f32),
         shape((G, 16, rows), f32)), (HBM,) * 4, (sum_a, mine, grad_step), [HBM, VMEM, VMEM],
        [pltpu.VMEM((RIM, lane), f32), pltpu.VMEM((planes - 1, RIM, lane), f32), pltpu.VMEM((G, 16, rows), f32),
         pltpu.VMEM((planes - 1, G, 16, rows), f32), DMA((3,)), DMA((3,)), DMA((2 * G,)), DMA((2 * G,)),
         DMA((2,)), DMA((planes - 1,)), DMA((planes - 1,)), DMA((planes - 1,)), DMA((planes - 1,)), DMA((3,)), DMA((3,)), DMA(()),
         DMA((2 * G,)), DMA((2 * G,)), DMA(())],
    )
    widths = [w.shape[1] for w in (
        z_weight, x_weight, bc_weight, q_weight, k_weight, v_weight, o_weight, out_weight,
    )]
    gathered = (got_z, got_b, got_x, got_s)
    steps_ = rows // strip
    moved = pl.BlockSpec((tokens // steps_, width), lambda c: (c, 0))
    *weights, layer_out, grad_input = chunked(
        functools.partial(give_body, (bcs, quarter_half)), steps_,
        tuple(shape((rows, w), f32) for w in widths) + (shape((tokens, width), f32),) * 2,
        tuple(given(w) for w in widths) + (moved, moved),
        (jnp.full((1,), hi, jnp.int32),) + gathered + (layer_out, grad_input), [smem] + [got(v) for v in gathered] + [moved, moved], mib=40,
    )
    weights.insert(3, got_t[:, :heads].reshape(G * heads, rows).T)

    sums = sums.reshape(G, cores, RIM, lane)
    mine = lax.dynamic_index_in_dim(sums, hi, 1, False)
    o_conv_inner = mine[:, :K, :chan].transpose(1, 0, 2).reshape(K, G * chan)
    o_conv_state = sums[:, :, :K, chan : chan + bcs].transpose(2, 1, 0, 3).reshape(K, 2 * N)
    per = width // (planes * G)
    gains = jnp.sum(sums[:, :, 8:], axis=(0, 1)).reshape(2, width)
    gains = lax.dynamic_slice_in_dim(gains, (zi * G + pi) * per, per, 1)

    return (
        layer_out, grad_input, gains[1], gains[0], *weights, *ffn_out,
        o_conv_inner, o_conv_state,
        mine[:, 5, :heads].reshape(-1), mine[:, 5, 128 : 128 + heads].reshape(-1),
        mine[:, 5, 256 : 256 + heads].reshape(-1), mine[:, 4, :chan].reshape(-1),
    )


def solution(mesh):
    seq, cores = mesh.shape["seq"], mesh.shape["head"]
    planes = Mesh(mesh.devices.reshape(seq // G, G, cores), ("z", "p", "head"))
    s = ("z", "p")
    both, row, head, whole = P(s, "head"), P(s, None), P("head"), P()
    placed = (
        row, P(s), whole, whole, both, both, row, both, both, both, both, both, both, both, both, both,
        P(None, "head"), whole, head, head, head, head, row,
    )
    return jax.shard_map(
        on_device,
        mesh=planes,
        in_specs=placed,
        out_specs=(
            row, row, P(s), P(s), both, both, row, both, both, both, both, both, both, both, both, both,
            P(None, "head"), whole, head, head, head, head,
        ),
        check_vma=False,
    )
```

```python
import functools
import math

import jax
import jax.numpy as jnp
from jax import lax
from jax.experimental import pallas as pl
from jax.experimental.pallas import tpu as pltpu
from jax.sharding import Mesh, PartitionSpec as P

P_SIZE = 64
N = 256
HD = 128
K = 4
G = 4
CHUNK = 128
RIM = 16

highest = lax.Precision.HIGHEST
rope_base = 10000.0
norm_eps = 1e-05
bf16 = jnp.bfloat16
f32 = jnp.float32
MESH = pl.DeviceIdType.MESH
HBM = pl.BlockSpec(memory_space=pl.ANY)
VMEM = pl.BlockSpec(memory_space=pltpu.VMEM)
DMA = pltpu.SemaphoreType.DMA


def rcopy(src, dst, send, recv, **where):
    return pltpu.make_async_remote_copy(
        src_ref=src, dst_ref=dst, send_sem=send, recv_sem=recv, device_id=where, device_id_type=MESH
    )


def here():
    return lax.axis_index("z"), lax.axis_index("p"), lax.axis_index("head")


def ring(p, d):
    return lax.rem(p + d + G, G)


def greet(*partners):
    barrier = pltpu.get_barrier_semaphore()
    for where in partners:
        pl.semaphore_signal(barrier, inc=1, device_id=where, device_id_type=MESH)
    pl.semaphore_wait(barrier, len(partners))


def plane_partners(p, c):
    return [{"p": ring(p, d)} for d in range(1, G)] + [{"head": 1 - c}]


def line_partners(z, planes):
    return [{"z": lax.rem(z + d, planes)} for d in range(1, planes)]


def beside(p):
    return p + 1 - 2 * lax.rem(p, 2), lax.rem(p + 2, G), G - 1 - p


class Spread:
    sems = [DMA((2,)), DMA((2,)), DMA((2,)), DMA((2,)), DMA((4,)), DMA((4,)), DMA(())]

    def __init__(self, block, out, start, rows, sems, cores=True):
        self.block, self.out, self.first, self.rows, self.cores = block, out, start, rows, cores
        self.s1, self.r1, self.s2, self.r2, self.s3, self.r3, self.keep = sems
        _, self.p, self.c = here()
        self.around = beside(self.p)

    def spot(self, q, half=None):
        first, rows = self.first(q, self.c), self.rows
        if half is not None:
            first, rows = first + half * (rows // 2), rows // 2
        return self.out.at[pl.ds(first, rows)]

    def over(self, i):
        return rcopy(self.block, self.spot(self.p), self.s1.at[i], self.r1.at[i], p=self.around[i])

    def relay(self, i):
        spot = self.spot(self.around[i], i)
        return rcopy(spot, spot, self.s2.at[i], self.r2.at[i], p=self.around[1 - i])

    def relayed(self, i):
        spot = self.spot(self.around[2], 1 - i)
        return rcopy(spot, spot, self.s2.at[1 - i], self.r2.at[1 - i], p=self.around[i])

    def across(self, i):
        spot = self.spot(self.p if i == 3 else self.around[i])
        return rcopy(self.block if i == 3 else spot, spot, self.s3.at[i], self.r3.at[i], head=1 - self.c)

    def mine(self):
        return pltpu.make_async_copy(self.block, self.spot(self.p), self.keep)

    def start(self):
        for i in (0, 1):
            self.over(i).start()
        if self.cores:
            self.across(3).start()
        self.mine().start()

    def pass_on(self):
        for i in (0, 1):
            self.over(i).wait_recv()
            self.relay(i).start()
            if self.cores:
                self.across(i).start()
        for i in (0, 1):
            self.relayed(i).wait_recv()
        if self.cores:
            self.across(2).start()

    def finish(self):
        self.mine().wait()
        for i in (0, 1):
            self.over(i).wait_send()
            self.relay(i).wait_send()
        if self.cores:
            for i in range(4):
                self.across(i).wait()


class Collect:
    @staticmethod
    def scratch(rows, width, cores=True):
        return [
            pltpu.VMEM((4, rows, width) if cores else (1, 16, 128), bf16), pltpu.VMEM((3, rows, width), bf16),
            pltpu.VMEM((2, rows // 2, width), bf16), pltpu.VMEM((2, rows, width), bf16),
            pltpu.VMEM((rows, width), f32), DMA((4,)), DMA((4,)), DMA((6,)), DMA((6,)),
        ]

    def __init__(self, part, rows, scratch, strip=16, cores=True):
        self.part, self.rows, self.strip, self.cores = part, rows, strip, cores
        self.cx, self.out, self.rd, self.rx, self.total, self.s1, self.r1, self.s2, self.r2 = scratch
        _, self.p, self.c = here()
        self.around = beside(self.p)

    def first(self, q, c):
        return pl.multiple_of(((q * 2 + c) if self.cores else q) * self.rows, 16)

    def owner(self, i):
        return self.p if i == 3 else self.around[i]

    def across(self, i):
        spot = self.part.at[pl.ds(self.first(self.owner(i), 1 - self.c), self.rows)]
        return rcopy(spot, self.cx.at[i], self.s1.at[i], self.r1.at[i], head=1 - self.c)

    def over(self, i, half):
        at = pl.ds(half * (self.rows // 2), self.rows // 2)
        k = 2 * i + half
        if i == 2:
            return rcopy(self.out.at[2, at], self.rd.at[half], self.s2.at[k], self.r2.at[k], p=self.around[half])
        return rcopy(self.out.at[i, at], self.rx.at[i, at], self.s2.at[k], self.r2.at[k], p=self.around[i])

    def strips(self, body, lo=0, hi=None):
        hi = self.rows if hi is None else hi

        def one(n, carry):
            body(lo + n * self.strip)
            return carry

        lax.fori_loop(0, (hi - lo) // self.strip, one, 0)

    def at(self, first):
        return pl.ds(pl.multiple_of(first, self.strip), self.strip)

    def add(self, i, half=None, relayed=None):
        first = self.first(self.owner(i), self.c)
        size = self.rows // 2

        def one(at):
            v = self.part[self.at(first + at)].astype(f32)
            if self.cores:
                v = v + self.cx[i, self.at(at)].astype(f32)
            if relayed is not None:
                v = v + self.rd[relayed, self.at(at - half * size)].astype(f32)
            if i == 3:
                self.total[self.at(at)] = v
            else:
                self.out[i, self.at(at)] = v.astype(bf16)

        if half is None:
            self.strips(one)
        else:
            self.strips(one, half * size, (half + 1) * size)

    def start(self):
        if self.cores:
            for i in (2, 0, 1, 3):
                self.across(i).start()

    def crossed(self, i):
        if self.cores:
            self.across(i).wait_recv()

    def begin(self):
        self.crossed(2)
        for half in (0, 1):
            self.add(2, half)
            self.over(2, half).start()
        for i in (0, 1):
            self.crossed(i)
            self.add(i, i)
            self.over(i, i).start()
        self.crossed(3)
        self.add(3)

    def relay(self):
        for i in (0, 1):
            self.over(2, 1 - i).wait_recv()
            self.add(i, 1 - i, 1 - i)
            self.over(i, 1 - i).start()

    def middle(self):
        self.begin()
        self.relay()

    def arrive(self):
        for half in (0, 1):
            for i in (0, 1):
                self.over(i, i if half == 0 else 1 - i).wait_recv()

    def sum_of(self, at):
        r = self.at(at)
        return self.total[r] + self.rx[0, r].astype(f32) + self.rx[1, r].astype(f32)

    def finish(self):
        if self.cores:
            for i in range(4):
                self.across(i).wait_send()
        for i in range(3):
            for half in (0, 1):
                self.over(i, half).wait_send()


def call(body, name_id, outs, out_specs, ins, in_specs, scratch, us=20, mib=12):
    ins = [pltpu.with_memory_space_constraint(v, pltpu.HBM) if s is HBM and v.size > 20000 else v for v, s in zip(ins, in_specs)]
    if isinstance(outs, tuple):
        outs = tuple(pltpu.HBM(v.shape, v.dtype) if s is HBM else v for v, s in zip(outs, out_specs))
    elif out_specs is HBM:
        outs = pltpu.HBM(outs.shape, outs.dtype)
    return pl.pallas_call(
        body,
        out_shape=outs,
        in_specs=in_specs,
        out_specs=out_specs,
        scratch_shapes=scratch,
        cost_estimate=pl.CostEstimate(flops=0, bytes_accessed=us * 3_500_000, transcendentals=0),
        compiler_params=pltpu.CompilerParams(
            collective_id=name_id, has_side_effects=True, vmem_limit_bytes=mib * 2**20
        ),
    )(*ins)


def shape(dims, kind):
    return jax.ShapeDtypeStruct(dims, kind)


def exchange_copies(pieces, sems, keep):
    _, p, _ = here()
    away, own = [], []
    for i, (source, width, target, first, led, *part) in enumerate(pieces):
        whole, skip = part or (width, 0)
        rows = source.shape[-2]
        spot = target.at[pl.ds(pl.multiple_of(p * rows, 16), rows), pl.ds(first, width)]
        for d in range(G):
            q = ring(p, d)
            taken = source.at[q] if led else source.at[:, pl.ds(pl.multiple_of(q * whole + skip, 128), width)]
            if d:
                away.append(rcopy(taken, spot, sems[0].at[d - 1, i], sems[1].at[d - 1, i], p=q))
            else:
                own.append(pltpu.make_async_copy(taken, spot, keep.at[i]))
    return away, own


def exchange_a_body(x_ref, small_ref, out_ref, send, recv, keep):
    _, p, c = here()
    greet(*[{"p": ring(p, d)} for d in range(1, G)])
    xw = x_ref.shape[1] // G
    pieces = [(x_ref, xw, out_ref, 0, False), (small_ref, small_ref.shape[2], out_ref, xw, True)]
    away, own = exchange_copies(pieces, (send, recv), keep)
    for copy in away + own:
        copy.start()
    for copy in own + away:
        copy.wait()


def exchange_b_body(z_ref, q_ref, out_ref, o_ref, wb, send, recv, keep):
    _, p, c = here()
    greet(*[{"p": ring(p, d)} for d in range(1, G)])
    pieces, at = [], 0
    for ref in (z_ref, q_ref, out_ref, o_ref):
        pieces.append((ref, ref.shape[1] // G, wb, at, False))
        at += ref.shape[1] // G
    away, own = exchange_copies(pieces, (send, recv), keep)
    for copy in away + own:
        copy.start()
    for copy in own + away:
        copy.wait()


def start_body(planes, first, docs, steps, n1, all_docs, all_steps, *sems):
    z, p, c = here()
    greet(*plane_partners(p, c), *line_partners(z, planes))
    rim_s, rim_r, ps, pr, zs, zr, dk = sems[:7]
    rows = first.shape[0]
    a = Spread(first, n1, lambda q, k: pl.multiple_of(RIM + (q * 2 + k) * rows, 16), rows, sems[7:])
    near = [
        rcopy(have(ring(p, d)), every.at[z, p], ps.at[i, d - 1], pr.at[i, d - 1], p=ring(p, d))
        for i, (have, every) in enumerate(((lambda q: docs, all_docs), (lambda q: steps.at[q], all_steps))) for d in (1, 2, 3)
    ]
    own = [
        pltpu.make_async_copy(docs, all_docs.at[z, p], dk.at[0]), pltpu.make_async_copy(steps.at[p], all_steps.at[z, p], dk.at[1])
    ]
    a.start()
    for copy in near + own:
        copy.start()
    for copy in own + near:
        copy.wait()
    far = [
        rcopy(every.at[z], every.at[z], zs.at[i, d - 1], zr.at[i, d - 1], z=lax.rem(z + d, planes))
        for i, every in enumerate((all_docs, all_steps)) for d in range(1, planes)
    ]
    for copy in far:
        copy.start()
    a.pass_on()
    a.finish()
    last = n1.at[pl.ds(n1.shape[0] - RIM, RIM)]
    rim = rcopy(last, n1.at[pl.ds(0, RIM)], rim_s, rim_r, z=lax.rem(z + 1, planes))
    rim.start()
    for copy in far:
        copy.wait()
    rim.wait()


def spread_body(planes, block, kv, gate_w, up_w, down_w, out, lines, w1, w2, zs, zr, zk, send, recv, hold, *sems):
    z, p, c = here()
    greet(*plane_partners(p, c), *line_partners(z, planes))
    rows = block.shape[0]
    far = [rcopy(kv, lines.at[z], zs.at[d - 1], zr.at[d - 1], z=lax.rem(z + d, planes)) for d in range(1, planes)]
    keep = pltpu.make_async_copy(kv, lines.at[z], zk)
    for copy in far:
        copy.start()
    keep.start()
    s = Spread(block, out, lambda q, k: pl.multiple_of((k * G + q) * rows, 16), rows, sems)
    units = gate_w.shape[1] // G
    pieces = [
        (ref, part, to, i * part, False, units, skip)
        for to, part, skip in ((w1, w1.shape[1] // 3, 0), (w2, w2.shape[1] // 3, w1.shape[1] // 3))
        for i, ref in enumerate((gate_w, up_w, down_w))
    ]
    away, own = exchange_copies(pieces, (send, recv), hold)
    s.start()
    for copy in away + own:
        copy.start()
    s.pass_on()
    s.finish()
    for copy in own + away:
        copy.wait()
    keep.wait()
    for copy in far:
        copy.wait()


def state_copies(planes, upward, state, factor, states, factors, sems):
    z, _, _ = here()
    s1, r1, s2, r2 = sems
    way = 1 if upward else -1

    def pair(d):
        to = lax.rem(z + way * d + planes, planes)
        return (
            rcopy(state, states.at[d - 1], s1.at[d - 1], r1.at[d - 1], z=to),
            rcopy(factor, factors.at[d - 1], s2.at[d - 1], r2.at[d - 1], z=to),
        )

    def start():
        for d in range(1, planes):
            @pl.when((z + d < planes) if upward else (z - d >= 0))
            def _():
                for copy in pair(d):
                    copy.start()

    def wait():
        for d in range(1, planes):
            @pl.when((z - d >= 0) if upward else (z + d < planes))
            def _():
                for copy in pair(d):
                    copy.wait_recv()

            @pl.when((z + d < planes) if upward else (z - d >= 0))
            def _():
                for copy in pair(d):
                    copy.wait_send()

    return start, wait


def up_body(planes, state, factor, lines, low, states, factors, kv, ol, *sems):
    z, p, c = here()
    greet(*plane_partners(p, c), *line_partners(z, planes))
    start, wait = state_copies(planes, True, state, factor, states, factors, sems[:4])
    start()
    rows = low.shape[0]
    s = Spread(lines, kv, lambda q, k: q * planes, planes, sems[4:11], cores=False)
    b = Spread(low, ol, lambda q, k: pl.multiple_of((q * 2 + k) * rows, 16), rows, sems[11:18])
    s.start()
    b.start()
    s.pass_on()
    b.pass_on()
    s.finish()
    b.finish()
    wait()


def down_body(planes, state, factor, dkv, part, hidden, states, factors, kv, layer, *sems):
    z, p, c = here()
    greet(*plane_partners(p, c), *line_partners(z, planes))
    start, wait = state_copies(planes, False, state, factor, states, factors, sems[:4])
    start()
    k = Collect(dkv, kv.shape[0], sems[4:13], cores=False)
    s = Collect(part, hidden.shape[0], sems[13:])
    s.start()
    k.begin()
    s.begin()
    k.relay()
    s.relay()
    k.arrive()

    def sum_kv(at):
        kv[k.at(at)] = k.sum_of(at).astype(bf16)

    k.strips(sum_kv)
    s.arrive()

    def one(at):
        layer[s.at(at)] = hidden[s.at(at)] + s.sum_of(at)

    s.strips(one)
    k.finish()
    s.finish()
    wait()


def hidden_body(part, x_ref, gain, hidden, second, *scratch):
    _, p, c = here()
    greet(*plane_partners(p, c))
    rows = x_ref.shape[0]
    s = Collect(part, rows, scratch[:9])
    stage = scratch[9]
    s.start()
    s.middle()
    s.arrive()

    def one(at):
        r = s.at(at)
        h = x_ref[r] + s.sum_of(at)
        hidden[r] = h
        scale = lax.rsqrt(jnp.mean(h * h, axis=-1, keepdims=True) + norm_eps)
        stage[r] = (h * scale * gain[...]).astype(bf16)

    s.strips(one)
    g = Spread(stage, second, s.first, rows, scratch[10:17])
    g.start()
    g.pass_on()
    s.finish()
    g.finish()


def branch_body(part, hidden, cot, gain, d_hidden, gain_grad, branch, *scratch):
    _, p, c = here()
    greet(*plane_partners(p, c))
    rows = hidden.shape[0]
    s = Collect(part, rows, scratch[:9])
    stage = scratch[9]
    gain_grad[...] = jnp.zeros_like(gain_grad)
    s.start()
    s.middle()
    s.arrive()

    def one(at):
        r = s.at(at)
        h = hidden[r]
        scale = lax.rsqrt(jnp.mean(h * h, axis=-1, keepdims=True) + norm_eps)
        grad = s.sum_of(at)
        gain_grad[pl.ds(0, 1)] += jnp.sum(grad * h * scale, axis=0, keepdims=True)
        u = grad * gain[...]
        d = cot[r] + scale * u - h * (scale * scale * scale * jnp.mean(u * h, axis=-1, keepdims=True))
        d_hidden[r] = d
        stage[r] = d.astype(bf16)

    s.strips(one)
    g = Spread(stage, branch, s.first, rows, scratch[10:17])
    g.start()
    g.pass_on()
    s.finish()
    g.finish()


def final_body(part, x_ref, d_hidden, layer, gain, taps, norm, rows_ref, ffn, sum_z, sum_b, grad_in, layer_out, mine, got_z, got_b, *scratch):
    z, p, c = here()
    greet(*plane_partners(p, c))
    rows = x_ref.shape[0]
    s = Collect(part, rows, scratch[:9])
    stage, gain_row, es, er, ek, zs, zr, zk = scratch[9:]
    half = pl.ds(pl.multiple_of(c * rows, 16), rows)
    wide = got_z.shape[1]

    def halves(i, source, target):
        return (
            rcopy(source, target.at[half], es.at[i], er.at[i], head=1 - c),
            pltpu.make_async_copy(source, target.at[half], ek.at[i]),
        )

    def rows_of(v, q):
        cols = got_z.shape[2]
        return v.at[pl.ds(pl.multiple_of(q * wide, 16), wide), pl.ds(v.shape[1] - cols, cols)]

    s.start()
    first = halves(0, layer, layer_out)
    for copy in first:
        copy.start()
    lane = mine.shape[1]
    mine[...] = jnp.zeros_like(mine)
    mine[:K, : taps.shape[1]] = taps[:K]
    mine[4:5, : norm.shape[1]] = norm[:1]
    for j in range(3):
        mine[5:6, j * 128 : (j + 1) * 128] = rows_ref[j : j + 1]
    for j in range(4):
        mine[8 + j : 9 + j] = ffn[:1, j * lane : (j + 1) * lane]
    gain_row[...] = jnp.zeros_like(gain_row)
    s.middle()
    zb = []
    for i, (have, got) in enumerate(((sum_z, got_z), (sum_b, got_b))):
        for d in (1, 2, 3):
            zb.append(rcopy(rows_of(have, ring(p, d)), got.at[p], zs.at[i, d - 1], zr.at[i, d - 1], p=ring(p, d)))
        zb.append(pltpu.make_async_copy(rows_of(have, p), got.at[p], zk.at[i]))
    for copy in zb:
        copy.start()
    s.arrive()

    def one(at):
        r = s.at(at)
        v = x_ref[r]
        scale = lax.rsqrt(jnp.mean(v * v, axis=-1, keepdims=True) + norm_eps)
        grad = s.sum_of(at)
        gain_row[pl.ds(0, 1)] += jnp.sum(grad * v * scale, axis=0, keepdims=True)
        u = grad * gain[...]
        stage[r] = d_hidden[r] + scale * u - v * (scale * scale * scale * jnp.mean(u * v, axis=-1, keepdims=True))

    s.strips(one)
    second = halves(1, stage, grad_in)
    for copy in second:
        copy.start()
    for j in range(4):
        mine[12 + j : 13 + j] = gain_row[:1, j * lane : (j + 1) * lane]
    s.finish()
    for copy in first + second:
        copy.wait()
    for copy in zb:
        copy.wait()


def back_body(planes, dbc, dkv, d_silu_bc, gx, sum_1, sum_2, g_bc, rim_bc, rim_x, kv_out, got_1, got_2, *scratch):
    z, p, c = here()
    greet(*plane_partners(p, c), *line_partners(z, planes))
    (cx, bx, rbc, zkv, acc, xs, xr, bs, br, zs, zr, ms, mr, ws, wr, wk) = scratch
    rows = rbc.shape[1]
    across = rcopy(
        dbc.at[pl.ds(pl.multiple_of((1 - c) * G * rows, 16), G * rows)], cx, xs, xr, head=1 - c
    )
    across.start()
    grads = list(enumerate(((sum_1, got_1), (sum_2, got_2))))
    wide = got_1.shape[1]

    def rows_of(q):
        return pl.ds(pl.multiple_of(q * wide, 16), wide)

    w_over = [
        rcopy(have.at[rows_of(ring(p, d)), pl.ds(0, got.shape[2])], got.at[p], ws.at[i, d - 1], wr.at[i, d - 1], p=ring(p, d))
        for i, (have, got) in grads for d in (1, 2, 3)
    ]
    w_own = [
        pltpu.make_async_copy(have.at[rows_of(p), pl.ds(0, got.shape[2])], got.at[p], wk.at[i]) for i, (have, got) in grads
    ]
    for copy in w_over[3:] + w_own:
        copy.start()

    def kv_down(d):
        to = lax.rem(z - d + planes, planes)
        return rcopy(dkv.at[to], zkv.at[d - 1], zs.at[d - 1], zr.at[d - 1], z=to)

    for d in range(1, planes):
        @pl.when(z - d >= 0)
        def _():
            kv_down(d).start()

    across.wait_recv()
    bc_over = []
    for d in (1, 2, 3, 0):
        q = ring(p, d)
        own = dbc[pl.ds(pl.multiple_of((c * G + q) * rows, 16), rows)].astype(f32)
        own = own + cx[pl.ds(pl.multiple_of(q * rows, 16), rows)].astype(f32)
        if d:
            bx[d - 1] = own.astype(bf16)
            bc_over.append(rcopy(bx.at[d - 1], rbc.at[d - 1], bs.at[d - 1], br.at[d - 1], p=q))
            bc_over[-1].start()
        else:
            acc[...] = own
    for copy in w_over[:3]:
        copy.start()
    for copy in bc_over:
        copy.wait_recv()
    g = acc[...]
    for d in range(3):
        g = g + rbc[d].astype(f32)
    g_bc[...] = g * d_silu_bc[...]
    before = lax.rem(z - 1 + planes, planes)
    rims = [
        rcopy(g_bc.at[:, pl.ds(0, 128)], rim_bc, ms.at[0], mr.at[0], z=before),
        rcopy(gx.at[pl.ds(0, RIM)], rim_x, ms.at[1], mr.at[1], z=before),
    ]
    for copy in rims:
        copy.start()
    kv_out[...] = dkv[z].astype(f32)
    for d in range(1, planes):
        @pl.when(z + d < planes)
        def _():
            kv_down(d).wait_recv()
            kv_out[...] += zkv[d - 1].astype(f32)

        @pl.when(z - d >= 0)
        def _():
            kv_down(d).wait_send()

    for copy in rims:
        copy.wait()
    across.wait_send()
    for copy in bc_over:
        copy.wait_send()
    for copy in w_own + w_over:
        copy.wait()


def last_body(planes, sum_a, small, steps, got_x, got_s, sums, got_t, mine, others, t_own, t_far, xs, xr, ss, sr, keep, ls, lr,
              ts, tr, qs, qr, tk, gs, gr, gk):
    z, p, c = here()
    pairs = [(d, k) for k in (0, 1) for d in range(G) if d or k]
    greet(*[{"p": ring(p, d), "head": lax.rem(c + k, 2)} for d, k in pairs], *line_partners(z, planes))
    rows, chan = got_x.shape[1], got_x.shape[2]

    def part(q, first, cols):
        return sum_a.at[pl.ds(pl.multiple_of(q * rows, 16), rows), pl.ds(first, cols)]

    def narrow(d, k):
        cols, to = got_s.shape[2], got_s.at[c * G + p]
        i = k * G + d - 1
        return rcopy(part(ring(p, d), chan, cols), to, ss.at[i], sr.at[i], p=ring(p, d), head=lax.rem(c + k, 2))

    lines = [
        rcopy(small, others.at[d - 1], ls.at[d - 1], lr.at[d - 1], z=lax.rem(z + d, planes)) for d in range(1, planes)
    ] + [
        rcopy(steps.at[lax.rem(z + d, planes)], t_far.at[d - 1], ts.at[d - 1], tr.at[d - 1], z=lax.rem(z + d, planes))
        for d in range(1, planes)
    ]
    copies = [
        rcopy(part(ring(p, d), 0, chan), got_x.at[p], xs.at[d - 1], xr.at[d - 1], p=ring(p, d)) for d in (1, 2, 3)
    ] + [narrow(d, k) for d, k in pairs] + [
        pltpu.make_async_copy(part(p, 0, chan), got_x.at[p], keep.at[0]),
        pltpu.make_async_copy(part(p, chan, got_s.shape[2]), got_s.at[c * G + p], keep.at[1]),
    ]
    for copy in lines + copies:
        copy.start()
    for copy in lines:
        copy.wait()
    total = small[...]
    for d in range(1, planes):
        total = total + others[d - 1]
    mine[...] = total
    place = sums.at[pl.ds(pl.multiple_of((p * 2 + c) * RIM, RIM), RIM)]
    shares = [
        rcopy(mine, place, gs.at[k * G + d - 1], gr.at[k * G + d - 1], p=ring(p, d), head=lax.rem(c + k, 2)) for d, k in pairs
    ]
    shares.append(pltpu.make_async_copy(mine, place, gk))
    for copy in shares:
        copy.start()
    total = steps[z]
    for d in range(1, planes):
        total = total + t_far[d - 1]
    t_own[...] = total
    back = [rcopy(t_own.at[ring(p, d)], got_t.at[p], qs.at[d - 1], qr.at[d - 1], p=ring(p, d)) for d in (1, 2, 3)]
    back.append(pltpu.make_async_copy(t_own.at[p], got_t.at[p], tk))
    for copy in back:
        copy.start()
    for copy in copies + back + shares:
        copy.wait()


def give_ffn_body(f1, f2, *outs):
    units = (f1.shape[2] + f2.shape[2]) // 3
    for p in range(G):
        for i, ref in enumerate(outs):
            for got, skip in ((f1, 0), (f2, f1.shape[2] // 3)):
                part = got.shape[2] // 3
                at = p * units + skip
                ref[:, at : at + part] = got[p, :, i * part : (i + 1) * part].astype(f32)


def give_body(sizes, core_ref, zq, ob, x_, s_, layer, grad, z_o, x_o, bc_o, q_o, k_o, v_o, o_o, out_o, layer_o, grad_o):
    bcs, quarter = sizes
    layer_o[...] = layer[...]
    grad_o[...] = grad[...]
    chan = x_.shape[2]
    for p in range(G):
        for ref, got, first, cols in (
            (z_o, zq, 0, chan), (q_o, zq, chan, HD), (out_o, ob, 0, chan), (o_o, ob, chan, HD),
            (x_o, x_, 0, chan),
        ):
            ref[:, p * cols : (p + 1) * cols] = got[p, :, first : first + cols].astype(f32)

    def place(first, cols, target):
        i = iota((128, 128), 0) - first
        return ((i >= 0) & (i < cols) & (iota((128, 128), 1) == target(i))).astype(bf16)

    def bc_place(p):
        return (iota((128, 256), 0) + p * bcs == iota((128, 256), 1)).astype(bf16) * (iota((128, 256), 0) < bcs).astype(bf16)

    mine = core_ref[0]
    k_sum = v_sum = jnp.zeros((x_.shape[1], 128), f32)
    halves = []
    for k in (0, 1):
        total = jnp.zeros((x_.shape[1], 256), f32)
        for p in range(G):
            total = total + mm(s_[k * G + p], bc_place(p), 1, 0)
        halves.append(total)
    bc_o[:, :256] = halves[0]
    bc_o[:, 256:] = halves[1]
    for p in range(G):
        own = s_[mine * G + p]
        k_sum = k_sum + mm(own, place(bcs, 2 * quarter, lambda i: (i // quarter) * (quarter * G) + p * quarter + i % quarter), 1, 0)
        v_sum = v_sum + mm(own, place(bcs + 2 * quarter, 2 * quarter, lambda i: i + p * 2 * quarter), 1, 0)
    k_o[...] = k_sum
    v_o[...] = v_sum


def mm(a, b, ca, cb):
    return lax.dot_general(a.astype(bf16), b.astype(bf16), (((ca,), (cb,)), ((), ())), preferred_element_type=f32)


def mm_pieces(a, b, ca, cb, pieces, right=False):
    rest, total = (b if right else a), None
    for _ in range(pieces):
        piece = rest.astype(bf16)
        rest = rest - piece.astype(f32)
        part = mm(a, piece, ca, cb) if right else mm(piece, b, ca, cb)
        total = part if total is None else total + part
    return total


def iota(dims, axis):
    return lax.broadcasted_iota(jnp.int32, dims, axis)


def soft(v):
    return jnp.maximum(v, 0.0) + jnp.log1p(jnp.exp(-jnp.abs(v)))


def sig(v):
    return 1.0 / (1.0 + jnp.exp(-v))


def rates_of(raw, bias, rates, heads):
    lane = iota((CHUNK, 128), 1)
    step = jnp.where(lane < heads, soft(raw + bias), 0.0)
    log_decay = -jnp.exp(rates) * step
    lower = (iota((CHUNK, CHUNK), 0) >= iota((CHUNK, CHUNK), 1)).astype(f32)
    return step, log_decay, mm_pieces(lower, log_decay, 1, 0, 3, True)


def pair_of(v, pair):
    left = iota((CHUNK, 128), 1) < P_SIZE
    return jnp.where(left, v[:, 2 * pair : 2 * pair + 1], v[:, 2 * pair + 1 : 2 * pair + 2])


def lanes(v, pair):
    return v[:, pair * 128 : (pair + 1) * 128]


def halves_of(a, b):
    return jnp.where(iota(a.shape, 1) < P_SIZE, a, b)


def head_means(v):
    same = (iota((128, 128), 0) // P_SIZE == iota((128, 128), 1) // P_SIZE).astype(f32) / P_SIZE
    return jnp.concatenate([mm_pieces(lanes(v, k), same, 1, 0, 2) for k in range(v.shape[1] // 128)], axis=1)


def head_sums(v, heads):
    chan = v.shape[1]
    pick = (iota((chan, 128), 0) // P_SIZE == iota((chan, 128), 1)).astype(f32)
    return mm_pieces(v, pick, 1, 0, 3)


def scale_rows(v, factor, heads):
    return jnp.concatenate(
        [v[h * P_SIZE : (h + 1) * P_SIZE] * factor[h : h + 1, :1] for h in range(heads)], axis=0
    )


def conv_of(pa_ref, taps_ref, starts, place, c, chan, first):
    block = pa_ref[pl.ds(pl.multiple_of(c * CHUNK + RIM - 8, 8), CHUNK + 8), first : first + chan]
    total = jnp.zeros((CHUNK, chan), f32)
    for lag in range(K):
        back = K - 1 - lag
        total = total + jnp.where(place - back >= starts, block[8 - back : 8 - back + CHUNK] * taps_ref[lag : lag + 1], 0.0)
    return total


def places_of(base_ref, c):
    return base_ref[0] + c * CHUNK + iota((CHUNK, 1), 0)


def weights_of(h, cs, cs_t, visible):
    span = cs[:, h : h + 1] - cs_t[h : h + 1]
    return jnp.where(visible, jnp.exp(jnp.where(visible, span, 0.0)), 0.0)


def visible_of(base_ref, c, starts, place):
    across = base_ref[0] + c * CHUNK + iota((CHUNK, CHUNK), 1)
    return (starts <= across) & (across <= place)


def decays_of(cs, starts, place):
    first = place[:1]
    decay_in = jnp.where(starts < first, jnp.exp(cs), 0.0)
    closing = jnp.where(starts[CHUNK - 1 :] <= place, jnp.exp(cs[CHUNK - 1 :] - cs), 0.0)
    return decay_in, closing


def scan_body(heads, base_ref, raw_ref, pa_ref, bc_ref, starts_ref, taps_ref, bias_ref, rates_ref,
              y_ref, cv_ref, enter_ref, reach_ref, state_out, through_out, state, through):
    c = pl.program_id(0)
    chan = heads * P_SIZE

    @pl.when(c == 0)
    def _():
        state[...] = jnp.zeros_like(state)
        through[...] = jnp.ones_like(through)

    starts, place = starts_ref[...], places_of(base_ref, c)
    raw = raw_ref[...]
    step, _, cs = rates_of(raw, bias_ref[...], rates_ref[...], heads)
    cs_t = cs.T
    cv = conv_of(pa_ref, taps_ref, starts, place, c, chan, 0)
    cv_ref[...] = cv
    x = cv * sig(cv)
    b_rows, c_rows = bc_ref[:, :N], bc_ref[:, N:]
    inter = mm(c_rows, b_rows, 1, 1)
    visible = visible_of(base_ref, c, starts, place)
    decay_in, closing = decays_of(cs, starts, place)
    ends = decay_in.T
    for k in range(heads // 2):
        driven = lanes(x, k) * pair_of(step, k)
        mixed = [mm(weights_of(2 * k + i, cs, cs_t, visible) * inter, driven, 1, 0) for i in (0, 1)]
        y_ref[:, k * 128 : (k + 1) * 128] = halves_of(*mixed)
        local = mm(driven * pair_of(closing, k), b_rows, 0, 0)
        at = pl.ds(k * 128, 128)
        old = state[at]
        enter_ref[0, at] = old
        both = jnp.concatenate(
            [old[i * P_SIZE : (i + 1) * P_SIZE] * ends[2 * k + i : 2 * k + i + 1, CHUNK - 1 :] for i in (0, 1)], axis=0
        )
        state[at] = both + local
    factor = jnp.broadcast_to(ends[:8, CHUNK - 1 :], (8, 128))
    reach_ref[0, :8] = through[...]
    reach_ref[0, 8:] = factor
    through[...] = through[...] * factor
    state_out[...] = state[...].astype(bf16)
    through_out[...] = through[...]


def gate_parts(y_scan, cv, z, skip, gain):
    x = cv * sig(cv)
    ssm = y_scan + skip * x
    s = sig(z)
    gated = ssm * (z * s)
    r = lax.rsqrt(head_means(gated * gated) + norm_eps)
    return x, ssm, s, gated, r


def gate_body(heads, base_ref, raw_ref, bc_ref, starts_ref, bias_ref, rates_ref, y_ref, cv_ref, enter_ref, reach_ref,
              before_ref, z_ref, skip_ref, gain_ref, low_ref, scan_ref):
    c = pl.program_id(0)
    chan = heads * P_SIZE
    starts, place = starts_ref[...], places_of(base_ref, c)
    raw = raw_ref[...]
    _, _, cs = rates_of(raw, bias_ref[...], rates_ref[...], heads)
    decay_in, _ = decays_of(cs, starts, place)
    state_in = enter_ref[0] + scale_rows(before_ref[...], reach_ref[0], heads)
    c_rows = bc_ref[:, N:]
    off = [mm(c_rows, state_in[k * 128 : (k + 1) * 128], 1, 1) * pair_of(decay_in, k) for k in range(heads // 2)]
    y_scan = y_ref[...] + jnp.concatenate(off, axis=1)
    scan_ref[...] = y_scan
    _, _, _, gated, r = gate_parts(y_scan, cv_ref[...], z_ref[...], skip_ref[...], gain_ref[...])
    low_ref[...] = (gated * r * gain_ref[...]).astype(bf16)


def gate_back_body(heads, chunks, base_ref, raw_ref, bc_ref, starts_ref, bias_ref, rates_ref, d_ref, scan_ref, cv_ref,
                   reach_ref, z_ref, skip_ref, gain_ref, dz_ref, dy_ref, leave_ref, tail_ref, state_out, gain_out, state, tail):
    c = chunks - 1 - pl.program_id(0)
    chan = heads * P_SIZE

    @pl.when(c == chunks - 1)
    def _():
        state[...] = jnp.zeros_like(state)
        tail[...] = jnp.ones_like(tail)
        gain_out[...] = jnp.zeros_like(gain_out)

    starts, place = starts_ref[...], places_of(base_ref, c)
    raw = raw_ref[...]
    _, _, cs = rates_of(raw, bias_ref[...], rates_ref[...], heads)
    decay_in, _ = decays_of(cs, starts, place)
    z = z_ref[...]
    x, ssm, s, gated, r = gate_parts(scan_ref[...], cv_ref[...], z, skip_ref[...], gain_ref[...])
    d = d_ref[...]
    gain_out[:1] += jnp.sum(d * gated * r, axis=0, keepdims=True)
    u = d * gain_ref[...]
    d_gated = r * u - gated * (r * r * r * head_means(u * gated))
    dz_ref[...] = (d_gated * ssm * (s * (1.0 + z * (1.0 - s)))).astype(bf16)
    dy = d_gated * (z * s)
    dy_ref[...] = dy
    c_rows = bc_ref[:, N:]
    leave_ref[0] = state[...]
    tail_ref[0] = tail[...]
    factor = reach_ref[0, 8:]
    local = [mm(lanes(dy, k) * pair_of(decay_in, k), c_rows, 0, 0) for k in range(heads // 2)]
    state[...] = scale_rows(state[...], factor, heads) + jnp.concatenate(local, axis=0)
    tail[...] = tail[...] * factor
    state_out[...] = state[...].astype(bf16)


def scan_back_body(heads, base_ref, raw_ref, bc_ref, starts_ref, bias_ref, rates_ref, dy_ref, cv_ref,
                   enter_ref, reach_ref, before_ref, leave_ref, tail_ref, after_ref, skip_ref,
                   gx_ref, dbc_ref, raw_out, rows_out):
    c = pl.program_id(0)
    chan = heads * P_SIZE

    @pl.when(c == 0)
    def _():
        rows_out[...] = jnp.zeros_like(rows_out)

    starts, place = starts_ref[...], places_of(base_ref, c)
    raw = raw_ref[...]
    step, log_decay, cs = rates_of(raw, bias_ref[...], rates_ref[...], heads)
    cs_t = cs.T
    visible = visible_of(base_ref, c, starts, place)
    decay_in, closing = decays_of(cs, starts, place)
    b_rows, c_rows = bc_ref[:, :N], bc_ref[:, N:]
    inter = mm(c_rows, b_rows, 1, 1)
    cv = cv_ref[...]
    s = sig(cv)
    x = cv * s
    dy = dy_ref[...]
    state_in = enter_ref[0] + scale_rows(before_ref[...], reach_ref[0], heads)
    d_state = leave_ref[0] + scale_rows(after_ref[...], tail_ref[0], heads)
    left = iota((CHUNK, 128), 1) < P_SIZE
    d_inter = jnp.zeros((CHUNK, CHUNK), f32)
    d_b = jnp.zeros((CHUNK, N), f32)
    d_c = jnp.zeros((CHUNK, N), f32)
    inside, outside, closes, drives = [], [], [], []
    for k in range(heads // 2):
        at = slice(k * 128, (k + 1) * 128)
        driven = (lanes(x, k) * pair_of(step, k)).astype(bf16)
        dyk = lanes(dy, k)
        dyb = dyk.astype(bf16)
        d_mixed, y_mixed = [], []
        for i in (0, 1):
            w = weights_of(2 * k + i, cs, cs_t, visible)
            mix = (w * inter).astype(bf16)
            half = jnp.where(left if i == 0 else ~left, dyb, jnp.zeros_like(dyb))
            d_inter = d_inter + w * mm(half, driven, 1, 1)
            d_mixed.append(mm(mix, dyb, 0, 0))
            y_mixed.append(mm(mix, driven, 1, 0))
        d_mix = halves_of(*d_mixed)
        close = pair_of(closing, k)
        d_close = mm(b_rows, d_state[at], 1, 1)
        closed = driven.astype(f32) * close
        enter = pair_of(decay_in, k)
        y_off = mm(c_rows, state_in[at], 1, 1) * enter
        d_c = d_c + mm(dyk * enter, state_in[at], 1, 0)
        d_b = d_b + mm(closed, d_state[at], 1, 0)
        inside.append(dyb.astype(f32) * halves_of(*y_mixed) - driven.astype(f32) * d_mix)
        outside.append(dyk * y_off)
        closes.append(closed * d_close)
        drives.append(d_mix + close * d_close)
    d_c = d_c + mm(d_inter, b_rows, 1, 0)
    d_b = d_b + mm(d_inter, c_rows, 0, 0)
    dbc_ref[:N] = d_b.astype(bf16).T
    dbc_ref[N:] = d_c.astype(bf16).T
    d_driven = jnp.concatenate(drives, axis=1)
    closes = head_sums(jnp.concatenate(closes, axis=1), heads)
    d_cs = head_sums(jnp.concatenate(inside, axis=1) + jnp.concatenate(outside, axis=1), heads) - closes
    kept = head_sums_t(d_state * state_in, heads)
    whole = decay_in[CHUNK - 1 :] * kept + jnp.sum(closes, axis=0, keepdims=True)
    upper = (iota((CHUNK, CHUNK), 0) <= iota((CHUNK, CHUNK), 1)).astype(f32)
    d_la = mm_pieces(upper, d_cs, 1, 0, 3, True) + whole
    d_step = head_sums(d_driven * x, heads)
    d_raw = (d_step - jnp.exp(rates_ref[...]) * d_la) * sig(raw + bias_ref[...])
    d_raw = jnp.where(iota((CHUNK, 128), 1) < heads, d_raw, 0.0)
    raw_out[...] = d_raw.astype(bf16)
    rows_out[:1] += jnp.sum(d_la * log_decay, axis=0, keepdims=True)
    rows_out[1:2] += jnp.sum(d_raw, axis=0, keepdims=True)
    rows_out[2:3] += jnp.sum(head_sums(dy * x, heads), axis=0, keepdims=True)
    wide = jnp.concatenate([pair_of(step, k) for k in range(heads // 2)], axis=1)
    gx_ref[...] = (d_driven * wide + skip_ref[...] * dy) * (s * (1.0 + cv * (1.0 - s)))


def unshuffled(v, back=False):
    quarter = HD // 2 // G
    i, j = (iota((HD, HD), 1), iota((HD, HD), 0)) if back else (iota((HD, HD), 0), iota((HD, HD), 1))
    half, rest = i // (HD // 2), i % (HD // 2)
    to = (rest // quarter) * 2 * quarter + half * quarter + rest % quarter
    return mm_pieces(v, (to == j).astype(f32), 1, 0, 2 if back else 1)


def keys_of(kv_ref, begin, size, tokens):
    plane, at = begin // tokens, pl.ds(pl.multiple_of(begin % tokens, 128), size)
    half = kv_ref.shape[2] // 2
    keys = jnp.concatenate([kv_ref[p, plane, :half, at] for p in range(G)], axis=0)
    values = jnp.concatenate([kv_ref[p, plane, half:, at] for p in range(G)], axis=0)
    return plane, at, keys, values


def seen_of(begin, size, starts, place):
    at = begin + iota((starts.shape[0], size), 1)
    return (at >= starts) & (at <= place)


def attend_body(size, tokens, base_ref, first_ref, q_ref, starts_ref, cos_ref, sin_ref, kv_ref,
                query_ref, low_ref, out_ref, mass_ref):
    i = pl.program_id(0)
    rows = q_ref.shape[0]
    v = q_ref[...]
    turned = (v * cos_ref[...] - pltpu.roll(v, HD // 2, 1) * sin_ref[...]) * HD ** (-0.5)
    query = unshuffled(turned.astype(bf16).astype(f32)).astype(bf16)
    query_ref[...] = query
    starts = starts_ref[...]
    place = base_ref[0] + i * rows + iota((rows, 1), 0)

    def step(n, carry):
        peak, mass, total = carry
        begin = n * size
        _, _, keys, values = keys_of(kv_ref, begin, size, tokens)
        scores = jnp.where(seen_of(begin, size, starts, place), mm(query, keys, 1, 0), -1e30)
        new = jnp.maximum(peak, jnp.max(scores, axis=1, keepdims=True))
        probs = jnp.where(scores > -1e29, jnp.exp(scores - new), 0.0)
        keep = jnp.exp(peak - new)
        return new, mass * keep + jnp.sum(probs, axis=1, keepdims=True), total * keep + mm(probs, values, 1, 1)

    begin = first_ref[i] // size
    end = (base_ref[0] + (i + 1) * rows - 1) // size + 1
    start = (jnp.full((rows, 1), -1e30, f32), jnp.zeros((rows, 1), f32), jnp.zeros((rows, HD), f32))
    peak, mass, total = lax.fori_loop(begin, end, step, start)
    attended = total / mass
    out_ref[...] = attended
    low_ref[...] = attended.astype(bf16)
    mass_ref[...] = peak + jnp.log(mass)


def attend_back_body(size, tokens, base_ref, first_ref, query_ref, starts_ref, cos_ref, sin_ref, kv_ref, d_ref, out_ref, mass_ref,
                     dq_ref, dkv_ref, d_keys, d_values):
    i = pl.program_id(0)
    rows = query_ref.shape[0]

    @pl.when(i == 0)
    def _():
        d_keys[...] = jnp.zeros_like(d_keys)
        d_values[...] = jnp.zeros_like(d_values)

    query = query_ref[...]
    d_low = d_ref[...].astype(bf16)
    balance = jnp.sum(d_low.astype(f32) * out_ref[...], axis=1, keepdims=True)
    query_t, d_t = query.T, d_low.T
    starts, mass = starts_ref[...], mass_ref[...]
    place = base_ref[0] + i * rows + iota((rows, 1), 0)

    def step(n, total):
        begin = n * size
        plane, at, keys, values = keys_of(kv_ref, begin, size, tokens)
        seen = seen_of(begin, size, starts, place)
        probs = jnp.where(seen, jnp.exp(jnp.where(seen, mm(query, keys, 1, 0) - mass, 0.0)), 0.0)
        d_scores = (probs * (mm(d_low, values, 1, 0) - balance)).astype(bf16)
        d_keys[plane, :, at] += mm(query_t, d_scores, 1, 0)
        d_values[plane, :, at] += mm(d_t, probs, 1, 0)
        return total + mm(d_scores, keys, 1, 1)

    begin = first_ref[i] // size
    end = (base_ref[0] + (i + 1) * rows - 1) // size + 1
    d_query = unshuffled(lax.fori_loop(begin, end, step, jnp.zeros((rows, HD), f32)), True)
    d_query = (d_query * cos_ref[...] + pltpu.roll(d_query, HD // 2, 1) * sin_ref[...]) * HD ** (-0.5)
    dq_ref[...] = d_query.astype(bf16)

    @pl.when(i == pl.num_programs(0) - 1)
    def _():
        half = dkv_ref.shape[2] // 2

        def give(plane, carry):
            for p in range(G):
                dkv_ref[p, plane, :half] = d_keys[plane, p * half : (p + 1) * half].astype(bf16)
                dkv_ref[p, plane, half:] = d_values[plane, p * half : (p + 1) * half].astype(bf16)
            return carry

        lax.fori_loop(0, dkv_ref.shape[1], give, 0)


def ffn_units(part, second, low, w_ref):
    gate = mm(second, w_ref[:, :part], 1, 0)
    up = mm(second, w_ref[:, part : 2 * part], 1, 0)
    d_act = mm(low, w_ref[:, 2 * part :], 1, 0)
    s = sig(gate)
    silu = gate * s
    return jnp.concatenate(
        [(d_act * up * (s * (1.0 + gate * (1.0 - s)))).astype(bf16), (d_act * silu).astype(bf16), (silu * up).astype(bf16)],
        axis=1,
    )


def ffn_body(part, second_ref, low_ref, w_ref, *refs):
    *done, h_ref, layer_ref, back_ref = refs
    h = ffn_units(part, second_ref[...], low_ref[...], w_ref)
    h_ref[...] = h
    two = 2 * part
    layer = mm(h[:, two:], w_ref[:, two:], 1, 1)
    back = mm(h[:, :two], w_ref[:, :two], 1, 1)
    if done:
        layer = layer + done[0][...].astype(f32)
        back = back + done[1][...].astype(f32)
    layer_ref[...] = layer.astype(bf16)
    back_ref[...] = back.astype(bf16)


def token_grad_body(widths, *refs):
    count = len(widths)
    tokens, narrow, out_ref, turned = refs[:count], refs[count : 2 * count], refs[2 * count], refs[2 * count + 1]
    at = [sum(widths[:i]) for i in range(count)]

    @pl.when(pl.program_id(0) == 0)
    def _():
        for first, n, ref in zip(at, widths, narrow):
            turned[first : first + n] = ref[...].T

    for first, n, ref in zip(at, widths, tokens):
        rows = ref[ref.shape[0] - turned.shape[1] :]
        out_ref[:, first : first + n] = mm(turned[first : first + n], rows, 1, 0).astype(bf16).T


def finish_body(chunks, chan, base_ref, pa_ref, gx_ref, rim_x, g_bc, rim_bc, dkv, starts_ref, taps_ref, cos_ref, sin_ref,
                out_ref, taps_out):
    c = pl.program_id(0)
    wide = chan + 128

    @pl.when(c == 0)
    def _():
        taps_out[...] = jnp.zeros_like(taps_out)

    rows = g_bc.shape[0]
    here_ = pl.ds(pl.multiple_of(c * CHUNK, CHUNK), CHUNK)
    last = c == chunks - 1
    ahead_at = jnp.minimum((c + 1) * CHUNK, (chunks - 1) * CHUNK)
    next_ = pl.ds(pl.multiple_of(ahead_at, CHUNK), CHUNK)

    def put(first):
        return (iota((rows, 128), 1) == iota((rows, 128), 0) + first).astype(f32)

    bc_here = mm_pieces(g_bc[:, here_], put(0), 0, 0, 3)
    bc_next = mm_pieces(jnp.where(last, rim_bc[...], g_bc[:, next_]), put(0), 0, 0, 3)[:8]
    gx_next = jnp.where(last, rim_x[:8], gx_ref[pl.ds(pl.multiple_of(ahead_at, 8), 8)])
    longer = jnp.concatenate([
        jnp.concatenate([gx_ref[here_], bc_here], axis=1), jnp.concatenate([gx_next, bc_next], axis=1)
    ], axis=0)
    starts = starts_ref[pl.ds(pl.multiple_of(c * CHUNK, 8), CHUNK + 8)]
    place = places_of(base_ref, c)
    block = pa_ref[pl.ds(pl.multiple_of(c * CHUNK + RIM - 8, 8), CHUNK + 8), :wide]
    total = jnp.zeros((CHUNK, wide), f32)
    for lag in range(K):
        ahead = K - 1 - lag
        seen = place >= starts[ahead : ahead + CHUNK]
        total = total + jnp.where(seen, longer[ahead : ahead + CHUNK], 0.0) * taps_ref[lag : lag + 1]
        valid = place - ahead >= starts[:CHUNK]
        part = jnp.where(valid, longer[:CHUNK] * block[8 - ahead : 8 - ahead + CHUNK], 0.0)
        taps_out[lag : lag + 1] += jnp.sum(part, axis=0, keepdims=True)
    quarter = cos_ref.shape[0]
    kv = dkv[:, here_]
    a, b = kv[:quarter], kv[quarter : 2 * quarter]
    cosine, sine = cos_ref[:, here_], sin_ref[:, here_]
    kv = jnp.concatenate([a * cosine + b * sine, b * cosine - a * sine, kv[2 * quarter :]], axis=0)
    out_ref[:, :chan] = total[:, :chan].astype(bf16)
    out_ref[:, chan:wide] = (total[:, chan:] + mm(kv, put(rows), 0, 0)).astype(bf16)


def prepare_body(chan, base_ref, pa_ref, starts_ref, taps_ref, cos_ref, sin_ref, bc_ref, slope_ref, kv_ref):
    c = pl.program_id(0)
    cv = conv_of(pa_ref, taps_ref, starts_ref[...], places_of(base_ref, c), c, 128, chan).T
    rows, quarter = bc_ref.shape[0], cos_ref.shape[0]
    cv = cv[:rows]
    s = sig(cv)
    bc_ref[...] = (cv * s).astype(bf16)
    slope_ref[...] = s * (1.0 + cv * (1.0 - s))
    kv = pa_ref[pl.ds(pl.multiple_of(c * CHUNK + RIM, 16), CHUNK), chan : chan + 128].T[rows:]
    a, b = kv[:quarter], kv[quarter : 2 * quarter]
    cosine, sine = cos_ref[...], sin_ref[...]
    kv_ref[:quarter] = (a * cosine - b * sine).astype(bf16)
    kv_ref[quarter : 2 * quarter] = (b * cosine + a * sine).astype(bf16)
    kv_ref[2 * quarter :] = kv[2 * quarter :].astype(bf16)


def back_part_body(da_ref, dz_ref, raw_ref, wa_ref, wz_ref, ws_ref, out_ref):
    total = mm(da_ref[...], wa_ref[...], 1, 1) + mm(dz_ref[...], wz_ref[...], 1, 1) + mm(raw_ref[...], ws_ref[...], 1, 0)
    out_ref[...] = total.astype(bf16)


def head_sums_t(v, heads):
    column = jnp.sum(v, axis=1, keepdims=True)
    pick = (iota((v.shape[0], 128), 0) // P_SIZE == iota((v.shape[0], 128), 1)).astype(f32)
    return jnp.sum(column * pick, axis=0, keepdims=True)


def chunked(body, chunks, outs, out_specs, ins, in_specs, scratch=(), mib=16, near=(), keep=()):
    ins = [
        pltpu.with_memory_space_constraint(v, pltpu.HBM) if s.memory_space is None and v.size > 20000 and i not in near else v
        for i, (v, s) in enumerate(zip(ins, in_specs))
    ]
    if isinstance(outs, tuple):
        outs = tuple(
            (pltpu.VMEM if i in keep else pltpu.HBM)(v.shape, v.dtype) if v.size > 20000 else v for i, v in enumerate(outs)
        )
    else:
        outs = (pltpu.VMEM if keep else pltpu.HBM)(outs.shape, outs.dtype)
    return pl.pallas_call(
        body,
        grid=(chunks,),
        out_shape=outs,
        in_specs=in_specs,
        out_specs=out_specs,
        scratch_shapes=list(scratch),
        cost_estimate=pl.CostEstimate(flops=2_000_000_000, bytes_accessed=40_000_000, transcendentals=0),
        compiler_params=pltpu.CompilerParams(vmem_limit_bytes=mib * 2**20),
    )(*ins)


def dot(a, b, ca, cb):
    return lax.dot_general(a, b, (((ca,), (cb,)), ((), ())), preferred_element_type=f32)


def exact(text, *operands):
    return jnp.einsum(text, *operands, precision=highest, preferred_element_type=f32)


def d_silu(v):
    s = jax.nn.sigmoid(v)
    return s * (1.0 + v * (1.0 - s))


def shifted(block, axis, distance):
    count = lax.axis_size(axis)
    route = [(i - distance, i) for i in range(count) if 0 <= i - distance < count]
    return lax.ppermute(block, axis, route)


def rope_tables(offsets, first, count):
    half = HD // 2
    index = (first + jnp.arange(count)).astype(f32)
    freqs = rope_base ** (-2.0 * index / HD)
    angles = offsets.astype(f32)[:, None] * freqs[None, :]
    return jnp.cos(angles), jnp.sin(angles)


def turn(v, cosine, sine):
    half = v.shape[-1] // 2
    a, b = v[:, :half], v[:, half:]
    return jnp.concatenate([a * cosine - b * sine, b * cosine + a * sine], axis=-1)


def conv_rows(padded, taps, starts, places):
    length = starts.shape[0]
    total = jnp.zeros((length, padded.shape[1]), f32)
    for lag in range(K):
        back = K - 1 - lag
        valid = (places - back >= starts)[:, None]
        total = total + jnp.where(valid, padded[RIM - back : RIM - back + length] * taps[lag][None, :], 0.0)
    return total


def mixer_row(v):
    return v.reshape(1, -1)


def on_device(
    layer_input, doc_start, mixer_gain, ffn_gain,
    z_weight, x_weight, bc_weight, dt_weight, q_weight, k_weight, v_weight,
    o_weight, out_weight, gate_weight, up_weight, down_weight,
    conv_inner, conv_state, decay_log, dt_bias, skip_coef, ssm_gain, cotangent,
):
    tokens, width = layer_input.shape
    rows = z_weight.shape[0]
    planes = lax.axis_size("z")
    cores = lax.axis_size("head")
    zi, pi, hi = (lax.axis_index(a) for a in ("z", "p", "head"))
    T = tokens * G
    total_tokens = T * planes
    offset = zi * T
    places = offset + jnp.arange(T, dtype=jnp.int32)
    own = tokens // cores
    heads = decay_log.shape[0] // G
    chan = heads * P_SIZE
    bcs = 2 * N // cores // G
    quarter_half = HD // 2 // G

    def my_slice(v, size, index, axis):
        return lax.dynamic_slice_in_dim(v, index * size, size, axis)

    taps_inner = my_slice(conv_inner, chan, pi, 1)
    taps_state = my_slice(conv_state, bcs, hi * G + pi, 1)
    rates = my_slice(decay_log, heads, pi, 0)
    bias = my_slice(dt_bias, heads, pi, 0)
    skip = my_slice(skip_coef, heads, pi, 0)
    gain_s = my_slice(ssm_gain, chan, pi, 0)

    def cut(w):
        return w.reshape(rows, G, -1)

    bc_mine = lax.dynamic_slice_in_dim(bc_weight, hi * (2 * N // cores), 2 * N // cores, 1)
    k_cut = jnp.moveaxis(k_weight.reshape(rows, 2, G, quarter_half), 2, 1).reshape(rows, G, -1)
    small_w = jnp.concatenate([cut(bc_mine), k_cut, cut(v_weight)], axis=2)
    small_w = jnp.moveaxis(small_w, 1, 0)
    a_cols = chan + 128
    own_steps = jnp.pad(dt_weight.T.reshape(G, heads, rows), ((0, 0), (0, 16 - heads), (0, 0)))

    def gather(w):
        return lax.all_gather(w, "z", axis=0, tiled=True)

    exchange_sems = lambda n: [DMA((3, n)), DMA((3, n)), DMA((n,))]
    wa = gather(call(
        exchange_a_body, 0, shape((G * rows, a_cols), bf16), HBM,
        (x_weight, small_w), [HBM] * 2, exchange_sems(2),
    ))

    def half(v):
        return lax.dynamic_slice_in_dim(v, hi * own, own, 0)

    x_own, cot_own = half(layer_input), half(cotangent)
    r1 = lax.rsqrt(jnp.mean(x_own * x_own, axis=-1, keepdims=True) + norm_eps)
    first_own = (x_own * r1 * mixer_gain).astype(bf16)
    wb = gather(call(
        exchange_b_body, 9, shape((G * rows, 2 * (chan + HD)), bf16), HBM,
        (z_weight, q_weight, out_weight, o_weight), [HBM] * 4, exchange_sems(4),
    ))
    first_rim, docs, steps = call(
        functools.partial(start_body, planes), 1,
        (shape((RIM + T, width), bf16), shape((planes, G, 8, tokens), jnp.int32), shape((planes, G, 16, rows), bf16)), (HBM,) * 3,
        (first_own, jnp.broadcast_to(doc_start[None], (8, tokens)), own_steps), [VMEM] * 3,
        [DMA(()), DMA(()), DMA((2, 3)), DMA((2, 3)), DMA((2, planes - 1)), DMA((2, planes - 1)), DMA((2,))] + Spread.sems, us=25,
    )
    w_step = jnp.pad(steps.transpose(2, 0, 1, 3).reshape(16, width), ((0, 112), (0, 0)))
    w_zqob = wb
    wz, wb = wb[:, : chan + HD], wb[:, chan + HD :]
    first = first_rim[RIM:]
    all_starts = docs[:, :, 0].reshape(-1)
    starts = lax.dynamic_slice_in_dim(all_starts, offset, T, 0)

    def line_sum(grad):
        return lax.psum_scatter(grad, "z", scatter_dimension=0, tiled=True)

    raw = dot(first, w_step, 1, 1)
    pa = dot(first_rim, wa, 1, 0)
    zq = dot(first, wz, 1, 0)
    offsets = places - starts
    cos_q, sin_q = rope_tables(offsets, 0, HD // 2)
    cos_row = jnp.concatenate([cos_q, cos_q], axis=1)
    sin_row = jnp.concatenate([sin_q, -sin_q], axis=1)
    cos_k, sin_k = (v.T for v in rope_tables(offsets, pi * quarter_half, quarter_half))
    kvr = 4 * quarter_half
    L = CHUNK
    nc = T // L
    base = jnp.full((1,), offset, jnp.int32)
    starts_col = starts[:, None]
    smem = pl.BlockSpec(memory_space=pltpu.SMEM)
    taps_pair = jnp.concatenate([taps_state, jnp.zeros((K, 128 - bcs), f32)], axis=1)
    along = lambda rows_: pl.BlockSpec((rows_, L), lambda c: (0, c))
    bc_low, slope_bc, kv_own = chunked(
        functools.partial(prepare_body, chan), nc,
        (shape((bcs, T), bf16), shape((bcs, T), f32), shape((kvr, T), bf16)), (along(bcs), along(bcs), along(kvr)),
        (base, pa, starts_col, taps_pair, cos_k, sin_k),
        [smem, pl.BlockSpec(pa.shape, lambda c: (0, 0)), pl.BlockSpec((L, 1), lambda c: (c, 0)), pl.BlockSpec((K, 128), lambda c: (0, 0)),
         along(quarter_half), along(quarter_half)],
    )
    line_sems = [DMA((planes - 1,)), DMA((planes - 1,))]
    units = gate_weight.shape[1] // G
    parts = (units - 128, 128)
    bc_t, kv_line, w1, w2 = call(
        functools.partial(spread_body, planes), 2,
        (shape((2 * N, T), bf16), shape((planes, kvr, T), bf16)) + tuple(shape((G * rows, 3 * n), bf16) for n in parts), (HBM,) * 4,
        (bc_low, kv_own, gate_weight, up_weight, down_weight), [HBM] * 5,
        line_sems + [DMA(())] + exchange_sems(6) + Spread.sems, us=28,
    )
    w1, w2 = gather(w1), gather(w2)
    bc_all = bc_t.T


    def row128(v):
        return jnp.pad(v, (0, 128 - v.shape[0]))[None]

    bias_row, rates_row = row128(bias), row128(rates)
    skip_row, gain_row = jnp.repeat(skip, P_SIZE)[None], gain_s[None]

    def specs(turned=False):
        at = (lambda c: nc - 1 - c) if turned else (lambda c: c)
        return (
            lambda cols: pl.BlockSpec((L, cols), lambda c: (at(c), 0)),
            lambda *dims: pl.BlockSpec(dims, lambda c: (0,) * len(dims)),
            lambda rows, cols: pl.BlockSpec((1, rows, cols), lambda c: (at(c), 0, 0)),
        )

    tile, fixed, stack = specs()
    pa_spec = fixed(*pa.shape)
    y_diag, cv_x, enter, reach, state, through = chunked(
        functools.partial(scan_body, heads), nc,
        (shape((T, chan), f32), shape((T, chan), f32), shape((nc, chan, N), f32), shape((nc, 16, 128), f32),
         shape((chan, N), bf16), shape((8, 128), f32)),
        (tile(chan), tile(chan), stack(chan, N), stack(16, 128), fixed(chan, N), fixed(8, 128)),
        (base, raw, pa, bc_all, starts_col, taps_inner, bias_row, rates_row),
        [smem, tile(128), pa_spec, tile(2 * N), tile(1), fixed(K, chan), fixed(1, 128), fixed(1, 128)],
        [pltpu.VMEM((chan, N), f32), pltpu.VMEM((8, 128), f32)],
    )

    def entering(upward, states, factors):
        total = jnp.zeros((chan, N), f32)
        for d in reversed(range(1, planes)):
            there = (zi - d >= 0) if upward else (zi + d < planes)
            factor = jnp.repeat(factors[d - 1, :heads, :1], P_SIZE, axis=0)
            total = jnp.where(there, total * factor + states[d - 1].astype(f32), total)
        return total

    state_shapes = (shape((planes - 1, chan, N), bf16), shape((planes - 1, 8, 128), f32))
    states, factors, kv_all, out_low = call(
        functools.partial(up_body, planes), 3, state_shapes + (shape((G * planes, kvr, T), bf16), shape((T, width), bf16)), (HBM,) * 4,
        (state, through, kv_line, cot_own.astype(bf16)), [HBM] * 4, line_sems * 2 + Spread.sems * 2, us=38,
    )
    before = entering(True, states, factors)
    ssm_low, y_scan = chunked(
        functools.partial(gate_body, heads), nc,
        (shape((T, chan), bf16), shape((T, chan), f32)), (tile(chan), tile(chan)),
        (base, raw, bc_all, starts_col, bias_row, rates_row, y_diag, cv_x, enter, reach, before, zq, skip_row, gain_row),
        [smem, tile(128), tile(2 * N), tile(1), fixed(1, 128), fixed(1, 128), tile(chan), tile(chan), stack(chan, N),
         stack(16, 128), fixed(chan, N), tile(chan), fixed(1, chan), fixed(1, chan)],
    )

    size = math.gcd(512, T)
    qrows = math.gcd(256, T)
    kv_all = kv_all.reshape(G, planes, kvr, T)
    firsts = starts.reshape(-1, qrows)[:, 0]

    def column(at, cols):
        return pl.BlockSpec((qrows, cols), lambda i: (i, at))

    kv_spec = pl.BlockSpec((G, planes, kvr, T), lambda i: (0, 0, 0, 0))
    at_q = chan // HD
    query, att_low, attended, log_mass = chunked(
        functools.partial(attend_body, size, T), T // qrows,
        (shape((T, HD), bf16), shape((T, HD), bf16), shape((T, HD), f32), shape((T, 1), f32)),
        (column(0, HD), column(0, HD), column(0, HD), column(0, 1)),
        (base, firsts, zq, starts_col, cos_row, sin_row, kv_all),
        [smem, smem, column(at_q, HD), column(0, 1), column(0, HD), column(0, HD), kv_spec], mib=12 + 2 * planes,
    )

    both_low = jnp.concatenate([ssm_low, att_low], axis=1)
    collect = Collect.scratch(own, width) + [pltpu.VMEM((own, width), bf16)] + Spread.sems
    hidden, second = call(
        hidden_body, 4, (shape((own, width), f32), shape((T, width), bf16)), (VMEM, HBM),
        (dot(both_low, wb, 1, 1).astype(bf16), x_own, mixer_row(ffn_gain)), [VMEM] * 3, collect, us=50,
    )
    ftile = math.gcd(256, T)

    def rows_spec(cols):
        return pl.BlockSpec((ftile, cols), lambda i: (i, 0))

    def all_spec(v):
        return pl.BlockSpec(v.shape, lambda i: (0,) * len(v.shape))

    def ffn(w, *done):
        wide = w.shape[1]
        return chunked(
            functools.partial(ffn_body, wide // 3), T // ftile,
            (shape((T, wide), bf16), shape((T, width), bf16), shape((T, width), bf16)),
            (rows_spec(wide), rows_spec(width), rows_spec(width)),
            (second, out_low, w) + done, [rows_spec(width), rows_spec(width), all_spec(w)] + [rows_spec(width)] * len(done), mib=36, keep=(1, 2) if done else (),
        )

    def token_grads(*groups):
        tile_d = math.gcd(512, width)
        widths = tuple(n for *_, n in groups)
        return chunked(
            functools.partial(token_grad_body, widths), width // tile_d, shape((width, sum(widths)), bf16),
            pl.BlockSpec((tile_d, sum(widths)), lambda i: (i, 0)),
            tuple(g[0] for g in groups) + tuple(g[1] for g in groups),
            [pl.BlockSpec((g[0].shape[0], tile_d), lambda i: (0, i)) for g in groups]
            + [pl.BlockSpec((T, n), lambda i, at=at: (0, at)) for _, _, at, n in groups],
            [pltpu.VMEM((sum(widths), T), bf16)], mib=32,
        )

    def ffn_grads(h, *more):
        n = h.shape[1] // 3
        return token_grads((second, h, 0, 2 * n), (out_low, h, 2, n), *more)

    h1, part_l, part_c = ffn(w1)
    grad_1 = ffn_grads(h1)
    w2, grad_1 = lax.optimization_barrier((w2, grad_1))
    sum_1 = line_sum(grad_1)
    h2, part_l, part_c = ffn(w2, part_l, part_c)
    d_hidden, grad_ffn, branch = call(
        branch_body, 5, (shape((own, width), f32), shape((8, width), f32), shape((T, width), bf16)), (VMEM, VMEM, HBM),
        (part_c, hidden, cot_own, mixer_row(ffn_gain)), [VMEM] * 4, collect, us=50,
    )
    h2, branch = lax.optimization_barrier((h2, branch))
    grad_2b = ffn_grads(h2, (branch, both_low, 0, chan + HD))
    d_both = dot(branch, wb, 1, 0)

    back, _, back_stack = specs(True)
    dz_low, dy, leave, tail, g_state, grad_gain_s = chunked(
        functools.partial(gate_back_body, heads, nc), nc,
        (shape((T, chan), bf16), shape((T, chan), f32), shape((nc, chan, N), f32), shape((nc, 8, 128), f32),
         shape((chan, N), bf16), shape((8, chan), f32)),
        (back(chan), back(chan), back_stack(chan, N), back_stack(8, 128), fixed(chan, N), fixed(8, chan)),
        (base, raw, bc_all, starts_col, bias_row, rates_row, d_both, y_scan, cv_x, reach, zq, skip_row, gain_row),
        [smem, back(128), back(2 * N), back(1), fixed(1, 128), fixed(1, 128), back(chan), back(chan), back(chan),
         back_stack(16, 128), back(chan), fixed(1, chan), fixed(1, chan)],
        [pltpu.VMEM((chan, N), f32), pltpu.VMEM((8, 128), f32)],
    )
    grad_2b, sum_1, dz_low = lax.optimization_barrier((grad_2b, sum_1, dz_low))
    sum_2 = line_sum(grad_2b)

    dq_low, dkv = chunked(
        functools.partial(attend_back_body, size, T), T // qrows,
        (shape((T, HD), bf16), shape((G, planes, kvr, T), bf16)), (column(0, HD), kv_spec),
        (base, firsts, query, starts_col, cos_row, sin_row, kv_all, d_both, attended, log_mass),
        [smem, smem, column(0, HD), column(0, 1), column(0, HD), column(0, HD), kv_spec, column(at_q, HD), column(0, HD),
         column(0, 1)],
        [pltpu.VMEM((planes, HD, T), f32), pltpu.VMEM((planes, HD, T), f32)], mib=14 + 3 * planes,
    )
    dzq_low = jnp.concatenate([dz_low, dq_low], axis=1)
    grad_z = dot(first, dzq_low, 0, 0).astype(bf16)
    g_state, sum_1, grad_z = lax.optimization_barrier((g_state, sum_1, grad_z))
    states, factors, dkv, layer_own = call(
        functools.partial(down_body, planes), 6, state_shapes + (shape((planes * kvr, T), bf16), shape((own, width), f32)),
        (HBM,) * 2 + (VMEM,) * 2, (g_state, through, dkv.reshape(-1, T), part_l, hidden), [HBM] * 2 + [VMEM] * 3,
        line_sems * 2 + Collect.scratch(planes * kvr, T, False) + Collect.scratch(own, width), us=45, mib=14 + 2 * planes,
    )
    states, grad_z = lax.optimization_barrier((states, grad_z))
    sum_z = line_sum(grad_z)
    after = entering(False, states, factors)
    gx, d_bc_all, d_raw, grad_rows = chunked(
        functools.partial(scan_back_body, heads), nc,
        (shape((T, chan), f32), shape((2 * N, T), bf16), shape((T, 128), bf16), shape((8, 128), f32)),
        (tile(chan), pl.BlockSpec((2 * N, L), lambda c: (0, c)), tile(128), fixed(8, 128)),
        (base, raw, bc_all, starts_col, bias_row, rates_row, dy, cv_x, enter, reach, before, leave, tail, after, skip_row),
        [smem, tile(128), tile(2 * N), tile(1), fixed(1, 128), fixed(1, 128), tile(chan), tile(chan),
         stack(chan, N), stack(16, 128), fixed(chan, N), stack(chan, N), stack(8, 128), fixed(chan, N), fixed(1, chan)],
    )

    d_bc_t, sum_2 = lax.optimization_barrier((d_bc_all, sum_2))
    g_bc, rim_bc, rim_x, dkv, got_1, got_2 = call(
        functools.partial(back_body, planes), 7,
        (shape((bcs, T), f32), shape((bcs, 128), f32), shape((RIM, chan), f32), shape((kvr, T), f32))
        + tuple(shape((G, rows, v.shape[1]), bf16) for v in (h1, h2)), (VMEM,) * 4 + (HBM,) * 2,
        (d_bc_t, dkv.reshape(planes, kvr, T), slope_bc, gx, sum_1, sum_2), [VMEM] * 3 + [HBM] * 3,
        [pltpu.VMEM((G * bcs, T), bf16), pltpu.VMEM((3, bcs, T), bf16), pltpu.VMEM((3, bcs, T), bf16),
         pltpu.VMEM((planes - 1, kvr, T), bf16), pltpu.VMEM((bcs, T), f32), DMA(()), DMA(()), DMA((3,)), DMA((3,)),
         DMA((planes - 1,)), DMA((planes - 1,)), DMA((2,)), DMA((2,)), DMA((2, 3)), DMA((2, 3)), DMA((2,))], us=30,
    )
    strip = min(64, rows)

    def got(v):
        return pl.BlockSpec((v.shape[0], strip, v.shape[2]), lambda c: (0, c, 0))

    def given(cols):
        return pl.BlockSpec((strip, cols), lambda c: (c, 0))

    ffn_out = chunked(
        give_ffn_body, rows // strip, (shape((rows, G * units), f32),) * 3, (given(G * units),) * 3,
        (got_1, got_2), [got(got_1), got(got_2)], mib=24,
    )
    gx, *ffn_out = lax.optimization_barrier((gx, *ffn_out))
    starts_long = jnp.concatenate([all_starts, jnp.full((8,), total_tokens, jnp.int32)])
    starts_long = lax.dynamic_slice_in_dim(starts_long, offset, T + 8, 0)[:, None]
    taps_both = jnp.concatenate([taps_inner, taps_pair], axis=1)
    da_low, grad_taps = chunked(
        functools.partial(finish_body, nc, chan), nc,
        (shape((T, a_cols), bf16), shape((8, chan + 128), f32)), (tile(a_cols), fixed(8, chan + 128)),
        (base, pa, gx, rim_x, g_bc, rim_bc, dkv, starts_long, taps_both, cos_k, sin_k),
        [smem, pa_spec, fixed(T, chan), fixed(RIM, chan), fixed(bcs, T), fixed(bcs, 128), fixed(kvr, T),
         fixed(T + 8, 1), fixed(K, chan + 128), fixed(quarter_half, T), fixed(quarter_half, T)], near=(3, 4, 5, 6),
    )
    grad_a = dot(first, da_low, 0, 0).astype(bf16)
    grad_a, sum_z = lax.optimization_barrier((grad_a, sum_z))
    sum_a = line_sum(grad_a)
    lane = width // 4
    part_a = chunked(
        back_part_body, T // ftile, shape((T, width), bf16), rows_spec(width), (da_low, dzq_low, d_raw, wa, w_zqob, w_step),
        [rows_spec(v.shape[1]) for v in (da_low, dzq_low, d_raw)] + [all_spec(v) for v in (wa, wz, w_step)], mib=28, keep=(0,),
    )
    grad_step = dot(d_raw, first, 0, 0)[:16].reshape(16, planes, G, rows).transpose(1, 2, 0, 3)
    groups = (shape((G, rows, chan + HD), bf16),) * 2
    grad_input, layer_out, mine, got_z, got_b = call(
        final_body, 8,
        (shape((tokens, width), f32), shape((tokens, width), f32), shape((RIM, lane), f32)) + groups, (HBM, HBM, VMEM, HBM, HBM),
        (part_a, x_own, d_hidden, layer_own, mixer_row(mixer_gain), grad_taps, grad_gain_s, grad_rows, grad_ffn, sum_z, sum_2),
        [VMEM] * 9 + [HBM] * 2,
        Collect.scratch(own, width)
        + [pltpu.VMEM((own, width), f32), pltpu.VMEM((8, width), f32), DMA((2,)), DMA((2,)), DMA((2,)),
           DMA((2, 3)), DMA((2, 3)), DMA((2,))], us=40,
    )

    got_x, got_s, sums, got_t = call(
        functools.partial(last_body, planes), 10,
        (shape((G, rows, chan), bf16), shape((2 * G, rows, a_cols - chan), bf16), shape((2 * G * RIM, lane), f32),
         shape((G, 16, rows), f32)), (HBM,) * 4, (sum_a, mine, grad_step), [HBM, VMEM, VMEM],
        [pltpu.VMEM((RIM, lane), f32), pltpu.VMEM((planes - 1, RIM, lane), f32), pltpu.VMEM((G, 16, rows), f32),
         pltpu.VMEM((planes - 1, G, 16, rows), f32), DMA((3,)), DMA((3,)), DMA((2 * G,)), DMA((2 * G,)),
         DMA((2,)), DMA((planes - 1,)), DMA((planes - 1,)), DMA((planes - 1,)), DMA((planes - 1,)), DMA((3,)), DMA((3,)), DMA(()),
         DMA((2 * G,)), DMA((2 * G,)), DMA(())],
    )
    widths = [w.shape[1] for w in (
        z_weight, x_weight, bc_weight, q_weight, k_weight, v_weight, o_weight, out_weight,
    )]
    gathered = (got_z, got_b, got_x, got_s)
    steps_ = rows // strip
    moved = pl.BlockSpec((tokens // steps_, width), lambda c: (c, 0))
    *weights, layer_out, grad_input = chunked(
        functools.partial(give_body, (bcs, quarter_half)), steps_,
        tuple(shape((rows, w), f32) for w in widths) + (shape((tokens, width), f32),) * 2,
        tuple(given(w) for w in widths) + (moved, moved),
        (jnp.full((1,), hi, jnp.int32),) + gathered + (layer_out, grad_input), [smem] + [got(v) for v in gathered] + [moved, moved], mib=40,
    )
    weights.insert(3, got_t[:, :heads].reshape(G * heads, rows).T)

    sums = sums.reshape(G, cores, RIM, lane)
    mine = lax.dynamic_index_in_dim(sums, hi, 1, False)
    o_conv_inner = mine[:, :K, :chan].transpose(1, 0, 2).reshape(K, G * chan)
    o_conv_state = sums[:, :, :K, chan : chan + bcs].transpose(2, 1, 0, 3).reshape(K, 2 * N)
    per = width // (planes * G)
    gains = jnp.sum(sums[:, :, 8:], axis=(0, 1)).reshape(2, width)
    gains = lax.dynamic_slice_in_dim(gains, (zi * G + pi) * per, per, 1)

    return (
        layer_out, grad_input, gains[1], gains[0], *weights, *ffn_out,
        o_conv_inner, o_conv_state,
        mine[:, 5, :heads].reshape(-1), mine[:, 5, 128 : 128 + heads].reshape(-1),
        mine[:, 5, 256 : 256 + heads].reshape(-1), mine[:, 4, :chan].reshape(-1),
    )


def solution(mesh):
    seq, cores = mesh.shape["seq"], mesh.shape["head"]
    planes = Mesh(mesh.devices.reshape(seq // G, G, cores), ("z", "p", "head"))
    s = ("z", "p")
    both, row, head, whole = P(s, "head"), P(s, None), P("head"), P()
    placed = (
        row, P(s), whole, whole, both, both, row, both, both, both, both, both, both, both, both, both,
        P(None, "head"), whole, head, head, head, head, row,
    )
    return jax.shard_map(
        on_device,
        mesh=planes,
        in_specs=placed,
        out_specs=(
            row, row, P(s), P(s), both, both, row, both, both, both, both, both, both, both, both, both,
            P(None, "head"), whole, head, head, head, head,
        ),
        check_vma=False,
    )
```
